32 devices in a mesh: groups: 2 (over y), expert: 4 (over z), dp: 2 (over x), pipe: 2 (over core).
Axes of the slice: x: 2, y: 2, z: 4, core: 2. Of those that a mesh axis runs over, the one named last changes fastest.
Arguments:
- tokens: bfloat16 [256, 4096], P(('groups', 'expert'), ('dp', 'pipe')), parts along dimension 0, may hold values from -6 to 6
- routes: int32 [256, 4], P('groups'), parts along dimension 0, may hold values from 0 to 15, all different within a row; in each aligned block of 32 rows (0 to 31, 32 to 63, ...) at most 16 rows name the same one
- gate_weights: float32 [256, 4], P('groups'), parts along dimension 0, may hold values from 0.1 to 0.6
- teacher_gate: bfloat16 [4096, 14336], P(('dp', 'pipe'), 'expert'), may hold values from -0.09375 to 0.09375
- teacher_up: bfloat16 [4096, 14336], P(('dp', 'pipe'), 'expert'), may hold values from -0.09375 to 0.09375
- teacher_down: bfloat16 [14336, 4096], P('expert', ('dp', 'pipe')), may hold values from -0.046875 to 0.046875
- expert_gate: bfloat16 [4096, 14336], P(('dp', 'pipe'), 'expert'), may hold values from -0.09375 to 0.09375
- expert_up: bfloat16 [4096, 14336], P(('dp', 'pipe'), 'expert'), may hold values from -0.09375 to 0.09375
- expert_down: bfloat16 [14336, 4096], P('expert', ('dp', 'pipe')), may hold values from -0.1875 to 0.1875
Outputs:
- student_out: bfloat16 [256, 4096], P(('groups', 'expert'), ('dp', 'pipe')), parts along dimension 0
- grad_gate: bfloat16 [8192, 14336], P(('groups', 'dp', 'pipe'), 'expert'), parts along dimension 0
- grad_up: bfloat16 [8192, 14336], P(('groups', 'dp', 'pipe'), 'expert'), parts along dimension 0
- grad_down: bfloat16 [28672, 4096], P(('groups', 'expert'), ('dp', 'pipe')), parts along dimension 0
The draws below stay inside these ranges and needn't reach their ends.
There are 2 independent parts, one for each index of `groups`. The reference program is written for one: setup_inputs(seed, part) draws one part's arguments, and reference() takes and returns one part's arrays. A program takes and returns all parts, laid end to end along the dimension named above; an argument that names none is the same for every part. Nothing has to cross between parts.
Inputs may be any that keep to these rules, and one draw needn't show every extreme that they name: `routes`: the 4 experts of a row differ. In each aligned block of 32 rows (the tokens of one index of expert) no expert is named by more than 16 rows, a bound that some block reaches.
All inputs are finite; a program needn't handle non-finite values.
Results may differ from the reference program's by a relative error of at most 0.028.
Values may be sent and summed in bfloat16 or wider, within the bound.
No kernel may reach another device: no remote copies, remote signals or barrier semaphores. Data moves between devices by JAX's collectives and lax.ppermute only.
A program may use at most 192 MiB of HBM per device.

```python
import math
import jax
import jax.numpy as jnp
import numpy as np
from jax import lax

D = 4096
H = 896
EXPERTS = 16
TOP = 4
TOK_DEV = 32
FFT = 14336
TOKENS = 128
CAP = 16
N_DP = 2
N_PIPE = 2


def levels(own_key, extent, split, least, largest):
    loudness = 1.0
    for dim, shards_of in split:
        steps = jax.random.uniform(jax.random.fold_in(jax.random.fold_in(own_key, 6), dim), (shards_of,), jnp.float32, least / len(split), largest / len(split))
        loudness = loudness * jnp.repeat(jnp.exp(steps), extent[dim] // shards_of).reshape((-1,) + (1,) * (len(extent) - 1 - dim))
    return loudness


def deal_out(stream_key, own, number, rows, amount, top, reach, slope):
    sequence = jax.random.permutation(stream_key, amount)
    crowded, ordinary = load_shares(amount, rows * top, reach, slope, True), load_shares(amount, rows * top, reach, slope, False)
    places = jnp.arange(amount)

    def named(lengths, offset_by):
        used = int((lengths > 0).sum())
        fixed = max(1, used // 4)
        passed = fixed + (places - fixed + offset_by * (used - fixed)) % max(1, amount - fixed)
        return jnp.zeros((amount,), jnp.int32).at[sequence[jnp.where(places < fixed, places, passed)]].set(jnp.asarray(lengths, jnp.int32))

    lengths = jnp.where(number % 4 == 0, named(crowded, number // 4), named(ordinary, number - number // 4 - 1))
    mixed = jax.random.permutation(jax.random.fold_in(own, 3), amount)
    giver, taker = mixed[0:amount // 2 * 2:2], mixed[1:amount // 2 * 2:2]
    room = jnp.minimum(lengths[giver] - 1, reach - lengths[taker]) // 2
    room = jnp.where((giver == sequence[0]) | (taker == sequence[0]) | (lengths[taker] == 0), 0, jnp.maximum(room, 0))
    passed = jax.random.randint(jax.random.fold_in(own, 4), (amount // 2,), 0, 1 << 20) % (room + 1)
    lengths = lengths.at[giver].add(-passed).at[taker].add(passed)
    members = jnp.searchsorted(jnp.cumsum(lengths), jnp.arange(rows * top), side="right").astype(jnp.int32)
    grid = members.reshape(top, rows).T
    grid = grid[jax.random.permutation(jax.random.fold_in(own, 1), rows)]
    offset_by = jax.random.randint(jax.random.fold_in(own, 2), (rows, 1), 0, top)
    return jnp.take_along_axis(grid, (jnp.arange(top)[None, :] + offset_by) % top, axis=1)


def load_shares(amount, total, most, skew, full):
    weights = [(1 << 20) // math.isqrt(grade ** skew) + 1 for grade in range(1, amount + 1)]
    largest = most if full else min(most, max(-(-total // amount), total * weights[0] // sum(weights)))
    least = 1 if total - largest >= amount - 1 else 0
    given, rest = [largest] + [least] * (amount - 1), total - largest - least * (amount - 1)
    while rest > 0:
        candidates = [i for i in range(1, amount) if given[i] < largest] or [i for i in range(1, amount) if given[i] < most]
        pool, remaining = sum([weights[i] for i in candidates]), rest
        for i in candidates:
            extra = min(most - given[i], max(1, remaining * weights[i] // pool), rest)
            given[i] = given[i] + extra
            rest = rest - extra
    return np.array(given)


def normal_values(rng, extent, scale, limit, cuts=(), held_as=jnp.bfloat16):
    result = scale * jax.random.normal(rng, extent, jnp.float32)
    if cuts:
        result = result * levels(rng, extent, cuts, -0.22, 0.18)
    return jnp.clip(result, -limit, limit).astype(held_as)


def setup_inputs(seed: int = 0, part: int = 0) -> dict:
    key_of = jax.random.split(jax.random.key(seed), 10)
    own_keys = jax.random.split(jax.random.fold_in(key_of[9], part), 10)
    tokens = normal_values(own_keys[0], (TOKENS, D), 1.0, 6.0, ((0, 4), (1, 4)))
    routes_keys = jax.random.split(jax.random.fold_in(own_keys[1], 1), TOKENS // TOK_DEV)
    routes_turns = jax.random.permutation(jax.random.fold_in(own_keys[1], 3), TOKENS // TOK_DEV)
    routes = jax.vmap(lambda own, number: deal_out(jax.random.fold_in(own_keys[1], 2), own, number, TOK_DEV, EXPERTS, TOP, CAP, 2))(routes_keys, routes_turns).reshape((TOKENS, TOP))
    gate_weights = jnp.clip(jax.random.uniform(own_keys[2], (TOKENS, TOP), jnp.float32, 0.1, 0.6), 0.1, 0.6)
    teacher_gate = normal_values(key_of[3], (D, FFT), D ** -0.5, 0.09375, ((0, 4), (1, 4)))
    teacher_up = normal_values(key_of[4], (D, FFT), D ** -0.5, 0.09375, ((0, 4), (1, 4)))
    teacher_down = normal_values(key_of[5], (FFT, D), FFT ** -0.5, 0.046875, ((0, 4), (1, 4)))
    expert_gate = normal_values(key_of[6], (D, EXPERTS * H), D ** -0.5, 0.09375, ((0, 4), (1, 4)))
    expert_up = normal_values(key_of[7], (D, EXPERTS * H), D ** -0.5, 0.09375, ((0, 4), (1, 4)))
    expert_down = normal_values(key_of[8], (EXPERTS * H, D), H ** -0.5, 0.1875, ((0, 4), (1, 4)))
    return {"tokens": tokens, "routes": routes, "gate_weights": gate_weights, "teacher_gate": teacher_gate, "teacher_up": teacher_up, "teacher_down": teacher_down, "expert_gate": expert_gate, "expert_up": expert_up, "expert_down": expert_down}


def blockwise(operand, weights, pieces):
    width = operand.shape[1] // pieces
    left_blocks = operand.reshape(operand.shape[0], pieces, width).transpose(1, 0, 2)
    right_blocks = weights.reshape(pieces, width, weights.shape[1])

    def accumulate(running, operands):
        partial_sum = jnp.dot(operands[0], operands[1], preferred_element_type=jnp.float32)
        rounded = lax.optimization_barrier(partial_sum.astype(jnp.bfloat16))
        return running + rounded.astype(jnp.float32), None

    initial = jnp.zeros((operand.shape[0], weights.shape[1]), jnp.float32)
    running, unused = lax.scan(accumulate, initial, (left_blocks, right_blocks))
    return running


def reference(tokens, routes, gate_weights, teacher_gate, teacher_up, teacher_down, expert_gate, expert_up, expert_down):
    pieces = N_DP * N_PIPE
    teacher_pre_gate = blockwise(tokens, teacher_gate, pieces)
    teacher_pre_up = blockwise(tokens, teacher_up, pieces)
    teacher_hidden = (jax.nn.silu(teacher_pre_gate) * teacher_pre_up).astype(jnp.bfloat16)
    target = jnp.dot(teacher_hidden, teacher_down, preferred_element_type=jnp.float32)
    gate_stack = expert_gate.reshape(D, EXPERTS, H).transpose(1, 0, 2)
    up_stack = expert_up.reshape(D, EXPERTS, H).transpose(1, 0, 2)
    down_stack = expert_down.reshape(EXPERTS, H, D)
    expert_ids = jnp.arange(EXPERTS, dtype=jnp.int32)
    matched = routes[:, :, None] == expert_ids[None, None, :]
    route_weight = jnp.sum(jnp.where(matched, gate_weights[:, :, None], jnp.zeros((), jnp.float32)), axis=1)
    route_stack = route_weight.T

    def expert_forward(gate_w, up_w, down_w):
        pre_gate = blockwise(tokens, gate_w, pieces)
        pre_up = blockwise(tokens, up_w, pieces)
        hidden = (jax.nn.silu(pre_gate) * pre_up).astype(jnp.bfloat16)
        output = jnp.dot(hidden, down_w, preferred_element_type=jnp.float32)
        return pre_gate, pre_up, hidden, output

    def forward_step(running, operands):
        gate_w, up_w, down_w, weight_col = operands
        outputs = expert_forward(gate_w, up_w, down_w)
        return running + weight_col[:, None] * outputs[3], None

    student_sum, unused = lax.scan(forward_step, jnp.zeros((TOKENS, D), jnp.float32), (gate_stack, up_stack, down_stack, route_stack))
    student_out = student_sum.astype(jnp.bfloat16)
    residual = (student_sum - target).astype(jnp.bfloat16)

    def backward_step(carry, operands):
        gate_w, up_w, down_w, weight_col = operands
        pre_gate, pre_up, hidden, output = expert_forward(gate_w, up_w, down_w)
        output_grad = (weight_col[:, None] * residual.astype(jnp.float32)).astype(jnp.bfloat16)
        hidden_grad = blockwise(output_grad, down_w.T, pieces)
        sigmoid_gate = jax.nn.sigmoid(pre_gate)
        gate_grad = (hidden_grad * pre_up * sigmoid_gate * (1.0 + pre_gate * (1.0 - sigmoid_gate))).astype(jnp.bfloat16)
        up_grad = (hidden_grad * pre_gate * sigmoid_gate).astype(jnp.bfloat16)
        down_grad = jnp.dot(hidden.T, output_grad, preferred_element_type=jnp.float32).astype(jnp.bfloat16)
        gate_grad_w = jnp.dot(tokens.T, gate_grad, preferred_element_type=jnp.float32).astype(jnp.bfloat16)
        up_grad_w = jnp.dot(tokens.T, up_grad, preferred_element_type=jnp.float32).astype(jnp.bfloat16)
        return carry, (gate_grad_w, up_grad_w, down_grad)

    unused_carry, grads = lax.scan(backward_step, jnp.zeros((), jnp.float32), (gate_stack, up_stack, down_stack, route_stack))
    grad_gate = grads[0].transpose(1, 0, 2).reshape(D, EXPERTS * H)
    grad_up = grads[1].transpose(1, 0, 2).reshape(D, EXPERTS * H)
    grad_down = grads[2].reshape(EXPERTS * H, D)
    return student_out, grad_gate, grad_up, grad_down
```

```python
import functools

import jax
import jax.numpy as jnp
from jax import lax
from jax.experimental import pallas as pl
from jax.experimental.pallas import tpu as pltpu
from jax.sharding import PartitionSpec as P

H = 896
BF = jnp.bfloat16
F32 = jnp.float32
VMEM_BYTES = 48 * 1024 * 1024


def shift(value, axis, count, by):
    return lax.ppermute(value, axis, [(i, (i + by) % count) for i in range(count)])


def call(kernel, grid, in_specs, out_specs, out_shape, flops, moved):
    return pl.pallas_call(
        kernel,
        grid=grid,
        in_specs=in_specs,
        out_specs=out_specs,
        out_shape=out_shape,
        compiler_params=pltpu.CompilerParams(vmem_limit_bytes=VMEM_BYTES),
        cost_estimate=pl.CostEstimate(flops=flops, bytes_accessed=moved, transcendentals=0),
    )


def dot(a, b, contract_a=1, contract_b=0):
    return lax.dot_general(
        a, b, (((contract_a,), (contract_b,)), ((), ())), preferred_element_type=F32
    )


def expert_pre_kernel(picker, tokens, gate, up, keep, send):
    half = keep.shape[2]
    rows = dot(picker[0], tokens[...]).astype(BF)
    for which, weight in enumerate((gate, up)):
        product = dot(rows, weight[...]).astype(BF)
        keep[0, which] = product[:half]
        send[0, which] = product[half:]


def expert_pre(picker, tokens, gate, up, first, count):
    slots, token_count = picker.shape[1:]
    width = tokens.shape[1]
    halves = jax.ShapeDtypeStruct((count, 2, slots // 2, H), BF)
    half_spec = pl.BlockSpec((1, 2, slots // 2, H), lambda i: (i, 0, 0, 0))
    weight_spec = pl.BlockSpec((width, H), lambda i: (0, first + i))
    return call(
        expert_pre_kernel,
        (count,),
        [
            pl.BlockSpec((1, slots, token_count), lambda i: (first + i, 0, 0)),
            pl.BlockSpec((token_count, width), lambda i: (0, 0)),
            weight_spec,
            weight_spec,
        ],
        (half_spec, half_spec),
        (halves, halves),
        count * 4 * slots * width * H,
        count * 4 * width * H,
    )(picker, tokens, gate, up)


def student_kernel(picker, hidden, weight, out, total):
    step = pl.program_id(0)
    dense = dot(picker[0], hidden[0], 0, 0).astype(BF)
    product = dot(dense, weight[...])

    @pl.when(step == 0)
    def _():
        total[...] = product

    @pl.when(step > 0)
    def _():
        total[...] += product

    @pl.when(step == pl.num_programs(0) - 1)
    def _():
        out[...] = total[...].astype(BF)


def student_product(picker, hidden, down):
    count, slots, token_count = picker.shape
    width = down.shape[1]
    return pl.pallas_call(
        student_kernel,
        grid=(count,),
        in_specs=[
            pl.BlockSpec((1, slots, token_count), lambda i: (i, 0, 0)),
            pl.BlockSpec((1, slots, H), lambda i: (i, 0, 0)),
            pl.BlockSpec((H, width), lambda i: (i, 0)),
        ],
        out_specs=pl.BlockSpec((token_count, width), lambda i: (0, 0)),
        out_shape=jax.ShapeDtypeStruct((token_count, width), BF),
        scratch_shapes=[pltpu.VMEM((token_count, width), F32)],
        compiler_params=pltpu.CompilerParams(vmem_limit_bytes=VMEM_BYTES),
        cost_estimate=pl.CostEstimate(
            flops=count * 2 * token_count * width * H,
            bytes_accessed=count * 2 * width * H,
            transcendentals=0,
        ),
    )(picker, hidden, down)


def hidden_grad_kernel(picker, residual, weight, keep, send):
    half = keep.shape[1]
    rows = dot(picker[0], residual[...]).astype(BF)
    product = dot(rows, weight[...], 1, 1).astype(BF)
    keep[0] = product[:half]
    send[0] = product[half:]


def hidden_grad_parts(picker, residual, down):
    count, slots, token_count = picker.shape
    width = down.shape[1]
    halves = jax.ShapeDtypeStruct((count, slots // 2, H), BF)
    half_spec = pl.BlockSpec((1, slots // 2, H), lambda i: (i, 0, 0))
    return call(
        hidden_grad_kernel,
        (count,),
        [
            pl.BlockSpec((1, slots, token_count), lambda i: (i, 0, 0)),
            pl.BlockSpec((token_count, width), lambda i: (0, 0)),
            pl.BlockSpec((H, width), lambda i: (i, 0)),
        ],
        (half_spec, half_spec),
        (halves, halves),
        count * 2 * slots * width * H,
        count * 2 * width * H,
    )(picker, residual, down)


def down_grad_kernel(picker, residual, hidden, out):
    rows = dot(picker[0], residual[...]).astype(BF)
    out[...] = dot(hidden[0], rows, 0, 0).astype(BF)


def down_grad(picker, residual, hidden):
    count, slots, token_count = picker.shape
    width = residual.shape[1]
    return call(
        down_grad_kernel,
        (count,),
        [
            pl.BlockSpec((1, slots, token_count), lambda i: (i, 0, 0)),
            pl.BlockSpec((token_count, width), lambda i: (0, 0)),
            pl.BlockSpec((1, slots, H), lambda i: (i, 0, 0)),
        ],
        pl.BlockSpec((H, width), lambda i: (i, 0)),
        jax.ShapeDtypeStruct((count * H, width), BF),
        count * 2 * slots * width * H,
        count * 2 * width * H,
    )(picker, residual, hidden)


def input_grad_kernel(picker, tokens, gate_grad, up_grad, out_gate, out_up):
    rows = dot(picker[0], tokens[...]).astype(BF)
    out_gate[...] = dot(rows, gate_grad[0], 0, 0).astype(BF)
    out_up[...] = dot(rows, up_grad[0], 0, 0).astype(BF)


def input_grads(picker, tokens, gate_grad, up_grad):
    count, slots, token_count = picker.shape
    width = tokens.shape[1]
    grad_spec = pl.BlockSpec((1, slots, H), lambda i: (i, 0, 0))
    out_spec = pl.BlockSpec((width, H), lambda i: (0, i))
    out = jax.ShapeDtypeStruct((width, count * H), BF)
    return call(
        input_grad_kernel,
        (count,),
        [
            pl.BlockSpec((1, slots, token_count), lambda i: (i, 0, 0)),
            pl.BlockSpec((token_count, width), lambda i: (0, 0)),
            grad_spec,
            grad_spec,
        ],
        (out_spec, out_spec),
        (out, out),
        count * 4 * slots * width * H,
        count * 4 * width * H,
    )(picker, tokens, gate_grad, up_grad)


def add(a, b):
    return (a.astype(F32) + b.astype(F32)).astype(BF)


def split_rows(value, count):
    rows = value.shape[-2] // count
    return [value[..., i * rows : (i + 1) * rows, :] for i in range(count)]


def scatter_dp(value, count):
    pieces = split_rows(value, count)
    total = pieces[0].astype(F32)
    for s in range(1, count):
        total = total + shift(pieces[s], "dp", count, s).astype(F32)
    return total


def gather_dp(value, count):
    return jnp.concatenate(
        [value] + [shift(value, "dp", count, -s) for s in range(1, count)], axis=-2
    )


def reduce_dp(value, count):
    if count == 2:
        other = shift(value, "dp", count, 1)
        first, second = split_rows(other, 2)
        return value.astype(F32) + jnp.concatenate([second, first], axis=-2).astype(F32)
    return gather_dp(scatter_dp(value, count).astype(BF), count).astype(F32)


def body(
    tokens,
    routes,
    gate_weights,
    teacher_gate,
    teacher_up,
    teacher_down,
    expert_gate,
    expert_up,
    expert_down,
):
    ranks = lax.axis_size("expert")
    dps = lax.axis_size("dp")
    pipes = lax.axis_size("pipe")
    rank = lax.axis_index("expert")
    dp = lax.axis_index("dp")
    pipe = lax.axis_index("pipe")
    block, width = tokens.shape
    token_count = block * ranks
    capacity = block // 2
    slots = capacity * ranks
    experts = expert_gate.shape[1] // H
    per_piece = ranks // (pipes * dps)

    base = jnp.concatenate(
        [tokens] + [shift(tokens, "expert", ranks, -s) for s in range(1, ranks)], axis=0
    )

    def own_order(table):
        twice = jnp.concatenate([table, table], axis=0)
        return lax.dynamic_slice_in_dim(twice, rank * block, token_count, axis=0)

    names = own_order(routes).T
    shares = own_order(gate_weights).T
    ids = rank * experts + jnp.arange(experts, dtype=jnp.int32)
    matched = names[None, :, :] == ids[:, None, None]
    routed = jnp.any(matched, axis=1)
    weight = jnp.sum(jnp.where(matched, shares[None, :, :], 0.0), axis=1)
    at = jnp.arange(token_count, dtype=jnp.int32)
    earlier = ((at[:, None] // block == at[None, :] // block) & (at[:, None] < at[None, :])).astype(BF)
    within = jnp.dot(routed.astype(BF), earlier, preferred_element_type=F32).astype(jnp.int32)
    at_block = at // block
    at_pipe = at_block // (dps * per_piece)
    at_dp = at_block // per_piece % dps
    place = ((at_pipe + pipes - pipe) % pipes * dps + (at_dp + dps - dp) % dps) * per_piece
    place = (place + at_block % per_piece) * capacity
    slot_of = jnp.where(routed, within + place[None, :], -1)
    picked = slot_of[:, None, :] == jnp.arange(slots, dtype=jnp.int32)[None, :, None]
    picker = picked.astype(BF)
    slot_weight = jnp.sum(jnp.where(picked, weight[:, None, :], 0.0), axis=2)[:, :, None]

    pieces = base.reshape(pipes, dps, per_piece * block, width)
    pieces = jnp.concatenate([pieces, pieces], axis=0)
    pieces = lax.dynamic_slice_in_dim(pieces, pipe, pipes, axis=0)
    pieces = jnp.concatenate([pieces, pieces], axis=1)
    ordered = lax.dynamic_slice_in_dim(pieces, dp, dps, axis=1).reshape(token_count, width)

    def teacher_part(first, size):
        sums = []
        for table in (teacher_gate, teacher_up):
            product = jnp.dot(
                ordered, table[:, first : first + size], preferred_element_type=F32
            ).astype(BF)
            keep, send = split_rows(product, 2)
            half = add(keep, shift(send, "pipe", pipes, 1))
            sums.append(scatter_dp(half, dps))
        hidden = (jax.nn.silu(sums[0]) * sums[1]).astype(BF)
        hidden = gather_dp(hidden, dps)
        other = shift(hidden, "pipe", pipes, 1)
        return jnp.concatenate([hidden, other], axis=0)

    chunks = 2 if teacher_gate.shape[1] % 256 == 0 else 1
    size = teacher_gate.shape[1] // chunks
    hidden = jnp.concatenate([teacher_part(i * size, size) for i in range(chunks)], axis=1)
    hidden = hidden.reshape(pipes, dps, per_piece * block, hidden.shape[1])
    hidden = jnp.concatenate([hidden, hidden], axis=1)
    hidden = lax.dynamic_slice_in_dim(hidden, (dps - dp) % dps, dps, axis=1)
    hidden = jnp.concatenate([hidden, hidden], axis=0)
    hidden = lax.dynamic_slice_in_dim(hidden, (pipes - pipe) % pipes, pipes, axis=0)
    hidden = hidden.reshape(token_count, -1)

    def to_owners(product):
        blocks = split_rows(product, ranks)
        total = blocks[0].astype(F32)
        for s in range(1, ranks):
            total = total + shift(blocks[s], "expert", ranks, s).astype(F32)
        return total

    target = to_owners(jnp.dot(hidden, teacher_down, preferred_element_type=F32).astype(BF))

    group = 2 if experts % 2 == 0 else 1
    pre_gate, pre_up, weighted = [], [], []
    for first in range(0, experts, group):
        keep, send = expert_pre(picker, base, expert_gate, expert_up, first, group)
        half = add(keep, shift(send, "pipe", pipes, 1))
        total = reduce_dp(half, dps)
        mine = slot_weight[first : first + group, : slots // 2]
        part = (jax.nn.silu(total[:, 0]) * total[:, 1] * mine).astype(BF)
        pre_gate.append(total[:, 0])
        pre_up.append(total[:, 1])
        weighted.append(jnp.concatenate([part, shift(part, "pipe", pipes, 1)], axis=1))
    pre_gate = jnp.concatenate(pre_gate, axis=0)
    pre_up = jnp.concatenate(pre_up, axis=0)
    weighted = jnp.concatenate(weighted, axis=0)

    student_sum = to_owners(student_product(picker, weighted, expert_down))
    residual = (student_sum - target).astype(BF)
    residuals = jnp.concatenate(
        [residual] + [shift(residual, "expert", ranks, -s) for s in range(1, ranks)], axis=0
    )

    keep, send = hidden_grad_parts(picker, residuals, expert_down)
    half = add(keep, shift(send, "pipe", pipes, 1))
    hidden_grad = reduce_dp(half, dps) * slot_weight[:, : slots // 2]
    sig = jax.nn.sigmoid(pre_gate)
    gate_grad = (hidden_grad * pre_up * sig * (1.0 + pre_gate * (1.0 - sig))).astype(BF)
    up_grad = (hidden_grad * pre_gate * sig).astype(BF)
    gate_grad = jnp.concatenate([gate_grad, shift(gate_grad, "pipe", pipes, 1)], axis=1)
    up_grad = jnp.concatenate([up_grad, shift(up_grad, "pipe", pipes, 1)], axis=1)

    grad_down = down_grad(picker, residuals, weighted)
    grad_gate, grad_up = input_grads(picker, base, gate_grad, up_grad)
    return (student_sum.astype(BF), grad_gate, grad_up, grad_down)


def solution(mesh):
    placed = (
        P(("groups", "expert"), ("dp", "pipe")),
        P("groups", None),
        P("groups", None),
        P(("dp", "pipe"), "expert"),
        P(("dp", "pipe"), "expert"),
        P("expert", ("dp", "pipe")),
        P(("dp", "pipe"), "expert"),
        P(("dp", "pipe"), "expert"),
        P("expert", ("dp", "pipe")),
    )
    return jax.shard_map(
        body,
        mesh=mesh,
        in_specs=placed,
        out_specs=(
            P(("groups", "expert"), ("dp", "pipe")),
            P(("groups", "dp", "pipe"), "expert"),
            P(("groups", "dp", "pipe"), "expert"),
            P(("groups", "expert"), ("dp", "pipe")),
        ),
        check_vma=False,
    )
```

```python
import functools

import jax
import jax.numpy as jnp
from jax import lax
from jax.experimental import pallas as pl
from jax.experimental.pallas import tpu as pltpu
from jax.sharding import PartitionSpec as P

H = 896
BF = jnp.bfloat16
F32 = jnp.float32


def shift(value, axis, count, by):
    return lax.ppermute(value, axis, [(i, (i + by) % count) for i in range(count)])


def dot(a, b, contract_a=1, contract_b=0):
    return lax.dot_general(
        a, b, (((contract_a,), (contract_b,)), ((), ())), preferred_element_type=F32
    )


def whole():
    return pl.BlockSpec(memory_space=pltpu.VMEM)


def in_hbm():
    return pl.BlockSpec(memory_space=pltpu.HBM)


def anywhere():
    return pl.BlockSpec(memory_space=pl.ANY)


def scalars():
    return pl.BlockSpec(memory_space=pltpu.SMEM)


def prepare_kernel(
    ranks, capacity, dps, pipes, place, routes, shares, gate, up, picker, weights, gate_out, up_out, sems
):
    pieces = 8
    rows = gate.shape[0] // pieces
    copies = []
    for which, (source, target) in enumerate(((gate, gate_out), (up, up_out))):
        for i in range(pieces):
            part = pl.ds(i * rows, rows)
            copies.append(
                pltpu.make_async_copy(source.at[part], target.at[part], sems.at[which, i])
            )
    for copy in copies:
        copy.start()
    rank, dp, pipe = place[0], place[1], place[2]
    experts, slots, token_count = picker.shape
    block = token_count // ranks
    per_piece = ranks // (dps * pipes)
    lane = lax.broadcasted_iota(jnp.int32, (token_count, 128), 1)
    names = lane + rank * experts
    weight = jnp.zeros((token_count, 128), F32)
    routed = jnp.zeros((token_count, 128), F32)
    for k in range(routes.shape[1]):
        hit = (routes[:, k : k + 1] == names) & (lane < experts)
        weight = weight + jnp.where(hit, shares[:, k : k + 1], 0.0)
        routed = routed + jnp.where(hit, 1.0, 0.0)
    weight = weight.T
    t_from = lax.broadcasted_iota(jnp.int32, (token_count, token_count), 0)
    t_to = lax.broadcasted_iota(jnp.int32, (token_count, token_count), 1)
    earlier = jnp.where((t_from // block == t_to // block) & (t_from < t_to), 1.0, 0.0)
    routed = routed.T
    within = dot(routed.astype(BF), earlier.astype(BF)).astype(jnp.int32)
    at_block = lax.broadcasted_iota(jnp.int32, (1, token_count), 1) // block
    at_pipe = lax.rem(at_block // (dps * per_piece) + pipes - pipe, pipes)
    at_dp = lax.rem(lax.rem(at_block // per_piece, dps) + dps - dp, dps)
    first = ((at_pipe * dps + at_dp) * per_piece + lax.rem(at_block, per_piece)) * capacity
    slot = jnp.where(routed > 0.0, within + first, -1)
    ids = lax.broadcasted_iota(jnp.int32, (slots, token_count), 0)
    for e in range(experts):
        hit = slot[e : e + 1] == ids
        picker[e] = jnp.where(hit, 1.0, 0.0).astype(BF)
        weights[e] = jnp.sum(jnp.where(hit, weight[e : e + 1], 0.0), axis=1, keepdims=True)
    for copy in copies:
        copy.wait()


def prepare(place, routes, shares, gate, up, ranks, dps, pipes, block, experts):
    capacity = block // 2
    token_count = block * ranks
    slots = capacity * ranks
    return pl.pallas_call(
        functools.partial(prepare_kernel, ranks, capacity, dps, pipes),
        in_specs=[scalars(), whole(), whole(), in_hbm(), in_hbm()],
        out_specs=(whole(), whole(), whole(), whole()),
        out_shape=(
            jax.ShapeDtypeStruct((experts, slots, token_count), BF),
            jax.ShapeDtypeStruct((experts, slots, 1), F32),
            pltpu.VMEM(gate.shape, BF),
            pltpu.VMEM(up.shape, BF),
        ),
        scratch_shapes=[pltpu.SemaphoreType.DMA((2, 8))],
        compiler_params=pltpu.CompilerParams(vmem_limit_bytes=8 * 1024 * 1024),
        cost_estimate=pl.CostEstimate(
            flops=0, bytes_accessed=4 * gate.size, transcendentals=0
        ),
    )(place, routes, shares, gate, up)


def tile_of(size):
    return 256 if size % 256 == 0 else 128


def teacher_kernel(first, size, dps, pipes, place, tokens, gate, up, keep, send):
    dp, pipe = place[1], place[2]
    rows = tokens.shape[0] // (dps * pipes)
    half = dps * rows
    parts = []
    for j1 in range(pipes):
        for j0 in range(dps):
            piece = lax.rem(pipe + j1, pipes) * dps + lax.rem(dp + j0, dps)
            parts.append(tokens[pl.ds(pl.multiple_of(piece * rows, rows), rows), :])
    ordered = jnp.concatenate(parts, axis=0)
    tile = tile_of(size)
    for which, weight in enumerate((gate, up)):
        for i in range(size // tile):
            product = dot(ordered, weight[:, first + i * tile : first + (i + 1) * tile]).astype(BF)
            keep[which, :, i * tile : (i + 1) * tile] = product[:half]
            send[which, :, i * tile : (i + 1) * tile] = product[half:]


def teacher_pre(place, tokens, gate, up, first, size, dps, pipes):
    token_count, width = tokens.shape
    half = jax.ShapeDtypeStruct((2, token_count // pipes, size), BF)
    return pl.pallas_call(
        functools.partial(teacher_kernel, first, size, dps, pipes),
        in_specs=[scalars(), whole(), whole(), whole()],
        out_specs=(whole(), whole()),
        out_shape=(half, half),
        compiler_params=pltpu.CompilerParams(vmem_limit_bytes=8 * 1024 * 1024),
        cost_estimate=pl.CostEstimate(
            flops=4 * token_count * width * size, bytes_accessed=4 * width * size, transcendentals=0
        ),
    )(place, tokens, gate, up)


def expert_kernel(first, picker, tokens, gate, up, before, keep, send):
    half = keep.shape[2]
    for i in range(keep.shape[0]):
        e = first + i
        rows = dot(picker[e], tokens[...]).astype(BF)
        for which, weight in enumerate((gate, up)):
            product = dot(rows, weight[:, e * H : (e + 1) * H]).astype(BF)
            keep[i, which] = product[:half]
            send[i, which] = product[half:]


def expert_pre(picker, tokens, gate, up, before, first, count):
    slots = picker.shape[1]
    width = tokens.shape[1]
    halves = jax.ShapeDtypeStruct((count, 2, slots // 2, H), BF)
    return pl.pallas_call(
        functools.partial(expert_kernel, first),
        in_specs=[whole(), whole(), whole(), whole(), anywhere()],
        out_specs=(whole(), whole()),
        out_shape=(halves, halves),
        compiler_params=pltpu.CompilerParams(vmem_limit_bytes=8 * 1024 * 1024),
        cost_estimate=pl.CostEstimate(
            flops=count * 4 * slots * width * H,
            bytes_accessed=count * 4 * width * H,
            transcendentals=0,
        ),
    )(picker, tokens, gate, up, before)


def spread_kernel(picker, hidden, out):
    for e in range(picker.shape[0]):
        out[:, e * H : (e + 1) * H] = dot(picker[e], hidden[e], 0, 0).astype(BF)


def spread(picker, hidden):
    count, slots, token_count = picker.shape
    return pl.pallas_call(
        spread_kernel,
        in_specs=[whole(), whole()],
        out_specs=whole(),
        out_shape=jax.ShapeDtypeStruct((token_count, count * H), BF),
        compiler_params=pltpu.CompilerParams(vmem_limit_bytes=8 * 1024 * 1024),
    )(picker, hidden)


def pick_kernel(first, picker, dense, keep, send):
    half = keep.shape[1]
    for i in range(keep.shape[0]):
        e = first + i
        rows = dot(picker[e], dense[:, e * H : (e + 1) * H]).astype(BF)
        keep[i] = rows[:half]
        send[i] = rows[half:]


def pick(picker, dense, first, count):
    slots = picker.shape[1]
    halves = jax.ShapeDtypeStruct((count, slots // 2, H), BF)
    return pl.pallas_call(
        functools.partial(pick_kernel, first),
        in_specs=[whole(), whole()],
        out_specs=(whole(), whole()),
        out_shape=(halves, halves),
        compiler_params=pltpu.CompilerParams(vmem_limit_bytes=8 * 1024 * 1024),
    )(picker, dense)


def hidden_grad_act_kernel(first, swap, mine, other, pre, weight, before, out):
    count, rows = mine.shape[:2]
    for i in range(count):
        total = mine[i].astype(F32)
        if swap:
            flipped = jnp.concatenate([other[i, rows // 2 :], other[i, : rows // 2]], axis=0)
            total = total + flipped.astype(F32)
        total = total * weight[first + i, :rows]
        pre_gate, pre_up = pre[i, 0], pre[i, 1]
        sig = jax.nn.sigmoid(pre_gate)
        gate_grad = total * pre_up * sig * (1.0 + pre_gate * (1.0 - sig))
        up_grad = total * pre_gate * sig
        out[i, 0] = gate_grad.astype(BF)
        out[i, 1] = up_grad.astype(BF)


def hidden_grad_act(mine, other, swap, pre, weight, before, first):
    count, rows, width = mine.shape
    return pl.pallas_call(
        functools.partial(hidden_grad_act_kernel, first, swap),
        in_specs=[whole(), whole(), whole(), whole(), anywhere()],
        out_specs=whole(),
        out_shape=jax.ShapeDtypeStruct((count, 2, rows, width), BF),
        compiler_params=pltpu.CompilerParams(vmem_limit_bytes=8 * 1024 * 1024),
    )(mine, other, pre, weight, before)


def down_grad_kernel(picker, residual, hidden, before, out):
    rows = dot(picker[0], residual[...]).astype(BF)
    out[...] = dot(hidden[0], rows, 0, 0).astype(BF)


def down_grad(picker, residual, hidden, before):
    count, slots, token_count = picker.shape
    width = residual.shape[1]
    split = 2 if width % 256 == 0 else 1
    part = width // split
    return pl.pallas_call(
        down_grad_kernel,
        grid=(count, split),
        in_specs=[
            pl.BlockSpec((1, slots, token_count), lambda i, j: (i, 0, 0)),
            pl.BlockSpec((token_count, part), lambda i, j: (0, j)),
            pl.BlockSpec((1, slots, H), lambda i, j: (i, 0, 0)),
            anywhere(),
        ],
        out_specs=pl.BlockSpec((H, part), lambda i, j: (i, j)),
        out_shape=jax.ShapeDtypeStruct((count * H, width), BF),
        compiler_params=pltpu.CompilerParams(vmem_limit_bytes=16 * 1024 * 1024),
        cost_estimate=pl.CostEstimate(
            flops=count * 2 * slots * width * H,
            bytes_accessed=count * 2 * width * H,
            transcendentals=0,
        ),
    )(picker, residual, hidden, before)


def input_grad_kernel(picker, tokens, mine, theirs, *rest):
    out_gate, out_up = rest[-2:]
    rows = dot(picker[0], tokens[...]).astype(BF)
    for which, out in enumerate((out_gate, out_up)):
        grad = jnp.concatenate([mine[0, which], theirs[0, which]], axis=0)
        out[...] = dot(rows, grad, 0, 0).astype(BF)


def input_grads(picker, tokens, mine, theirs, first, so_far):
    experts, slots, token_count = picker.shape
    width = tokens.shape[1]
    count = mine.shape[0]
    split = 2 if width % 256 == 0 else 1
    part = width // split
    grad_spec = pl.BlockSpec((1, 2, slots // 2, H), lambda i, j: (i, 0, 0, 0))
    out_spec = pl.BlockSpec((part, H), lambda i, j: (j, first + i))
    out = jax.ShapeDtypeStruct((width, experts * H), BF)
    extra = () if so_far is None else so_far
    return pl.pallas_call(
        input_grad_kernel,
        grid=(count, split),
        in_specs=[
            pl.BlockSpec((1, slots, token_count), lambda i, j: (first + i, 0, 0)),
            pl.BlockSpec((token_count, part), lambda i, j: (0, j)),
            grad_spec,
            grad_spec,
        ]
        + [in_hbm()] * len(extra),
        out_specs=(out_spec, out_spec),
        out_shape=(out, out),
        input_output_aliases={4 + i: i for i in range(len(extra))},
        compiler_params=pltpu.CompilerParams(vmem_limit_bytes=16 * 1024 * 1024),
        cost_estimate=pl.CostEstimate(
            flops=count * 4 * slots * width * H,
            bytes_accessed=count * 4 * width * H,
            transcendentals=0,
        ),
    )(picker, tokens, mine, theirs, *extra)


def add(a, b):
    return (a.astype(F32) + b.astype(F32)).astype(BF)


def split_rows(value, count):
    rows = value.shape[-2] // count
    return [value[..., i * rows : (i + 1) * rows, :] for i in range(count)]


def scatter_dp(value, count):
    pieces = split_rows(value, count)
    total = pieces[0].astype(F32)
    for s in range(1, count):
        total = total + shift(pieces[s], "dp", count, s).astype(F32)
    return total


def gather_dp(value, count):
    return jnp.concatenate(
        [value] + [shift(value, "dp", count, -s) for s in range(1, count)], axis=-2
    )


def reduce_dp(value, count):
    if count == 2:
        first, second = split_rows(shift(value, "dp", count, 1), 2)
        return value.astype(F32) + jnp.concatenate([second, first], axis=-2).astype(F32)
    return gather_dp(scatter_dp(value, count).astype(BF), count).astype(F32)


def body(
    tokens,
    routes,
    gate_weights,
    teacher_gate,
    teacher_up,
    teacher_down,
    expert_gate,
    expert_up,
    expert_down,
):
    ranks = lax.axis_size("expert")
    dps = lax.axis_size("dp")
    pipes = lax.axis_size("pipe")
    rank = lax.axis_index("expert")
    dp = lax.axis_index("dp")
    pipe = lax.axis_index("pipe")
    block, width = tokens.shape
    token_count = block * ranks
    experts = expert_gate.shape[1] // H
    slots = block // 2 * ranks
    place = jnp.stack([rank, dp, pipe]).astype(jnp.int32)

    def gather_tokens(mine):
        whole_rows = jnp.zeros((token_count, mine.shape[1]), BF)
        whole_rows = lax.dynamic_update_slice(whole_rows, mine, (rank * block, 0))
        for s in range(1, ranks):
            theirs = shift(mine, "expert", ranks, -s)
            at = (rank + s) % ranks * block
            whole_rows = lax.dynamic_update_slice(whole_rows, theirs, (at, 0))
        return whole_rows

    def to_owners(product):
        def block_of(s):
            return lax.dynamic_slice_in_dim(product, (rank + s) % ranks * block, block, axis=0)

        total = block_of(0).astype(F32)
        for s in range(1, ranks):
            total = total + shift(block_of(s), "expert", ranks, s).astype(F32)
        return total

    base = gather_tokens(tokens)
    picker, slot_weight, gate_near, up_near = prepare(
        place, routes, gate_weights, teacher_gate, teacher_up, ranks, dps, pipes, block, experts
    )

    chunks = 2 if teacher_gate.shape[1] % 512 == 0 else 1
    size = teacher_gate.shape[1] // chunks
    halves = []
    for i in range(chunks):
        keep, send = teacher_pre(place, base, gate_near, up_near, i * size, size, dps, pipes)
        halves.append(add(keep, shift(send, "pipe", pipes, 1)))

    group = 2 if experts % 2 == 0 else 1
    firsts = range(0, experts, group)
    expert_halves = []
    for first in firsts:
        keep, send = expert_pre(picker, base, expert_gate, expert_up, halves[0], first, group)
        expert_halves.append(add(keep, shift(send, "pipe", pipes, 1)))

    hiddens = []
    for half in halves:
        total = scatter_dp(half, dps)
        hidden = gather_dp((jax.nn.silu(total[0]) * total[1]).astype(BF), dps)
        hiddens.append(jnp.concatenate([hidden, shift(hidden, "pipe", pipes, 1)], axis=0))
    hidden = jnp.concatenate(hiddens, axis=1)
    hidden = hidden.reshape(pipes, dps, token_count // (pipes * dps), hidden.shape[1])
    hidden = jnp.concatenate([hidden, hidden], axis=1)
    hidden = lax.dynamic_slice_in_dim(hidden, (dps - dp) % dps, dps, axis=1)
    hidden = jnp.concatenate([hidden, hidden], axis=0)
    hidden = lax.dynamic_slice_in_dim(hidden, (pipes - pipe) % pipes, pipes, axis=0)
    hidden = hidden.reshape(token_count, -1)
    target = to_owners(jnp.dot(hidden, teacher_down, preferred_element_type=F32).astype(BF))

    pre, weighted = [], []
    for first, half in zip(firsts, expert_halves):
        total = reduce_dp(half, dps)
        mine = slot_weight[first : first + group, : slots // 2]
        part = (jax.nn.silu(total[:, 0]) * total[:, 1] * mine).astype(BF)
        pre.append(total)
        weighted.append(jnp.concatenate([part, shift(part, "pipe", pipes, 1)], axis=1))
    weighted = jnp.concatenate(weighted, axis=0)

    dense = spread(picker, weighted)
    student_sum = to_owners(jnp.dot(dense, expert_down, preferred_element_type=F32).astype(BF))
    residual = gather_tokens((student_sum - target).astype(BF))

    dense_grad = lax.dot_general(
        residual, expert_down, (((1,), (1,)), ((), ())), preferred_element_type=F32
    ).astype(BF)
    sums = []
    for first in firsts:
        keep, send = pick(picker, dense_grad, first, group)
        sums.append(add(keep, shift(send, "pipe", pipes, 1)))
    others = []
    if dps == 2:
        others = [shift(value, "dp", dps, 1) for value in sums]
    else:
        sums = [gather_dp(scatter_dp(value, dps).astype(BF), dps) for value in sums]
        others = sums
    grad_down = down_grad(picker, residual, weighted, sums[0])
    grads = None
    for i, first in enumerate(firsts):
        mine = hidden_grad_act(
            sums[i], others[i], dps == 2, pre[i], slot_weight, grad_down, first
        )
        grads = input_grads(picker, base, mine, shift(mine, "pipe", pipes, 1), first, grads)
    return (student_sum.astype(BF), grads[0], grads[1], grad_down)


def solution(mesh):
    placed = (
        P(("groups", "expert"), ("dp", "pipe")),
        P("groups", None),
        P("groups", None),
        P(("dp", "pipe"), "expert"),
        P(("dp", "pipe"), "expert"),
        P("expert", ("dp", "pipe")),
        P(("dp", "pipe"), "expert"),
        P(("dp", "pipe"), "expert"),
        P("expert", ("dp", "pipe")),
    )
    return jax.shard_map(
        body,
        mesh=mesh,
        in_specs=placed,
        out_specs=(
            P(("groups", "expert"), ("dp", "pipe")),
            P(("groups", "dp", "pipe"), "expert"),
            P(("groups", "dp", "pipe"), "expert"),
            P(("groups", "expert"), ("dp", "pipe")),
        ),
        check_vma=False,
    )
```

```python
import functools

import jax
import jax.numpy as jnp
from jax import lax
from jax.experimental import pallas as pl
from jax.experimental.pallas import tpu as pltpu
from jax.sharding import PartitionSpec as P

H = 896
BF = jnp.bfloat16
F32 = jnp.float32


def shift(value, axis, count, by):
    return lax.ppermute(value, axis, [(i, (i + by) % count) for i in range(count)])


def dot(a, b, contract_a=1, contract_b=0):
    return lax.dot_general(
        a, b, (((contract_a,), (contract_b,)), ((), ())), preferred_element_type=F32
    )


def whole():
    return pl.BlockSpec(memory_space=pltpu.VMEM)


def in_hbm():
    return pl.BlockSpec(memory_space=pltpu.HBM)


def anywhere():
    return pl.BlockSpec(memory_space=pl.ANY)


def scalars():
    return pl.BlockSpec(memory_space=pltpu.SMEM)


def load_start(pairs, sems, pieces):
    copies = []
    for which, (source, target) in enumerate(pairs):
        rows = source.shape[0] // pieces
        for i in range(pieces):
            part = pl.ds(i * rows, rows)
            copies.append(
                pltpu.make_async_copy(source.at[part], target.at[part], sems.at[which, i])
            )
    for copy in copies:
        copy.start()
    return copies


def far(value):
    return pltpu.with_memory_space_constraint(value, pltpu.HBM)


def prepare_kernel(
    ranks, capacity, dps, pipes, place, routes, shares, gate, up, picker, weights, gate_out, up_out, sems
):
    copies = load_start(((gate, gate_out), (up, up_out)), sems, 8)
    rank, dp, pipe = place[0], place[1], place[2]
    experts, slots, token_count = picker.shape
    block = token_count // ranks
    per_piece = ranks // (dps * pipes)
    row = lax.broadcasted_iota(jnp.int32, (8, token_count), 0)
    names = row + rank * experts
    weight = jnp.zeros((8, token_count), F32)
    routed = jnp.zeros((8, token_count), F32)
    for k in range(routes.shape[0]):
        hit = (routes[k : k + 1, :] == names) & (row < experts)
        weight = weight + jnp.where(hit, shares[k : k + 1, :], 0.0)
        routed = routed + jnp.where(hit, 1.0, 0.0)
    t_from = lax.broadcasted_iota(jnp.int32, (token_count, token_count), 0)
    t_to = lax.broadcasted_iota(jnp.int32, (token_count, token_count), 1)
    earlier = jnp.where((t_from // block == t_to // block) & (t_from < t_to), 1.0, 0.0)
    within = dot(routed.astype(BF), earlier.astype(BF)).astype(jnp.int32)
    at_block = lax.broadcasted_iota(jnp.int32, (1, token_count), 1) // block
    at_pipe = lax.rem(at_block // (dps * per_piece) + pipes - pipe, pipes)
    at_dp = lax.rem(lax.rem(at_block // per_piece, dps) + dps - dp, dps)
    first = ((at_pipe * dps + at_dp) * per_piece + lax.rem(at_block, per_piece)) * capacity
    slot = jnp.where(routed > 0.0, within + first, -1)
    ids = lax.broadcasted_iota(jnp.int32, (slots, token_count), 0)
    for e in range(experts):
        hit = slot[e : e + 1] == ids
        picker[e] = jnp.where(hit, 1.0, 0.0).astype(BF)
        weights[e] = jnp.sum(jnp.where(hit, weight[e : e + 1], 0.0), axis=1, keepdims=True)
    for copy in copies:
        copy.wait()


def prepare(place, routes, shares, gate, up, ranks, dps, pipes, block, experts):
    assert experts <= 8
    capacity = block // 2
    token_count = block * ranks
    slots = capacity * ranks
    return pl.pallas_call(
        functools.partial(prepare_kernel, ranks, capacity, dps, pipes),
        in_specs=[scalars(), whole(), whole(), in_hbm(), in_hbm()],
        out_specs=(whole(), whole(), whole(), whole()),
        out_shape=(
            jax.ShapeDtypeStruct((experts, slots, token_count), BF),
            jax.ShapeDtypeStruct((experts, slots, 1), F32),
            pltpu.VMEM(gate.shape, BF),
            pltpu.VMEM(up.shape, BF),
        ),
        scratch_shapes=[pltpu.SemaphoreType.DMA((2, 8))],
        compiler_params=pltpu.CompilerParams(vmem_limit_bytes=8 * 1024 * 1024),
        cost_estimate=pl.CostEstimate(
            flops=0, bytes_accessed=4 * gate.size, transcendentals=0
        ),
    )(place, routes, shares, far(gate), far(up))


def load_kernel(source, before, out, sems):
    for copy in load_start(((source, out),), sems, 8):
        copy.wait()


def load(source, before):
    return pl.pallas_call(
        load_kernel,
        in_specs=[in_hbm(), anywhere()],
        out_specs=whole(),
        out_shape=pltpu.VMEM(source.shape, source.dtype),
        scratch_shapes=[pltpu.SemaphoreType.DMA((1, 8))],
        compiler_params=pltpu.CompilerParams(vmem_limit_bytes=4 * 1024 * 1024),
        cost_estimate=pl.CostEstimate(
            flops=0, bytes_accessed=2 * source.size, transcendentals=0
        ),
    )(far(source), before)


def add_kernel(a, b, before, out):
    out[...] = (a[...].astype(F32) + b[...].astype(F32)).astype(BF)


def add_after(a, b, before):
    return pl.pallas_call(
        add_kernel,
        in_specs=[whole(), whole(), anywhere()],
        out_specs=whole(),
        out_shape=jax.ShapeDtypeStruct(a.shape, BF),
        compiler_params=pltpu.CompilerParams(vmem_limit_bytes=4 * 1024 * 1024),
    )(a, b, before)


def tile_of(size):
    return 256 if size % 256 == 0 else 128


def teacher_kernel(first, size, dps, pipes, place, tokens, gate, up, keep, send):
    dp, pipe = place[1], place[2]
    rows = tokens.shape[0] // (dps * pipes)
    half = dps * rows
    parts = []
    for j1 in range(pipes):
        for j0 in range(dps):
            piece = lax.rem(pipe + j1, pipes) * dps + lax.rem(dp + j0, dps)
            parts.append(tokens[pl.ds(pl.multiple_of(piece * rows, rows), rows), :])
    ordered = jnp.concatenate(parts, axis=0)
    tile = tile_of(size)
    for which, weight in enumerate((gate, up)):
        for i in range(size // tile):
            product = dot(ordered, weight[:, first + i * tile : first + (i + 1) * tile]).astype(BF)
            keep[which, :, i * tile : (i + 1) * tile] = product[:half]
            send[which, :, i * tile : (i + 1) * tile] = product[half:]


def teacher_pre(place, tokens, gate, up, first, size, dps, pipes):
    token_count, width = tokens.shape
    half = jax.ShapeDtypeStruct((2, token_count // pipes, size), BF)
    return pl.pallas_call(
        functools.partial(teacher_kernel, first, size, dps, pipes),
        in_specs=[scalars(), whole(), whole(), whole()],
        out_specs=(whole(), whole()),
        out_shape=(half, half),
        compiler_params=pltpu.CompilerParams(vmem_limit_bytes=8 * 1024 * 1024),
        cost_estimate=pl.CostEstimate(
            flops=4 * token_count * width * size, bytes_accessed=4 * width * size, transcendentals=0
        ),
    )(place, tokens, gate, up)


def expert_kernel(first, picker, tokens, gate, up, before, keep, send, held, sems):
    half = keep.shape[2]
    count = keep.shape[0]
    pieces = sems.shape[2]
    rows_each = gate.shape[0] // pieces
    copies = {}
    for i in range(count):
        for which, weight in enumerate((gate, up)):
            for p in range(pieces):
                part = pl.ds(p * rows_each, rows_each)
                columns = pl.ds((first + i) * H, H)
                copies[i, which, p] = pltpu.make_async_copy(
                    weight.at[part, columns], held.at[i, which, part], sems.at[i, which, p]
                )
                copies[i, which, p].start()
    for i in range(count):
        rows = dot(picker[first + i], tokens[...]).astype(BF)
        for which in range(2):
            for p in range(pieces):
                copies[i, which, p].wait()
            product = dot(rows, held[i, which]).astype(BF)
            keep[i, which] = product[:half]
            send[i, which] = product[half:]


def expert_pre(picker, tokens, gate, up, before, first, count):
    slots = picker.shape[1]
    width = tokens.shape[1]
    halves = jax.ShapeDtypeStruct((count, 2, slots // 2, H), BF)
    return pl.pallas_call(
        functools.partial(expert_kernel, first),
        in_specs=[whole(), whole(), in_hbm(), in_hbm(), anywhere()],
        out_specs=(whole(), whole()),
        out_shape=(halves, halves),
        scratch_shapes=[
            pltpu.VMEM((count, 2, width, H), BF),
            pltpu.SemaphoreType.DMA((count, 2, 4)),
        ],
        compiler_params=pltpu.CompilerParams(vmem_limit_bytes=16 * 1024 * 1024),
        cost_estimate=pl.CostEstimate(
            flops=count * 4 * slots * width * H,
            bytes_accessed=count * 4 * width * H,
            transcendentals=0,
        ),
    )(picker, tokens, far(gate), far(up), before)


def hidden_act_kernel(first, swap, mine, other, weight, pre, out):
    count, _, rows = mine.shape[:3]
    for i in range(count):
        totals = []
        for which in range(2):
            total = mine[i, which].astype(F32)
            if swap:
                theirs = other[i, which].astype(F32)
                total = total + jnp.concatenate([theirs[rows // 2 :], theirs[: rows // 2]], axis=0)
            pre[i, which] = total
            totals.append(total)
        gate, up = totals
        out[i] = (gate * jax.nn.sigmoid(gate) * up * weight[first + i, :rows]).astype(BF)


def hidden_act(mine, other, swap, weight, first):
    count, _, rows, width = mine.shape
    return pl.pallas_call(
        functools.partial(hidden_act_kernel, first, swap),
        in_specs=[whole(), whole(), whole()],
        out_specs=(whole(), whole()),
        out_shape=(
            jax.ShapeDtypeStruct(mine.shape, F32),
            jax.ShapeDtypeStruct((count, rows, width), BF),
        ),
        compiler_params=pltpu.CompilerParams(vmem_limit_bytes=8 * 1024 * 1024),
    )(mine, other, weight)


def join_kernel(dps, pipes, place, *refs):
    out = refs[-1]
    dp, pipe = place[1], place[2]
    rows = out.shape[0] // (dps * pipes)
    at = 0
    for i in range((len(refs) - 1) // 2):
        size = refs[2 * i].shape[1]
        for j1 in range(pipes):
            for j0 in range(dps):
                piece = lax.rem(pipe + j1, pipes) * dps + lax.rem(dp + j0, dps)
                target = pl.ds(pl.multiple_of(piece * rows, rows), rows)
                out[target, at : at + size] = refs[2 * i + j1][j0 * rows : (j0 + 1) * rows, :]
        at += size


def join(place, parts, dps, pipes):
    assert pipes == 2
    flat = [value for pair in parts for value in pair]
    rows = flat[0].shape[0] * pipes
    width = sum(pair[0].shape[1] for pair in parts)
    return pl.pallas_call(
        functools.partial(join_kernel, dps, pipes),
        in_specs=[scalars()] + [whole()] * len(flat),
        out_specs=whole(),
        out_shape=jax.ShapeDtypeStruct((rows, width), BF),
        compiler_params=pltpu.CompilerParams(vmem_limit_bytes=8 * 1024 * 1024),
    )(place, *flat)


def spread_kernel(picker, hidden, out):
    for e in range(picker.shape[0]):
        out[:, e * H : (e + 1) * H] = dot(picker[e], hidden[e], 0, 0).astype(BF)


def spread(picker, hidden):
    count, slots, token_count = picker.shape
    return pl.pallas_call(
        spread_kernel,
        in_specs=[whole(), whole()],
        out_specs=whole(),
        out_shape=jax.ShapeDtypeStruct((token_count, count * H), BF),
        compiler_params=pltpu.CompilerParams(vmem_limit_bytes=8 * 1024 * 1024),
    )(picker, hidden)


def flip_kernel(dense, tokens, before, dense_out, tokens_out):
    dense_out[...] = dense[...].astype(F32).T.astype(BF)
    tokens_out[...] = tokens[...].astype(F32).T.astype(BF)


def flip(dense, tokens, before):
    return pl.pallas_call(
        flip_kernel,
        in_specs=[whole(), whole(), anywhere()],
        out_specs=(whole(), whole()),
        out_shape=(
            jax.ShapeDtypeStruct(dense.shape[::-1], BF),
            jax.ShapeDtypeStruct(tokens.shape[::-1], BF),
        ),
        compiler_params=pltpu.CompilerParams(vmem_limit_bytes=16 * 1024 * 1024),
    )(dense, tokens, before)


def hidden_grad_kernel(first, picker, residual, down, keep, send):
    half = keep.shape[1]
    for i in range(keep.shape[0]):
        e = first + i
        rows = dot(picker[e], residual[...]).astype(BF)
        product = dot(down[e * H : (e + 1) * H, :], rows, 1, 1).T.astype(BF)
        keep[i] = product[:half]
        send[i] = product[half:]


def hidden_grad_parts(picker, residual, down, first, count):
    slots = picker.shape[1]
    halves = jax.ShapeDtypeStruct((count, slots // 2, H), BF)
    return pl.pallas_call(
        functools.partial(hidden_grad_kernel, first),
        in_specs=[whole(), whole(), whole()],
        out_specs=(whole(), whole()),
        out_shape=(halves, halves),
        compiler_params=pltpu.CompilerParams(vmem_limit_bytes=8 * 1024 * 1024),
    )(picker, residual, down)


def hidden_grad_act_kernel(first, swap, mine, other, pre, weight, before, out):
    count, rows = mine.shape[:2]
    for i in range(count):
        total = mine[i].astype(F32)
        if swap:
            flipped = jnp.concatenate([other[i, rows // 2 :], other[i, : rows // 2]], axis=0)
            total = total + flipped.astype(F32)
        total = total * weight[first + i, :rows]
        pre_gate, pre_up = pre[i, 0], pre[i, 1]
        sig = jax.nn.sigmoid(pre_gate)
        gate_grad = total * pre_up * sig * (1.0 + pre_gate * (1.0 - sig))
        up_grad = total * pre_gate * sig
        out[i, 0] = gate_grad.astype(BF)
        out[i, 1] = up_grad.astype(BF)


def hidden_grad_act(mine, other, swap, pre, weight, before, first):
    count, rows, width = mine.shape
    return pl.pallas_call(
        functools.partial(hidden_grad_act_kernel, first, swap),
        in_specs=[whole(), whole(), whole(), whole(), anywhere()],
        out_specs=whole(),
        out_shape=jax.ShapeDtypeStruct((count, 2, rows, width), BF),
        compiler_params=pltpu.CompilerParams(vmem_limit_bytes=8 * 1024 * 1024),
    )(mine, other, pre, weight, before)


def down_grad_kernel(hidden, residual, before, out, done):
    out[...] = dot(hidden[...], residual[...]).astype(BF)
    done[...] = jnp.zeros_like(done)


def down_grad(hidden, residual, before):
    rows, token_count = hidden.shape
    width = residual.shape[1]
    return pl.pallas_call(
        down_grad_kernel,
        grid=(rows // H,),
        in_specs=[
            pl.BlockSpec((H, token_count), lambda i: (i, 0)),
            pl.BlockSpec((token_count, width), lambda i: (0, 0)),
            anywhere(),
        ],
        out_specs=(
            pl.BlockSpec((H, width), lambda i: (i, 0)),
            pl.BlockSpec((8, 128), lambda i: (0, 0)),
        ),
        out_shape=(
            jax.ShapeDtypeStruct((rows, width), BF),
            jax.ShapeDtypeStruct((8, 128), F32),
        ),
        compiler_params=pltpu.CompilerParams(vmem_limit_bytes=16 * 1024 * 1024),
        cost_estimate=pl.CostEstimate(
            flops=2 * rows * width * token_count,
            bytes_accessed=2 * rows * width,
            transcendentals=0,
        ),
    )(hidden, residual, before)


def input_grad_kernel(picker, tokens, mine, theirs, *rest):
    out_gate, out_up = rest[-2:]
    for which, out in enumerate((out_gate, out_up)):
        grad = jnp.concatenate([mine[0, which], theirs[0, which]], axis=0)
        dense = dot(picker[0], grad, 0, 0).astype(BF)
        out[...] = dot(tokens[...], dense).astype(BF)


def input_grads(picker, tokens, mine, theirs, first, so_far):
    experts, slots, token_count = picker.shape
    width = tokens.shape[0]
    count = mine.shape[0]
    split = 2 if width % 256 == 0 else 1
    part = width // split
    grad_spec = pl.BlockSpec((1, 2, slots // 2, H), lambda i, j: (i, 0, 0, 0))
    out_spec = pl.BlockSpec((part, H), lambda i, j: (j, first + i))
    out = jax.ShapeDtypeStruct((width, experts * H), BF)
    extra = () if so_far is None else so_far
    return pl.pallas_call(
        input_grad_kernel,
        grid=(count, split),
        in_specs=[
            pl.BlockSpec((1, slots, token_count), lambda i, j: (first + i, 0, 0)),
            pl.BlockSpec((part, token_count), lambda i, j: (j, 0)),
            grad_spec,
            grad_spec,
        ]
        + [in_hbm()] * len(extra),
        out_specs=(out_spec, out_spec),
        out_shape=(out, out),
        input_output_aliases={4 + i: i for i in range(len(extra))},
        compiler_params=pltpu.CompilerParams(vmem_limit_bytes=16 * 1024 * 1024),
        cost_estimate=pl.CostEstimate(
            flops=count * 4 * token_count * width * H,
            bytes_accessed=count * 4 * width * H,
            transcendentals=0,
        ),
    )(picker, tokens, mine, theirs, *[far(value) for value in extra])


def add(a, b):
    return (a.astype(F32) + b.astype(F32)).astype(BF)


def split_rows(value, count):
    rows = value.shape[-2] // count
    return [value[..., i * rows : (i + 1) * rows, :] for i in range(count)]


def scatter_dp(value, count):
    pieces = split_rows(value, count)
    total = pieces[0].astype(F32)
    for s in range(1, count):
        total = total + shift(pieces[s], "dp", count, s).astype(F32)
    return total


def gather_dp(value, count):
    return jnp.concatenate(
        [value] + [shift(value, "dp", count, -s) for s in range(1, count)], axis=-2
    )


def exchange_dp(value, count):
    if count == 2:
        return value, shift(value, "dp", count, 1)
    total = gather_dp(scatter_dp(value, count).astype(BF), count)
    return total, total


def body(
    tokens,
    routes,
    gate_weights,
    teacher_gate,
    teacher_up,
    teacher_down,
    expert_gate,
    expert_up,
    expert_down,
):
    ranks = lax.axis_size("expert")
    dps = lax.axis_size("dp")
    pipes = lax.axis_size("pipe")
    rank = lax.axis_index("expert")
    dp = lax.axis_index("dp")
    pipe = lax.axis_index("pipe")
    block, width = tokens.shape
    token_count = block * ranks
    experts = expert_gate.shape[1] // H
    slots = block // 2 * ranks
    place = jnp.stack([rank, dp, pipe]).astype(jnp.int32)

    def gather_tokens(mine):
        whole_rows = jnp.zeros((token_count, mine.shape[1]), BF)
        whole_rows = lax.dynamic_update_slice(whole_rows, mine, (rank * block, 0))
        for s in range(1, ranks):
            theirs = shift(mine, "expert", ranks, -s)
            at = (rank + s) % ranks * block
            whole_rows = lax.dynamic_update_slice(whole_rows, theirs, (at, 0))
        return whole_rows

    def to_owners(product):
        def block_of(s):
            return lax.dynamic_slice_in_dim(product, (rank + s) % ranks * block, block, axis=0)

        total = block_of(0).astype(F32)
        for s in range(1, ranks):
            total = total + shift(block_of(s), "expert", ranks, s).astype(F32)
        return total

    base = gather_tokens(tokens)
    picker, slot_weight, gate_near, up_near = prepare(
        place, routes.T, gate_weights.T, teacher_gate, teacher_up, ranks, dps, pipes, block, experts
    )

    chunks = 2 if teacher_gate.shape[1] % 512 == 0 else 1
    size = teacher_gate.shape[1] // chunks
    halves = []
    for i in range(chunks):
        keep, send = teacher_pre(place, base, gate_near, up_near, i * size, size, dps, pipes)
        halves.append(add(keep, shift(send, "pipe", pipes, 1)))

    group = 2 if experts % 2 == 0 else 1
    firsts = range(0, experts, group)
    parts = []
    last = halves[-1]
    for first in firsts:
        keep, send = expert_pre(picker, base, expert_gate, expert_up, last, first, group)
        last = keep
        parts.append((keep, shift(send, "pipe", pipes, 1)))
    teacher_down = load(teacher_down, last)
    expert_down = load(expert_down, teacher_down)

    hiddens = []
    for half in halves:
        total = scatter_dp(half, dps)
        hidden = gather_dp((jax.nn.silu(total[0]) * total[1]).astype(BF), dps)
        hiddens.append((hidden, shift(hidden, "pipe", pipes, 1)))
    hidden = join(place, hiddens, dps, pipes)
    target = to_owners(jnp.dot(hidden, teacher_down, preferred_element_type=F32).astype(BF))

    pre, weighted = [], []
    for first, (keep, theirs) in zip(firsts, parts):
        mine, other = exchange_dp(add(keep, theirs), dps)
        total, part = hidden_act(mine, other, dps == 2, slot_weight, first)
        pre.append(total)
        weighted.append(jnp.concatenate([part, shift(part, "pipe", pipes, 1)], axis=1))
    weighted = jnp.concatenate(weighted, axis=0)

    dense = spread(picker, weighted)
    product = jnp.dot(dense, expert_down, preferred_element_type=F32).astype(BF)
    student_sum = to_owners(product)
    dense_flipped, base_flipped = flip(dense, base, product)
    residual = gather_tokens((student_sum - target).astype(BF))

    sums = []
    for first in firsts:
        keep, send = hidden_grad_parts(picker, residual, expert_down, first, group)
        sums.append(add(keep, shift(send, "pipe", pipes, 1)))
    pairs = [exchange_dp(value, dps) for value in sums]
    grad_down, done = down_grad(dense_flipped, residual, sums[-1])
    grads = None
    for i, first in enumerate(firsts):
        mine = hidden_grad_act(*pairs[i], dps == 2, pre[i], slot_weight, done, first)
        theirs = shift(mine, "pipe", pipes, 1)
        grads = input_grads(picker, base_flipped, mine, theirs, first, grads)
    return (student_sum.astype(BF), grads[0], grads[1], grad_down)


def solution(mesh):
    placed = (
        P(("groups", "expert"), ("dp", "pipe")),
        P("groups", None),
        P("groups", None),
        P(("dp", "pipe"), "expert"),
        P(("dp", "pipe"), "expert"),
        P("expert", ("dp", "pipe")),
        P(("dp", "pipe"), "expert"),
        P(("dp", "pipe"), "expert"),
        P("expert", ("dp", "pipe")),
    )
    return jax.shard_map(
        body,
        mesh=mesh,
        in_specs=placed,
        out_specs=(
            P(("groups", "expert"), ("dp", "pipe")),
            P(("groups", "dp", "pipe"), "expert"),
            P(("groups", "dp", "pipe"), "expert"),
            P(("groups", "expert"), ("dp", "pipe")),
        ),
        check_vma=False,
    )
```

```python
import functools

import jax
import jax.numpy as jnp
from jax import lax
from jax.experimental import pallas as pl
from jax.experimental.pallas import tpu as pltpu
from jax.sharding import PartitionSpec as P

H = 896
BF = jnp.bfloat16
F32 = jnp.float32


def shift(value, axis, count, by):
    return lax.ppermute(value, axis, [(i, (i + by) % count) for i in range(count)])


def dot(a, b, contract_a=1, contract_b=0):
    return lax.dot_general(
        a, b, (((contract_a,), (contract_b,)), ((), ())), preferred_element_type=F32
    )


def whole():
    return pl.BlockSpec(memory_space=pltpu.VMEM)


def in_hbm():
    return pl.BlockSpec(memory_space=pltpu.HBM)


def anywhere():
    return pl.BlockSpec(memory_space=pl.ANY)


def scalars():
    return pl.BlockSpec(memory_space=pltpu.SMEM)


def load_start(pairs, sems, pieces):
    copies = []
    for which, (source, target) in enumerate(pairs):
        rows = source.shape[0] // pieces
        for i in range(pieces):
            part = pl.ds(i * rows, rows)
            copies.append(
                pltpu.make_async_copy(source.at[part], target.at[part], sems.at[which, i])
            )
    for copy in copies:
        copy.start()
    return copies


def far(value):
    return pltpu.with_memory_space_constraint(value, pltpu.HBM)


def prepare_kernel(
    ranks,
    capacity,
    dps,
    pipes,
    place,
    far_routes,
    far_shares,
    gate,
    up,
    picker,
    weights,
    gate_out,
    up_out,
    routes,
    shares,
    sems,
    table_sems,
):
    tables = [
        pltpu.make_async_copy(far_routes, routes, table_sems.at[0]),
        pltpu.make_async_copy(far_shares, shares, table_sems.at[1]),
    ]
    for copy in tables:
        copy.start()
    copies = load_start(((gate, gate_out), (up, up_out)), sems, 8)
    for copy in tables:
        copy.wait()
    rank, dp, pipe = place[0], place[1], place[2]
    experts, slots, token_count = picker.shape
    block = token_count // ranks
    per_piece = ranks // (dps * pipes)
    row = lax.broadcasted_iota(jnp.int32, (8, token_count), 0)
    names = row + rank * experts
    weight = jnp.zeros((8, token_count), F32)
    routed = jnp.zeros((8, token_count), F32)
    for k in range(routes.shape[0]):
        hit = (routes[k : k + 1, :] == names) & (row < experts)
        weight = weight + jnp.where(hit, shares[k : k + 1, :], 0.0)
        routed = routed + jnp.where(hit, 1.0, 0.0)
    t_from = lax.broadcasted_iota(jnp.int32, (token_count, token_count), 0)
    t_to = lax.broadcasted_iota(jnp.int32, (token_count, token_count), 1)
    earlier = jnp.where((t_from // block == t_to // block) & (t_from < t_to), 1.0, 0.0)
    within = dot(routed.astype(BF), earlier.astype(BF)).astype(jnp.int32)
    at_block = lax.broadcasted_iota(jnp.int32, (1, token_count), 1) // block
    at_pipe = lax.rem(at_block // (dps * per_piece) + pipes - pipe, pipes)
    at_dp = lax.rem(lax.rem(at_block // per_piece, dps) + dps - dp, dps)
    first = ((at_pipe * dps + at_dp) * per_piece + lax.rem(at_block, per_piece)) * capacity
    slot = jnp.where(routed > 0.0, within + first, -1)
    ids = lax.broadcasted_iota(jnp.int32, (slots, token_count), 0)
    for e in range(experts):
        hit = slot[e : e + 1] == ids
        picker[e] = jnp.where(hit, 1.0, 0.0).astype(BF)
        weights[e] = jnp.sum(jnp.where(hit, weight[e : e + 1], 0.0), axis=1, keepdims=True)
    for copy in copies:
        copy.wait()


def prepare(place, routes, shares, gate, up, ranks, dps, pipes, block, experts):
    assert experts <= 8
    capacity = block // 2
    token_count = block * ranks
    slots = capacity * ranks
    return pl.pallas_call(
        functools.partial(prepare_kernel, ranks, capacity, dps, pipes),
        in_specs=[scalars(), in_hbm(), in_hbm(), in_hbm(), in_hbm()],
        out_specs=(whole(), whole(), whole(), whole()),
        out_shape=(
            jax.ShapeDtypeStruct((experts, slots, token_count), BF),
            jax.ShapeDtypeStruct((experts, slots, 1), F32),
            pltpu.VMEM(gate.shape, BF),
            pltpu.VMEM(up.shape, BF),
        ),
        scratch_shapes=[
            pltpu.VMEM(routes.shape, routes.dtype),
            pltpu.VMEM(shares.shape, shares.dtype),
            pltpu.SemaphoreType.DMA((2, 8)),
            pltpu.SemaphoreType.DMA((2,)),
        ],
        compiler_params=pltpu.CompilerParams(vmem_limit_bytes=8 * 1024 * 1024),
        cost_estimate=pl.CostEstimate(
            flops=0, bytes_accessed=4 * gate.size, transcendentals=0
        ),
    )(place, far(routes), far(shares), far(gate), far(up))


def load_kernel(source, before, out, sems):
    for copy in load_start(((source, out),), sems, 8):
        copy.wait()


def load(source, before):
    return pl.pallas_call(
        load_kernel,
        in_specs=[in_hbm(), anywhere()],
        out_specs=whole(),
        out_shape=pltpu.VMEM(source.shape, source.dtype),
        scratch_shapes=[pltpu.SemaphoreType.DMA((1, 8))],
        compiler_params=pltpu.CompilerParams(vmem_limit_bytes=4 * 1024 * 1024),
        cost_estimate=pl.CostEstimate(
            flops=0, bytes_accessed=2 * source.size, transcendentals=0
        ),
    )(far(source), before)


def pair_kernel(*refs):
    out = refs[-1]
    rows = out.shape[0] // (len(refs) - 2)
    for i, value in enumerate(refs[:-2]):
        out[i * rows : (i + 1) * rows, :] = value[...]


def pair(values, before):
    rows, width = values[0].shape
    return pl.pallas_call(
        pair_kernel,
        in_specs=[whole()] * len(values) + [anywhere()],
        out_specs=whole(),
        out_shape=jax.ShapeDtypeStruct((rows * len(values), width), BF),
        compiler_params=pltpu.CompilerParams(vmem_limit_bytes=4 * 1024 * 1024),
    )(*values, before)


def residual_kernel(ranks, *refs):
    student = refs[0][...].astype(F32)
    target = refs[ranks][...].astype(F32)
    for i in range(1, ranks):
        student = student + refs[i][...].astype(F32)
        target = target + refs[ranks + i][...].astype(F32)
    refs[-2][...] = student.astype(BF)
    refs[-1][...] = (student - target).astype(BF)


def residual_of(student, target, before):
    ranks = len(student)
    block = jax.ShapeDtypeStruct(student[0].shape, BF)
    return pl.pallas_call(
        functools.partial(residual_kernel, ranks),
        in_specs=[whole()] * (2 * ranks) + [anywhere()] * len(before),
        out_specs=(whole(), whole()),
        out_shape=(block, block),
        compiler_params=pltpu.CompilerParams(vmem_limit_bytes=4 * 1024 * 1024),
    )(*student, *target, *before)


def tile_of(size):
    return 256 if size % 256 == 0 else 128


def teacher_kernel(first, size, dps, pipes, place, tokens, gate, up, keep, send):
    dp, pipe = place[1], place[2]
    rows = tokens.shape[0] // (dps * pipes)
    half = dps * rows
    parts = []
    for j1 in range(pipes):
        for j0 in range(dps):
            piece = lax.rem(pipe + j1, pipes) * dps + lax.rem(dp + j0, dps)
            parts.append(tokens[pl.ds(pl.multiple_of(piece * rows, rows), rows), :])
    ordered = jnp.concatenate(parts, axis=0)
    tile = tile_of(size)
    for which, weight in enumerate((gate, up)):
        for i in range(size // tile):
            product = dot(ordered, weight[:, first + i * tile : first + (i + 1) * tile]).astype(BF)
            keep[which, :, i * tile : (i + 1) * tile] = product[:half]
            send[which, :, i * tile : (i + 1) * tile] = product[half:]


def teacher_pre(place, tokens, gate, up, first, size, dps, pipes):
    token_count, width = tokens.shape
    half = jax.ShapeDtypeStruct((2, token_count // pipes, size), BF)
    return pl.pallas_call(
        functools.partial(teacher_kernel, first, size, dps, pipes),
        in_specs=[scalars(), whole(), whole(), whole()],
        out_specs=(whole(), whole()),
        out_shape=(half, half),
        compiler_params=pltpu.CompilerParams(vmem_limit_bytes=8 * 1024 * 1024),
        cost_estimate=pl.CostEstimate(
            flops=4 * token_count * width * size, bytes_accessed=4 * width * size, transcendentals=0
        ),
    )(place, tokens, gate, up)


def expert_kernel(first, picker, tokens, gate, up, before, keep, send, held, sems):
    half = keep.shape[2]
    count = keep.shape[0]
    pieces = sems.shape[2]
    rows_each = gate.shape[0] // pieces
    copies = {}
    for i in range(count):
        for which, weight in enumerate((gate, up)):
            for p in range(pieces):
                part = pl.ds(p * rows_each, rows_each)
                columns = pl.ds((first + i) * H, H)
                copies[i, which, p] = pltpu.make_async_copy(
                    weight.at[part, columns], held.at[i, which, part], sems.at[i, which, p]
                )
                copies[i, which, p].start()
    for i in range(count):
        rows = dot(picker[first + i], tokens[...]).astype(BF)
        for which in range(2):
            for p in range(pieces):
                copies[i, which, p].wait()
            product = dot(rows, held[i, which]).astype(BF)
            keep[i, which] = product[:half]
            send[i, which] = product[half:]


def expert_pre(picker, tokens, gate, up, before, first, count):
    slots = picker.shape[1]
    width = tokens.shape[1]
    halves = jax.ShapeDtypeStruct((count, 2, slots // 2, H), BF)
    return pl.pallas_call(
        functools.partial(expert_kernel, first),
        in_specs=[whole(), whole(), in_hbm(), in_hbm(), anywhere()],
        out_specs=(whole(), whole()),
        out_shape=(halves, halves),
        scratch_shapes=[
            pltpu.VMEM((count, 2, width, H), BF),
            pltpu.SemaphoreType.DMA((count, 2, 4)),
        ],
        compiler_params=pltpu.CompilerParams(vmem_limit_bytes=16 * 1024 * 1024),
        cost_estimate=pl.CostEstimate(
            flops=count * 4 * slots * width * H,
            bytes_accessed=count * 4 * width * H,
            transcendentals=0,
        ),
    )(picker, tokens, far(gate), far(up), before)


def hidden_act_kernel(first, swap, mine, other, weight, pre, out):
    count, _, rows = mine.shape[:3]
    for i in range(count):
        totals = []
        for which in range(2):
            total = mine[i, which].astype(F32)
            if swap:
                theirs = other[i, which].astype(F32)
                total = total + jnp.concatenate([theirs[rows // 2 :], theirs[: rows // 2]], axis=0)
            pre[i, which] = total
            totals.append(total)
        gate, up = totals
        out[i] = (gate * jax.nn.sigmoid(gate) * up * weight[first + i, :rows]).astype(BF)


def hidden_act(mine, other, swap, weight, first):
    count, _, rows, width = mine.shape
    return pl.pallas_call(
        functools.partial(hidden_act_kernel, first, swap),
        in_specs=[whole(), whole(), whole()],
        out_specs=(whole(), whole()),
        out_shape=(
            jax.ShapeDtypeStruct(mine.shape, F32),
            jax.ShapeDtypeStruct((count, rows, width), BF),
        ),
        compiler_params=pltpu.CompilerParams(vmem_limit_bytes=8 * 1024 * 1024),
    )(mine, other, weight)


def join_kernel(dps, pipes, place, *refs):
    out = refs[-1]
    dp, pipe = place[1], place[2]
    rows = out.shape[0] // (dps * pipes)
    at = 0
    for i in range((len(refs) - 2) // 2):
        size = refs[2 * i].shape[1]
        for j1 in range(pipes):
            for j0 in range(dps):
                piece = lax.rem(pipe + j1, pipes) * dps + lax.rem(dp + j0, dps)
                target = pl.ds(pl.multiple_of(piece * rows, rows), rows)
                out[target, at : at + size] = refs[2 * i + j1][j0 * rows : (j0 + 1) * rows, :]
        at += size


def join(place, parts, before, dps, pipes):
    assert pipes == 2
    flat = [value for pair in parts for value in pair]
    rows = flat[0].shape[0] * pipes
    width = sum(pair[0].shape[1] for pair in parts)
    return pl.pallas_call(
        functools.partial(join_kernel, dps, pipes),
        in_specs=[scalars()] + [whole()] * len(flat) + [anywhere()],
        out_specs=whole(),
        out_shape=jax.ShapeDtypeStruct((rows, width), BF),
        compiler_params=pltpu.CompilerParams(vmem_limit_bytes=8 * 1024 * 1024),
    )(place, *flat, before)


def spread_kernel(picker, hidden, out):
    for e in range(picker.shape[0]):
        out[:, e * H : (e + 1) * H] = dot(picker[e], hidden[e], 0, 0).astype(BF)


def spread(picker, hidden):
    count, slots, token_count = picker.shape
    return pl.pallas_call(
        spread_kernel,
        in_specs=[whole(), whole()],
        out_specs=whole(),
        out_shape=jax.ShapeDtypeStruct((token_count, count * H), BF),
        compiler_params=pltpu.CompilerParams(vmem_limit_bytes=8 * 1024 * 1024),
    )(picker, hidden)


def flip_kernel(dense, tokens, before, dense_out, tokens_out):
    dense_out[...] = dense[...].astype(F32).T.astype(BF)
    tokens_out[...] = tokens[...].astype(F32).T.astype(BF)


def flip(dense, tokens, before):
    return pl.pallas_call(
        flip_kernel,
        in_specs=[whole(), whole(), anywhere()],
        out_specs=(whole(), whole()),
        out_shape=(
            jax.ShapeDtypeStruct(dense.shape[::-1], BF),
            jax.ShapeDtypeStruct(tokens.shape[::-1], BF),
        ),
        compiler_params=pltpu.CompilerParams(vmem_limit_bytes=16 * 1024 * 1024),
    )(dense, tokens, before)


def hidden_grad_kernel(first, picker, residual, down, before, keep, send):
    half = keep.shape[1]
    for i in range(keep.shape[0]):
        e = first + i
        rows = dot(picker[e], residual[...]).astype(BF)
        product = dot(down[e * H : (e + 1) * H, :], rows, 1, 1).T.astype(BF)
        keep[i] = product[:half]
        send[i] = product[half:]


def hidden_grad_parts(picker, residual, down, before, first, count):
    slots = picker.shape[1]
    halves = jax.ShapeDtypeStruct((count, slots // 2, H), BF)
    return pl.pallas_call(
        functools.partial(hidden_grad_kernel, first),
        in_specs=[whole(), whole(), whole(), anywhere()],
        out_specs=(whole(), whole()),
        out_shape=(halves, halves),
        compiler_params=pltpu.CompilerParams(vmem_limit_bytes=8 * 1024 * 1024),
    )(picker, residual, down, before)


def hidden_grad_act_kernel(first, swap, mine, other, pre, weight, before, out):
    count, rows = mine.shape[:2]
    for i in range(count):
        total = mine[i].astype(F32)
        if swap:
            flipped = jnp.concatenate([other[i, rows // 2 :], other[i, : rows // 2]], axis=0)
            total = total + flipped.astype(F32)
        total = total * weight[first + i, :rows]
        pre_gate, pre_up = pre[i, 0], pre[i, 1]
        sig = jax.nn.sigmoid(pre_gate)
        gate_grad = total * pre_up * sig * (1.0 + pre_gate * (1.0 - sig))
        up_grad = total * pre_gate * sig
        out[i, 0] = gate_grad.astype(BF)
        out[i, 1] = up_grad.astype(BF)


def hidden_grad_act(mine, other, swap, pre, weight, before, first):
    count, rows, width = mine.shape
    return pl.pallas_call(
        functools.partial(hidden_grad_act_kernel, first, swap),
        in_specs=[whole(), whole(), whole(), whole(), anywhere()],
        out_specs=whole(),
        out_shape=jax.ShapeDtypeStruct((count, 2, rows, width), BF),
        compiler_params=pltpu.CompilerParams(vmem_limit_bytes=8 * 1024 * 1024),
    )(mine, other, pre, weight, before)


def down_grad_kernel(hidden, residual, before, out, done, held, sems):
    tiles = sems.shape[0]
    rows = hidden.shape[0] // tiles
    copies = []
    for i in range(tiles):
        part = pl.ds(i * rows, rows)
        held[part, :] = dot(hidden[part, :], residual[...]).astype(BF)
        copies.append(pltpu.make_async_copy(held.at[part], out.at[part], sems.at[i]))
        copies[-1].start()
    done[...] = jnp.zeros_like(done)
    for copy in copies:
        copy.wait()


def down_grad(hidden, residual, before):
    rows, token_count = hidden.shape
    width = residual.shape[1]
    return pl.pallas_call(
        down_grad_kernel,
        in_specs=[whole(), whole(), anywhere()],
        out_specs=(in_hbm(), whole()),
        out_shape=(
            jax.ShapeDtypeStruct((rows, width), BF),
            jax.ShapeDtypeStruct((8, 128), F32),
        ),
        scratch_shapes=[
            pltpu.VMEM((rows, width), BF),
            pltpu.SemaphoreType.DMA((rows // (H // 2),)),
        ],
        compiler_params=pltpu.CompilerParams(vmem_limit_bytes=16 * 1024 * 1024),
        cost_estimate=pl.CostEstimate(
            flops=2 * rows * width * token_count,
            bytes_accessed=2 * rows * width,
            transcendentals=0,
        ),
    )(hidden, residual, before)


def input_grad_kernel(first, picker, tokens, mine, theirs, *rest):
    outs, held, sems = rest[-4:-2], rest[-2], rest[-1]
    count = mine.shape[0]
    splits = sems.shape[2]
    rows = tokens.shape[0] // splits
    copies = []
    for i in range(count):
        for which in range(2):
            grad = jnp.concatenate([mine[i, which], theirs[i, which]], axis=0)
            dense = dot(picker[first + i], grad, 0, 0).astype(BF)
            for r in range(splits):
                part = pl.ds(r * rows, rows)
                columns = pl.ds((first + i) * H, H)
                held[i, which, part] = dot(tokens[part, :], dense).astype(BF)
                copies.append(
                    pltpu.make_async_copy(
                        held.at[i, which, part], outs[which].at[part, columns], sems.at[i, which, r]
                    )
                )
                copies[-1].start()
    for copy in copies:
        copy.wait()


def input_grads(picker, tokens, mine, theirs, first, so_far):
    experts, slots, token_count = picker.shape
    width = tokens.shape[0]
    count = mine.shape[0]
    out = jax.ShapeDtypeStruct((width, experts * H), BF)
    extra = () if so_far is None else so_far
    return pl.pallas_call(
        functools.partial(input_grad_kernel, first),
        in_specs=[whole()] * 4 + [in_hbm()] * len(extra),
        out_specs=(in_hbm(), in_hbm()),
        out_shape=(out, out),
        scratch_shapes=[
            pltpu.VMEM((count, 2, width, H), BF),
            pltpu.SemaphoreType.DMA((count, 2, 2)),
        ],
        input_output_aliases={4 + i: i for i in range(len(extra))},
        compiler_params=pltpu.CompilerParams(vmem_limit_bytes=16 * 1024 * 1024),
        cost_estimate=pl.CostEstimate(
            flops=count * 4 * token_count * width * H,
            bytes_accessed=count * 4 * width * H,
            transcendentals=0,
        ),
    )(picker, tokens, mine, theirs, *[far(value) for value in extra])


def add(a, b):
    return (a.astype(F32) + b.astype(F32)).astype(BF)


def split_rows(value, count):
    rows = value.shape[-2] // count
    return [value[..., i * rows : (i + 1) * rows, :] for i in range(count)]


def scatter_dp(value, count):
    pieces = split_rows(value, count)
    total = pieces[0].astype(F32)
    for s in range(1, count):
        total = total + shift(pieces[s], "dp", count, s).astype(F32)
    return total


def gather_dp_parts(value, count):
    return [value] + [shift(value, "dp", count, -s) for s in range(1, count)]


def gather_dp(value, count):
    return jnp.concatenate(gather_dp_parts(value, count), axis=-2)


def exchange_dp(value, count):
    if count == 2:
        return value, shift(value, "dp", count, 1)
    total = gather_dp(scatter_dp(value, count).astype(BF), count)
    return total, total


def body(
    tokens,
    routes,
    gate_weights,
    teacher_gate,
    teacher_up,
    teacher_down,
    expert_gate,
    expert_up,
    expert_down,
):
    ranks = lax.axis_size("expert")
    dps = lax.axis_size("dp")
    pipes = lax.axis_size("pipe")
    rank = lax.axis_index("expert")
    dp = lax.axis_index("dp")
    pipe = lax.axis_index("pipe")
    block, width = tokens.shape
    token_count = block * ranks
    experts = expert_gate.shape[1] // H
    slots = block // 2 * ranks
    place = jnp.stack([rank, dp, pipe]).astype(jnp.int32)

    paired = ranks & (ranks - 1) == 0

    def to_partner(value, s):
        if paired:
            return lax.ppermute(value, "expert", [(i, i ^ s) for i in range(ranks)])
        return shift(value, "expert", ranks, s)

    def target_of(s):
        return rank ^ s if paired else (rank + s) % ranks

    def source_of(s):
        return rank ^ s if paired else (rank + ranks - s) % ranks

    def gather_tokens(mine):
        whole_rows = jnp.zeros((token_count, mine.shape[1]), BF)
        whole_rows = lax.dynamic_update_slice(whole_rows, mine, (rank * block, 0))
        for s in range(1, ranks):
            theirs = to_partner(mine, s)
            whole_rows = lax.dynamic_update_slice(whole_rows, theirs, (source_of(s) * block, 0))
        return whole_rows

    def to_owners(product):
        def block_of(r):
            return lax.dynamic_slice_in_dim(product, r * block, block, axis=0)

        return [block_of(rank)] + [to_partner(block_of(target_of(s)), s) for s in range(1, ranks)]

    base = gather_tokens(tokens)
    picker, slot_weight, gate_near, up_near = prepare(
        place, routes.T, gate_weights.T, teacher_gate, teacher_up, ranks, dps, pipes, block, experts
    )

    chunks = 2 if teacher_gate.shape[1] % 512 == 0 else 1
    size = teacher_gate.shape[1] // chunks
    halves = []
    for i in range(chunks):
        keep, send = teacher_pre(place, base, gate_near, up_near, i * size, size, dps, pipes)
        halves.append(add(keep, shift(send, "pipe", pipes, 1)))

    group = 2 if experts % 2 == 0 else 1
    firsts = range(0, experts, group)
    parts = []
    last = halves[-1]
    for first in firsts:
        keep, send = expert_pre(picker, base, expert_gate, expert_up, last, first, group)
        last = keep
        parts.append((keep, shift(send, "pipe", pipes, 1)))
    teacher_near = load(teacher_down, last)

    hiddens = []
    for half in halves:
        total = scatter_dp(half, dps)
        hidden = (jax.nn.silu(total[0]) * total[1]).astype(BF)
        hidden = pair(gather_dp_parts(hidden, dps), teacher_near)
        hiddens.append((hidden, shift(hidden, "pipe", pipes, 1)))
    expert_near = load(expert_down, hiddens[-1][0])
    hidden = join(place, hiddens, expert_near, dps, pipes)
    target = to_owners(jnp.dot(hidden, teacher_near, preferred_element_type=F32).astype(BF))

    pre, weighted = [], []
    for first, (keep, theirs) in zip(firsts, parts):
        mine, other = exchange_dp(add(keep, theirs), dps)
        total, part = hidden_act(mine, other, dps == 2, slot_weight, first)
        pre.append(total)
        weighted.append(jnp.concatenate([part, shift(part, "pipe", pipes, 1)], axis=1))
    weighted = jnp.concatenate(weighted, axis=0)

    dense = spread(picker, weighted)
    product = jnp.dot(dense, expert_near, preferred_element_type=F32).astype(BF)
    student = to_owners(product)
    dense_flipped, base_flipped = flip(dense, base, product)
    expert_near = load(expert_down, base_flipped)
    student_out, residual = residual_of(student, target, (expert_near,))
    residual = gather_tokens(residual)

    sums = []
    last = residual
    for first in firsts:
        keep, send = hidden_grad_parts(picker, residual, expert_near, last, first, group)
        last = keep
        sums.append(add(keep, shift(send, "pipe", pipes, 1)))
    pairs = [exchange_dp(value, dps) for value in sums]
    grad_down, done = down_grad(dense_flipped, residual, sums[-1])
    grads = None
    for i, first in enumerate(firsts):
        mine = hidden_grad_act(*pairs[i], dps == 2, pre[i], slot_weight, done, first)
        theirs = shift(mine, "pipe", pipes, 1)
        grads = input_grads(picker, base_flipped, mine, theirs, first, grads)
    return (student_out, grads[0], grads[1], grad_down)


def solution(mesh):
    placed = (
        P(("groups", "expert"), ("dp", "pipe")),
        P("groups", None),
        P("groups", None),
        P(("dp", "pipe"), "expert"),
        P(("dp", "pipe"), "expert"),
        P("expert", ("dp", "pipe")),
        P(("dp", "pipe"), "expert"),
        P(("dp", "pipe"), "expert"),
        P("expert", ("dp", "pipe")),
    )
    return jax.shard_map(
        body,
        mesh=mesh,
        in_specs=placed,
        out_specs=(
            P(("groups", "expert"), ("dp", "pipe")),
            P(("groups", "dp", "pipe"), "expert"),
            P(("groups", "dp", "pipe"), "expert"),
            P(("groups", "expert"), ("dp", "pipe")),
        ),
        check_vma=False,
    )
```

```python
import functools

import jax
import jax.numpy as jnp
from jax import lax
from jax.experimental import pallas as pl
from jax.experimental.pallas import tpu as pltpu
from jax.sharding import PartitionSpec as P

H = 896
BF = jnp.bfloat16
F32 = jnp.float32


def shift(value, axis, count, by):
    return lax.ppermute(value, axis, [(i, (i + by) % count) for i in range(count)])


def dot(a, b, contract_a=1, contract_b=0):
    return lax.dot_general(
        a, b, (((contract_a,), (contract_b,)), ((), ())), preferred_element_type=F32
    )


def whole():
    return pl.BlockSpec(memory_space=pltpu.VMEM)


def in_hbm():
    return pl.BlockSpec(memory_space=pltpu.HBM)


def anywhere():
    return pl.BlockSpec(memory_space=pl.ANY)


def scalars():
    return pl.BlockSpec(memory_space=pltpu.SMEM)


def load_start(pairs, sems, pieces):
    copies = []
    for which, (source, target) in enumerate(pairs):
        rows = source.shape[0] // pieces
        for i in range(pieces):
            part = pl.ds(i * rows, rows)
            copies.append(
                pltpu.make_async_copy(source.at[part], target.at[part], sems.at[which, i])
            )
    for copy in copies:
        copy.start()
    return copies


def far(value):
    return pltpu.with_memory_space_constraint(value, pltpu.HBM)


def prepare_kernel(
    ranks,
    capacity,
    dps,
    pipes,
    place,
    far_routes,
    far_shares,
    gate,
    up,
    picker,
    weights,
    gate_out,
    up_out,
    routes,
    shares,
    sems,
    table_sems,
):
    tables = [
        pltpu.make_async_copy(far_routes, routes, table_sems.at[0]),
        pltpu.make_async_copy(far_shares, shares, table_sems.at[1]),
    ]
    for copy in tables:
        copy.start()
    copies = load_start(((gate, gate_out), (up, up_out)), sems, 8)
    for copy in tables:
        copy.wait()
    rank, dp, pipe = place[0], place[1], place[2]
    experts, slots, token_count = picker.shape
    block = token_count // ranks
    per_piece = ranks // (dps * pipes)
    row = lax.broadcasted_iota(jnp.int32, (8, token_count), 0)
    names = row + rank * experts
    weight = jnp.zeros((8, token_count), F32)
    routed = jnp.zeros((8, token_count), F32)
    for k in range(routes.shape[0]):
        hit = (routes[k : k + 1, :] == names) & (row < experts)
        weight = weight + jnp.where(hit, shares[k : k + 1, :], 0.0)
        routed = routed + jnp.where(hit, 1.0, 0.0)
    t_from = lax.broadcasted_iota(jnp.int32, (token_count, token_count), 0)
    t_to = lax.broadcasted_iota(jnp.int32, (token_count, token_count), 1)
    earlier = jnp.where((t_from // block == t_to // block) & (t_from < t_to), 1.0, 0.0)
    within = dot(routed.astype(BF), earlier.astype(BF)).astype(jnp.int32)
    at_block = lax.broadcasted_iota(jnp.int32, (1, token_count), 1) // block
    at_pipe = lax.rem(at_block // (dps * per_piece) + pipes - pipe, pipes)
    at_dp = lax.rem(lax.rem(at_block // per_piece, dps) + dps - dp, dps)
    first = ((at_pipe * dps + at_dp) * per_piece + lax.rem(at_block, per_piece)) * capacity
    slot = jnp.where(routed > 0.0, within + first, -1)
    ids = lax.broadcasted_iota(jnp.int32, (slots, token_count), 0)
    for e in range(experts):
        hit = slot[e : e + 1] == ids
        picker[e] = jnp.where(hit, 1.0, 0.0).astype(BF)
        weights[e] = jnp.sum(jnp.where(hit, weight[e : e + 1], 0.0), axis=1, keepdims=True)
    for copy in copies:
        copy.wait()


def prepare(place, routes, shares, gate, up, ranks, dps, pipes, block, experts):
    assert experts <= 8
    capacity = block // 2
    token_count = block * ranks
    slots = capacity * ranks
    return pl.pallas_call(
        functools.partial(prepare_kernel, ranks, capacity, dps, pipes),
        in_specs=[scalars(), in_hbm(), in_hbm(), in_hbm(), in_hbm()],
        out_specs=(whole(), whole(), whole(), whole()),
        out_shape=(
            jax.ShapeDtypeStruct((experts, slots, token_count), BF),
            jax.ShapeDtypeStruct((experts, slots, 1), F32),
            pltpu.VMEM(gate.shape, BF),
            pltpu.VMEM(up.shape, BF),
        ),
        scratch_shapes=[
            pltpu.VMEM(routes.shape, routes.dtype),
            pltpu.VMEM(shares.shape, shares.dtype),
            pltpu.SemaphoreType.DMA((2, 8)),
            pltpu.SemaphoreType.DMA((2,)),
        ],
        compiler_params=pltpu.CompilerParams(vmem_limit_bytes=8 * 1024 * 1024),
        cost_estimate=pl.CostEstimate(
            flops=0, bytes_accessed=4 * gate.size, transcendentals=0
        ),
    )(place, far(routes), far(shares), far(gate), far(up))


def residual_kernel(ranks, *refs):
    student = refs[0][...].astype(F32)
    target = refs[ranks][...].astype(F32)
    for i in range(1, ranks):
        student = student + refs[i][...].astype(F32)
        target = target + refs[ranks + i][...].astype(F32)
    refs[-2][...] = student.astype(BF)
    refs[-1][...] = (student - target).astype(BF)


def residual_of(student, target, before):
    ranks = len(student)
    block = jax.ShapeDtypeStruct(student[0].shape, BF)
    return pl.pallas_call(
        functools.partial(residual_kernel, ranks),
        in_specs=[whole()] * (2 * ranks) + [anywhere()] * len(before),
        out_specs=(whole(), whole()),
        out_shape=(block, block),
        compiler_params=pltpu.CompilerParams(vmem_limit_bytes=4 * 1024 * 1024),
    )(*student, *target, *before)


def tile_of(size):
    return 256 if size % 256 == 0 else 128


def teacher_kernel(first, size, dps, pipes, place, tokens, gate, up, keep, send):
    dp, pipe = place[1], place[2]
    rows = tokens.shape[0] // (dps * pipes)
    half = dps * rows
    parts = []
    for j1 in range(pipes):
        for j0 in range(dps):
            piece = lax.rem(pipe + j1, pipes) * dps + lax.rem(dp + j0, dps)
            parts.append(tokens[pl.ds(pl.multiple_of(piece * rows, rows), rows), :])
    ordered = jnp.concatenate(parts, axis=0)
    tile = tile_of(size)
    for which, weight in enumerate((gate, up)):
        for i in range(size // tile):
            product = dot(ordered, weight[:, first + i * tile : first + (i + 1) * tile]).astype(BF)
            keep[which, :, i * tile : (i + 1) * tile] = product[:half]
            send[which, :, i * tile : (i + 1) * tile] = product[half:]


def teacher_pre(place, tokens, gate, up, first, size, dps, pipes):
    token_count, width = tokens.shape
    half = jax.ShapeDtypeStruct((2, token_count // pipes, size), BF)
    return pl.pallas_call(
        functools.partial(teacher_kernel, first, size, dps, pipes),
        in_specs=[scalars(), whole(), whole(), whole()],
        out_specs=(whole(), whole()),
        out_shape=(half, half),
        compiler_params=pltpu.CompilerParams(vmem_limit_bytes=8 * 1024 * 1024),
        cost_estimate=pl.CostEstimate(
            flops=4 * token_count * width * size, bytes_accessed=4 * width * size, transcendentals=0
        ),
    )(place, tokens, gate, up)


def expert_kernel(first, picker, tokens, gate, up, before, keep, send, held, sems):
    half = keep.shape[2]
    count = keep.shape[0]
    pieces = sems.shape[2]
    rows_each = gate.shape[0] // pieces
    copies = {}
    for i in range(count):
        for which, weight in enumerate((gate, up)):
            for p in range(pieces):
                part = pl.ds(p * rows_each, rows_each)
                columns = pl.ds((first + i) * H, H)
                copies[i, which, p] = pltpu.make_async_copy(
                    weight.at[part, columns], held.at[i, which, part], sems.at[i, which, p]
                )
                copies[i, which, p].start()
    for i in range(count):
        rows = dot(picker[first + i], tokens[...]).astype(BF)
        for which in range(2):
            for p in range(pieces):
                copies[i, which, p].wait()
            product = dot(rows, held[i, which]).astype(BF)
            keep[i, which] = product[:half]
            send[i, which] = product[half:]


def expert_pre(picker, tokens, gate, up, before, first, count):
    slots = picker.shape[1]
    width = tokens.shape[1]
    halves = jax.ShapeDtypeStruct((count, 2, slots // 2, H), BF)
    return pl.pallas_call(
        functools.partial(expert_kernel, first),
        in_specs=[whole(), whole(), in_hbm(), in_hbm(), anywhere()],
        out_specs=(whole(), whole()),
        out_shape=(halves, halves),
        scratch_shapes=[
            pltpu.VMEM((count, 2, width, H), BF),
            pltpu.SemaphoreType.DMA((count, 2, 4)),
        ],
        compiler_params=pltpu.CompilerParams(vmem_limit_bytes=16 * 1024 * 1024),
        cost_estimate=pl.CostEstimate(
            flops=count * 4 * slots * width * H,
            bytes_accessed=count * 4 * width * H,
            transcendentals=0,
        ),
    )(picker, tokens, far(gate), far(up), before)


def hidden_act_kernel(first, swap, mine, other, weight, pre, out):
    count, _, rows = mine.shape[:3]
    for i in range(count):
        totals = []
        for which in range(2):
            total = mine[i, which].astype(F32)
            if swap:
                theirs = other[i, which].astype(F32)
                total = total + jnp.concatenate([theirs[rows // 2 :], theirs[: rows // 2]], axis=0)
            pre[i, which] = total
            totals.append(total)
        gate, up = totals
        out[i] = (gate * jax.nn.sigmoid(gate) * up * weight[first + i, :rows]).astype(BF)


def hidden_act(mine, other, swap, weight, first):
    count, _, rows, width = mine.shape
    return pl.pallas_call(
        functools.partial(hidden_act_kernel, first, swap),
        in_specs=[whole(), whole(), whole()],
        out_specs=(whole(), whole()),
        out_shape=(
            jax.ShapeDtypeStruct(mine.shape, F32),
            jax.ShapeDtypeStruct((count, rows, width), BF),
        ),
        compiler_params=pltpu.CompilerParams(vmem_limit_bytes=8 * 1024 * 1024),
    )(mine, other, weight)


def join_kernel(dps, pipes, place, *refs):
    out = refs[-1]
    dp, pipe = place[1], place[2]
    rows = out.shape[0] // (dps * pipes)
    at = 0
    for i in range((len(refs) - 1) // 2):
        size = refs[2 * i].shape[1]
        for j1 in range(pipes):
            for j0 in range(dps):
                piece = lax.rem(pipe + j1, pipes) * dps + lax.rem(dp + j0, dps)
                target = pl.ds(pl.multiple_of(piece * rows, rows), rows)
                out[target, at : at + size] = refs[2 * i + j1][j0 * rows : (j0 + 1) * rows, :]
        at += size


def join(place, parts, dps, pipes):
    assert pipes == 2
    flat = [value for pair in parts for value in pair]
    rows = flat[0].shape[0] * pipes
    width = sum(pair[0].shape[1] for pair in parts)
    return pl.pallas_call(
        functools.partial(join_kernel, dps, pipes),
        in_specs=[scalars()] + [whole()] * len(flat),
        out_specs=whole(),
        out_shape=jax.ShapeDtypeStruct((rows, width), BF),
        compiler_params=pltpu.CompilerParams(vmem_limit_bytes=8 * 1024 * 1024),
    )(place, *flat)


def spread_kernel(picker, hidden, out):
    for e in range(picker.shape[0]):
        out[:, e * H : (e + 1) * H] = dot(picker[e], hidden[e], 0, 0).astype(BF)


def spread(picker, hidden):
    count, slots, token_count = picker.shape
    return pl.pallas_call(
        spread_kernel,
        in_specs=[whole(), whole()],
        out_specs=whole(),
        out_shape=jax.ShapeDtypeStruct((token_count, count * H), BF),
        compiler_params=pltpu.CompilerParams(vmem_limit_bytes=8 * 1024 * 1024),
    )(picker, hidden)


def flip_kernel(dense, tokens, before, dense_out, tokens_out):
    dense_out[...] = dense[...].astype(F32).T.astype(BF)
    tokens_out[...] = tokens[...].astype(F32).T.astype(BF)


def flip(dense, tokens, before):
    return pl.pallas_call(
        flip_kernel,
        in_specs=[whole(), whole(), anywhere()],
        out_specs=(whole(), whole()),
        out_shape=(
            jax.ShapeDtypeStruct(dense.shape[::-1], BF),
            jax.ShapeDtypeStruct(tokens.shape[::-1], BF),
        ),
        compiler_params=pltpu.CompilerParams(vmem_limit_bytes=16 * 1024 * 1024),
    )(dense, tokens, before)


def hidden_grad_kernel(first, picker, residual, down, before, keep, send):
    half = keep.shape[1]
    for i in range(keep.shape[0]):
        e = first + i
        rows = dot(picker[e], residual[...]).astype(BF)
        product = dot(down[e * H : (e + 1) * H, :], rows, 1, 1).T.astype(BF)
        keep[i] = product[:half]
        send[i] = product[half:]


def hidden_grad_parts(picker, residual, down, before, first, count):
    slots = picker.shape[1]
    halves = jax.ShapeDtypeStruct((count, slots // 2, H), BF)
    return pl.pallas_call(
        functools.partial(hidden_grad_kernel, first),
        in_specs=[whole(), whole(), whole(), anywhere()],
        out_specs=(whole(), whole()),
        out_shape=(halves, halves),
        compiler_params=pltpu.CompilerParams(vmem_limit_bytes=8 * 1024 * 1024),
    )(picker, residual, down, before)


def hidden_grad_act_kernel(first, swap, mine, other, pre, weight, before, out):
    count, rows = mine.shape[:2]
    for i in range(count):
        total = mine[i].astype(F32)
        if swap:
            flipped = jnp.concatenate([other[i, rows // 2 :], other[i, : rows // 2]], axis=0)
            total = total + flipped.astype(F32)
        total = total * weight[first + i, :rows]
        pre_gate, pre_up = pre[i, 0], pre[i, 1]
        sig = jax.nn.sigmoid(pre_gate)
        gate_grad = total * pre_up * sig * (1.0 + pre_gate * (1.0 - sig))
        up_grad = total * pre_gate * sig
        out[i, 0] = gate_grad.astype(BF)
        out[i, 1] = up_grad.astype(BF)


def hidden_grad_act(mine, other, swap, pre, weight, before, first):
    count, rows, width = mine.shape
    return pl.pallas_call(
        functools.partial(hidden_grad_act_kernel, first, swap),
        in_specs=[whole(), whole(), whole(), whole(), anywhere()],
        out_specs=whole(),
        out_shape=jax.ShapeDtypeStruct((count, 2, rows, width), BF),
        compiler_params=pltpu.CompilerParams(vmem_limit_bytes=8 * 1024 * 1024),
    )(mine, other, pre, weight, before)


def down_grad_kernel(first, hidden, residual, before, *rest):
    out, done, held, sems = rest[-4:]
    tiles = sems.shape[0]
    rows = H // 2
    copies = []
    for i in range(tiles):
        here = pl.ds(i * rows, rows)
        part = pl.ds(first * H + i * rows, rows)
        held[here, :] = dot(hidden[part, :], residual[...]).astype(BF)
        copies.append(pltpu.make_async_copy(held.at[here], out.at[part], sems.at[i]))
        copies[-1].start()
    done[...] = jnp.zeros_like(done)
    for copy in copies:
        copy.wait()


def down_grad(hidden, residual, before, first, count, so_far):
    rows, token_count = hidden.shape
    width = residual.shape[1]
    extra = () if so_far is None else (so_far,)
    return pl.pallas_call(
        functools.partial(down_grad_kernel, first),
        in_specs=[whole(), whole(), anywhere()] + [in_hbm()] * len(extra),
        out_specs=(in_hbm(), whole()),
        out_shape=(
            jax.ShapeDtypeStruct((rows, width), BF),
            jax.ShapeDtypeStruct((8, 128), F32),
        ),
        scratch_shapes=[
            pltpu.VMEM((count * H, width), BF),
            pltpu.SemaphoreType.DMA((2 * count,)),
        ],
        input_output_aliases={3: 0} if extra else {},
        compiler_params=pltpu.CompilerParams(vmem_limit_bytes=16 * 1024 * 1024),
        cost_estimate=pl.CostEstimate(
            flops=2 * count * H * width * token_count,
            bytes_accessed=2 * count * H * width,
            transcendentals=0,
        ),
    )(hidden, residual, before, *[far(value) for value in extra])


def input_grad_kernel(first, picker, tokens, mine, theirs, *rest):
    outs, held, sems = rest[-4:-2], rest[-2], rest[-1]
    count = mine.shape[0]
    splits = sems.shape[2]
    rows = tokens.shape[0] // splits
    copies = []
    for i in range(count):
        for which in range(2):
            grad = jnp.concatenate([mine[i, which], theirs[i, which]], axis=0)
            dense = dot(picker[first + i], grad, 0, 0).astype(BF)
            for r in range(splits):
                part = pl.ds(r * rows, rows)
                columns = pl.ds((first + i) * H, H)
                held[i, which, part] = dot(tokens[part, :], dense).astype(BF)
                copies.append(
                    pltpu.make_async_copy(
                        held.at[i, which, part], outs[which].at[part, columns], sems.at[i, which, r]
                    )
                )
                copies[-1].start()
    for copy in copies:
        copy.wait()


def input_grads(picker, tokens, mine, theirs, first, so_far):
    experts, slots, token_count = picker.shape
    width = tokens.shape[0]
    count = mine.shape[0]
    out = jax.ShapeDtypeStruct((width, experts * H), BF)
    extra = () if so_far is None else so_far
    return pl.pallas_call(
        functools.partial(input_grad_kernel, first),
        in_specs=[whole()] * 4 + [in_hbm()] * len(extra),
        out_specs=(in_hbm(), in_hbm()),
        out_shape=(out, out),
        scratch_shapes=[
            pltpu.VMEM((count, 2, width, H), BF),
            pltpu.SemaphoreType.DMA((count, 2, 2)),
        ],
        input_output_aliases={4 + i: i for i in range(len(extra))},
        compiler_params=pltpu.CompilerParams(vmem_limit_bytes=16 * 1024 * 1024),
        cost_estimate=pl.CostEstimate(
            flops=count * 4 * token_count * width * H,
            bytes_accessed=count * 4 * width * H,
            transcendentals=0,
        ),
    )(picker, tokens, mine, theirs, *[far(value) for value in extra])


def add(a, b):
    return (a.astype(F32) + b.astype(F32)).astype(BF)


def split_rows(value, count):
    rows = value.shape[-2] // count
    return [value[..., i * rows : (i + 1) * rows, :] for i in range(count)]


def scatter_dp(value, count):
    pieces = split_rows(value, count)
    total = pieces[0].astype(F32)
    for s in range(1, count):
        total = total + shift(pieces[s], "dp", count, s).astype(F32)
    return total


def gather_dp_parts(value, count):
    return [value] + [shift(value, "dp", count, -s) for s in range(1, count)]


def gather_dp(value, count):
    return jnp.concatenate(gather_dp_parts(value, count), axis=-2)


def exchange_dp(value, count):
    if count == 2:
        return value, shift(value, "dp", count, 1)
    total = gather_dp(scatter_dp(value, count).astype(BF), count)
    return total, total


def body(
    tokens,
    routes,
    gate_weights,
    teacher_gate,
    teacher_up,
    teacher_down,
    expert_gate,
    expert_up,
    expert_down,
):
    ranks = lax.axis_size("expert")
    dps = lax.axis_size("dp")
    pipes = lax.axis_size("pipe")
    rank = lax.axis_index("expert")
    dp = lax.axis_index("dp")
    pipe = lax.axis_index("pipe")
    block, width = tokens.shape
    token_count = block * ranks
    experts = expert_gate.shape[1] // H
    slots = block // 2 * ranks
    place = jnp.stack([rank, dp, pipe]).astype(jnp.int32)

    paired = ranks & (ranks - 1) == 0

    def to_partner(value, s):
        if paired:
            return lax.ppermute(value, "expert", [(i, i ^ s) for i in range(ranks)])
        return shift(value, "expert", ranks, s)

    def target_of(s):
        return rank ^ s if paired else (rank + s) % ranks

    def source_of(s):
        return rank ^ s if paired else (rank + ranks - s) % ranks

    def gather_tokens(mine):
        whole_rows = jnp.zeros((token_count, mine.shape[1]), BF)
        whole_rows = lax.dynamic_update_slice(whole_rows, mine, (rank * block, 0))
        for s in range(1, ranks):
            theirs = to_partner(mine, s)
            whole_rows = lax.dynamic_update_slice(whole_rows, theirs, (source_of(s) * block, 0))
        return whole_rows

    def to_owners(product):
        def block_of(r):
            return lax.dynamic_slice_in_dim(product, r * block, block, axis=0)

        return [block_of(rank)] + [to_partner(block_of(target_of(s)), s) for s in range(1, ranks)]

    base = gather_tokens(tokens)
    picker, slot_weight, gate_near, up_near = prepare(
        place, routes.T, gate_weights.T, teacher_gate, teacher_up, ranks, dps, pipes, block, experts
    )

    chunks = 2 if teacher_gate.shape[1] % 512 == 0 else 1
    size = teacher_gate.shape[1] // chunks
    halves = []
    for i in range(chunks):
        keep, send = teacher_pre(place, base, gate_near, up_near, i * size, size, dps, pipes)
        halves.append(add(keep, shift(send, "pipe", pipes, 1)))

    group = 2 if experts % 2 == 0 else 1
    firsts = range(0, experts, group)
    parts = []
    last = halves[-1]
    for first in firsts:
        keep, send = expert_pre(picker, base, expert_gate, expert_up, last, first, group)
        last = keep
        parts.append((keep, shift(send, "pipe", pipes, 1)))
    hiddens = []
    for half in halves:
        total = scatter_dp(half, dps)
        hidden = (jax.nn.silu(total[0]) * total[1]).astype(BF)
        hidden = jnp.concatenate(gather_dp_parts(hidden, dps), axis=0)
        hiddens.append((hidden, shift(hidden, "pipe", pipes, 1)))
    hidden = join(place, hiddens, dps, pipes)
    target = to_owners(jnp.dot(hidden, teacher_down, preferred_element_type=F32).astype(BF))

    pre, weighted = [], []
    for first, (keep, theirs) in zip(firsts, parts):
        mine, other = exchange_dp(add(keep, theirs), dps)
        total, part = hidden_act(mine, other, dps == 2, slot_weight, first)
        pre.append(total)
        weighted.append(jnp.concatenate([part, shift(part, "pipe", pipes, 1)], axis=1))
    weighted = jnp.concatenate(weighted, axis=0)

    dense = spread(picker, weighted)
    product = jnp.dot(dense, expert_down, preferred_element_type=F32).astype(BF)
    student = to_owners(product)
    dense_flipped, base_flipped = flip(dense, base, product)
    student_out, residual = residual_of(student, target, (base_flipped,))
    residual = gather_tokens(residual)

    sums = []
    last = residual
    for first in firsts:
        keep, send = hidden_grad_parts(picker, residual, expert_down, last, first, group)
        last = keep
        sums.append(add(keep, shift(send, "pipe", pipes, 1)))
    pairs = [exchange_dp(value, dps) for value in sums]
    grads = None
    grad_down = None
    last = sums[-1]
    activations = []
    for i, first in enumerate(firsts):
        grad_down, done = down_grad(dense_flipped, residual, last, first, group, grad_down)
        last = hidden_grad_act(*pairs[i], dps == 2, pre[i], slot_weight, done, first)
        activations.append((last, shift(last, "pipe", pipes, 1)))
    for (mine, theirs), first in zip(activations, firsts):
        grads = input_grads(picker, base_flipped, mine, theirs, first, grads)
    return (student_out, grads[0], grads[1], grad_down)


def solution(mesh):
    placed = (
        P(("groups", "expert"), ("dp", "pipe")),
        P("groups", None),
        P("groups", None),
        P(("dp", "pipe"), "expert"),
        P(("dp", "pipe"), "expert"),
        P("expert", ("dp", "pipe")),
        P(("dp", "pipe"), "expert"),
        P(("dp", "pipe"), "expert"),
        P("expert", ("dp", "pipe")),
    )
    return jax.shard_map(
        body,
        mesh=mesh,
        in_specs=placed,
        out_specs=(
            P(("groups", "expert"), ("dp", "pipe")),
            P(("groups", "dp", "pipe"), "expert"),
            P(("groups", "dp", "pipe"), "expert"),
            P(("groups", "expert"), ("dp", "pipe")),
        ),
        check_vma=False,
    )
```

```python
import functools

import jax
import jax.numpy as jnp
from jax import lax
from jax.experimental import pallas as pl
from jax.experimental.pallas import tpu as pltpu
from jax.sharding import PartitionSpec as P

H = 896
BF = jnp.bfloat16
F32 = jnp.float32


def shift(value, axis, count, by):
    return lax.ppermute(value, axis, [(i, (i + by) % count) for i in range(count)])


def dot(a, b, contract_a=1, contract_b=0):
    return lax.dot_general(
        a, b, (((contract_a,), (contract_b,)), ((), ())), preferred_element_type=F32
    )


def whole():
    return pl.BlockSpec(memory_space=pltpu.VMEM)


def in_hbm():
    return pl.BlockSpec(memory_space=pltpu.HBM)


def anywhere():
    return pl.BlockSpec(memory_space=pl.ANY)


def scalars():
    return pl.BlockSpec(memory_space=pltpu.SMEM)


def load_start(pairs, sems, pieces):
    copies = []
    for which, (source, target) in enumerate(pairs):
        rows = source.shape[0] // pieces
        for i in range(pieces):
            part = pl.ds(i * rows, rows)
            copies.append(
                pltpu.make_async_copy(source.at[part], target.at[part], sems.at[which, i])
            )
    for copy in copies:
        copy.start()
    return copies


def far(value):
    return pltpu.with_memory_space_constraint(value, pltpu.HBM)


def prepare_kernel(
    ranks,
    capacity,
    dps,
    pipes,
    place,
    far_routes,
    far_shares,
    gate,
    up,
    picker,
    weights,
    gate_out,
    up_out,
    routes,
    shares,
    sems,
    table_sems,
):
    tables = [
        pltpu.make_async_copy(far_routes, routes, table_sems.at[0]),
        pltpu.make_async_copy(far_shares, shares, table_sems.at[1]),
    ]
    for copy in tables:
        copy.start()
    copies = load_start(((gate, gate_out), (up, up_out)), sems, 8)
    for copy in tables:
        copy.wait()
    rank, dp, pipe = place[0], place[1], place[2]
    experts, slots, token_count = picker.shape
    block = token_count // ranks
    per_piece = ranks // (dps * pipes)
    row = lax.broadcasted_iota(jnp.int32, (8, token_count), 0)
    names = row + rank * experts
    weight = jnp.zeros((8, token_count), F32)
    routed = jnp.zeros((8, token_count), F32)
    for k in range(routes.shape[0]):
        hit = (routes[k : k + 1, :] == names) & (row < experts)
        weight = weight + jnp.where(hit, shares[k : k + 1, :], 0.0)
        routed = routed + jnp.where(hit, 1.0, 0.0)
    t_from = lax.broadcasted_iota(jnp.int32, (token_count, token_count), 0)
    t_to = lax.broadcasted_iota(jnp.int32, (token_count, token_count), 1)
    earlier = jnp.where((t_from // block == t_to // block) & (t_from < t_to), 1.0, 0.0)
    within = dot(routed.astype(BF), earlier.astype(BF)).astype(jnp.int32)
    at_block = lax.broadcasted_iota(jnp.int32, (1, token_count), 1) // block
    at_pipe = lax.rem(at_block // (dps * per_piece) + pipes - pipe, pipes)
    at_dp = lax.rem(lax.rem(at_block // per_piece, dps) + dps - dp, dps)
    first = ((at_pipe * dps + at_dp) * per_piece + lax.rem(at_block, per_piece)) * capacity
    slot = jnp.where(routed > 0.0, within + first, -1)
    ids = lax.broadcasted_iota(jnp.int32, (slots, token_count), 0)
    for e in range(experts):
        hit = slot[e : e + 1] == ids
        picker[e] = jnp.where(hit, 1.0, 0.0).astype(BF)
        weights[e] = jnp.sum(jnp.where(hit, weight[e : e + 1], 0.0), axis=1, keepdims=True)
    for copy in copies:
        copy.wait()


def prepare(place, routes, shares, gate, up, ranks, dps, pipes, block, experts):
    assert experts <= 8
    capacity = block // 2
    token_count = block * ranks
    slots = capacity * ranks
    return pl.pallas_call(
        functools.partial(prepare_kernel, ranks, capacity, dps, pipes),
        in_specs=[scalars(), in_hbm(), in_hbm(), in_hbm(), in_hbm()],
        out_specs=(whole(), whole(), whole(), whole()),
        out_shape=(
            jax.ShapeDtypeStruct((experts, slots, token_count), BF),
            jax.ShapeDtypeStruct((experts, slots, 1), F32),
            pltpu.VMEM(gate.shape, BF),
            pltpu.VMEM(up.shape, BF),
        ),
        scratch_shapes=[
            pltpu.VMEM(routes.shape, routes.dtype),
            pltpu.VMEM(shares.shape, shares.dtype),
            pltpu.SemaphoreType.DMA((2, 8)),
            pltpu.SemaphoreType.DMA((2,)),
        ],
        compiler_params=pltpu.CompilerParams(vmem_limit_bytes=8 * 1024 * 1024),
        cost_estimate=pl.CostEstimate(
            flops=0, bytes_accessed=4 * gate.size, transcendentals=0
        ),
    )(place, far(routes), far(shares), far(gate), far(up))


def residual_kernel(ranks, *refs):
    student = refs[0][...].astype(F32)
    target = refs[ranks][...].astype(F32)
    for i in range(1, ranks):
        student = student + refs[i][...].astype(F32)
        target = target + refs[ranks + i][...].astype(F32)
    refs[-2][...] = student.astype(BF)
    refs[-1][...] = (student - target).astype(BF)


def residual_of(student, target, before):
    ranks = len(student)
    block = jax.ShapeDtypeStruct(student[0].shape, BF)
    return pl.pallas_call(
        functools.partial(residual_kernel, ranks),
        in_specs=[whole()] * (2 * ranks) + [anywhere()] * len(before),
        out_specs=(whole(), whole()),
        out_shape=(block, block),
        compiler_params=pltpu.CompilerParams(vmem_limit_bytes=4 * 1024 * 1024),
    )(*student, *target, *before)


def tile_of(size):
    return 256 if size % 256 == 0 else 128


def teacher_kernel(first, size, dps, pipes, place, tokens, gate, up, keep, send):
    dp, pipe = place[1], place[2]
    rows = tokens.shape[0] // (dps * pipes)
    half = dps * rows
    parts = []
    for j1 in range(pipes):
        for j0 in range(dps):
            piece = lax.rem(pipe + j1, pipes) * dps + lax.rem(dp + j0, dps)
            parts.append(tokens[pl.ds(pl.multiple_of(piece * rows, rows), rows), :])
    ordered = jnp.concatenate(parts, axis=0)
    tile = tile_of(size)
    for which, weight in enumerate((gate, up)):
        for i in range(size // tile):
            product = dot(ordered, weight[:, first + i * tile : first + (i + 1) * tile]).astype(BF)
            keep[which, :, i * tile : (i + 1) * tile] = product[:half]
            send[which, :, i * tile : (i + 1) * tile] = product[half:]


def teacher_pre(place, tokens, gate, up, first, size, dps, pipes):
    token_count, width = tokens.shape
    half = jax.ShapeDtypeStruct((2, token_count // pipes, size), BF)
    return pl.pallas_call(
        functools.partial(teacher_kernel, first, size, dps, pipes),
        in_specs=[scalars(), whole(), whole(), whole()],
        out_specs=(whole(), whole()),
        out_shape=(half, half),
        compiler_params=pltpu.CompilerParams(vmem_limit_bytes=8 * 1024 * 1024),
        cost_estimate=pl.CostEstimate(
            flops=4 * token_count * width * size, bytes_accessed=4 * width * size, transcendentals=0
        ),
    )(place, tokens, gate, up)


def expert_kernel(first, picker, tokens, gate, up, before, keep, send, held, sems):
    half = keep.shape[2]
    count = keep.shape[0]
    pieces = sems.shape[2]
    rows_each = gate.shape[0] // pieces
    copies = {}
    for i in range(count):
        for which, weight in enumerate((gate, up)):
            for p in range(pieces):
                part = pl.ds(p * rows_each, rows_each)
                columns = pl.ds((first + i) * H, H)
                copies[i, which, p] = pltpu.make_async_copy(
                    weight.at[part, columns], held.at[i, which, part], sems.at[i, which, p]
                )
                copies[i, which, p].start()
    for i in range(count):
        rows = dot(picker[first + i], tokens[...]).astype(BF)
        for which in range(2):
            for p in range(pieces):
                copies[i, which, p].wait()
            product = dot(rows, held[i, which]).astype(BF)
            keep[i, which] = product[:half]
            send[i, which] = product[half:]


def expert_pre(picker, tokens, gate, up, before, first, count):
    slots = picker.shape[1]
    width = tokens.shape[1]
    halves = jax.ShapeDtypeStruct((count, 2, slots // 2, H), BF)
    return pl.pallas_call(
        functools.partial(expert_kernel, first),
        in_specs=[whole(), whole(), in_hbm(), in_hbm(), anywhere()],
        out_specs=(whole(), whole()),
        out_shape=(halves, halves),
        scratch_shapes=[
            pltpu.VMEM((count, 2, width, H), BF),
            pltpu.SemaphoreType.DMA((count, 2, 4)),
        ],
        compiler_params=pltpu.CompilerParams(vmem_limit_bytes=16 * 1024 * 1024),
        cost_estimate=pl.CostEstimate(
            flops=count * 4 * slots * width * H,
            bytes_accessed=count * 4 * width * H,
            transcendentals=0,
        ),
    )(picker, tokens, far(gate), far(up), before)


def hidden_act_kernel(first, swap, mine, other, weight, *rest):
    pre, out = rest[-2:]
    count, _, rows = mine.shape[:3]
    for i in range(count):
        totals = []
        for which in range(2):
            total = mine[i, which].astype(F32)
            if swap:
                theirs = other[i, which].astype(F32)
                total = total + jnp.concatenate([theirs[rows // 2 :], theirs[: rows // 2]], axis=0)
            pre[i, which] = total
            totals.append(total)
        gate, up = totals
        out[i] = (gate * jax.nn.sigmoid(gate) * up * weight[first + i, :rows]).astype(BF)


def hidden_act(mine, other, swap, weight, before, first):
    count, _, rows, width = mine.shape
    return pl.pallas_call(
        functools.partial(hidden_act_kernel, first, swap),
        in_specs=[whole(), whole(), whole()] + [anywhere()] * len(before),
        out_specs=(whole(), whole()),
        out_shape=(
            jax.ShapeDtypeStruct(mine.shape, F32),
            jax.ShapeDtypeStruct((count, rows, width), BF),
        ),
        compiler_params=pltpu.CompilerParams(vmem_limit_bytes=8 * 1024 * 1024),
    )(mine, other, weight, *before)


def join_kernel(dps, pipes, place, *refs):
    out = refs[-1]
    dp, pipe = place[1], place[2]
    rows = out.shape[0] // (dps * pipes)
    at = 0
    for i in range((len(refs) - 1) // 2):
        size = refs[2 * i].shape[1]
        for j1 in range(pipes):
            for j0 in range(dps):
                piece = lax.rem(pipe + j1, pipes) * dps + lax.rem(dp + j0, dps)
                target = pl.ds(pl.multiple_of(piece * rows, rows), rows)
                out[target, at : at + size] = refs[2 * i + j1][j0 * rows : (j0 + 1) * rows, :]
        at += size


def join(place, parts, dps, pipes):
    assert pipes == 2
    flat = [value for pair in parts for value in pair]
    rows = flat[0].shape[0] * pipes
    width = sum(pair[0].shape[1] for pair in parts)
    return pl.pallas_call(
        functools.partial(join_kernel, dps, pipes),
        in_specs=[scalars()] + [whole()] * len(flat),
        out_specs=whole(),
        out_shape=jax.ShapeDtypeStruct((rows, width), BF),
        compiler_params=pltpu.CompilerParams(vmem_limit_bytes=8 * 1024 * 1024),
    )(place, *flat)


def spread_kernel(picker, hidden, out):
    for e in range(picker.shape[0]):
        out[:, e * H : (e + 1) * H] = dot(picker[e], hidden[e], 0, 0).astype(BF)


def spread(picker, hidden):
    count, slots, token_count = picker.shape
    return pl.pallas_call(
        spread_kernel,
        in_specs=[whole(), whole()],
        out_specs=whole(),
        out_shape=jax.ShapeDtypeStruct((token_count, count * H), BF),
        compiler_params=pltpu.CompilerParams(vmem_limit_bytes=8 * 1024 * 1024),
    )(picker, hidden)


def flip_kernel(dense, tokens, before, dense_out, tokens_out):
    dense_out[...] = dense[...].astype(F32).T.astype(BF)
    tokens_out[...] = tokens[...].astype(F32).T.astype(BF)


def flip(dense, tokens, before):
    return pl.pallas_call(
        flip_kernel,
        in_specs=[whole(), whole(), anywhere()],
        out_specs=(whole(), whole()),
        out_shape=(
            jax.ShapeDtypeStruct(dense.shape[::-1], BF),
            jax.ShapeDtypeStruct(tokens.shape[::-1], BF),
        ),
        compiler_params=pltpu.CompilerParams(vmem_limit_bytes=16 * 1024 * 1024),
    )(dense, tokens, before)


def hidden_grad_kernel(first, picker, residual, down, before, keep, send):
    half = keep.shape[1]
    for i in range(keep.shape[0]):
        e = first + i
        rows = dot(picker[e], residual[...]).astype(BF)
        product = dot(down[e * H : (e + 1) * H, :], rows, 1, 1).T.astype(BF)
        keep[i] = product[:half]
        send[i] = product[half:]


def hidden_grad_parts(picker, residual, down, before, first, count):
    slots = picker.shape[1]
    halves = jax.ShapeDtypeStruct((count, slots // 2, H), BF)
    return pl.pallas_call(
        functools.partial(hidden_grad_kernel, first),
        in_specs=[whole(), whole(), whole(), anywhere()],
        out_specs=(whole(), whole()),
        out_shape=(halves, halves),
        compiler_params=pltpu.CompilerParams(vmem_limit_bytes=8 * 1024 * 1024),
    )(picker, residual, down, before)


def hidden_grad_act_kernel(first, swap, mine, other, pre, weight, before, out):
    count, rows = mine.shape[:2]
    for i in range(count):
        total = mine[i].astype(F32)
        if swap:
            flipped = jnp.concatenate([other[i, rows // 2 :], other[i, : rows // 2]], axis=0)
            total = total + flipped.astype(F32)
        total = total * weight[first + i, :rows]
        pre_gate, pre_up = pre[i, 0], pre[i, 1]
        sig = jax.nn.sigmoid(pre_gate)
        gate_grad = total * pre_up * sig * (1.0 + pre_gate * (1.0 - sig))
        up_grad = total * pre_gate * sig
        out[i, 0] = gate_grad.astype(BF)
        out[i, 1] = up_grad.astype(BF)


def hidden_grad_act(mine, other, swap, pre, weight, before, first):
    count, rows, width = mine.shape
    return pl.pallas_call(
        functools.partial(hidden_grad_act_kernel, first, swap),
        in_specs=[whole(), whole(), whole(), whole(), anywhere()],
        out_specs=whole(),
        out_shape=jax.ShapeDtypeStruct((count, 2, rows, width), BF),
        compiler_params=pltpu.CompilerParams(vmem_limit_bytes=8 * 1024 * 1024),
    )(mine, other, pre, weight, before)


def down_grad_kernel(hidden, residual, before, out, done, held, sems):
    tiles = sems.shape[0]
    rows = hidden.shape[0] // tiles
    copies = []
    for i in range(tiles):
        part = pl.ds(i * rows, rows)
        held[part, :] = dot(hidden[part, :], residual[...]).astype(BF)
        copies.append(pltpu.make_async_copy(held.at[part], out.at[part], sems.at[i]))
        copies[-1].start()
    done[...] = jnp.zeros_like(done)
    for copy in copies:
        copy.wait()


def down_grad(hidden, residual, before):
    rows, token_count = hidden.shape
    width = residual.shape[1]
    return pl.pallas_call(
        down_grad_kernel,
        in_specs=[whole(), whole(), anywhere()],
        out_specs=(in_hbm(), whole()),
        out_shape=(
            jax.ShapeDtypeStruct((rows, width), BF),
            jax.ShapeDtypeStruct((8, 128), F32),
        ),
        scratch_shapes=[
            pltpu.VMEM((rows, width), BF),
            pltpu.SemaphoreType.DMA((rows // (H // 2),)),
        ],
        compiler_params=pltpu.CompilerParams(vmem_limit_bytes=16 * 1024 * 1024),
        cost_estimate=pl.CostEstimate(
            flops=2 * rows * width * token_count,
            bytes_accessed=2 * rows * width,
            transcendentals=0,
        ),
    )(hidden, residual, before)


def input_grad_kernel(group, picker, tokens, *rest):
    outs, held, sems = rest[-4:-2], rest[-2], rest[-1]
    count = picker.shape[0]
    splits = sems.shape[2]
    rows = tokens.shape[0] // splits
    copies = []
    for i in range(count):
        for which in range(2):
            mine, theirs = rest[i // group * 2], rest[i // group * 2 + 1]
            grad = jnp.concatenate([mine[i % group, which], theirs[i % group, which]], axis=0)
            dense = dot(picker[i], grad, 0, 0).astype(BF)
            for r in range(splits):
                part = pl.ds(r * rows, rows)
                columns = pl.ds(i * H, H)
                held[i, which, part] = dot(tokens[part, :], dense).astype(BF)
                copies.append(
                    pltpu.make_async_copy(
                        held.at[i, which, part], outs[which].at[part, columns], sems.at[i, which, r]
                    )
                )
                copies[-1].start()
    for copy in copies:
        copy.wait()


def input_grads(picker, tokens, parts):
    count, slots, token_count = picker.shape
    width = tokens.shape[0]
    out = jax.ShapeDtypeStruct((width, count * H), BF)
    return pl.pallas_call(
        functools.partial(input_grad_kernel, count // len(parts)),
        in_specs=[whole()] * (2 + 2 * len(parts)),
        out_specs=(in_hbm(), in_hbm()),
        out_shape=(out, out),
        scratch_shapes=[
            pltpu.VMEM((count, 2, width, H), BF),
            pltpu.SemaphoreType.DMA((count, 2, 2)),
        ],
        compiler_params=pltpu.CompilerParams(vmem_limit_bytes=24 * 1024 * 1024),
        cost_estimate=pl.CostEstimate(
            flops=count * 4 * token_count * width * H,
            bytes_accessed=count * 4 * width * H,
            transcendentals=0,
        ),
    )(picker, tokens, *[value for pair in parts for value in pair])


def add(a, b):
    return (a.astype(F32) + b.astype(F32)).astype(BF)


def split_rows(value, count):
    rows = value.shape[-2] // count
    return [value[..., i * rows : (i + 1) * rows, :] for i in range(count)]


def scatter_dp(value, count):
    pieces = split_rows(value, count)
    total = pieces[0].astype(F32)
    for s in range(1, count):
        total = total + shift(pieces[s], "dp", count, s).astype(F32)
    return total


def gather_dp_parts(value, count):
    return [value] + [shift(value, "dp", count, -s) for s in range(1, count)]


def gather_dp(value, count):
    return jnp.concatenate(gather_dp_parts(value, count), axis=-2)


def exchange_dp(value, count):
    if count == 2:
        return value, shift(value, "dp", count, 1)
    total = gather_dp(scatter_dp(value, count).astype(BF), count)
    return total, total


def body(
    tokens,
    routes,
    gate_weights,
    teacher_gate,
    teacher_up,
    teacher_down,
    expert_gate,
    expert_up,
    expert_down,
):
    ranks = lax.axis_size("expert")
    dps = lax.axis_size("dp")
    pipes = lax.axis_size("pipe")
    rank = lax.axis_index("expert")
    dp = lax.axis_index("dp")
    pipe = lax.axis_index("pipe")
    block, width = tokens.shape
    token_count = block * ranks
    experts = expert_gate.shape[1] // H
    slots = block // 2 * ranks
    place = jnp.stack([rank, dp, pipe]).astype(jnp.int32)

    paired = ranks & (ranks - 1) == 0

    def to_partner(value, s):
        if paired:
            return lax.ppermute(value, "expert", [(i, i ^ s) for i in range(ranks)])
        return shift(value, "expert", ranks, s)

    def target_of(s):
        return rank ^ s if paired else (rank + s) % ranks

    def source_of(s):
        return rank ^ s if paired else (rank + ranks - s) % ranks

    def gather_tokens(mine):
        whole_rows = jnp.zeros((token_count, mine.shape[1]), BF)
        whole_rows = lax.dynamic_update_slice(whole_rows, mine, (rank * block, 0))
        for s in range(1, ranks):
            theirs = to_partner(mine, s)
            whole_rows = lax.dynamic_update_slice(whole_rows, theirs, (source_of(s) * block, 0))
        return whole_rows

    def to_owners(product):
        def block_of(r):
            return lax.dynamic_slice_in_dim(product, r * block, block, axis=0)

        return [block_of(rank)] + [to_partner(block_of(target_of(s)), s) for s in range(1, ranks)]

    base = gather_tokens(tokens)
    picker, slot_weight, gate_near, up_near = prepare(
        place, routes.T, gate_weights.T, teacher_gate, teacher_up, ranks, dps, pipes, block, experts
    )

    chunks = 2 if teacher_gate.shape[1] % 512 == 0 else 1
    size = teacher_gate.shape[1] // chunks
    halves = []
    for i in range(chunks):
        keep, send = teacher_pre(place, base, gate_near, up_near, i * size, size, dps, pipes)
        halves.append(add(keep, shift(send, "pipe", pipes, 1)))

    group = 2 if experts % 2 == 0 else 1
    firsts = range(0, experts, group)
    parts = []
    last = halves[-1]
    for first in firsts:
        keep, send = expert_pre(picker, base, expert_gate, expert_up, last, first, group)
        last = keep
        parts.append((keep, shift(send, "pipe", pipes, 1)))
    hiddens = []
    for half in halves:
        total = scatter_dp(half, dps)
        hidden = (jax.nn.silu(total[0]) * total[1]).astype(BF)
        hidden = jnp.concatenate(gather_dp_parts(hidden, dps), axis=0)
        hiddens.append((hidden, shift(hidden, "pipe", pipes, 1)))
    hidden = join(place, hiddens, dps, pipes)
    target = to_owners(jnp.dot(hidden, teacher_down, preferred_element_type=F32).astype(BF))

    pre, weighted = [], []
    for first, (keep, theirs) in zip(firsts, parts):
        mine, other = exchange_dp(add(keep, theirs), dps)
        total, part = hidden_act(mine, other, dps == 2, slot_weight, target[-2:], first)
        pre.append(total)
        weighted.append(jnp.concatenate([part, shift(part, "pipe", pipes, 1)], axis=1))
    weighted = jnp.concatenate(weighted, axis=0)

    dense = spread(picker, weighted)
    product = jnp.dot(dense, expert_down, preferred_element_type=F32).astype(BF)
    student = to_owners(product)
    dense_flipped, base_flipped = flip(dense, base, product)
    student_out, residual = residual_of(student, target, (base_flipped,))
    residual = gather_tokens(residual)

    sums = []
    last = residual
    for first in firsts:
        keep, send = hidden_grad_parts(picker, residual, expert_down, last, first, group)
        last = keep
        sums.append(add(keep, shift(send, "pipe", pipes, 1)))
    pairs = [exchange_dp(value, dps) for value in sums]
    grad_down, done = down_grad(dense_flipped, residual, sums[-1])
    activations = []
    for i, first in enumerate(firsts):
        mine = hidden_grad_act(*pairs[i], dps == 2, pre[i], slot_weight, done, first)
        activations.append((mine, shift(mine, "pipe", pipes, 1)))
    grads = input_grads(picker, base_flipped, activations)
    return (student_out, grads[0], grads[1], grad_down)


def solution(mesh):
    placed = (
        P(("groups", "expert"), ("dp", "pipe")),
        P("groups", None),
        P("groups", None),
        P(("dp", "pipe"), "expert"),
        P(("dp", "pipe"), "expert"),
        P("expert", ("dp", "pipe")),
        P(("dp", "pipe"), "expert"),
        P(("dp", "pipe"), "expert"),
        P("expert", ("dp", "pipe")),
    )
    return jax.shard_map(
        body,
        mesh=mesh,
        in_specs=placed,
        out_specs=(
            P(("groups", "expert"), ("dp", "pipe")),
            P(("groups", "dp", "pipe"), "expert"),
            P(("groups", "dp", "pipe"), "expert"),
            P(("groups", "expert"), ("dp", "pipe")),
        ),
        check_vma=False,
    )
```

```python
import functools

import jax
import jax.numpy as jnp
from jax import lax
from jax.experimental import pallas as pl
from jax.experimental.pallas import tpu as pltpu
from jax.sharding import PartitionSpec as P

H = 896
BF = jnp.bfloat16
F32 = jnp.float32


def shift(value, axis, count, by):
    return lax.ppermute(value, axis, [(i, (i + by) % count) for i in range(count)])


def dot(a, b, contract_a=1, contract_b=0):
    return lax.dot_general(
        a, b, (((contract_a,), (contract_b,)), ((), ())), preferred_element_type=F32
    )


def whole():
    return pl.BlockSpec(memory_space=pltpu.VMEM)


def in_hbm():
    return pl.BlockSpec(memory_space=pltpu.HBM)


def anywhere():
    return pl.BlockSpec(memory_space=pl.ANY)


def scalars():
    return pl.BlockSpec(memory_space=pltpu.SMEM)


def load_start(pairs, sems, pieces):
    copies = []
    for which, (source, target) in enumerate(pairs):
        rows = source.shape[0] // pieces
        for i in range(pieces):
            part = pl.ds(i * rows, rows)
            copies.append(
                pltpu.make_async_copy(source.at[part], target.at[part], sems.at[which, i])
            )
    for copy in copies:
        copy.start()
    return copies


def far(value):
    return pltpu.with_memory_space_constraint(value, pltpu.HBM)


def prepare_kernel(
    ranks,
    capacity,
    dps,
    pipes,
    place,
    far_routes,
    far_shares,
    gate,
    up,
    picker,
    weights,
    gate_out,
    up_out,
    routes,
    shares,
    sems,
    table_sems,
):
    tables = [
        pltpu.make_async_copy(far_routes, routes, table_sems.at[0]),
        pltpu.make_async_copy(far_shares, shares, table_sems.at[1]),
    ]
    for copy in tables:
        copy.start()
    copies = load_start(((gate, gate_out), (up, up_out)), sems, 8)
    for copy in tables:
        copy.wait()
    rank, dp, pipe = place[0], place[1], place[2]
    experts, slots, token_count = picker.shape
    block = token_count // ranks
    per_piece = ranks // (dps * pipes)
    row = lax.broadcasted_iota(jnp.int32, (8, token_count), 0)
    names = row + rank * experts
    weight = jnp.zeros((8, token_count), F32)
    routed = jnp.zeros((8, token_count), F32)
    for k in range(routes.shape[0]):
        hit = (routes[k : k + 1, :] == names) & (row < experts)
        weight = weight + jnp.where(hit, shares[k : k + 1, :], 0.0)
        routed = routed + jnp.where(hit, 1.0, 0.0)
    t_from = lax.broadcasted_iota(jnp.int32, (token_count, token_count), 0)
    t_to = lax.broadcasted_iota(jnp.int32, (token_count, token_count), 1)
    earlier = jnp.where((t_from // block == t_to // block) & (t_from < t_to), 1.0, 0.0)
    within = dot(routed.astype(BF), earlier.astype(BF)).astype(jnp.int32)
    at_block = lax.broadcasted_iota(jnp.int32, (1, token_count), 1) // block
    at_pipe = lax.rem(at_block // (dps * per_piece) + pipes - pipe, pipes)
    at_dp = lax.rem(lax.rem(at_block // per_piece, dps) + dps - dp, dps)
    first = ((at_pipe * dps + at_dp) * per_piece + lax.rem(at_block, per_piece)) * capacity
    slot = jnp.where(routed > 0.0, within + first, -1)
    ids = lax.broadcasted_iota(jnp.int32, (slots, token_count), 0)
    for e in range(experts):
        hit = slot[e : e + 1] == ids
        picker[e] = jnp.where(hit, 1.0, 0.0).astype(BF)
        weights[e] = jnp.sum(jnp.where(hit, weight[e : e + 1], 0.0), axis=1, keepdims=True)
    for copy in copies:
        copy.wait()


def prepare(place, routes, shares, gate, up, ranks, dps, pipes, block, experts):
    assert experts <= 8
    capacity = block // 2
    token_count = block * ranks
    slots = capacity * ranks
    return pl.pallas_call(
        functools.partial(prepare_kernel, ranks, capacity, dps, pipes),
        in_specs=[scalars(), in_hbm(), in_hbm(), in_hbm(), in_hbm()],
        out_specs=(whole(), whole(), whole(), whole()),
        out_shape=(
            jax.ShapeDtypeStruct((experts, slots, token_count), BF),
            jax.ShapeDtypeStruct((experts, slots, 1), F32),
            pltpu.VMEM(gate.shape, BF),
            pltpu.VMEM(up.shape, BF),
        ),
        scratch_shapes=[
            pltpu.VMEM(routes.shape, routes.dtype),
            pltpu.VMEM(shares.shape, shares.dtype),
            pltpu.SemaphoreType.DMA((2, 8)),
            pltpu.SemaphoreType.DMA((2,)),
        ],
        compiler_params=pltpu.CompilerParams(vmem_limit_bytes=8 * 1024 * 1024),
        cost_estimate=pl.CostEstimate(
            flops=0, bytes_accessed=4 * gate.size, transcendentals=0
        ),
    )(place, far(routes), far(shares), far(gate), far(up))


def residual_kernel(student_parts, target_parts, before, out, residual):
    student = student_parts[0].astype(F32)
    target = target_parts[0].astype(F32)
    for i in range(1, student_parts.shape[0]):
        student = student + student_parts[i].astype(F32)
        target = target + target_parts[i].astype(F32)
    out[...] = student.astype(BF)
    residual[...] = (student - target).astype(BF)


def residual_of(student, target, before):
    block = jax.ShapeDtypeStruct(student.shape[1:], BF)
    return pl.pallas_call(
        residual_kernel,
        in_specs=[whole(), whole(), anywhere()],
        out_specs=(whole(), whole()),
        out_shape=(block, block),
        compiler_params=pltpu.CompilerParams(vmem_limit_bytes=4 * 1024 * 1024),
    )(student, target, before)


def tile_of(size):
    return 256 if size % 256 == 0 else 128


def teacher_kernel(first, size, dps, pipes, place, tokens, gate, up, keep, send):
    dp, pipe = place[1], place[2]
    rows = tokens.shape[0] // (dps * pipes)
    half = dps * rows
    parts = []
    for j1 in range(pipes):
        for j0 in range(dps):
            piece = lax.rem(pipe + j1, pipes) * dps + lax.rem(dp + j0, dps)
            parts.append(tokens[pl.ds(pl.multiple_of(piece * rows, rows), rows), :])
    ordered = jnp.concatenate(parts, axis=0)
    tile = tile_of(size)
    for which, weight in enumerate((gate, up)):
        for i in range(size // tile):
            product = dot(ordered, weight[:, first + i * tile : first + (i + 1) * tile]).astype(BF)
            keep[which, :, i * tile : (i + 1) * tile] = product[:half]
            send[which, :, i * tile : (i + 1) * tile] = product[half:]


def teacher_pre(place, tokens, gate, up, first, size, dps, pipes):
    token_count, width = tokens.shape
    half = jax.ShapeDtypeStruct((2, token_count // pipes, size), BF)
    return pl.pallas_call(
        functools.partial(teacher_kernel, first, size, dps, pipes),
        in_specs=[scalars(), whole(), whole(), whole()],
        out_specs=(whole(), whole()),
        out_shape=(half, half),
        compiler_params=pltpu.CompilerParams(vmem_limit_bytes=8 * 1024 * 1024),
        cost_estimate=pl.CostEstimate(
            flops=4 * token_count * width * size, bytes_accessed=4 * width * size, transcendentals=0
        ),
    )(place, tokens, gate, up)


def expert_kernel(first, picker, tokens, gate, up, before, keep, send, held, sems):
    half = keep.shape[2]
    count = keep.shape[0]
    pieces = sems.shape[2]
    rows_each = gate.shape[0] // pieces
    copies = {}
    for i in range(count):
        for which, weight in enumerate((gate, up)):
            for p in range(pieces):
                part = pl.ds(p * rows_each, rows_each)
                columns = pl.ds((first + i) * H, H)
                copies[i, which, p] = pltpu.make_async_copy(
                    weight.at[part, columns], held.at[i, which, part], sems.at[i, which, p]
                )
                copies[i, which, p].start()
    for i in range(count):
        rows = dot(picker[first + i], tokens[...]).astype(BF)
        for which in range(2):
            for p in range(pieces):
                copies[i, which, p].wait()
            product = dot(rows, held[i, which]).astype(BF)
            keep[i, which] = product[:half]
            send[i, which] = product[half:]


def expert_pre(picker, tokens, gate, up, before, first, count):
    slots = picker.shape[1]
    width = tokens.shape[1]
    halves = jax.ShapeDtypeStruct((count, 2, slots // 2, H), BF)
    return pl.pallas_call(
        functools.partial(expert_kernel, first),
        in_specs=[whole(), whole(), in_hbm(), in_hbm(), anywhere()],
        out_specs=(whole(), whole()),
        out_shape=(halves, halves),
        scratch_shapes=[
            pltpu.VMEM((count, 2, width, H), BF),
            pltpu.SemaphoreType.DMA((count, 2, 4)),
        ],
        compiler_params=pltpu.CompilerParams(vmem_limit_bytes=16 * 1024 * 1024),
        cost_estimate=pl.CostEstimate(
            flops=count * 4 * slots * width * H,
            bytes_accessed=count * 4 * width * H,
            transcendentals=0,
        ),
    )(picker, tokens, far(gate), far(up), before)


def hidden_act_kernel(first, swap, mine, other, weight, *rest):
    pre, out = rest[-2:]
    count, _, rows = mine.shape[:3]
    for i in range(count):
        totals = []
        for which in range(2):
            total = mine[i, which].astype(F32)
            if swap:
                theirs = other[i, which].astype(F32)
                total = total + jnp.concatenate([theirs[rows // 2 :], theirs[: rows // 2]], axis=0)
            pre[i, which] = total
            totals.append(total)
        gate, up = totals
        out[i] = (gate * jax.nn.sigmoid(gate) * up * weight[first + i, :rows]).astype(BF)


def hidden_act(mine, other, swap, weight, before, first):
    count, _, rows, width = mine.shape
    return pl.pallas_call(
        functools.partial(hidden_act_kernel, first, swap),
        in_specs=[whole(), whole(), whole()] + [anywhere()] * len(before),
        out_specs=(whole(), whole()),
        out_shape=(
            jax.ShapeDtypeStruct(mine.shape, F32),
            jax.ShapeDtypeStruct((count, rows, width), BF),
        ),
        compiler_params=pltpu.CompilerParams(vmem_limit_bytes=8 * 1024 * 1024),
    )(mine, other, weight, *before)


def join_kernel(dps, pipes, place, *refs):
    out = refs[-1]
    dp, pipe = place[1], place[2]
    rows = out.shape[0] // (dps * pipes)
    at = 0
    for i in range((len(refs) - 1) // 2):
        size = refs[2 * i].shape[1]
        for j1 in range(pipes):
            for j0 in range(dps):
                piece = lax.rem(pipe + j1, pipes) * dps + lax.rem(dp + j0, dps)
                target = pl.ds(pl.multiple_of(piece * rows, rows), rows)
                out[target, at : at + size] = refs[2 * i + j1][j0 * rows : (j0 + 1) * rows, :]
        at += size


def join(place, parts, dps, pipes):
    assert pipes == 2
    flat = [value for pair in parts for value in pair]
    rows = flat[0].shape[0] * pipes
    width = sum(pair[0].shape[1] for pair in parts)
    return pl.pallas_call(
        functools.partial(join_kernel, dps, pipes),
        in_specs=[scalars()] + [whole()] * len(flat),
        out_specs=whole(),
        out_shape=jax.ShapeDtypeStruct((rows, width), BF),
        compiler_params=pltpu.CompilerParams(vmem_limit_bytes=8 * 1024 * 1024),
    )(place, *flat)


def spread_kernel(picker, hidden, out):
    for e in range(picker.shape[0]):
        out[:, e * H : (e + 1) * H] = dot(picker[e], hidden[e], 0, 0).astype(BF)


def spread(picker, hidden):
    count, slots, token_count = picker.shape
    return pl.pallas_call(
        spread_kernel,
        in_specs=[whole(), whole()],
        out_specs=whole(),
        out_shape=jax.ShapeDtypeStruct((token_count, count * H), BF),
        compiler_params=pltpu.CompilerParams(vmem_limit_bytes=8 * 1024 * 1024),
    )(picker, hidden)


def flip_kernel(dense, tokens, before, dense_out, tokens_out):
    dense_out[...] = dense[...].astype(F32).T.astype(BF)
    tokens_out[...] = tokens[...].astype(F32).T.astype(BF)


def flip(dense, tokens, before):
    return pl.pallas_call(
        flip_kernel,
        in_specs=[whole(), whole(), anywhere()],
        out_specs=(whole(), whole()),
        out_shape=(
            jax.ShapeDtypeStruct(dense.shape[::-1], BF),
            jax.ShapeDtypeStruct(tokens.shape[::-1], BF),
        ),
        compiler_params=pltpu.CompilerParams(vmem_limit_bytes=16 * 1024 * 1024),
    )(dense, tokens, before)


def hidden_grad_kernel(first, picker, residual, down, before, keep, send):
    half = keep.shape[1]
    for i in range(keep.shape[0]):
        e = first + i
        rows = dot(picker[e], residual[...]).astype(BF)
        product = dot(down[e * H : (e + 1) * H, :], rows, 1, 1).T.astype(BF)
        keep[i] = product[:half]
        send[i] = product[half:]


def hidden_grad_parts(picker, residual, down, before, first, count):
    slots = picker.shape[1]
    halves = jax.ShapeDtypeStruct((count, slots // 2, H), BF)
    return pl.pallas_call(
        functools.partial(hidden_grad_kernel, first),
        in_specs=[whole(), whole(), whole(), anywhere()],
        out_specs=(whole(), whole()),
        out_shape=(halves, halves),
        compiler_params=pltpu.CompilerParams(vmem_limit_bytes=8 * 1024 * 1024),
    )(picker, residual, down, before)


def hidden_grad_act_kernel(first, swap, mine, other, pre, weight, before, out):
    count, rows = mine.shape[:2]
    for i in range(count):
        total = mine[i].astype(F32)
        if swap:
            flipped = jnp.concatenate([other[i, rows // 2 :], other[i, : rows // 2]], axis=0)
            total = total + flipped.astype(F32)
        total = total * weight[first + i, :rows]
        pre_gate, pre_up = pre[i, 0], pre[i, 1]
        sig = jax.nn.sigmoid(pre_gate)
        gate_grad = total * pre_up * sig * (1.0 + pre_gate * (1.0 - sig))
        up_grad = total * pre_gate * sig
        out[i, 0] = gate_grad.astype(BF)
        out[i, 1] = up_grad.astype(BF)


def hidden_grad_act(mine, other, swap, pre, weight, before, first):
    count, rows, width = mine.shape
    return pl.pallas_call(
        functools.partial(hidden_grad_act_kernel, first, swap),
        in_specs=[whole(), whole(), whole(), whole(), anywhere()],
        out_specs=whole(),
        out_shape=jax.ShapeDtypeStruct((count, 2, rows, width), BF),
        compiler_params=pltpu.CompilerParams(vmem_limit_bytes=8 * 1024 * 1024),
    )(mine, other, pre, weight, before)


def down_grad_kernel(hidden, residual, before, out, done, held, sems):
    tiles = sems.shape[0]
    rows = hidden.shape[0] // tiles
    copies = []
    for i in range(tiles):
        part = pl.ds(i * rows, rows)
        held[part, :] = dot(hidden[part, :], residual[...]).astype(BF)
        copies.append(pltpu.make_async_copy(held.at[part], out.at[part], sems.at[i]))
        copies[-1].start()
    done[...] = jnp.zeros_like(done)
    for copy in copies:
        copy.wait()


def down_grad(hidden, residual, before):
    rows, token_count = hidden.shape
    width = residual.shape[1]
    return pl.pallas_call(
        down_grad_kernel,
        in_specs=[whole(), whole(), anywhere()],
        out_specs=(in_hbm(), whole()),
        out_shape=(
            jax.ShapeDtypeStruct((rows, width), BF),
            jax.ShapeDtypeStruct((8, 128), F32),
        ),
        scratch_shapes=[
            pltpu.VMEM((rows, width), BF),
            pltpu.SemaphoreType.DMA((rows // (H // 2),)),
        ],
        compiler_params=pltpu.CompilerParams(vmem_limit_bytes=16 * 1024 * 1024),
        cost_estimate=pl.CostEstimate(
            flops=2 * rows * width * token_count,
            bytes_accessed=2 * rows * width,
            transcendentals=0,
        ),
    )(hidden, residual, before)


def input_grad_kernel(group, picker, tokens, *rest):
    outs, held, sems = rest[-4:-2], rest[-2], rest[-1]
    count = picker.shape[0]
    splits = sems.shape[2]
    rows = tokens.shape[0] // splits
    copies = []
    for i in range(count):
        for which in range(2):
            mine, theirs = rest[i // group * 2], rest[i // group * 2 + 1]
            grad = jnp.concatenate([mine[i % group, which], theirs[i % group, which]], axis=0)
            dense = dot(picker[i], grad, 0, 0).astype(BF)
            for r in range(splits):
                part = pl.ds(r * rows, rows)
                columns = pl.ds(i * H, H)
                held[i, which, part] = dot(tokens[part, :], dense).astype(BF)
                copies.append(
                    pltpu.make_async_copy(
                        held.at[i, which, part], outs[which].at[part, columns], sems.at[i, which, r]
                    )
                )
                copies[-1].start()
    for copy in copies:
        copy.wait()


def input_grads(picker, tokens, parts):
    count, slots, token_count = picker.shape
    width = tokens.shape[0]
    out = jax.ShapeDtypeStruct((width, count * H), BF)
    return pl.pallas_call(
        functools.partial(input_grad_kernel, count // len(parts)),
        in_specs=[whole()] * (2 + 2 * len(parts)),
        out_specs=(in_hbm(), in_hbm()),
        out_shape=(out, out),
        scratch_shapes=[
            pltpu.VMEM((count, 2, width, H), BF),
            pltpu.SemaphoreType.DMA((count, 2, 2)),
        ],
        compiler_params=pltpu.CompilerParams(vmem_limit_bytes=24 * 1024 * 1024),
        cost_estimate=pl.CostEstimate(
            flops=count * 4 * token_count * width * H,
            bytes_accessed=count * 4 * width * H,
            transcendentals=0,
        ),
    )(picker, tokens, *[value for pair in parts for value in pair])


def add(a, b):
    return (a.astype(F32) + b.astype(F32)).astype(BF)


def split_rows(value, count):
    rows = value.shape[-2] // count
    return [value[..., i * rows : (i + 1) * rows, :] for i in range(count)]


def scatter_dp(value, count):
    pieces = split_rows(value, count)
    total = pieces[0].astype(F32)
    for s in range(1, count):
        total = total + shift(pieces[s], "dp", count, s).astype(F32)
    return total


def gather_dp_parts(value, count):
    return [value] + [shift(value, "dp", count, -s) for s in range(1, count)]


def gather_dp(value, count):
    return jnp.concatenate(gather_dp_parts(value, count), axis=-2)


def exchange_dp(value, count):
    if count == 2:
        return value, shift(value, "dp", count, 1)
    total = gather_dp(scatter_dp(value, count).astype(BF), count)
    return total, total


def body(
    tokens,
    routes,
    gate_weights,
    teacher_gate,
    teacher_up,
    teacher_down,
    expert_gate,
    expert_up,
    expert_down,
):
    ranks = lax.axis_size("expert")
    dps = lax.axis_size("dp")
    pipes = lax.axis_size("pipe")
    rank = lax.axis_index("expert")
    dp = lax.axis_index("dp")
    pipe = lax.axis_index("pipe")
    block, width = tokens.shape
    token_count = block * ranks
    experts = expert_gate.shape[1] // H
    slots = block // 2 * ranks
    place = jnp.stack([rank, dp, pipe]).astype(jnp.int32)

    paired = ranks & (ranks - 1) == 0

    def to_partner(value, s):
        if paired:
            return lax.ppermute(value, "expert", [(i, i ^ s) for i in range(ranks)])
        return shift(value, "expert", ranks, s)

    def target_of(s):
        return rank ^ s if paired else (rank + s) % ranks

    def source_of(s):
        return rank ^ s if paired else (rank + ranks - s) % ranks

    def gather_tokens(mine):
        whole_rows = jnp.zeros((token_count, mine.shape[1]), BF)
        whole_rows = lax.dynamic_update_slice(whole_rows, mine, (rank * block, 0))
        for s in range(1, ranks):
            theirs = to_partner(mine, s)
            whole_rows = lax.dynamic_update_slice(whole_rows, theirs, (source_of(s) * block, 0))
        return whole_rows

    def to_owners(product):
        blocks = product.reshape(ranks, block, width)
        return lax.all_to_all(blocks, "expert", split_axis=0, concat_axis=0)

    base = gather_tokens(tokens)
    picker, slot_weight, gate_near, up_near = prepare(
        place, routes.T, gate_weights.T, teacher_gate, teacher_up, ranks, dps, pipes, block, experts
    )

    chunks = 2 if teacher_gate.shape[1] % 512 == 0 else 1
    size = teacher_gate.shape[1] // chunks
    halves = []
    for i in range(chunks):
        keep, send = teacher_pre(place, base, gate_near, up_near, i * size, size, dps, pipes)
        halves.append(add(keep, shift(send, "pipe", pipes, 1)))

    group = 2 if experts % 2 == 0 else 1
    firsts = range(0, experts, group)
    parts = []
    last = halves[-1]
    for first in firsts:
        keep, send = expert_pre(picker, base, expert_gate, expert_up, last, first, group)
        last = keep
        parts.append((keep, shift(send, "pipe", pipes, 1)))
    hiddens = []
    for half in halves:
        total = scatter_dp(half, dps)
        hidden = (jax.nn.silu(total[0]) * total[1]).astype(BF)
        hidden = jnp.concatenate(gather_dp_parts(hidden, dps), axis=0)
        hiddens.append((hidden, shift(hidden, "pipe", pipes, 1)))
    hidden = join(place, hiddens, dps, pipes)
    target = to_owners(jnp.dot(hidden, teacher_down, preferred_element_type=F32).astype(BF))

    pre, weighted = [], []
    for first, (keep, theirs) in zip(firsts, parts):
        mine, other = exchange_dp(add(keep, theirs), dps)
        total, part = hidden_act(mine, other, dps == 2, slot_weight, [target], first)
        pre.append(total)
        weighted.append(jnp.concatenate([part, shift(part, "pipe", pipes, 1)], axis=1))
    weighted = jnp.concatenate(weighted, axis=0)

    dense = spread(picker, weighted)
    product = jnp.dot(dense, expert_down, preferred_element_type=F32).astype(BF)
    student = to_owners(product)
    dense_flipped, base_flipped = flip(dense, base, product)
    student_out, residual = residual_of(student, target, base_flipped)
    residual = jnp.broadcast_to(residual[None], (ranks, block, width))
    residual = lax.all_to_all(residual, "expert", split_axis=0, concat_axis=0)
    residual = residual.reshape(token_count, width)

    sums = []
    last = residual
    for first in firsts:
        keep, send = hidden_grad_parts(picker, residual, expert_down, last, first, group)
        last = keep
        sums.append(add(keep, shift(send, "pipe", pipes, 1)))
    pairs = [exchange_dp(value, dps) for value in sums]
    grad_down, done = down_grad(dense_flipped, residual, sums[-1])
    activations = []
    for i, first in enumerate(firsts):
        mine = hidden_grad_act(*pairs[i], dps == 2, pre[i], slot_weight, done, first)
        activations.append((mine, shift(mine, "pipe", pipes, 1)))
    grads = input_grads(picker, base_flipped, activations)
    return (student_out, grads[0], grads[1], grad_down)


def solution(mesh):
    placed = (
        P(("groups", "expert"), ("dp", "pipe")),
        P("groups", None),
        P("groups", None),
        P(("dp", "pipe"), "expert"),
        P(("dp", "pipe"), "expert"),
        P("expert", ("dp", "pipe")),
        P(("dp", "pipe"), "expert"),
        P(("dp", "pipe"), "expert"),
        P("expert", ("dp", "pipe")),
    )
    return jax.shard_map(
        body,
        mesh=mesh,
        in_specs=placed,
        out_specs=(
            P(("groups", "expert"), ("dp", "pipe")),
            P(("groups", "dp", "pipe"), "expert"),
            P(("groups", "dp", "pipe"), "expert"),
            P(("groups", "expert"), ("dp", "pipe")),
        ),
        check_vma=False,
    )
```

```python
import functools

import jax
import jax.numpy as jnp
from jax import lax
from jax.experimental import pallas as pl
from jax.experimental.pallas import tpu as pltpu
from jax.sharding import PartitionSpec as P

H = 896
BF = jnp.bfloat16
F32 = jnp.float32


def shift(value, axis, count, by):
    return lax.ppermute(value, axis, [(i, (i + by) % count) for i in range(count)])


def dot(a, b, contract_a=1, contract_b=0):
    return lax.dot_general(
        a, b, (((contract_a,), (contract_b,)), ((), ())), preferred_element_type=F32
    )


def whole():
    return pl.BlockSpec(memory_space=pltpu.VMEM)


def in_hbm():
    return pl.BlockSpec(memory_space=pltpu.HBM)


def anywhere():
    return pl.BlockSpec(memory_space=pl.ANY)


def scalars():
    return pl.BlockSpec(memory_space=pltpu.SMEM)


def load_start(pairs, sems, pieces):
    copies = []
    for which, (source, target) in enumerate(pairs):
        rows = source.shape[0] // pieces
        for i in range(pieces):
            part = pl.ds(i * rows, rows)
            copies.append(
                pltpu.make_async_copy(source.at[part], target.at[part], sems.at[which, i])
            )
    for copy in copies:
        copy.start()
    return copies


def far(value):
    return pltpu.with_memory_space_constraint(value, pltpu.HBM)


def prepare_kernel(
    ranks,
    capacity,
    dps,
    pipes,
    place,
    far_routes,
    far_shares,
    gate,
    picker,
    weights,
    gate_out,
    routes,
    shares,
    sems,
    table_sems,
):
    tables = [
        pltpu.make_async_copy(far_routes, routes, table_sems.at[0]),
        pltpu.make_async_copy(far_shares, shares, table_sems.at[1]),
    ]
    for copy in tables:
        copy.start()
    copies = load_start(((gate, gate_out),), sems, 8)
    for copy in tables:
        copy.wait()
    rank, dp, pipe = place[0], place[1], place[2]
    experts, slots, token_count = picker.shape
    block = token_count // ranks
    per_piece = ranks // (dps * pipes)
    row = lax.broadcasted_iota(jnp.int32, (8, token_count), 0)
    names = row + rank * experts
    weight = jnp.zeros((8, token_count), F32)
    routed = jnp.zeros((8, token_count), F32)
    for k in range(routes.shape[0]):
        hit = (routes[k : k + 1, :] == names) & (row < experts)
        weight = weight + jnp.where(hit, shares[k : k + 1, :], 0.0)
        routed = routed + jnp.where(hit, 1.0, 0.0)
    t_from = lax.broadcasted_iota(jnp.int32, (token_count, token_count), 0)
    t_to = lax.broadcasted_iota(jnp.int32, (token_count, token_count), 1)
    earlier = jnp.where((t_from // block == t_to // block) & (t_from < t_to), 1.0, 0.0)
    within = dot(routed.astype(BF), earlier.astype(BF)).astype(jnp.int32)
    at_block = lax.broadcasted_iota(jnp.int32, (1, token_count), 1) // block
    at_pipe = lax.rem(at_block // (dps * per_piece) + pipes - pipe, pipes)
    at_dp = lax.rem(lax.rem(at_block // per_piece, dps) + dps - dp, dps)
    first = ((at_pipe * dps + at_dp) * per_piece + lax.rem(at_block, per_piece)) * capacity
    slot = jnp.where(routed > 0.0, within + first, -1)
    ids = lax.broadcasted_iota(jnp.int32, (slots, token_count), 0)
    for e in range(experts):
        hit = slot[e : e + 1] == ids
        picker[e] = jnp.where(hit, 1.0, 0.0).astype(BF)
        weights[e] = jnp.sum(jnp.where(hit, weight[e : e + 1], 0.0), axis=1, keepdims=True)
    for copy in copies:
        copy.wait()


def prepare(place, routes, shares, gate, ranks, dps, pipes, block, experts):
    assert experts <= 8
    capacity = block // 2
    token_count = block * ranks
    slots = capacity * ranks
    return pl.pallas_call(
        functools.partial(prepare_kernel, ranks, capacity, dps, pipes),
        in_specs=[scalars(), in_hbm(), in_hbm(), in_hbm()],
        out_specs=(whole(), whole(), whole()),
        out_shape=(
            jax.ShapeDtypeStruct((experts, slots, token_count), BF),
            jax.ShapeDtypeStruct((experts, slots, 1), F32),
            pltpu.VMEM(gate.shape, BF),
        ),
        scratch_shapes=[
            pltpu.VMEM(routes.shape, routes.dtype),
            pltpu.VMEM(shares.shape, shares.dtype),
            pltpu.SemaphoreType.DMA((1, 8)),
            pltpu.SemaphoreType.DMA((2,)),
        ],
        compiler_params=pltpu.CompilerParams(vmem_limit_bytes=8 * 1024 * 1024),
        cost_estimate=pl.CostEstimate(
            flops=0, bytes_accessed=8 * gate.size, transcendentals=0
        ),
    )(place, far(routes), far(shares), far(gate))


def residual_kernel(counts, *refs):
    sums = []
    at = 0
    for count in counts:
        total = refs[at][...].astype(F32)
        for i in range(1, count):
            total = total + refs[at + i][...].astype(F32)
        sums.append(total)
        at += count
    student, target = sums
    refs[-2][...] = student.astype(BF)
    refs[-1][...] = (student - target).astype(BF)


def residual_of(student, target, before):
    block = jax.ShapeDtypeStruct(student[0].shape, BF)
    return pl.pallas_call(
        functools.partial(residual_kernel, (len(student), len(target))),
        in_specs=[whole()] * (len(student) + len(target)) + [anywhere()] * len(before),
        out_specs=(whole(), whole()),
        out_shape=(block, block),
        compiler_params=pltpu.CompilerParams(vmem_limit_bytes=4 * 1024 * 1024),
    )(*student, *target, *before)


def order_kernel(dps, pipes, place, tokens, *rest):
    out = rest[-1]
    dp, pipe = place[1], place[2]
    rows = tokens.shape[0] // (dps * pipes)
    at = 0
    for j1 in range(pipes):
        for j0 in range(dps):
            piece = lax.rem(pipe + j1, pipes) * dps + lax.rem(dp + j0, dps)
            out[at : at + rows, :] = tokens[pl.ds(pl.multiple_of(piece * rows, rows), rows), :]
            at += rows


def order(place, tokens, before, dps, pipes):
    return pl.pallas_call(
        functools.partial(order_kernel, dps, pipes),
        in_specs=[scalars(), whole()] + [anywhere()] * len(before),
        out_specs=whole(),
        out_shape=jax.ShapeDtypeStruct(tokens.shape, BF),
        compiler_params=pltpu.CompilerParams(vmem_limit_bytes=4 * 1024 * 1024),
    )(place, tokens, *before)


def expert_kernel(first, picker, tokens, gate, up, *rest):
    keep, send, held, sems = rest[-4:]
    half = keep.shape[2]
    count = keep.shape[0]
    pieces = sems.shape[2]
    rows_each = gate.shape[0] // pieces
    copies = {}
    for i in range(count):
        for which, weight in enumerate((gate, up)):
            for p in range(pieces):
                part = pl.ds(p * rows_each, rows_each)
                columns = pl.ds((first + i) * H, H)
                copies[i, which, p] = pltpu.make_async_copy(
                    weight.at[part, columns], held.at[i, which, part], sems.at[i, which, p]
                )
                copies[i, which, p].start()
    for i in range(count):
        rows = dot(picker[first + i], tokens[...]).astype(BF)
        for which in range(2):
            for p in range(pieces):
                copies[i, which, p].wait()
            product = dot(rows, held[i, which]).astype(BF)
            keep[i, which] = product[:half]
            send[i, which] = product[half:]


def expert_pre(picker, tokens, gate, up, before, first, count):
    slots = picker.shape[1]
    width = tokens.shape[1]
    halves = jax.ShapeDtypeStruct((count, 2, slots // 2, H), BF)
    return pl.pallas_call(
        functools.partial(expert_kernel, first),
        in_specs=[whole(), whole(), in_hbm(), in_hbm()] + [anywhere()] * len(before),
        out_specs=(whole(), whole()),
        out_shape=(halves, halves),
        scratch_shapes=[
            pltpu.VMEM((count, 2, width, H), BF),
            pltpu.SemaphoreType.DMA((count, 2, 4)),
        ],
        compiler_params=pltpu.CompilerParams(vmem_limit_bytes=16 * 1024 * 1024),
        cost_estimate=pl.CostEstimate(
            flops=count * 4 * slots * width * H,
            bytes_accessed=count * 4 * width * H,
            transcendentals=0,
        ),
    )(picker, tokens, far(gate), far(up), *before)


def hidden_act_kernel(first, swap, mine, other, weight, *rest):
    pre, out = rest[-2:]
    count, _, rows = mine.shape[:3]
    for i in range(count):
        totals = []
        for which in range(2):
            total = mine[i, which].astype(F32)
            if swap:
                theirs = other[i, which].astype(F32)
                total = total + jnp.concatenate([theirs[rows // 2 :], theirs[: rows // 2]], axis=0)
            pre[i, which] = total
            totals.append(total)
        gate, up = totals
        out[i] = (gate * jax.nn.sigmoid(gate) * up * weight[first + i, :rows]).astype(BF)


def hidden_act(mine, other, swap, weight, before, first):
    count, _, rows, width = mine.shape
    return pl.pallas_call(
        functools.partial(hidden_act_kernel, first, swap),
        in_specs=[whole(), whole(), whole()] + [anywhere()] * len(before),
        out_specs=(whole(), whole()),
        out_shape=(
            jax.ShapeDtypeStruct(mine.shape, F32),
            jax.ShapeDtypeStruct((count, rows, width), BF),
        ),
        compiler_params=pltpu.CompilerParams(vmem_limit_bytes=8 * 1024 * 1024),
    )(mine, other, weight, *before)


def join_kernel(ranks, dps, pipes, place, *refs):
    out = refs[-1]
    rank, dp, pipe = place[0], place[1], place[2]
    chunks = (len(refs) - 1) // 2
    chunk_rows = out.shape[0] // chunks
    rows = chunk_rows // (dps * pipes)
    for i in range(chunks):
        chunk = lax.rem(rank // (ranks // chunks) + i, chunks)
        for j1 in range(pipes):
            for j0 in range(dps):
                piece = lax.rem(pipe + j1, pipes) * dps + lax.rem(dp + j0, dps)
                at = pl.multiple_of(chunk * chunk_rows + piece * rows, rows)
                out[pl.ds(at, rows), :] = refs[2 * i + j1][j0 * rows : (j0 + 1) * rows, :]


def join(place, parts, ranks, dps, pipes):
    assert pipes == 2
    flat = [value for pair in parts for value in pair]
    rows, width = flat[0].shape
    return pl.pallas_call(
        functools.partial(join_kernel, ranks, dps, pipes),
        in_specs=[scalars()] + [whole()] * len(flat),
        out_specs=whole(),
        out_shape=jax.ShapeDtypeStruct((rows * len(flat), width), BF),
        compiler_params=pltpu.CompilerParams(vmem_limit_bytes=8 * 1024 * 1024),
    )(place, *flat)


def spread_kernel(picker, hidden, out):
    for e in range(picker.shape[0]):
        out[:, e * H : (e + 1) * H] = dot(picker[e], hidden[e], 0, 0).astype(BF)


def spread(picker, hidden):
    count, slots, token_count = picker.shape
    return pl.pallas_call(
        spread_kernel,
        in_specs=[whole(), whole()],
        out_specs=whole(),
        out_shape=jax.ShapeDtypeStruct((token_count, count * H), BF),
        compiler_params=pltpu.CompilerParams(vmem_limit_bytes=8 * 1024 * 1024),
    )(picker, hidden)


def flip_kernel(dense, tokens, before, dense_out, tokens_out):
    dense_out[...] = dense[...].astype(F32).T.astype(BF)
    tokens_out[...] = tokens[...].astype(F32).T.astype(BF)


def flip(dense, tokens, before):
    return pl.pallas_call(
        flip_kernel,
        in_specs=[whole(), whole(), anywhere()],
        out_specs=(whole(), whole()),
        out_shape=(
            jax.ShapeDtypeStruct(dense.shape[::-1], BF),
            jax.ShapeDtypeStruct(tokens.shape[::-1], BF),
        ),
        compiler_params=pltpu.CompilerParams(vmem_limit_bytes=16 * 1024 * 1024),
    )(dense, tokens, before)


def hidden_grad_kernel(first, picker, residual, down, before, keep, send):
    half = keep.shape[1]
    for i in range(keep.shape[0]):
        e = first + i
        rows = dot(picker[e], residual[...]).astype(BF)
        product = dot(down[e * H : (e + 1) * H, :], rows, 1, 1).T.astype(BF)
        keep[i] = product[:half]
        send[i] = product[half:]


def hidden_grad_parts(picker, residual, down, before, first, count):
    slots = picker.shape[1]
    halves = jax.ShapeDtypeStruct((count, slots // 2, H), BF)
    return pl.pallas_call(
        functools.partial(hidden_grad_kernel, first),
        in_specs=[whole(), whole(), whole(), anywhere()],
        out_specs=(whole(), whole()),
        out_shape=(halves, halves),
        compiler_params=pltpu.CompilerParams(vmem_limit_bytes=8 * 1024 * 1024),
    )(picker, residual, down, before)


def hidden_grad_act_kernel(first, swap, mine, other, pre, weight, before, out):
    count, rows = mine.shape[:2]
    for i in range(count):
        total = mine[i].astype(F32)
        if swap:
            flipped = jnp.concatenate([other[i, rows // 2 :], other[i, : rows // 2]], axis=0)
            total = total + flipped.astype(F32)
        total = total * weight[first + i, :rows]
        pre_gate, pre_up = pre[i, 0], pre[i, 1]
        sig = jax.nn.sigmoid(pre_gate)
        gate_grad = total * pre_up * sig * (1.0 + pre_gate * (1.0 - sig))
        up_grad = total * pre_gate * sig
        out[i, 0] = gate_grad.astype(BF)
        out[i, 1] = up_grad.astype(BF)


def hidden_grad_act(mine, other, swap, pre, weight, before, first):
    count, rows, width = mine.shape
    return pl.pallas_call(
        functools.partial(hidden_grad_act_kernel, first, swap),
        in_specs=[whole(), whole(), whole(), whole(), anywhere()],
        out_specs=whole(),
        out_shape=jax.ShapeDtypeStruct((count, 2, rows, width), BF),
        compiler_params=pltpu.CompilerParams(vmem_limit_bytes=8 * 1024 * 1024),
    )(mine, other, pre, weight, before)


def down_grad_kernel(hidden, residual, before, out, done, held, sems):
    tiles = sems.shape[0]
    rows = hidden.shape[0] // tiles
    copies = []
    for i in range(tiles):
        part = pl.ds(i * rows, rows)
        held[part, :] = dot(hidden[part, :], residual[...]).astype(BF)
        copies.append(pltpu.make_async_copy(held.at[part], out.at[part], sems.at[i]))
        copies[-1].start()
    done[...] = jnp.zeros_like(done)
    for copy in copies:
        copy.wait()


def down_grad(hidden, residual, before):
    rows, token_count = hidden.shape
    width = residual.shape[1]
    return pl.pallas_call(
        down_grad_kernel,
        in_specs=[whole(), whole(), anywhere()],
        out_specs=(in_hbm(), whole()),
        out_shape=(
            jax.ShapeDtypeStruct((rows, width), BF),
            jax.ShapeDtypeStruct((8, 128), F32),
        ),
        scratch_shapes=[
            pltpu.VMEM((rows, width), BF),
            pltpu.SemaphoreType.DMA((rows // (H // 2),)),
        ],
        compiler_params=pltpu.CompilerParams(vmem_limit_bytes=16 * 1024 * 1024),
        cost_estimate=pl.CostEstimate(
            flops=2 * rows * width * token_count,
            bytes_accessed=2 * rows * width,
            transcendentals=0,
        ),
    )(hidden, residual, before)


def input_grad_kernel(group, picker, tokens, *rest):
    outs, held, sems = rest[-4:-2], rest[-2], rest[-1]
    count = picker.shape[0]
    splits = sems.shape[2]
    rows = tokens.shape[0] // splits
    copies = []
    for i in range(count):
        for which in range(2):
            mine, theirs = rest[i // group * 2], rest[i // group * 2 + 1]
            grad = jnp.concatenate([mine[i % group, which], theirs[i % group, which]], axis=0)
            dense = dot(picker[i], grad, 0, 0).astype(BF)
            for r in range(splits):
                part = pl.ds(r * rows, rows)
                columns = pl.ds(i * H, H)
                held[i, which, part] = dot(tokens[part, :], dense).astype(BF)
                copies.append(
                    pltpu.make_async_copy(
                        held.at[i, which, part], outs[which].at[part, columns], sems.at[i, which, r]
                    )
                )
                copies[-1].start()
    for copy in copies:
        copy.wait()


def input_grads(picker, tokens, parts):
    count, slots, token_count = picker.shape
    width = tokens.shape[0]
    out = jax.ShapeDtypeStruct((width, count * H), BF)
    return pl.pallas_call(
        functools.partial(input_grad_kernel, count // len(parts)),
        in_specs=[whole()] * (2 + 2 * len(parts)),
        out_specs=(in_hbm(), in_hbm()),
        out_shape=(out, out),
        scratch_shapes=[
            pltpu.VMEM((count, 2, width, H), BF),
            pltpu.SemaphoreType.DMA((count, 2, 2)),
        ],
        compiler_params=pltpu.CompilerParams(vmem_limit_bytes=24 * 1024 * 1024),
        cost_estimate=pl.CostEstimate(
            flops=count * 4 * token_count * width * H,
            bytes_accessed=count * 4 * width * H,
            transcendentals=0,
        ),
    )(picker, tokens, *[value for pair in parts for value in pair])


def add(a, b):
    return (a.astype(F32) + b.astype(F32)).astype(BF)


def split_rows(value, count):
    rows = value.shape[-2] // count
    return [value[..., i * rows : (i + 1) * rows, :] for i in range(count)]


def scatter_dp(value, count):
    pieces = split_rows(value, count)
    total = pieces[0].astype(F32)
    for s in range(1, count):
        total = total + shift(pieces[s], "dp", count, s).astype(F32)
    return total


def gather_dp_parts(value, count):
    return [value] + [shift(value, "dp", count, -s) for s in range(1, count)]


def gather_dp(value, count):
    return jnp.concatenate(gather_dp_parts(value, count), axis=-2)


def exchange_dp(value, count):
    if count == 2:
        return value, shift(value, "dp", count, 1)
    total = gather_dp(scatter_dp(value, count).astype(BF), count)
    return total, total


def body(
    tokens,
    routes,
    gate_weights,
    teacher_gate,
    teacher_up,
    teacher_down,
    expert_gate,
    expert_up,
    expert_down,
):
    ranks = lax.axis_size("expert")
    dps = lax.axis_size("dp")
    pipes = lax.axis_size("pipe")
    rank = lax.axis_index("expert")
    dp = lax.axis_index("dp")
    pipe = lax.axis_index("pipe")
    block, width = tokens.shape
    token_count = block * ranks
    experts = expert_gate.shape[1] // H
    slots = block // 2 * ranks
    place = jnp.stack([rank, dp, pipe]).astype(jnp.int32)

    paired = ranks & (ranks - 1) == 0

    def to_partner(value, s):
        if paired:
            return lax.ppermute(value, "expert", [(i, i ^ s) for i in range(ranks)])
        return shift(value, "expert", ranks, s)

    def target_of(s):
        return rank ^ s if paired else (rank + s) % ranks

    def source_of(s):
        return rank ^ s if paired else (rank + ranks - s) % ranks

    def place_rows(blocks):
        rows = jnp.zeros((token_count, blocks[0].shape[1]), BF)
        for s, value in enumerate(blocks):
            rows = lax.dynamic_update_slice(rows, value, (source_of(s) * block, 0))
        return rows

    def gather_blocks(mine):
        return [mine] + [to_partner(mine, s) for s in range(1, ranks)]

    def to_owners(product):
        def block_of(r):
            return lax.dynamic_slice_in_dim(product, r * block, block, axis=0)

        return [block_of(rank)] + [to_partner(block_of(target_of(s)), s) for s in range(1, ranks)]

    def to_owners_in_steps(product):
        blocks = product.reshape(ranks, block, width)
        mask = 1
        seen = None
        while mask < ranks:
            blocks = blocks.reshape(-1, 2, block, width)
            bit = rank // mask % 2
            keep = lax.dynamic_index_in_dim(blocks, bit, 1, keepdims=False)
            send = lax.dynamic_index_in_dim(blocks, 1 - bit, 1, keepdims=False)
            received = to_partner(send, mask)
            seen = received if seen is None else seen
            last = (keep[0], received[0])
            blocks = add(keep, received)
            mask *= 2
        return list(last), seen

    blocks = gather_blocks(tokens)
    base = place_rows(blocks)
    picker, slot_weight, gate_near = prepare(
        place, routes.T, gate_weights.T, teacher_gate, ranks, dps, pipes, block, experts
    )

    halved = paired and ranks > 2 and token_count // 2 % (16 * dps * pipes) == 0
    if halved:
        near = jnp.zeros((token_count // 2, width), BF)
        for s in range(ranks // 2):
            near = lax.dynamic_update_slice(
                near, blocks[s], (source_of(s) % (ranks // 2) * block, 0)
            )
        start = (1 - rank // (ranks // 2)) * (token_count // 2)
        chunks = [near, lax.dynamic_slice_in_dim(base, start, token_count // 2, axis=0)]
    else:
        chunks = [base]
    halves = []
    before = []
    for chunk in chunks:
        ordered = order(place, chunk, before, dps, pipes)
        products = [
            jnp.dot(ordered, weight, preferred_element_type=F32).astype(BF)
            for weight in (gate_near, teacher_up)
        ]
        cut = chunk.shape[0] // pipes
        keep = jnp.stack([value[:cut] for value in products])
        send = jnp.stack([value[cut:] for value in products])
        halves.append(add(keep, shift(send, "pipe", pipes, 1)))
        before = halves[-1:]

    group = 2 if experts % 2 == 0 else 1
    firsts = range(0, experts, group)
    parts = []
    before = halves
    for first in firsts:
        keep, send = expert_pre(picker, base, expert_gate, expert_up, before, first, group)
        before = [keep]
        parts.append((keep, shift(send, "pipe", pipes, 1)))
    hiddens = []
    for half in halves:
        total = scatter_dp(half, dps)
        hidden = (jax.nn.silu(total[0]) * total[1]).astype(BF)
        hidden = jnp.concatenate(gather_dp_parts(hidden, dps), axis=0)
        hiddens.append((hidden, shift(hidden, "pipe", pipes, 1)))
    hidden = join(place, hiddens, ranks, dps, pipes)
    product = jnp.dot(hidden, teacher_down, preferred_element_type=F32).astype(BF)
    if paired and ranks > 1:
        target, seen = to_owners_in_steps(product)
    else:
        target = to_owners(product)
        seen = target[-1]

    pre, weighted = [], []
    for first, (keep, theirs) in zip(firsts, parts):
        mine, other = exchange_dp(add(keep, theirs), dps)
        total, part = hidden_act(mine, other, dps == 2, slot_weight, [seen], first)
        pre.append(total)
        weighted.append(jnp.concatenate([part, shift(part, "pipe", pipes, 1)], axis=1))
    weighted = jnp.concatenate(weighted, axis=0)

    dense = spread(picker, weighted)
    product = jnp.dot(dense, expert_down, preferred_element_type=F32).astype(BF)
    student = to_owners(product)
    dense_flipped, base_flipped = flip(dense, base, product)
    student_out, residual = residual_of(student, target, (base_flipped,))
    residual = place_rows(gather_blocks(residual))

    sums = []
    last = residual
    for first in firsts:
        keep, send = hidden_grad_parts(picker, residual, expert_down, last, first, group)
        last = keep
        sums.append(add(keep, shift(send, "pipe", pipes, 1)))
    pairs = [exchange_dp(value, dps) for value in sums]
    grad_down, done = down_grad(dense_flipped, residual, sums[-1])
    activations = []
    for i, first in enumerate(firsts):
        mine = hidden_grad_act(*pairs[i], dps == 2, pre[i], slot_weight, done, first)
        activations.append((mine, shift(mine, "pipe", pipes, 1)))
    grads = input_grads(picker, base_flipped, activations)
    return (student_out, grads[0], grads[1], grad_down)


def solution(mesh):
    placed = (
        P(("groups", "expert"), ("dp", "pipe")),
        P("groups", None),
        P("groups", None),
        P(("dp", "pipe"), "expert"),
        P(("dp", "pipe"), "expert"),
        P("expert", ("dp", "pipe")),
        P(("dp", "pipe"), "expert"),
        P(("dp", "pipe"), "expert"),
        P("expert", ("dp", "pipe")),
    )
    return jax.shard_map(
        body,
        mesh=mesh,
        in_specs=placed,
        out_specs=(
            P(("groups", "expert"), ("dp", "pipe")),
            P(("groups", "dp", "pipe"), "expert"),
            P(("groups", "dp", "pipe"), "expert"),
            P(("groups", "expert"), ("dp", "pipe")),
        ),
        check_vma=False,
    )
```

```python
import functools

import jax
import jax.numpy as jnp
from jax import lax
from jax.experimental import pallas as pl
from jax.experimental.pallas import tpu as pltpu
from jax.sharding import PartitionSpec as P

H = 896
BF = jnp.bfloat16
F32 = jnp.float32


def shift(value, axis, count, by):
    return lax.ppermute(value, axis, [(i, (i + by) % count) for i in range(count)])


def dot(a, b, contract_a=1, contract_b=0):
    return lax.dot_general(
        a, b, (((contract_a,), (contract_b,)), ((), ())), preferred_element_type=F32
    )


def whole():
    return pl.BlockSpec(memory_space=pltpu.VMEM)


def in_hbm():
    return pl.BlockSpec(memory_space=pltpu.HBM)


def anywhere():
    return pl.BlockSpec(memory_space=pl.ANY)


def scalars():
    return pl.BlockSpec(memory_space=pltpu.SMEM)


def load_start(pairs, sems, pieces):
    copies = []
    for which, (source, target) in enumerate(pairs):
        rows = source.shape[0] // pieces
        for i in range(pieces):
            part = pl.ds(i * rows, rows)
            copies.append(
                pltpu.make_async_copy(source.at[part], target.at[part], sems.at[which, i])
            )
    for copy in copies:
        copy.start()
    return copies


def far(value):
    return pltpu.with_memory_space_constraint(value, pltpu.HBM)


def prepare_kernel(
    ranks,
    capacity,
    dps,
    pipes,
    place,
    far_routes,
    far_shares,
    gate,
    up,
    picker,
    weights,
    gate_out,
    up_out,
    routes,
    shares,
    sems,
    table_sems,
):
    tables = [
        pltpu.make_async_copy(far_routes, routes, table_sems.at[0]),
        pltpu.make_async_copy(far_shares, shares, table_sems.at[1]),
    ]
    for copy in tables:
        copy.start()
    copies = load_start(((gate, gate_out), (up, up_out)), sems, 8)
    for copy in tables:
        copy.wait()
    rank, dp, pipe = place[0], place[1], place[2]
    experts, slots, token_count = picker.shape
    block = token_count // ranks
    per_piece = ranks // (dps * pipes)
    row = lax.broadcasted_iota(jnp.int32, (8, token_count), 0)
    names = row + rank * experts
    weight = jnp.zeros((8, token_count), F32)
    routed = jnp.zeros((8, token_count), F32)
    for k in range(routes.shape[0]):
        hit = (routes[k : k + 1, :] == names) & (row < experts)
        weight = weight + jnp.where(hit, shares[k : k + 1, :], 0.0)
        routed = routed + jnp.where(hit, 1.0, 0.0)
    t_from = lax.broadcasted_iota(jnp.int32, (token_count, token_count), 0)
    t_to = lax.broadcasted_iota(jnp.int32, (token_count, token_count), 1)
    earlier = jnp.where((t_from // block == t_to // block) & (t_from < t_to), 1.0, 0.0)
    within = dot(routed.astype(BF), earlier.astype(BF)).astype(jnp.int32)
    at_block = lax.broadcasted_iota(jnp.int32, (1, token_count), 1) // block
    at_pipe = lax.rem(at_block // (dps * per_piece) + pipes - pipe, pipes)
    at_dp = lax.rem(lax.rem(at_block // per_piece, dps) + dps - dp, dps)
    first = ((at_pipe * dps + at_dp) * per_piece + lax.rem(at_block, per_piece)) * capacity
    slot = jnp.where(routed > 0.0, within + first, -1)
    ids = lax.broadcasted_iota(jnp.int32, (slots, token_count), 0)
    for e in range(experts):
        hit = slot[e : e + 1] == ids
        picker[e] = jnp.where(hit, 1.0, 0.0).astype(BF)
        weights[e] = jnp.sum(jnp.where(hit, weight[e : e + 1], 0.0), axis=1, keepdims=True)
    for copy in copies:
        copy.wait()


def prepare(place, routes, shares, gate, up, ranks, dps, pipes, block, experts):
    assert experts <= 8
    capacity = block // 2
    token_count = block * ranks
    slots = capacity * ranks
    return pl.pallas_call(
        functools.partial(prepare_kernel, ranks, capacity, dps, pipes),
        in_specs=[scalars(), in_hbm(), in_hbm(), in_hbm(), in_hbm()],
        out_specs=(whole(), whole(), whole(), whole()),
        out_shape=(
            jax.ShapeDtypeStruct((experts, slots, token_count), BF),
            jax.ShapeDtypeStruct((experts, slots, 1), F32),
            pltpu.VMEM(gate.shape, BF),
            pltpu.VMEM(up.shape, BF),
        ),
        scratch_shapes=[
            pltpu.VMEM(routes.shape, routes.dtype),
            pltpu.VMEM(shares.shape, shares.dtype),
            pltpu.SemaphoreType.DMA((2, 8)),
            pltpu.SemaphoreType.DMA((2,)),
        ],
        compiler_params=pltpu.CompilerParams(vmem_limit_bytes=8 * 1024 * 1024),
        cost_estimate=pl.CostEstimate(
            flops=0, bytes_accessed=4 * gate.size, transcendentals=0
        ),
    )(place, far(routes), far(shares), far(gate), far(up))


def residual_kernel(count, *refs):
    student = refs[0][...].astype(F32)
    for i in range(1, count):
        student = student + refs[i][...].astype(F32)
    refs[-2][...] = student.astype(BF)
    refs[-1][...] = (student - refs[count][...].astype(F32)).astype(BF)


def residual_of(student, target, before):
    block = jax.ShapeDtypeStruct(target.shape, BF)
    return pl.pallas_call(
        functools.partial(residual_kernel, len(student)),
        in_specs=[whole()] * (len(student) + 1) + [anywhere()] * len(before),
        out_specs=(whole(), whole()),
        out_shape=(block, block),
        compiler_params=pltpu.CompilerParams(vmem_limit_bytes=4 * 1024 * 1024),
    )(*student, target, *before)


def tile_of(size):
    return 256 if size % 256 == 0 else 128


def teacher_kernel(first, size, dps, pipes, place, tokens, gate, up, keep, send):
    dp, pipe = place[1], place[2]
    rows = tokens.shape[0] // (dps * pipes)
    half = dps * rows
    parts = []
    for j1 in range(pipes):
        for j0 in range(dps):
            piece = lax.rem(pipe + j1, pipes) * dps + lax.rem(dp + j0, dps)
            parts.append(tokens[pl.ds(pl.multiple_of(piece * rows, rows), rows), :])
    ordered = jnp.concatenate(parts, axis=0)
    tile = tile_of(size)
    for which, weight in enumerate((gate, up)):
        for i in range(size // tile):
            product = dot(ordered, weight[:, first + i * tile : first + (i + 1) * tile]).astype(BF)
            keep[which, :, i * tile : (i + 1) * tile] = product[:half]
            send[which, :, i * tile : (i + 1) * tile] = product[half:]


def teacher_pre(place, tokens, gate, up, first, size, dps, pipes):
    token_count, width = tokens.shape
    half = jax.ShapeDtypeStruct((2, token_count // pipes, size), BF)
    return pl.pallas_call(
        functools.partial(teacher_kernel, first, size, dps, pipes),
        in_specs=[scalars(), whole(), whole(), whole()],
        out_specs=(whole(), whole()),
        out_shape=(half, half),
        compiler_params=pltpu.CompilerParams(vmem_limit_bytes=8 * 1024 * 1024),
        cost_estimate=pl.CostEstimate(
            flops=4 * token_count * width * size, bytes_accessed=4 * width * size, transcendentals=0
        ),
    )(place, tokens, gate, up)


def expert_kernel(first, picker, tokens, gate, up, before, keep, send, held, sems):
    half = keep.shape[2]
    count = keep.shape[0]
    pieces = sems.shape[2]
    rows_each = gate.shape[0] // pieces
    copies = {}
    for i in range(count):
        for which, weight in enumerate((gate, up)):
            for p in range(pieces):
                part = pl.ds(p * rows_each, rows_each)
                columns = pl.ds((first + i) * H, H)
                copies[i, which, p] = pltpu.make_async_copy(
                    weight.at[part, columns], held.at[i, which, part], sems.at[i, which, p]
                )
                copies[i, which, p].start()
    for i in range(count):
        rows = dot(picker[first + i], tokens[...]).astype(BF)
        for which in range(2):
            for p in range(pieces):
                copies[i, which, p].wait()
            product = dot(rows, held[i, which]).astype(BF)
            keep[i, which] = product[:half]
            send[i, which] = product[half:]


def expert_pre(picker, tokens, gate, up, before, first, count):
    slots = picker.shape[1]
    width = tokens.shape[1]
    halves = jax.ShapeDtypeStruct((count, 2, slots // 2, H), BF)
    return pl.pallas_call(
        functools.partial(expert_kernel, first),
        in_specs=[whole(), whole(), in_hbm(), in_hbm(), anywhere()],
        out_specs=(whole(), whole()),
        out_shape=(halves, halves),
        scratch_shapes=[
            pltpu.VMEM((count, 2, width, H), BF),
            pltpu.SemaphoreType.DMA((count, 2, 4)),
        ],
        compiler_params=pltpu.CompilerParams(vmem_limit_bytes=16 * 1024 * 1024),
        cost_estimate=pl.CostEstimate(
            flops=count * 4 * slots * width * H,
            bytes_accessed=count * 4 * width * H,
            transcendentals=0,
        ),
    )(picker, tokens, far(gate), far(up), before)


def hidden_act_kernel(first, swap, mine, other, weight, *rest):
    pre, out = rest[-2:]
    count, _, rows = mine.shape[:3]
    for i in range(count):
        totals = []
        for which in range(2):
            total = mine[i, which].astype(F32)
            if swap:
                theirs = other[i, which].astype(F32)
                total = total + jnp.concatenate([theirs[rows // 2 :], theirs[: rows // 2]], axis=0)
            pre[i, which] = total
            totals.append(total)
        gate, up = totals
        out[i] = (gate * jax.nn.sigmoid(gate) * up * weight[first + i, :rows]).astype(BF)


def hidden_act(mine, other, swap, weight, before, first):
    count, _, rows, width = mine.shape
    return pl.pallas_call(
        functools.partial(hidden_act_kernel, first, swap),
        in_specs=[whole(), whole(), whole()] + [anywhere()] * len(before),
        out_specs=(whole(), whole()),
        out_shape=(
            jax.ShapeDtypeStruct(mine.shape, F32),
            jax.ShapeDtypeStruct((count, rows, width), BF),
        ),
        compiler_params=pltpu.CompilerParams(vmem_limit_bytes=8 * 1024 * 1024),
    )(mine, other, weight, *before)


def join_kernel(dps, pipes, place, *refs):
    out = refs[-1]
    dp, pipe = place[1], place[2]
    rows = out.shape[0] // (dps * pipes)
    at = 0
    for i in range((len(refs) - 1) // 2):
        size = refs[2 * i].shape[1]
        for j1 in range(pipes):
            for j0 in range(dps):
                piece = lax.rem(pipe + j1, pipes) * dps + lax.rem(dp + j0, dps)
                target = pl.ds(pl.multiple_of(piece * rows, rows), rows)
                out[target, at : at + size] = refs[2 * i + j1][j0 * rows : (j0 + 1) * rows, :]
        at += size


def join(place, parts, dps, pipes):
    assert pipes == 2
    flat = [value for pair in parts for value in pair]
    rows = flat[0].shape[0] * pipes
    width = sum(pair[0].shape[1] for pair in parts)
    return pl.pallas_call(
        functools.partial(join_kernel, dps, pipes),
        in_specs=[scalars()] + [whole()] * len(flat),
        out_specs=whole(),
        out_shape=jax.ShapeDtypeStruct((rows, width), BF),
        compiler_params=pltpu.CompilerParams(vmem_limit_bytes=8 * 1024 * 1024),
    )(place, *flat)


def spread_kernel(picker, hidden, out):
    for e in range(picker.shape[0]):
        out[:, e * H : (e + 1) * H] = dot(picker[e], hidden[e], 0, 0).astype(BF)


def spread(picker, hidden):
    count, slots, token_count = picker.shape
    return pl.pallas_call(
        spread_kernel,
        in_specs=[whole(), whole()],
        out_specs=whole(),
        out_shape=jax.ShapeDtypeStruct((token_count, count * H), BF),
        compiler_params=pltpu.CompilerParams(vmem_limit_bytes=8 * 1024 * 1024),
    )(picker, hidden)


def flip_kernel(dense, tokens, before, dense_out, tokens_out):
    dense_out[...] = dense[...].astype(F32).T.astype(BF)
    tokens_out[...] = tokens[...].astype(F32).T.astype(BF)


def flip(dense, tokens, before):
    return pl.pallas_call(
        flip_kernel,
        in_specs=[whole(), whole(), anywhere()],
        out_specs=(whole(), whole()),
        out_shape=(
            jax.ShapeDtypeStruct(dense.shape[::-1], BF),
            jax.ShapeDtypeStruct(tokens.shape[::-1], BF),
        ),
        compiler_params=pltpu.CompilerParams(vmem_limit_bytes=16 * 1024 * 1024),
    )(dense, tokens, before)


def hidden_grad_kernel(first, picker, residual, down, before, keep, send):
    half = keep.shape[1]
    for i in range(keep.shape[0]):
        e = first + i
        rows = dot(picker[e], residual[...]).astype(BF)
        product = dot(down[e * H : (e + 1) * H, :], rows, 1, 1).T.astype(BF)
        keep[i] = product[:half]
        send[i] = product[half:]


def hidden_grad_parts(picker, residual, down, before, first, count):
    slots = picker.shape[1]
    halves = jax.ShapeDtypeStruct((count, slots // 2, H), BF)
    return pl.pallas_call(
        functools.partial(hidden_grad_kernel, first),
        in_specs=[whole(), whole(), whole(), anywhere()],
        out_specs=(whole(), whole()),
        out_shape=(halves, halves),
        compiler_params=pltpu.CompilerParams(vmem_limit_bytes=8 * 1024 * 1024),
    )(picker, residual, down, before)


def hidden_grad_act_kernel(first, swap, mine, other, pre, weight, before, out):
    count, rows = mine.shape[:2]
    for i in range(count):
        total = mine[i].astype(F32)
        if swap:
            flipped = jnp.concatenate([other[i, rows // 2 :], other[i, : rows // 2]], axis=0)
            total = total + flipped.astype(F32)
        total = total * weight[first + i, :rows]
        pre_gate, pre_up = pre[i, 0], pre[i, 1]
        sig = jax.nn.sigmoid(pre_gate)
        gate_grad = total * pre_up * sig * (1.0 + pre_gate * (1.0 - sig))
        up_grad = total * pre_gate * sig
        out[i, 0] = gate_grad.astype(BF)
        out[i, 1] = up_grad.astype(BF)


def hidden_grad_act(mine, other, swap, pre, weight, before, first):
    count, rows, width = mine.shape
    return pl.pallas_call(
        functools.partial(hidden_grad_act_kernel, first, swap),
        in_specs=[whole(), whole(), whole(), whole(), anywhere()],
        out_specs=whole(),
        out_shape=jax.ShapeDtypeStruct((count, 2, rows, width), BF),
        compiler_params=pltpu.CompilerParams(vmem_limit_bytes=8 * 1024 * 1024),
    )(mine, other, pre, weight, before)


def down_grad_kernel(hidden, residual, before, out, done, held, sems):
    tiles = sems.shape[0]
    rows = hidden.shape[0] // tiles
    copies = []
    for i in range(tiles):
        part = pl.ds(i * rows, rows)
        held[part, :] = dot(hidden[part, :], residual[...]).astype(BF)
        copies.append(pltpu.make_async_copy(held.at[part], out.at[part], sems.at[i]))
        copies[-1].start()
    done[...] = jnp.zeros_like(done)
    for copy in copies:
        copy.wait()


def down_grad(hidden, residual, before):
    rows, token_count = hidden.shape
    width = residual.shape[1]
    return pl.pallas_call(
        down_grad_kernel,
        in_specs=[whole(), whole(), anywhere()],
        out_specs=(in_hbm(), whole()),
        out_shape=(
            jax.ShapeDtypeStruct((rows, width), BF),
            jax.ShapeDtypeStruct((8, 128), F32),
        ),
        scratch_shapes=[
            pltpu.VMEM((rows, width), BF),
            pltpu.SemaphoreType.DMA((rows // (H // 2),)),
        ],
        compiler_params=pltpu.CompilerParams(vmem_limit_bytes=16 * 1024 * 1024),
        cost_estimate=pl.CostEstimate(
            flops=2 * rows * width * token_count,
            bytes_accessed=2 * rows * width,
            transcendentals=0,
        ),
    )(hidden, residual, before)


def input_grad_kernel(group, picker, tokens, *rest):
    outs, held, sems = rest[-4:-2], rest[-2], rest[-1]
    count = picker.shape[0]
    splits = sems.shape[2]
    rows = tokens.shape[0] // splits
    copies = []
    for i in range(count):
        for which in range(2):
            mine, theirs = rest[i // group * 2], rest[i // group * 2 + 1]
            grad = jnp.concatenate([mine[i % group, which], theirs[i % group, which]], axis=0)
            dense = dot(picker[i], grad, 0, 0).astype(BF)
            for r in range(splits):
                part = pl.ds(r * rows, rows)
                columns = pl.ds(i * H, H)
                held[i, which, part] = dot(tokens[part, :], dense).astype(BF)
                copies.append(
                    pltpu.make_async_copy(
                        held.at[i, which, part], outs[which].at[part, columns], sems.at[i, which, r]
                    )
                )
                copies[-1].start()
    for copy in copies:
        copy.wait()


def input_grads(picker, tokens, parts):
    count, slots, token_count = picker.shape
    width = tokens.shape[0]
    out = jax.ShapeDtypeStruct((width, count * H), BF)
    return pl.pallas_call(
        functools.partial(input_grad_kernel, count // len(parts)),
        in_specs=[whole()] * (2 + 2 * len(parts)),
        out_specs=(in_hbm(), in_hbm()),
        out_shape=(out, out),
        scratch_shapes=[
            pltpu.VMEM((count, 2, width, H), BF),
            pltpu.SemaphoreType.DMA((count, 2, 2)),
        ],
        compiler_params=pltpu.CompilerParams(vmem_limit_bytes=24 * 1024 * 1024),
        cost_estimate=pl.CostEstimate(
            flops=count * 4 * token_count * width * H,
            bytes_accessed=count * 4 * width * H,
            transcendentals=0,
        ),
    )(picker, tokens, *[value for pair in parts for value in pair])


def add(a, b):
    return (a.astype(F32) + b.astype(F32)).astype(BF)


def split_rows(value, count):
    rows = value.shape[-2] // count
    return [value[..., i * rows : (i + 1) * rows, :] for i in range(count)]


def scatter_dp(value, count):
    pieces = split_rows(value, count)
    total = pieces[0].astype(F32)
    for s in range(1, count):
        total = total + shift(pieces[s], "dp", count, s).astype(F32)
    return total


def gather_dp_parts(value, count):
    return [value] + [shift(value, "dp", count, -s) for s in range(1, count)]


def gather_dp(value, count):
    return jnp.concatenate(gather_dp_parts(value, count), axis=-2)


def exchange_dp(value, count):
    if count == 2:
        return value, shift(value, "dp", count, 1)
    total = gather_dp(scatter_dp(value, count).astype(BF), count)
    return total, total


def body(
    tokens,
    routes,
    gate_weights,
    teacher_gate,
    teacher_up,
    teacher_down,
    expert_gate,
    expert_up,
    expert_down,
):
    ranks = lax.axis_size("expert")
    dps = lax.axis_size("dp")
    pipes = lax.axis_size("pipe")
    rank = lax.axis_index("expert")
    dp = lax.axis_index("dp")
    pipe = lax.axis_index("pipe")
    block, width = tokens.shape
    token_count = block * ranks
    experts = expert_gate.shape[1] // H
    slots = block // 2 * ranks
    place = jnp.stack([rank, dp, pipe]).astype(jnp.int32)

    paired = ranks & (ranks - 1) == 0

    def to_partner(value, s):
        if paired:
            return lax.ppermute(value, "expert", [(i, i ^ s) for i in range(ranks)])
        return shift(value, "expert", ranks, s)

    def target_of(s):
        return rank ^ s if paired else (rank + s) % ranks

    def source_of(s):
        return rank ^ s if paired else (rank + ranks - s) % ranks

    def gather_tokens(mine):
        whole_rows = jnp.zeros((token_count, mine.shape[1]), BF)
        whole_rows = lax.dynamic_update_slice(whole_rows, mine, (rank * block, 0))
        for s in range(1, ranks):
            theirs = to_partner(mine, s)
            whole_rows = lax.dynamic_update_slice(whole_rows, theirs, (source_of(s) * block, 0))
        return whole_rows

    def to_owners(product):
        def block_of(r):
            return lax.dynamic_slice_in_dim(product, r * block, block, axis=0)

        return [block_of(rank)] + [to_partner(block_of(target_of(s)), s) for s in range(1, ranks)]

    base = gather_tokens(tokens)
    picker, slot_weight, gate_near, up_near = prepare(
        place, routes.T, gate_weights.T, teacher_gate, teacher_up, ranks, dps, pipes, block, experts
    )

    chunks = 2 if teacher_gate.shape[1] % 512 == 0 else 1
    size = teacher_gate.shape[1] // chunks
    halves = []
    for i in range(chunks):
        keep, send = teacher_pre(place, base, gate_near, up_near, i * size, size, dps, pipes)
        halves.append(add(keep, shift(send, "pipe", pipes, 1)))

    group = 2 if experts % 2 == 0 else 1
    firsts = range(0, experts, group)
    parts = []
    last = halves[-1]
    for first in firsts:
        keep, send = expert_pre(picker, base, expert_gate, expert_up, last, first, group)
        last = keep
        parts.append((keep, shift(send, "pipe", pipes, 1)))
    hiddens = []
    for half in halves:
        total = scatter_dp(half, dps)
        hidden = (jax.nn.silu(total[0]) * total[1]).astype(BF)
        hidden = jnp.concatenate(gather_dp_parts(hidden, dps), axis=0)
        hiddens.append((hidden, shift(hidden, "pipe", pipes, 1)))
    hidden = join(place, hiddens, dps, pipes)
    product = jnp.dot(hidden, teacher_down, preferred_element_type=F32).astype(BF)
    target = lax.psum_scatter(product, "expert", scatter_dimension=0, tiled=True)

    pre, weighted = [], []
    for first, (keep, theirs) in zip(firsts, parts):
        mine, other = exchange_dp(add(keep, theirs), dps)
        total, part = hidden_act(mine, other, dps == 2, slot_weight, [product], first)
        pre.append(total)
        weighted.append(jnp.concatenate([part, shift(part, "pipe", pipes, 1)], axis=1))
    weighted = jnp.concatenate(weighted, axis=0)

    dense = spread(picker, weighted)
    product = jnp.dot(dense, expert_down, preferred_element_type=F32).astype(BF)
    student = to_owners(product)
    dense_flipped, base_flipped = flip(dense, base, product)
    student_out, residual = residual_of(student, target, (base_flipped,))
    residual = gather_tokens(residual)

    sums = []
    last = residual
    for first in firsts:
        keep, send = hidden_grad_parts(picker, residual, expert_down, last, first, group)
        last = keep
        sums.append(add(keep, shift(send, "pipe", pipes, 1)))
    pairs = [exchange_dp(value, dps) for value in sums]
    grad_down, done = down_grad(dense_flipped, residual, sums[-1])
    activations = []
    for i, first in enumerate(firsts):
        mine = hidden_grad_act(*pairs[i], dps == 2, pre[i], slot_weight, done, first)
        activations.append((mine, shift(mine, "pipe", pipes, 1)))
    grads = input_grads(picker, base_flipped, activations)
    return (student_out, grads[0], grads[1], grad_down)


def solution(mesh):
    placed = (
        P(("groups", "expert"), ("dp", "pipe")),
        P("groups", None),
        P("groups", None),
        P(("dp", "pipe"), "expert"),
        P(("dp", "pipe"), "expert"),
        P("expert", ("dp", "pipe")),
        P(("dp", "pipe"), "expert"),
        P(("dp", "pipe"), "expert"),
        P("expert", ("dp", "pipe")),
    )
    return jax.shard_map(
        body,
        mesh=mesh,
        in_specs=placed,
        out_specs=(
            P(("groups", "expert"), ("dp", "pipe")),
            P(("groups", "dp", "pipe"), "expert"),
            P(("groups", "dp", "pipe"), "expert"),
            P(("groups", "expert"), ("dp", "pipe")),
        ),
        check_vma=False,
    )
```

```python
import functools

import jax
import jax.numpy as jnp
from jax import lax
from jax.experimental import pallas as pl
from jax.experimental.pallas import tpu as pltpu
from jax.sharding import PartitionSpec as P

H = 896
BF = jnp.bfloat16
F32 = jnp.float32


def shift(value, axis, count, by):
    return lax.ppermute(value, axis, [(i, (i + by) % count) for i in range(count)])


def dot(a, b, contract_a=1, contract_b=0):
    return lax.dot_general(
        a, b, (((contract_a,), (contract_b,)), ((), ())), preferred_element_type=F32
    )


def whole():
    return pl.BlockSpec(memory_space=pltpu.VMEM)


def in_hbm():
    return pl.BlockSpec(memory_space=pltpu.HBM)


def anywhere():
    return pl.BlockSpec(memory_space=pl.ANY)


def scalars():
    return pl.BlockSpec(memory_space=pltpu.SMEM)


def load_start(pairs, sems, pieces):
    copies = []
    for which, (source, target) in enumerate(pairs):
        rows = source.shape[0] // pieces
        for i in range(pieces):
            part = pl.ds(i * rows, rows)
            copies.append(
                pltpu.make_async_copy(source.at[part], target.at[part], sems.at[which, i])
            )
    for copy in copies:
        copy.start()
    return copies


def far(value):
    return pltpu.with_memory_space_constraint(value, pltpu.HBM)


def prepare_kernel(
    ranks,
    capacity,
    dps,
    pipes,
    place,
    far_routes,
    far_shares,
    gate,
    up,
    picker,
    weights,
    gate_out,
    up_out,
    routes,
    shares,
    sems,
    table_sems,
):
    tables = [
        pltpu.make_async_copy(far_routes, routes, table_sems.at[0]),
        pltpu.make_async_copy(far_shares, shares, table_sems.at[1]),
    ]
    for copy in tables:
        copy.start()
    copies = load_start(((gate, gate_out), (up, up_out)), sems, 8)
    for copy in tables:
        copy.wait()
    rank, dp, pipe = place[0], place[1], place[2]
    experts, slots, token_count = picker.shape
    block = token_count // ranks
    per_piece = ranks // (dps * pipes)
    row = lax.broadcasted_iota(jnp.int32, (8, token_count), 0)
    names = row + rank * experts
    weight = jnp.zeros((8, token_count), F32)
    routed = jnp.zeros((8, token_count), F32)
    for k in range(routes.shape[0]):
        hit = (routes[k : k + 1, :] == names) & (row < experts)
        weight = weight + jnp.where(hit, shares[k : k + 1, :], 0.0)
        routed = routed + jnp.where(hit, 1.0, 0.0)
    t_from = lax.broadcasted_iota(jnp.int32, (token_count, token_count), 0)
    t_to = lax.broadcasted_iota(jnp.int32, (token_count, token_count), 1)
    earlier = jnp.where((t_from // block == t_to // block) & (t_from < t_to), 1.0, 0.0)
    within = dot(routed.astype(BF), earlier.astype(BF)).astype(jnp.int32)
    at_block = lax.broadcasted_iota(jnp.int32, (1, token_count), 1) // block
    at_pipe = lax.rem(at_block // (dps * per_piece) + pipes - pipe, pipes)
    at_dp = lax.rem(lax.rem(at_block // per_piece, dps) + dps - dp, dps)
    first = ((at_pipe * dps + at_dp) * per_piece + lax.rem(at_block, per_piece)) * capacity
    slot = jnp.where(routed > 0.0, within + first, -1)
    ids = lax.broadcasted_iota(jnp.int32, (slots, token_count), 0)
    for e in range(experts):
        hit = slot[e : e + 1] == ids
        picker[e] = jnp.where(hit, 1.0, 0.0).astype(BF)
        weights[e] = jnp.sum(jnp.where(hit, weight[e : e + 1], 0.0), axis=1, keepdims=True)
    for copy in copies:
        copy.wait()


def prepare(place, routes, shares, gate, up, ranks, dps, pipes, block, experts):
    assert experts <= 8
    capacity = block // 2
    token_count = block * ranks
    slots = capacity * ranks
    return pl.pallas_call(
        functools.partial(prepare_kernel, ranks, capacity, dps, pipes),
        in_specs=[scalars(), in_hbm(), in_hbm(), in_hbm(), in_hbm()],
        out_specs=(whole(), whole(), whole(), whole()),
        out_shape=(
            jax.ShapeDtypeStruct((experts, slots, token_count), BF),
            jax.ShapeDtypeStruct((experts, slots, 1), F32),
            pltpu.VMEM(gate.shape, BF),
            pltpu.VMEM(up.shape, BF),
        ),
        scratch_shapes=[
            pltpu.VMEM(routes.shape, routes.dtype),
            pltpu.VMEM(shares.shape, shares.dtype),
            pltpu.SemaphoreType.DMA((2, 8)),
            pltpu.SemaphoreType.DMA((2,)),
        ],
        compiler_params=pltpu.CompilerParams(vmem_limit_bytes=8 * 1024 * 1024),
        cost_estimate=pl.CostEstimate(
            flops=0, bytes_accessed=4 * gate.size, transcendentals=0
        ),
    )(place, far(routes), far(shares), far(gate), far(up))


def residual_kernel(ranks, *refs):
    student = refs[0][...].astype(F32)
    target = refs[ranks][...].astype(F32)
    for i in range(1, ranks):
        student = student + refs[i][...].astype(F32)
        target = target + refs[ranks + i][...].astype(F32)
    refs[-2][...] = student
    refs[-1][...] = (student - target).astype(BF)


def residual_of(student, target, before):
    ranks = len(student)
    shape = student[0].shape
    return pl.pallas_call(
        functools.partial(residual_kernel, ranks),
        in_specs=[whole()] * (2 * ranks) + [anywhere()] * len(before),
        out_specs=(whole(), whole()),
        out_shape=(jax.ShapeDtypeStruct(shape, F32), jax.ShapeDtypeStruct(shape, BF)),
        compiler_params=pltpu.CompilerParams(vmem_limit_bytes=4 * 1024 * 1024),
    )(*student, *target, *before)


def tile_of(size):
    return 256 if size % 256 == 0 else 128


def teacher_kernel(first, size, dps, pipes, place, tokens, gate, up, keep, send):
    dp, pipe = place[1], place[2]
    rows = tokens.shape[0] // (dps * pipes)
    half = dps * rows
    parts = []
    for j1 in range(pipes):
        for j0 in range(dps):
            piece = lax.rem(pipe + j1, pipes) * dps + lax.rem(dp + j0, dps)
            parts.append(tokens[pl.ds(pl.multiple_of(piece * rows, rows), rows), :])
    ordered = jnp.concatenate(parts, axis=0)
    tile = tile_of(size)
    for which, weight in enumerate((gate, up)):
        for i in range(size // tile):
            product = dot(ordered, weight[:, first + i * tile : first + (i + 1) * tile]).astype(BF)
            keep[which, :, i * tile : (i + 1) * tile] = product[:half]
            send[which, :, i * tile : (i + 1) * tile] = product[half:]


def teacher_pre(place, tokens, gate, up, first, size, dps, pipes):
    token_count, width = tokens.shape
    half = jax.ShapeDtypeStruct((2, token_count // pipes, size), BF)
    return pl.pallas_call(
        functools.partial(teacher_kernel, first, size, dps, pipes),
        in_specs=[scalars(), whole(), whole(), whole()],
        out_specs=(whole(), whole()),
        out_shape=(half, half),
        compiler_params=pltpu.CompilerParams(vmem_limit_bytes=8 * 1024 * 1024),
        cost_estimate=pl.CostEstimate(
            flops=4 * token_count * width * size, bytes_accessed=4 * width * size, transcendentals=0
        ),
    )(place, tokens, gate, up)


def expert_kernel(first, picker, tokens, gate, up, before, keep, send, held, sems):
    half = keep.shape[2]
    count = keep.shape[0]
    pieces = sems.shape[2]
    rows_each = gate.shape[0] // pieces
    copies = {}
    for i in range(count):
        for which, weight in enumerate((gate, up)):
            for p in range(pieces):
                part = pl.ds(p * rows_each, rows_each)
                columns = pl.ds((first + i) * H, H)
                copies[i, which, p] = pltpu.make_async_copy(
                    weight.at[part, columns], held.at[i, which, part], sems.at[i, which, p]
                )
                copies[i, which, p].start()
    for i in range(count):
        rows = dot(picker[first + i], tokens[...]).astype(BF)
        for which in range(2):
            for p in range(pieces):
                copies[i, which, p].wait()
            product = dot(rows, held[i, which]).astype(BF)
            keep[i, which] = product[:half]
            send[i, which] = product[half:]


def expert_pre(picker, tokens, gate, up, before, first, count):
    slots = picker.shape[1]
    width = tokens.shape[1]
    halves = jax.ShapeDtypeStruct((count, 2, slots // 2, H), BF)
    return pl.pallas_call(
        functools.partial(expert_kernel, first),
        in_specs=[whole(), whole(), in_hbm(), in_hbm(), anywhere()],
        out_specs=(whole(), whole()),
        out_shape=(halves, halves),
        scratch_shapes=[
            pltpu.VMEM((count, 2, width, H), BF),
            pltpu.SemaphoreType.DMA((count, 2, 4)),
        ],
        compiler_params=pltpu.CompilerParams(vmem_limit_bytes=16 * 1024 * 1024),
        cost_estimate=pl.CostEstimate(
            flops=count * 4 * slots * width * H,
            bytes_accessed=count * 4 * width * H,
            transcendentals=0,
        ),
    )(picker, tokens, far(gate), far(up), before)


def hidden_act_kernel(first, swap, mine, other, weight, *rest):
    pre, out = rest[-2:]
    count, _, rows = mine.shape[:3]
    for i in range(count):
        totals = []
        for which in range(2):
            total = mine[i, which].astype(F32)
            if swap:
                theirs = other[i, which].astype(F32)
                total = total + jnp.concatenate([theirs[rows // 2 :], theirs[: rows // 2]], axis=0)
            pre[i, which] = total
            totals.append(total)
        gate, up = totals
        out[i] = (gate * jax.nn.sigmoid(gate) * up * weight[first + i, :rows]).astype(BF)


def hidden_act(mine, other, swap, weight, before, first):
    count, _, rows, width = mine.shape
    return pl.pallas_call(
        functools.partial(hidden_act_kernel, first, swap),
        in_specs=[whole(), whole(), whole()] + [anywhere()] * len(before),
        out_specs=(whole(), whole()),
        out_shape=(
            jax.ShapeDtypeStruct(mine.shape, F32),
            jax.ShapeDtypeStruct((count, rows, width), BF),
        ),
        compiler_params=pltpu.CompilerParams(vmem_limit_bytes=8 * 1024 * 1024),
    )(mine, other, weight, *before)


def join_kernel(dps, pipes, place, *refs):
    out = refs[-1]
    dp, pipe = place[1], place[2]
    rows = out.shape[0] // (dps * pipes)
    at = 0
    for i in range((len(refs) - 1) // 2):
        size = refs[2 * i].shape[1]
        for j1 in range(pipes):
            for j0 in range(dps):
                piece = lax.rem(pipe + j1, pipes) * dps + lax.rem(dp + j0, dps)
                target = pl.ds(pl.multiple_of(piece * rows, rows), rows)
                out[target, at : at + size] = refs[2 * i + j1][j0 * rows : (j0 + 1) * rows, :]
        at += size


def join(place, parts, dps, pipes):
    assert pipes == 2
    flat = [value for pair in parts for value in pair]
    rows = flat[0].shape[0] * pipes
    width = sum(pair[0].shape[1] for pair in parts)
    return pl.pallas_call(
        functools.partial(join_kernel, dps, pipes),
        in_specs=[scalars()] + [whole()] * len(flat),
        out_specs=whole(),
        out_shape=jax.ShapeDtypeStruct((rows, width), BF),
        compiler_params=pltpu.CompilerParams(vmem_limit_bytes=8 * 1024 * 1024),
    )(place, *flat)


def spread_kernel(picker, hidden, out):
    for e in range(picker.shape[0]):
        out[:, e * H : (e + 1) * H] = dot(picker[e], hidden[e], 0, 0).astype(BF)


def spread(picker, hidden):
    count, slots, token_count = picker.shape
    return pl.pallas_call(
        spread_kernel,
        in_specs=[whole(), whole()],
        out_specs=whole(),
        out_shape=jax.ShapeDtypeStruct((token_count, count * H), BF),
        compiler_params=pltpu.CompilerParams(vmem_limit_bytes=8 * 1024 * 1024),
    )(picker, hidden)


def flip_kernel(dense, tokens, before, dense_out, tokens_out):
    dense_out[...] = dense[...].astype(F32).T.astype(BF)
    tokens_out[...] = tokens[...].astype(F32).T.astype(BF)


def flip(dense, tokens, before):
    return pl.pallas_call(
        flip_kernel,
        in_specs=[whole(), whole(), anywhere()],
        out_specs=(whole(), whole()),
        out_shape=(
            jax.ShapeDtypeStruct(dense.shape[::-1], BF),
            jax.ShapeDtypeStruct(tokens.shape[::-1], BF),
        ),
        compiler_params=pltpu.CompilerParams(vmem_limit_bytes=16 * 1024 * 1024),
    )(dense, tokens, before)


def hidden_grad_kernel(first, picker, residual, down, before, keep, send):
    half = keep.shape[1]
    for i in range(keep.shape[0]):
        e = first + i
        rows = dot(picker[e], residual[...]).astype(BF)
        product = dot(down[e * H : (e + 1) * H, :], rows, 1, 1).T.astype(BF)
        keep[i] = product[:half]
        send[i] = product[half:]


def hidden_grad_parts(picker, residual, down, before, first, count):
    slots = picker.shape[1]
    halves = jax.ShapeDtypeStruct((count, slots // 2, H), BF)
    return pl.pallas_call(
        functools.partial(hidden_grad_kernel, first),
        in_specs=[whole(), whole(), whole(), anywhere()],
        out_specs=(whole(), whole()),
        out_shape=(halves, halves),
        compiler_params=pltpu.CompilerParams(vmem_limit_bytes=8 * 1024 * 1024),
    )(picker, residual, down, before)


def hidden_grad_act_kernel(first, swap, mine, other, pre, weight, before, out):
    count, rows = mine.shape[:2]
    for i in range(count):
        total = mine[i].astype(F32)
        if swap:
            flipped = jnp.concatenate([other[i, rows // 2 :], other[i, : rows // 2]], axis=0)
            total = total + flipped.astype(F32)
        total = total * weight[first + i, :rows]
        pre_gate, pre_up = pre[i, 0], pre[i, 1]
        sig = jax.nn.sigmoid(pre_gate)
        gate_grad = total * pre_up * sig * (1.0 + pre_gate * (1.0 - sig))
        up_grad = total * pre_gate * sig
        out[i, 0] = gate_grad.astype(BF)
        out[i, 1] = up_grad.astype(BF)


def hidden_grad_act(mine, other, swap, pre, weight, before, first):
    count, rows, width = mine.shape
    return pl.pallas_call(
        functools.partial(hidden_grad_act_kernel, first, swap),
        in_specs=[whole(), whole(), whole(), whole(), anywhere()],
        out_specs=whole(),
        out_shape=jax.ShapeDtypeStruct((count, 2, rows, width), BF),
        compiler_params=pltpu.CompilerParams(vmem_limit_bytes=8 * 1024 * 1024),
    )(mine, other, pre, weight, before)


def down_grad_kernel(hidden, residual, before, out, done, held, sems):
    tiles = sems.shape[0]
    rows = hidden.shape[0] // tiles
    copies = []
    for i in range(tiles):
        part = pl.ds(i * rows, rows)
        held[part, :] = dot(hidden[part, :], residual[...]).astype(BF)
        copies.append(pltpu.make_async_copy(held.at[part], out.at[part], sems.at[i]))
        copies[-1].start()
    done[...] = jnp.zeros_like(done)
    for copy in copies:
        copy.wait()


def down_grad(hidden, residual, before):
    rows, token_count = hidden.shape
    width = residual.shape[1]
    return pl.pallas_call(
        down_grad_kernel,
        in_specs=[whole(), whole(), anywhere()],
        out_specs=(in_hbm(), whole()),
        out_shape=(
            jax.ShapeDtypeStruct((rows, width), BF),
            jax.ShapeDtypeStruct((8, 128), F32),
        ),
        scratch_shapes=[
            pltpu.VMEM((rows, width), BF),
            pltpu.SemaphoreType.DMA((rows // (H // 2),)),
        ],
        compiler_params=pltpu.CompilerParams(vmem_limit_bytes=16 * 1024 * 1024),
        cost_estimate=pl.CostEstimate(
            flops=2 * rows * width * token_count,
            bytes_accessed=2 * rows * width,
            transcendentals=0,
        ),
    )(hidden, residual, before)


def input_grad_kernel(group, picker, tokens, *rest):
    outs, held, sems = rest[-4:-2], rest[-2], rest[-1]
    count = picker.shape[0]
    splits = sems.shape[2]
    rows = tokens.shape[0] // splits
    copies = []
    for i in range(count):
        for which in range(2):
            mine, theirs = rest[i // group * 2], rest[i // group * 2 + 1]
            grad = jnp.concatenate([mine[i % group, which], theirs[i % group, which]], axis=0)
            dense = dot(picker[i], grad, 0, 0).astype(BF)
            for r in range(splits):
                part = pl.ds(r * rows, rows)
                columns = pl.ds(i * H, H)
                held[i, which, part] = dot(tokens[part, :], dense).astype(BF)
                copies.append(
                    pltpu.make_async_copy(
                        held.at[i, which, part], outs[which].at[part, columns], sems.at[i, which, r]
                    )
                )
                copies[-1].start()
    for copy in copies:
        copy.wait()


def input_grads(picker, tokens, parts):
    count, slots, token_count = picker.shape
    width = tokens.shape[0]
    out = jax.ShapeDtypeStruct((width, count * H), BF)
    return pl.pallas_call(
        functools.partial(input_grad_kernel, count // len(parts)),
        in_specs=[whole()] * (2 + 2 * len(parts)),
        out_specs=(in_hbm(), in_hbm()),
        out_shape=(out, out),
        scratch_shapes=[
            pltpu.VMEM((count, 2, width, H), BF),
            pltpu.SemaphoreType.DMA((count, 2, 2)),
        ],
        compiler_params=pltpu.CompilerParams(vmem_limit_bytes=24 * 1024 * 1024),
        cost_estimate=pl.CostEstimate(
            flops=count * 4 * token_count * width * H,
            bytes_accessed=count * 4 * width * H,
            transcendentals=0,
        ),
    )(picker, tokens, *[value for pair in parts for value in pair])


def add(a, b):
    return (a.astype(F32) + b.astype(F32)).astype(BF)


def split_rows(value, count):
    rows = value.shape[-2] // count
    return [value[..., i * rows : (i + 1) * rows, :] for i in range(count)]


def scatter_dp(value, count):
    pieces = split_rows(value, count)
    total = pieces[0].astype(F32)
    for s in range(1, count):
        total = total + shift(pieces[s], "dp", count, s).astype(F32)
    return total


def gather_dp_parts(value, count):
    return [value] + [shift(value, "dp", count, -s) for s in range(1, count)]


def gather_dp(value, count):
    return jnp.concatenate(gather_dp_parts(value, count), axis=-2)


def exchange_dp(value, count):
    if count == 2:
        return value, shift(value, "dp", count, 1)
    total = gather_dp(scatter_dp(value, count).astype(BF), count)
    return total, total


def body(
    tokens,
    routes,
    gate_weights,
    teacher_gate,
    teacher_up,
    teacher_down,
    expert_gate,
    expert_up,
    expert_down,
):
    ranks = lax.axis_size("expert")
    dps = lax.axis_size("dp")
    pipes = lax.axis_size("pipe")
    rank = lax.axis_index("expert")
    dp = lax.axis_index("dp")
    pipe = lax.axis_index("pipe")
    block, width = tokens.shape
    token_count = block * ranks
    experts = expert_gate.shape[1] // H
    slots = block // 2 * ranks
    place = jnp.stack([rank, dp, pipe]).astype(jnp.int32)

    paired = ranks & (ranks - 1) == 0

    def to_partner(value, s):
        if paired:
            return lax.ppermute(value, "expert", [(i, i ^ s) for i in range(ranks)])
        return shift(value, "expert", ranks, s)

    def target_of(s):
        return rank ^ s if paired else (rank + s) % ranks

    def source_of(s):
        return rank ^ s if paired else (rank + ranks - s) % ranks

    def place_rows(blocks):
        rows = jnp.zeros((token_count, blocks[0].shape[1]), BF)
        for s, value in enumerate(blocks):
            rows = lax.dynamic_update_slice(rows, value, (source_of(s) * block, 0))
        return rows

    def gather_tokens(mine):
        return place_rows([mine] + [to_partner(mine, s) for s in range(1, ranks)])

    def gather_forwarded(mine):
        if not paired or ranks != 4:
            return gather_tokens(mine)
        far = to_partner(mine, 2)
        return place_rows([mine, to_partner(mine, 1), far, to_partner(far, 1)])

    def to_owners(product):
        def block_of(r):
            return lax.dynamic_slice_in_dim(product, r * block, block, axis=0)

        return [block_of(rank)] + [to_partner(block_of(target_of(s)), s) for s in range(1, ranks)]

    base = gather_tokens(tokens)
    picker, slot_weight, gate_near, up_near = prepare(
        place, routes.T, gate_weights.T, teacher_gate, teacher_up, ranks, dps, pipes, block, experts
    )

    chunks = 2 if teacher_gate.shape[1] % 512 == 0 else 1
    size = teacher_gate.shape[1] // chunks
    halves = []
    for i in range(chunks):
        keep, send = teacher_pre(place, base, gate_near, up_near, i * size, size, dps, pipes)
        halves.append(add(keep, shift(send, "pipe", pipes, 1)))

    group = 2 if experts % 2 == 0 else 1
    firsts = range(0, experts, group)
    parts = []
    last = halves[-1]
    for first in firsts:
        keep, send = expert_pre(picker, base, expert_gate, expert_up, last, first, group)
        last = keep
        parts.append((keep, shift(send, "pipe", pipes, 1)))
    hiddens = []
    for half in halves:
        total = scatter_dp(half, dps)
        hidden = (jax.nn.silu(total[0]) * total[1]).astype(BF)
        hidden = jnp.concatenate(gather_dp_parts(hidden, dps), axis=0)
        hiddens.append((hidden, shift(hidden, "pipe", pipes, 1)))
    hidden = join(place, hiddens, dps, pipes)
    target = to_owners(jnp.dot(hidden, teacher_down, preferred_element_type=F32).astype(BF))

    pre, weighted = [], []
    for first, (keep, theirs) in zip(firsts, parts):
        mine, other = exchange_dp(add(keep, theirs), dps)
        total, part = hidden_act(mine, other, dps == 2, slot_weight, target[-1:], first)
        pre.append(total)
        weighted.append(jnp.concatenate([part, shift(part, "pipe", pipes, 1)], axis=1))
    weighted = jnp.concatenate(weighted, axis=0)

    dense = spread(picker, weighted)
    product = jnp.dot(dense, expert_down, preferred_element_type=F32).astype(BF)
    student = to_owners(product)
    dense_flipped, base_flipped = flip(dense, base, product)
    student_sum, residual = residual_of(student, target, (base_flipped,))
    residual = gather_forwarded(residual)

    sums = []
    last = residual
    for first in firsts:
        keep, send = hidden_grad_parts(picker, residual, expert_down, last, first, group)
        last = keep
        sums.append(add(keep, shift(send, "pipe", pipes, 1)))
    pairs = [exchange_dp(value, dps) for value in sums]
    grad_down, done = down_grad(dense_flipped, residual, sums[-1])
    activations = []
    for i, first in enumerate(firsts):
        mine = hidden_grad_act(*pairs[i], dps == 2, pre[i], slot_weight, done, first)
        activations.append((mine, shift(mine, "pipe", pipes, 1)))
    grads = input_grads(picker, base_flipped, activations)
    return (student_sum.astype(BF), grads[0], grads[1], grad_down)


def solution(mesh):
    placed = (
        P(("groups", "expert"), ("dp", "pipe")),
        P("groups", None),
        P("groups", None),
        P(("dp", "pipe"), "expert"),
        P(("dp", "pipe"), "expert"),
        P("expert", ("dp", "pipe")),
        P(("dp", "pipe"), "expert"),
        P(("dp", "pipe"), "expert"),
        P("expert", ("dp", "pipe")),
    )
    return jax.shard_map(
        body,
        mesh=mesh,
        in_specs=placed,
        out_specs=(
            P(("groups", "expert"), ("dp", "pipe")),
            P(("groups", "dp", "pipe"), "expert"),
            P(("groups", "dp", "pipe"), "expert"),
            P(("groups", "expert"), ("dp", "pipe")),
        ),
        check_vma=False,
    )
```

```python
import functools

import jax
import jax.numpy as jnp
from jax import lax
from jax.experimental import pallas as pl
from jax.experimental.pallas import tpu as pltpu
from jax.sharding import PartitionSpec as P

H = 896
BF = jnp.bfloat16
F32 = jnp.float32


def shift(value, axis, count, by):
    return lax.ppermute(value, axis, [(i, (i + by) % count) for i in range(count)])


def dot(a, b, contract_a=1, contract_b=0):
    return lax.dot_general(
        a, b, (((contract_a,), (contract_b,)), ((), ())), preferred_element_type=F32
    )


def whole():
    return pl.BlockSpec(memory_space=pltpu.VMEM)


def in_hbm():
    return pl.BlockSpec(memory_space=pltpu.HBM)


def anywhere():
    return pl.BlockSpec(memory_space=pl.ANY)


def scalars():
    return pl.BlockSpec(memory_space=pltpu.SMEM)


def load_start(pairs, sems, pieces):
    copies = []
    for which, (source, target) in enumerate(pairs):
        rows = source.shape[0] // pieces
        for i in range(pieces):
            part = pl.ds(i * rows, rows)
            copies.append(
                pltpu.make_async_copy(source.at[part], target.at[part], sems.at[which, i])
            )
    for copy in copies:
        copy.start()
    return copies


def far(value):
    return pltpu.with_memory_space_constraint(value, pltpu.HBM)


def prepare_kernel(
    near_first,
    ranks,
    capacity,
    dps,
    pipes,
    place,
    far_routes,
    far_shares,
    gate,
    up,
    picker,
    weights,
    gate_out,
    up_out,
    routes,
    shares,
    sems,
    table_sems,
):
    tables = [
        pltpu.make_async_copy(far_routes, routes, table_sems.at[0]),
        pltpu.make_async_copy(far_shares, shares, table_sems.at[1]),
    ]
    for copy in tables:
        copy.start()
    copies = load_start(((gate, gate_out), (up, up_out)), sems, 8)
    for copy in tables:
        copy.wait()
    rank, dp, pipe = place[0], place[1], place[2]
    experts, slots, token_count = picker.shape
    block = token_count // ranks
    per_piece = ranks // (dps * pipes)
    row = lax.broadcasted_iota(jnp.int32, (8, token_count), 0)
    names = row + rank * experts
    weight = jnp.zeros((8, token_count), F32)
    routed = jnp.zeros((8, token_count), F32)
    for k in range(routes.shape[0]):
        hit = (routes[k : k + 1, :] == names) & (row < experts)
        weight = weight + jnp.where(hit, shares[k : k + 1, :], 0.0)
        routed = routed + jnp.where(hit, 1.0, 0.0)
    if near_first:
        swapped = rank // 2 == 1
        weight = jnp.where(swapped, pltpu.roll(weight, token_count // 2, 1), weight)
        routed = jnp.where(swapped, pltpu.roll(routed, token_count // 2, 1), routed)
    t_from = lax.broadcasted_iota(jnp.int32, (token_count, token_count), 0)
    t_to = lax.broadcasted_iota(jnp.int32, (token_count, token_count), 1)
    earlier = jnp.where((t_from // block == t_to // block) & (t_from < t_to), 1.0, 0.0)
    within = dot(routed.astype(BF), earlier.astype(BF)).astype(jnp.int32)
    at_block = lax.broadcasted_iota(jnp.int32, (1, token_count), 1) // block
    if near_first:
        at_pipe = lax.rem(at_block + pipe, 2)
        first = (at_pipe * 2 + at_block // 2) * capacity
    else:
        at_pipe = lax.rem(at_block // (dps * per_piece) + pipes - pipe, pipes)
        at_dp = lax.rem(lax.rem(at_block // per_piece, dps) + dps - dp, dps)
        first = ((at_pipe * dps + at_dp) * per_piece + lax.rem(at_block, per_piece)) * capacity
    slot = jnp.where(routed > 0.0, within + first, -1)
    ids = lax.broadcasted_iota(jnp.int32, (slots, token_count), 0)
    for e in range(experts):
        hit = slot[e : e + 1] == ids
        picker[e] = jnp.where(hit, 1.0, 0.0).astype(BF)
        weights[e] = jnp.sum(jnp.where(hit, weight[e : e + 1], 0.0), axis=1, keepdims=True)
    for copy in copies:
        copy.wait()


def prepare(place, routes, shares, gate, up, near_first, ranks, dps, pipes, block, experts):
    assert experts <= 8
    capacity = block // 2
    token_count = block * ranks
    slots = capacity * ranks
    return pl.pallas_call(
        functools.partial(prepare_kernel, near_first, ranks, capacity, dps, pipes),
        in_specs=[scalars(), in_hbm(), in_hbm(), in_hbm(), in_hbm()],
        out_specs=(whole(), whole(), whole(), whole()),
        out_shape=(
            jax.ShapeDtypeStruct((experts, slots, token_count), BF),
            jax.ShapeDtypeStruct((experts, slots, 1), F32),
            pltpu.VMEM(gate.shape, BF),
            pltpu.VMEM(up.shape, BF),
        ),
        scratch_shapes=[
            pltpu.VMEM(routes.shape, routes.dtype),
            pltpu.VMEM(shares.shape, shares.dtype),
            pltpu.SemaphoreType.DMA((2, 8)),
            pltpu.SemaphoreType.DMA((2,)),
        ],
        compiler_params=pltpu.CompilerParams(vmem_limit_bytes=8 * 1024 * 1024),
        cost_estimate=pl.CostEstimate(
            flops=0, bytes_accessed=4 * gate.size, transcendentals=0
        ),
    )(place, far(routes), far(shares), far(gate), far(up))


def residual_kernel(ranks, *refs):
    student = refs[0][...].astype(F32)
    target = refs[ranks][...].astype(F32)
    for i in range(1, ranks):
        student = student + refs[i][...].astype(F32)
        target = target + refs[ranks + i][...].astype(F32)
    refs[-2][...] = student
    refs[-1][...] = (student - target).astype(BF)


def residual_of(student, target, before):
    ranks = len(student)
    shape = student[0].shape
    return pl.pallas_call(
        functools.partial(residual_kernel, ranks),
        in_specs=[whole()] * (2 * ranks) + [anywhere()] * len(before),
        out_specs=(whole(), whole()),
        out_shape=(jax.ShapeDtypeStruct(shape, F32), jax.ShapeDtypeStruct(shape, BF)),
        compiler_params=pltpu.CompilerParams(vmem_limit_bytes=4 * 1024 * 1024),
    )(*student, *target, *before)


def tile_of(size):
    return 256 if size % 256 == 0 else 128


def teacher_kernel(first, size, dps, pipes, place, tokens, gate, up, keep, send):
    dp, pipe = place[1], place[2]
    rows = tokens.shape[0] // (dps * pipes)
    half = dps * rows
    parts = []
    for j1 in range(pipes):
        for j0 in range(dps):
            piece = lax.rem(pipe + j1, pipes) * dps + lax.rem(dp + j0, dps)
            parts.append(tokens[pl.ds(pl.multiple_of(piece * rows, rows), rows), :])
    ordered = jnp.concatenate(parts, axis=0)
    tile = tile_of(size)
    for which, weight in enumerate((gate, up)):
        for i in range(size // tile):
            product = dot(ordered, weight[:, first + i * tile : first + (i + 1) * tile]).astype(BF)
            keep[which, :, i * tile : (i + 1) * tile] = product[:half]
            send[which, :, i * tile : (i + 1) * tile] = product[half:]


def teacher_pre(place, tokens, gate, up, first, size, dps, pipes):
    token_count, width = tokens.shape
    half = jax.ShapeDtypeStruct((2, token_count // pipes, size), BF)
    return pl.pallas_call(
        functools.partial(teacher_kernel, first, size, dps, pipes),
        in_specs=[scalars(), whole(), whole(), whole()],
        out_specs=(whole(), whole()),
        out_shape=(half, half),
        compiler_params=pltpu.CompilerParams(vmem_limit_bytes=8 * 1024 * 1024),
        cost_estimate=pl.CostEstimate(
            flops=4 * token_count * width * size, bytes_accessed=4 * width * size, transcendentals=0
        ),
    )(place, tokens, gate, up)


def expert_kernel(cuts, picker, tokens, gate, up, before, *rest):
    outs, held, sems = rest[:-2], rest[-2], rest[-1]
    count, slots = picker.shape[:2]
    pieces = sems.shape[2]
    rows_each = gate.shape[0] // pieces
    copies = {}
    for e in range(count):
        for which, weight in enumerate((gate, up)):
            for p in range(pieces):
                part = pl.ds(p * rows_each, rows_each)
                columns = pl.ds(e * H, H)
                copies[e, which, p] = pltpu.make_async_copy(
                    weight.at[part, columns], held.at[e, which, part], sems.at[e, which, p]
                )
                copies[e, which, p].start()
    for e in range(count):
        rows = dot(picker[e], tokens[...]).astype(BF)
        for which in range(2):
            for p in range(pieces):
                copies[e, which, p].wait()
            product = dot(rows, held[e, which]).astype(BF)
            for i, (low, high) in enumerate(cuts):
                outs[2 * i][e, which] = product[low:high]
                outs[2 * i + 1][e, which] = product[slots // 2 + low : slots // 2 + high]


def expert_pre(picker, tokens, gate, up, before, cuts):
    count, slots = picker.shape[:2]
    width = tokens.shape[1]
    outs = []
    for low, high in cuts:
        outs += [jax.ShapeDtypeStruct((count, 2, high - low, H), BF)] * 2
    return pl.pallas_call(
        functools.partial(expert_kernel, cuts),
        in_specs=[whole(), whole(), in_hbm(), in_hbm(), anywhere()],
        out_specs=tuple(whole() for _ in outs),
        out_shape=tuple(outs),
        scratch_shapes=[
            pltpu.VMEM((count, 2, width, H), BF),
            pltpu.SemaphoreType.DMA((count, 2, 4)),
        ],
        compiler_params=pltpu.CompilerParams(vmem_limit_bytes=24 * 1024 * 1024),
        cost_estimate=pl.CostEstimate(
            flops=count * 4 * slots * width * H,
            bytes_accessed=count * 4 * width * H,
            transcendentals=0,
        ),
    )(picker, tokens, far(gate), far(up), before)


def add_kernel(a, b, before, out):
    out[...] = (a[...].astype(F32) + b[...].astype(F32)).astype(BF)


def add_after(a, b, before):
    return pl.pallas_call(
        add_kernel,
        in_specs=[whole(), whole(), anywhere()],
        out_specs=whole(),
        out_shape=jax.ShapeDtypeStruct(a.shape, BF),
        compiler_params=pltpu.CompilerParams(vmem_limit_bytes=4 * 1024 * 1024),
    )(a, b, before)


def dp_total(mode, mine, other):
    total = mine.astype(F32)
    if mode == "add":
        total = total + other.astype(F32)
    if mode == "swap":
        theirs = other.astype(F32)
        rows = theirs.shape[0]
        total = total + jnp.concatenate([theirs[rows // 2 :], theirs[: rows // 2]], axis=0)
    return total


def hidden_act_kernel(mode, low, mine, other, weight, *rest):
    pre, out = rest[-2:]
    count, _, rows = mine.shape[:3]
    for i in range(count):
        gate = dp_total(mode, mine[i, 0], other[i, 0])
        up = dp_total(mode, mine[i, 1], other[i, 1])
        pre[i, 0] = gate
        pre[i, 1] = up
        out[i] = (gate * jax.nn.sigmoid(gate) * up * weight[i, low : low + rows]).astype(BF)


def hidden_act(mine, other, mode, weight, before, low):
    count, _, rows, width = mine.shape
    return pl.pallas_call(
        functools.partial(hidden_act_kernel, mode, low),
        in_specs=[whole(), whole(), whole()] + [anywhere()] * len(before),
        out_specs=(whole(), whole()),
        out_shape=(
            jax.ShapeDtypeStruct(mine.shape, F32),
            jax.ShapeDtypeStruct((count, rows, width), BF),
        ),
        compiler_params=pltpu.CompilerParams(vmem_limit_bytes=8 * 1024 * 1024),
    )(mine, other, weight, *before)


def pair_kernel(*refs):
    values, out = refs[:-2], refs[-1]
    rows = out.shape[0] // len(values)
    for i, value in enumerate(values):
        out[i * rows : (i + 1) * rows, :] = value[...]


def pair(values, before):
    rows, width = values[0].shape
    return pl.pallas_call(
        pair_kernel,
        in_specs=[whole()] * len(values) + [anywhere()],
        out_specs=whole(),
        out_shape=jax.ShapeDtypeStruct((rows * len(values), width), BF),
        compiler_params=pltpu.CompilerParams(vmem_limit_bytes=4 * 1024 * 1024),
    )(*values, before)


def join_kernel(dps, pipes, place, *refs):
    out = refs[-1]
    dp, pipe = place[1], place[2]
    rows = out.shape[0] // (dps * pipes)
    at = 0
    for i in range((len(refs) - 1) // 2):
        size = refs[2 * i].shape[1]
        for j1 in range(pipes):
            for j0 in range(dps):
                piece = lax.rem(pipe + j1, pipes) * dps + lax.rem(dp + j0, dps)
                target = pl.ds(pl.multiple_of(piece * rows, rows), rows)
                out[target, at : at + size] = refs[2 * i + j1][j0 * rows : (j0 + 1) * rows, :]
        at += size


def join(place, parts, dps, pipes):
    assert pipes == 2
    flat = [value for pair in parts for value in pair]
    rows = flat[0].shape[0] * pipes
    width = sum(pair[0].shape[1] for pair in parts)
    return pl.pallas_call(
        functools.partial(join_kernel, dps, pipes),
        in_specs=[scalars()] + [whole()] * len(flat),
        out_specs=whole(),
        out_shape=jax.ShapeDtypeStruct((rows, width), BF),
        compiler_params=pltpu.CompilerParams(vmem_limit_bytes=8 * 1024 * 1024),
    )(place, *flat)


def slot_rows(table, low, high):
    half = table.shape[0] // 2
    return jnp.concatenate([table[low:high], table[half + low : half + high]], axis=0)


def spread_kernel(cut, tokens, picker, mine, theirs, out):
    for e in range(picker.shape[0]):
        hidden = jnp.concatenate([mine[e], theirs[e]], axis=0)
        dense = dot(slot_rows(picker[e], *cut), hidden, 0, 0)[tokens[0] : tokens[1]]
        out[:, e * H : (e + 1) * H] = dense.astype(BF)


def spread(picker, mine, theirs, cut, tokens):
    count = picker.shape[0]
    return pl.pallas_call(
        functools.partial(spread_kernel, cut, tokens),
        in_specs=[whole()] * 3,
        out_specs=whole(),
        out_shape=jax.ShapeDtypeStruct((tokens[1] - tokens[0], count * H), BF),
        compiler_params=pltpu.CompilerParams(vmem_limit_bytes=8 * 1024 * 1024),
    )(picker, mine, theirs)


def flip_kernel(*refs):
    dense_out, tokens_out = refs[-2:]
    tokens = refs[-4]
    dense = jnp.concatenate([value[...].astype(F32) for value in refs[:-4]], axis=0)
    dense_out[...] = dense.T.astype(BF)
    tokens_out[...] = tokens[...].astype(F32).T.astype(BF)


def flip(dense, tokens, before):
    return pl.pallas_call(
        flip_kernel,
        in_specs=[whole()] * (len(dense) + 1) + [anywhere()],
        out_specs=(whole(), whole()),
        out_shape=(
            jax.ShapeDtypeStruct((dense[0].shape[1], tokens.shape[0]), BF),
            jax.ShapeDtypeStruct(tokens.shape[::-1], BF),
        ),
        compiler_params=pltpu.CompilerParams(vmem_limit_bytes=16 * 1024 * 1024),
    )(*dense, tokens, before)


def hidden_grad_kernel(cut, picker, residual, down, before, keep, send):
    rows = keep.shape[1]
    for e in range(keep.shape[0]):
        picked = dot(slot_rows(picker[e], *cut), residual[...]).astype(BF)
        product = dot(down[e * H : (e + 1) * H, :], picked, 1, 1).T.astype(BF)
        keep[e] = product[:rows]
        send[e] = product[rows:]


def hidden_grad_parts(picker, residual, down, before, cut):
    count = picker.shape[0]
    part = jax.ShapeDtypeStruct((count, cut[1] - cut[0], H), BF)
    return pl.pallas_call(
        functools.partial(hidden_grad_kernel, cut),
        in_specs=[whole(), whole(), whole(), anywhere()],
        out_specs=(whole(), whole()),
        out_shape=(part, part),
        compiler_params=pltpu.CompilerParams(vmem_limit_bytes=8 * 1024 * 1024),
    )(picker, residual, down, before)


def hidden_grad_act_kernel(mode, low, mine, other, pre, weight, before, out):
    count, rows = mine.shape[:2]
    for i in range(count):
        total = dp_total(mode, mine[i], other[i]) * weight[i, low : low + rows]
        pre_gate, pre_up = pre[i, 0], pre[i, 1]
        sig = jax.nn.sigmoid(pre_gate)
        gate_grad = total * pre_up * sig * (1.0 + pre_gate * (1.0 - sig))
        up_grad = total * pre_gate * sig
        out[i, 0] = gate_grad.astype(BF)
        out[i, 1] = up_grad.astype(BF)


def hidden_grad_act(mine, other, mode, pre, weight, before, low):
    count, rows, width = mine.shape
    return pl.pallas_call(
        functools.partial(hidden_grad_act_kernel, mode, low),
        in_specs=[whole(), whole(), whole(), whole(), anywhere()],
        out_specs=whole(),
        out_shape=jax.ShapeDtypeStruct((count, 2, rows, width), BF),
        compiler_params=pltpu.CompilerParams(vmem_limit_bytes=8 * 1024 * 1024),
    )(mine, other, pre, weight, before)


def down_grad_kernel(hidden, residual, before, out, done, held, sems):
    tiles = sems.shape[0]
    rows = hidden.shape[0] // tiles
    copies = []
    for i in range(tiles):
        part = pl.ds(i * rows, rows)
        held[part, :] = dot(hidden[part, :], residual[...]).astype(BF)
        copies.append(pltpu.make_async_copy(held.at[part], out.at[part], sems.at[i]))
        copies[-1].start()
    done[...] = jnp.zeros_like(done)
    for copy in copies:
        copy.wait()


def down_grad(hidden, residual, before):
    rows, token_count = hidden.shape
    width = residual.shape[1]
    return pl.pallas_call(
        down_grad_kernel,
        in_specs=[whole(), whole(), anywhere()],
        out_specs=(in_hbm(), whole()),
        out_shape=(
            jax.ShapeDtypeStruct((rows, width), BF),
            jax.ShapeDtypeStruct((8, 128), F32),
        ),
        scratch_shapes=[
            pltpu.VMEM((rows, width), BF),
            pltpu.SemaphoreType.DMA((rows // (H // 2),)),
        ],
        compiler_params=pltpu.CompilerParams(vmem_limit_bytes=16 * 1024 * 1024),
        cost_estimate=pl.CostEstimate(
            flops=2 * rows * width * token_count,
            bytes_accessed=2 * rows * width,
            transcendentals=0,
        ),
    )(hidden, residual, before)


def input_grad_kernel(picker, tokens, *rest):
    parts, outs, held, sems = rest[:-4], rest[-4:-2], rest[-2], rest[-1]
    count = picker.shape[0]
    splits = sems.shape[2]
    rows = tokens.shape[0] // splits
    copies = []
    for i in range(count):
        for which in range(2):
            grad = jnp.concatenate([value[i, which] for value in parts], axis=0)
            dense = dot(picker[i], grad, 0, 0).astype(BF)
            for r in range(splits):
                part = pl.ds(r * rows, rows)
                columns = pl.ds(i * H, H)
                held[i, which, part] = dot(tokens[part, :], dense).astype(BF)
                copies.append(
                    pltpu.make_async_copy(
                        held.at[i, which, part], outs[which].at[part, columns], sems.at[i, which, r]
                    )
                )
                copies[-1].start()
    for copy in copies:
        copy.wait()


def input_grads(picker, tokens, parts):
    count, slots, token_count = picker.shape
    width = tokens.shape[0]
    out = jax.ShapeDtypeStruct((width, count * H), BF)
    return pl.pallas_call(
        input_grad_kernel,
        in_specs=[whole()] * (2 + len(parts)),
        out_specs=(in_hbm(), in_hbm()),
        out_shape=(out, out),
        scratch_shapes=[
            pltpu.VMEM((count, 2, width, H), BF),
            pltpu.SemaphoreType.DMA((count, 2, 2)),
        ],
        compiler_params=pltpu.CompilerParams(vmem_limit_bytes=24 * 1024 * 1024),
        cost_estimate=pl.CostEstimate(
            flops=count * 4 * token_count * width * H,
            bytes_accessed=count * 4 * width * H,
            transcendentals=0,
        ),
    )(picker, tokens, *parts)


def add(a, b):
    return (a.astype(F32) + b.astype(F32)).astype(BF)


def split_rows(value, count):
    rows = value.shape[-2] // count
    return [value[..., i * rows : (i + 1) * rows, :] for i in range(count)]


def scatter_dp(value, count):
    pieces = split_rows(value, count)
    total = pieces[0].astype(F32)
    for s in range(1, count):
        total = total + shift(pieces[s], "dp", count, s).astype(F32)
    return total


def gather_dp_parts(value, count):
    return [value] + [shift(value, "dp", count, -s) for s in range(1, count)]


def gather_dp(value, count):
    return jnp.concatenate(gather_dp_parts(value, count), axis=-2)


def exchange_dp(value, count, same_order):
    if count == 2:
        return value, shift(value, "dp", count, 1), "add" if same_order else "swap"
    total = gather_dp(scatter_dp(value, count).astype(BF), count)
    return total, total, "whole"


def body(
    tokens,
    routes,
    gate_weights,
    teacher_gate,
    teacher_up,
    teacher_down,
    expert_gate,
    expert_up,
    expert_down,
):
    ranks = lax.axis_size("expert")
    dps = lax.axis_size("dp")
    pipes = lax.axis_size("pipe")
    rank = lax.axis_index("expert")
    dp = lax.axis_index("dp")
    pipe = lax.axis_index("pipe")
    block, width = tokens.shape
    token_count = block * ranks
    experts = expert_gate.shape[1] // H
    slots = block // 2 * ranks
    place = jnp.stack([rank, dp, pipe]).astype(jnp.int32)

    near_first = (ranks, dps, pipes) == (4, 2, 2)
    offset = rank // 2 * 2 if near_first else 0
    capacity = slots // ranks
    if near_first:
        cuts = [(capacity, 2 * capacity), (0, capacity)]
        token_cuts = [(token_count // 2, token_count), (0, token_count // 2)]
    else:
        cuts = [(0, slots // 2)]
        token_cuts = [(0, token_count)]

    paired = ranks & (ranks - 1) == 0

    def to_partner(value, s):
        if paired:
            return lax.ppermute(value, "expert", [(i, i ^ s) for i in range(ranks)])
        return shift(value, "expert", ranks, s)

    def target_of(s):
        return rank ^ s if paired else (rank + s) % ranks

    def source_of(s):
        return rank ^ s if paired else (rank + ranks - s) % ranks

    def place_rows(rows, blocks):
        for s, value in blocks:
            at = (source_of(s) ^ offset) * block
            rows = lax.dynamic_update_slice(rows, value, (at, 0))
        return rows

    def gather_tokens(mine):
        rows = place_rows(jnp.zeros((token_count, mine.shape[1]), BF), [(0, mine)])
        near = range(1, 2 if near_first else ranks)
        near_rows = place_rows(rows, [(s, to_partner(mine, s)) for s in near])
        rest = range(2, ranks if near_first else 2)
        return near_rows, place_rows(near_rows, [(s, to_partner(mine, s)) for s in rest])

    def to_owners(product, first, count, low):
        received = []
        for s in range(first, first + count):
            at = (target_of(s) ^ offset) * block - low
            sent = lax.dynamic_slice_in_dim(product, at, block, axis=0)
            received.append(to_partner(sent, s) if s else sent)
        return received

    _, base = gather_tokens(tokens)
    picker, slot_weight, gate_near, up_near = prepare(
        place,
        routes.T,
        gate_weights.T,
        teacher_gate,
        teacher_up,
        near_first,
        ranks,
        dps,
        pipes,
        block,
        experts,
    )

    chunks = 2 if teacher_gate.shape[1] % 512 == 0 else 1
    size = teacher_gate.shape[1] // chunks
    halves = []
    for i in range(chunks):
        keep, send = teacher_pre(place, base, gate_near, up_near, i * size, size, dps, pipes)
        halves.append(add(keep, shift(send, "pipe", pipes, 1)))

    outs = expert_pre(picker, base, expert_gate, expert_up, halves[-1], cuts)
    parts, half = [], halves[-1]
    for i in range(len(cuts)):
        half = add_after(outs[2 * i], shift(outs[2 * i + 1], "pipe", pipes, 1), half)
        parts.append(exchange_dp(half, dps, near_first))
    hiddens = []
    for half in halves:
        total = scatter_dp(half, dps)
        hidden = (jax.nn.silu(total[0]) * total[1]).astype(BF)
        hidden = pair(gather_dp_parts(hidden, dps), parts[0][0])
        hiddens.append((hidden, shift(hidden, "pipe", pipes, 1)))
    hidden = join(place, hiddens, dps, pipes)
    product = jnp.dot(hidden, teacher_down, preferred_element_type=F32).astype(BF)
    target = to_owners(product, 0, ranks, 0)

    pre, dense, student = [], [], []
    for (mine, other, mode), cut, rows in zip(parts, cuts, token_cuts):
        total, part = hidden_act(mine, other, mode, slot_weight, [product], cut[0])
        pre.append(total)
        dense.append(spread(picker, part, shift(part, "pipe", pipes, 1), cut, rows))
        product = jnp.dot(dense[-1], expert_down, preferred_element_type=F32).astype(BF)
        count = (rows[1] - rows[0]) // block
        student = to_owners(product, rows[0] // block, count, rows[0]) + student
    dense_flipped, base_flipped = flip(dense[::-1], base, product)
    student_sum, residual = residual_of(student, target, (base_flipped,))

    residuals = gather_tokens(residual)
    sums, last = [], residual
    for rows, cut in zip(residuals[-len(cuts) :], cuts[::-1]):
        keep, send = hidden_grad_parts(picker, rows, expert_down, last, cut)
        last = keep
        sums.append(add(keep, shift(send, "pipe", pipes, 1)))
    exchanged = [exchange_dp(value, dps, near_first) for value in sums]
    grad_down, done = down_grad(dense_flipped, residuals[-1], sums[-1])
    mine, theirs = [], []
    for (own, other, mode), total, cut in zip(exchanged, pre[::-1], cuts[::-1]):
        part = hidden_grad_act(own, other, mode, total, slot_weight, done, cut[0])
        mine.append(part)
        theirs.append(shift(part, "pipe", pipes, 1))
    grads = input_grads(picker, base_flipped, mine + theirs)
    return (student_sum.astype(BF), grads[0], grads[1], grad_down)


def solution(mesh):
    placed = (
        P(("groups", "expert"), ("dp", "pipe")),
        P("groups", None),
        P("groups", None),
        P(("dp", "pipe"), "expert"),
        P(("dp", "pipe"), "expert"),
        P("expert", ("dp", "pipe")),
        P(("dp", "pipe"), "expert"),
        P(("dp", "pipe"), "expert"),
        P("expert", ("dp", "pipe")),
    )
    return jax.shard_map(
        body,
        mesh=mesh,
        in_specs=placed,
        out_specs=(
            P(("groups", "expert"), ("dp", "pipe")),
            P(("groups", "dp", "pipe"), "expert"),
            P(("groups", "dp", "pipe"), "expert"),
            P(("groups", "expert"), ("dp", "pipe")),
        ),
        check_vma=False,
    )
```

```python
import functools

import jax
import jax.numpy as jnp
from jax import lax
from jax.experimental import pallas as pl
from jax.experimental.pallas import tpu as pltpu
from jax.sharding import PartitionSpec as P

H = 896
BF = jnp.bfloat16
F32 = jnp.float32


def shift(value, axis, count, by):
    return lax.ppermute(value, axis, [(i, (i + by) % count) for i in range(count)])


def dot(a, b, contract_a=1, contract_b=0):
    return lax.dot_general(
        a, b, (((contract_a,), (contract_b,)), ((), ())), preferred_element_type=F32
    )


def whole():
    return pl.BlockSpec(memory_space=pltpu.VMEM)


def in_hbm():
    return pl.BlockSpec(memory_space=pltpu.HBM)


def anywhere():
    return pl.BlockSpec(memory_space=pl.ANY)


def scalars():
    return pl.BlockSpec(memory_space=pltpu.SMEM)


def load_start(pairs, sems, pieces):
    copies = []
    for which, (source, target) in enumerate(pairs):
        rows = source.shape[0] // pieces
        for i in range(pieces):
            part = pl.ds(i * rows, rows)
            copies.append(
                pltpu.make_async_copy(source.at[part], target.at[part], sems.at[which, i])
            )
    for copy in copies:
        copy.start()
    return copies


def far(value):
    return pltpu.with_memory_space_constraint(value, pltpu.HBM)


def prepare_kernel(
    near_first,
    ranks,
    capacity,
    dps,
    pipes,
    place,
    far_routes,
    far_shares,
    gate,
    up,
    picker,
    weights,
    gate_out,
    up_out,
    routes,
    shares,
    sems,
    table_sems,
):
    tables = [
        pltpu.make_async_copy(far_routes, routes, table_sems.at[0]),
        pltpu.make_async_copy(far_shares, shares, table_sems.at[1]),
    ]
    for copy in tables:
        copy.start()
    copies = load_start(((gate, gate_out), (up, up_out)), sems, 8)
    for copy in tables:
        copy.wait()
    rank, dp, pipe = place[0], place[1], place[2]
    experts, slots, token_count = picker.shape
    block = token_count // ranks
    per_piece = ranks // (dps * pipes)
    row = lax.broadcasted_iota(jnp.int32, (8, token_count), 0)
    names = row + rank * experts
    weight = jnp.zeros((8, token_count), F32)
    routed = jnp.zeros((8, token_count), F32)
    for k in range(routes.shape[0]):
        hit = (routes[k : k + 1, :] == names) & (row < experts)
        weight = weight + jnp.where(hit, shares[k : k + 1, :], 0.0)
        routed = routed + jnp.where(hit, 1.0, 0.0)
    if near_first:
        swapped = rank // 2 == 1
        weight = jnp.where(swapped, pltpu.roll(weight, token_count // 2, 1), weight)
        routed = jnp.where(swapped, pltpu.roll(routed, token_count // 2, 1), routed)
    t_from = lax.broadcasted_iota(jnp.int32, (token_count, token_count), 0)
    t_to = lax.broadcasted_iota(jnp.int32, (token_count, token_count), 1)
    earlier = jnp.where((t_from // block == t_to // block) & (t_from < t_to), 1.0, 0.0)
    within = dot(routed.astype(BF), earlier.astype(BF)).astype(jnp.int32)
    at_block = lax.broadcasted_iota(jnp.int32, (1, token_count), 1) // block
    if near_first:
        at_pipe = lax.rem(at_block + pipe, 2)
        first = (at_pipe * 2 + at_block // 2) * capacity
    else:
        at_pipe = lax.rem(at_block // (dps * per_piece) + pipes - pipe, pipes)
        at_dp = lax.rem(lax.rem(at_block // per_piece, dps) + dps - dp, dps)
        first = ((at_pipe * dps + at_dp) * per_piece + lax.rem(at_block, per_piece)) * capacity
    slot = jnp.where(routed > 0.0, within + first, -1)
    ids = lax.broadcasted_iota(jnp.int32, (slots, token_count), 0)
    for e in range(experts):
        hit = slot[e : e + 1] == ids
        picker[e] = jnp.where(hit, 1.0, 0.0).astype(BF)
        weights[e] = jnp.sum(jnp.where(hit, weight[e : e + 1], 0.0), axis=1, keepdims=True)
    for copy in copies:
        copy.wait()


def prepare(place, routes, shares, gate, up, near_first, ranks, dps, pipes, block, experts):
    assert experts <= 8
    capacity = block // 2
    token_count = block * ranks
    slots = capacity * ranks
    return pl.pallas_call(
        functools.partial(prepare_kernel, near_first, ranks, capacity, dps, pipes),
        in_specs=[scalars(), in_hbm(), in_hbm(), in_hbm(), in_hbm()],
        out_specs=(whole(), whole(), whole(), whole()),
        out_shape=(
            jax.ShapeDtypeStruct((experts, slots, token_count), BF),
            jax.ShapeDtypeStruct((experts, slots, 1), F32),
            pltpu.VMEM(gate.shape, BF),
            pltpu.VMEM(up.shape, BF),
        ),
        scratch_shapes=[
            pltpu.VMEM(routes.shape, routes.dtype),
            pltpu.VMEM(shares.shape, shares.dtype),
            pltpu.SemaphoreType.DMA((2, 8)),
            pltpu.SemaphoreType.DMA((2,)),
        ],
        compiler_params=pltpu.CompilerParams(vmem_limit_bytes=8 * 1024 * 1024),
        cost_estimate=pl.CostEstimate(
            flops=0, bytes_accessed=4 * gate.size, transcendentals=0
        ),
    )(place, far(routes), far(shares), far(gate), far(up))


def residual_kernel(ranks, *refs):
    student = refs[0][...].astype(F32)
    target = refs[ranks][...].astype(F32)
    for i in range(1, ranks):
        student = student + refs[i][...].astype(F32)
        target = target + refs[ranks + i][...].astype(F32)
    refs[-2][...] = student
    refs[-1][...] = (student - target).astype(BF)


def residual_of(student, target, before):
    ranks = len(student)
    shape = student[0].shape
    return pl.pallas_call(
        functools.partial(residual_kernel, ranks),
        in_specs=[whole()] * (2 * ranks) + [anywhere()] * len(before),
        out_specs=(whole(), whole()),
        out_shape=(jax.ShapeDtypeStruct(shape, F32), jax.ShapeDtypeStruct(shape, BF)),
        compiler_params=pltpu.CompilerParams(vmem_limit_bytes=4 * 1024 * 1024),
    )(*student, *target, *before)


def tile_of(size):
    return 256 if size % 256 == 0 else 128


def teacher_kernel(first, size, dps, pipes, place, tokens, gate, up, keep, send):
    dp, pipe = place[1], place[2]
    rows = tokens.shape[0] // (dps * pipes)
    half = dps * rows
    parts = []
    for j1 in range(pipes):
        for j0 in range(dps):
            piece = lax.rem(pipe + j1, pipes) * dps + lax.rem(dp + j0, dps)
            parts.append(tokens[pl.ds(pl.multiple_of(piece * rows, rows), rows), :])
    ordered = jnp.concatenate(parts, axis=0)
    tile = tile_of(size)
    for which, weight in enumerate((gate, up)):
        for i in range(size // tile):
            product = dot(ordered, weight[:, first + i * tile : first + (i + 1) * tile]).astype(BF)
            keep[which, :, i * tile : (i + 1) * tile] = product[:half]
            send[which, :, i * tile : (i + 1) * tile] = product[half:]


def teacher_pre(place, tokens, gate, up, first, size, dps, pipes):
    token_count, width = tokens.shape
    half = jax.ShapeDtypeStruct((2, token_count // pipes, size), BF)
    return pl.pallas_call(
        functools.partial(teacher_kernel, first, size, dps, pipes),
        in_specs=[scalars(), whole(), whole(), whole()],
        out_specs=(whole(), whole()),
        out_shape=(half, half),
        compiler_params=pltpu.CompilerParams(vmem_limit_bytes=8 * 1024 * 1024),
        cost_estimate=pl.CostEstimate(
            flops=4 * token_count * width * size, bytes_accessed=4 * width * size, transcendentals=0
        ),
    )(place, tokens, gate, up)


def expert_kernel(cuts, picker, tokens, gate, up, before, *rest):
    outs, held, sems = rest[:-2], rest[-2], rest[-1]
    count, slots = picker.shape[:2]
    depth, _, pieces = sems.shape
    rows_each = gate.shape[0] // pieces

    def copies(e, which):
        weight = (gate, up)[which]
        found = []
        for p in range(pieces):
            part = pl.ds(p * rows_each, rows_each)
            found.append(
                pltpu.make_async_copy(
                    weight.at[part, pl.ds(e * H, H)],
                    held.at[e % depth, which, part],
                    sems.at[e % depth, which, p],
                )
            )
        return found

    for e in range(min(depth, count)):
        for which in range(2):
            for copy in copies(e, which):
                copy.start()
    for e in range(count):
        rows = dot(picker[e], tokens[...]).astype(BF)
        for which in range(2):
            for copy in copies(e, which):
                copy.wait()
            product = dot(rows, held[e % depth, which]).astype(BF)
            for i, (low, high) in enumerate(cuts):
                outs[2 * i][e, which] = product[low:high]
                outs[2 * i + 1][e, which] = product[slots // 2 + low : slots // 2 + high]
            if e + depth < count:
                for copy in copies(e + depth, which):
                    copy.start()


def expert_pre(picker, tokens, gate, up, before, cuts):
    count, slots = picker.shape[:2]
    width = tokens.shape[1]
    outs = []
    for low, high in cuts:
        outs += [jax.ShapeDtypeStruct((count, 2, high - low, H), BF)] * 2
    return pl.pallas_call(
        functools.partial(expert_kernel, cuts),
        in_specs=[whole(), whole(), in_hbm(), in_hbm(), anywhere()],
        out_specs=tuple(whole() for _ in outs),
        out_shape=tuple(outs),
        scratch_shapes=[
            pltpu.VMEM((min(count, 2), 2, width, H), BF),
            pltpu.SemaphoreType.DMA((min(count, 2), 2, 4)),
        ],
        compiler_params=pltpu.CompilerParams(vmem_limit_bytes=12 * 1024 * 1024),
        cost_estimate=pl.CostEstimate(
            flops=count * 4 * slots * width * H,
            bytes_accessed=count * 4 * width * H,
            transcendentals=0,
        ),
    )(picker, tokens, far(gate), far(up), before)


def add_kernel(a, b, before, out):
    out[...] = (a[...].astype(F32) + b[...].astype(F32)).astype(BF)


def add_after(a, b, before):
    return pl.pallas_call(
        add_kernel,
        in_specs=[whole(), whole(), anywhere()],
        out_specs=whole(),
        out_shape=jax.ShapeDtypeStruct(a.shape, BF),
        compiler_params=pltpu.CompilerParams(vmem_limit_bytes=4 * 1024 * 1024),
    )(a, b, before)


def dp_total(mode, mine, other):
    total = mine.astype(F32)
    if mode == "add":
        total = total + other.astype(F32)
    if mode == "swap":
        theirs = other.astype(F32)
        rows = theirs.shape[0]
        total = total + jnp.concatenate([theirs[rows // 2 :], theirs[: rows // 2]], axis=0)
    return total


def hidden_act_kernel(mode, low, mine, other, weight, *rest):
    pre, out = rest[-2:]
    count, _, rows = mine.shape[:3]
    for i in range(count):
        gate = dp_total(mode, mine[i, 0], other[i, 0])
        up = dp_total(mode, mine[i, 1], other[i, 1])
        pre[i, 0] = gate
        pre[i, 1] = up
        out[i] = (gate * jax.nn.sigmoid(gate) * up * weight[i, low : low + rows]).astype(BF)


def hidden_act(mine, other, mode, weight, before, low):
    count, _, rows, width = mine.shape
    return pl.pallas_call(
        functools.partial(hidden_act_kernel, mode, low),
        in_specs=[whole(), whole(), whole()] + [anywhere()] * len(before),
        out_specs=(whole(), whole()),
        out_shape=(
            jax.ShapeDtypeStruct(mine.shape, F32),
            jax.ShapeDtypeStruct((count, rows, width), BF),
        ),
        compiler_params=pltpu.CompilerParams(vmem_limit_bytes=8 * 1024 * 1024),
    )(mine, other, weight, *before)


def pair_kernel(*refs):
    values, out = refs[:-2], refs[-1]
    rows = out.shape[0] // len(values)
    for i, value in enumerate(values):
        out[i * rows : (i + 1) * rows, :] = value[...]


def pair(values, before):
    rows, width = values[0].shape
    return pl.pallas_call(
        pair_kernel,
        in_specs=[whole()] * len(values) + [anywhere()],
        out_specs=whole(),
        out_shape=jax.ShapeDtypeStruct((rows * len(values), width), BF),
        compiler_params=pltpu.CompilerParams(vmem_limit_bytes=4 * 1024 * 1024),
    )(*values, before)


def join_kernel(dps, pipes, place, *refs):
    out = refs[-1]
    dp, pipe = place[1], place[2]
    rows = out.shape[0] // (dps * pipes)
    at = 0
    for i in range((len(refs) - 1) // 2):
        size = refs[2 * i].shape[1]
        for j1 in range(pipes):
            for j0 in range(dps):
                piece = lax.rem(pipe + j1, pipes) * dps + lax.rem(dp + j0, dps)
                target = pl.ds(pl.multiple_of(piece * rows, rows), rows)
                out[target, at : at + size] = refs[2 * i + j1][j0 * rows : (j0 + 1) * rows, :]
        at += size


def join(place, parts, dps, pipes):
    assert pipes == 2
    flat = [value for pair in parts for value in pair]
    rows = flat[0].shape[0] * pipes
    width = sum(pair[0].shape[1] for pair in parts)
    return pl.pallas_call(
        functools.partial(join_kernel, dps, pipes),
        in_specs=[scalars()] + [whole()] * len(flat),
        out_specs=whole(),
        out_shape=jax.ShapeDtypeStruct((rows, width), BF),
        compiler_params=pltpu.CompilerParams(vmem_limit_bytes=8 * 1024 * 1024),
    )(place, *flat)


def slot_rows(table, low, high):
    half = table.shape[0] // 2
    return jnp.concatenate([table[low:high], table[half + low : half + high]], axis=0)


def spread_kernel(cut, tokens, picker, mine, theirs, out):
    for e in range(picker.shape[0]):
        hidden = jnp.concatenate([mine[e], theirs[e]], axis=0)
        dense = dot(slot_rows(picker[e], *cut), hidden, 0, 0)[tokens[0] : tokens[1]]
        out[:, e * H : (e + 1) * H] = dense.astype(BF)


def spread(picker, mine, theirs, cut, tokens):
    count = picker.shape[0]
    return pl.pallas_call(
        functools.partial(spread_kernel, cut, tokens),
        in_specs=[whole()] * 3,
        out_specs=whole(),
        out_shape=jax.ShapeDtypeStruct((tokens[1] - tokens[0], count * H), BF),
        compiler_params=pltpu.CompilerParams(vmem_limit_bytes=8 * 1024 * 1024),
    )(picker, mine, theirs)


def flip_kernel(*refs):
    dense_out, tokens_out = refs[-2:]
    tokens = refs[-4]
    dense = jnp.concatenate([value[...].astype(F32) for value in refs[:-4]], axis=0)
    dense_out[...] = dense.T.astype(BF)
    tokens_out[...] = tokens[...].astype(F32).T.astype(BF)


def flip(dense, tokens, before):
    return pl.pallas_call(
        flip_kernel,
        in_specs=[whole()] * (len(dense) + 1) + [anywhere()],
        out_specs=(whole(), whole()),
        out_shape=(
            jax.ShapeDtypeStruct((dense[0].shape[1], tokens.shape[0]), BF),
            jax.ShapeDtypeStruct(tokens.shape[::-1], BF),
        ),
        compiler_params=pltpu.CompilerParams(vmem_limit_bytes=16 * 1024 * 1024),
    )(*dense, tokens, before)


def hidden_grad_kernel(first, picker, residual, down, before, keep, send):
    rows = keep.shape[1]
    for i in range(keep.shape[0]):
        e = first + i
        picked = dot(picker[e], residual[...]).astype(BF)
        product = dot(down[e * H : (e + 1) * H, :], picked, 1, 1).T.astype(BF)
        keep[i] = product[:rows]
        send[i] = product[rows:]


def hidden_grad_parts(picker, residual, down, before, first, count):
    part = jax.ShapeDtypeStruct((count, picker.shape[1] // 2, H), BF)
    return pl.pallas_call(
        functools.partial(hidden_grad_kernel, first),
        in_specs=[whole(), whole(), whole(), anywhere()],
        out_specs=(whole(), whole()),
        out_shape=(part, part),
        compiler_params=pltpu.CompilerParams(vmem_limit_bytes=8 * 1024 * 1024),
    )(picker, residual, down, before)


def hidden_grad_act_kernel(mode, first, mine, other, weight, before, *rest):
    pres, out = rest[:-1], rest[-1]
    count, rows = mine.shape[:2]
    for i in range(count):
        e = first + i
        total = dp_total(mode, mine[i], other[i]) * weight[e, :rows]
        pre_gate = jnp.concatenate([pre[e, 0] for pre in pres], axis=0)
        pre_up = jnp.concatenate([pre[e, 1] for pre in pres], axis=0)
        sig = jax.nn.sigmoid(pre_gate)
        gate_grad = total * pre_up * sig * (1.0 + pre_gate * (1.0 - sig))
        up_grad = total * pre_gate * sig
        out[i, 0] = gate_grad.astype(BF)
        out[i, 1] = up_grad.astype(BF)


def hidden_grad_act(mine, other, mode, pres, weight, before, first):
    count, rows, width = mine.shape
    return pl.pallas_call(
        functools.partial(hidden_grad_act_kernel, mode, first),
        in_specs=[whole(), whole(), whole(), anywhere()] + [whole()] * len(pres),
        out_specs=whole(),
        out_shape=jax.ShapeDtypeStruct((count, 2, rows, width), BF),
        compiler_params=pltpu.CompilerParams(vmem_limit_bytes=8 * 1024 * 1024),
    )(mine, other, weight, before, *pres)


def down_grad_kernel(hidden, residual, before, out, done, held, sems):
    tiles = sems.shape[0]
    rows = hidden.shape[0] // tiles
    copies = []
    for i in range(tiles):
        part = pl.ds(i * rows, rows)
        held[part, :] = dot(hidden[part, :], residual[...]).astype(BF)
        copies.append(pltpu.make_async_copy(held.at[part], out.at[part], sems.at[i]))
        copies[-1].start()
    done[...] = jnp.zeros_like(done)
    for copy in copies:
        copy.wait()


def down_grad(hidden, residual, before):
    rows, token_count = hidden.shape
    width = residual.shape[1]
    return pl.pallas_call(
        down_grad_kernel,
        in_specs=[whole(), whole(), anywhere()],
        out_specs=(in_hbm(), whole()),
        out_shape=(
            jax.ShapeDtypeStruct((rows, width), BF),
            jax.ShapeDtypeStruct((8, 128), F32),
        ),
        scratch_shapes=[
            pltpu.VMEM((rows, width), BF),
            pltpu.SemaphoreType.DMA((rows // (H // 2),)),
        ],
        compiler_params=pltpu.CompilerParams(vmem_limit_bytes=16 * 1024 * 1024),
        cost_estimate=pl.CostEstimate(
            flops=2 * rows * width * token_count,
            bytes_accessed=2 * rows * width,
            transcendentals=0,
        ),
    )(hidden, residual, before)


def input_grad_kernel(group, picker, tokens, *rest):
    outs, held, sems = rest[-4:-2], rest[-2], rest[-1]
    count = picker.shape[0]
    splits = sems.shape[2]
    rows = tokens.shape[0] // splits
    copies = []
    for i in range(count):
        for which in range(2):
            mine, theirs = rest[i // group * 2], rest[i // group * 2 + 1]
            grad = jnp.concatenate([mine[i % group, which], theirs[i % group, which]], axis=0)
            dense = dot(picker[i], grad, 0, 0).astype(BF)
            for r in range(splits):
                part = pl.ds(r * rows, rows)
                columns = pl.ds(i * H, H)
                held[i, which, part] = dot(tokens[part, :], dense).astype(BF)
                copies.append(
                    pltpu.make_async_copy(
                        held.at[i, which, part], outs[which].at[part, columns], sems.at[i, which, r]
                    )
                )
                copies[-1].start()
    for copy in copies:
        copy.wait()


def input_grads(picker, tokens, parts):
    count, slots, token_count = picker.shape
    width = tokens.shape[0]
    out = jax.ShapeDtypeStruct((width, count * H), BF)
    return pl.pallas_call(
        functools.partial(input_grad_kernel, count // len(parts)),
        in_specs=[whole()] * (2 + 2 * len(parts)),
        out_specs=(in_hbm(), in_hbm()),
        out_shape=(out, out),
        scratch_shapes=[
            pltpu.VMEM((count, 2, width, H), BF),
            pltpu.SemaphoreType.DMA((count, 2, 2)),
        ],
        compiler_params=pltpu.CompilerParams(vmem_limit_bytes=24 * 1024 * 1024),
        cost_estimate=pl.CostEstimate(
            flops=count * 4 * token_count * width * H,
            bytes_accessed=count * 4 * width * H,
            transcendentals=0,
        ),
    )(picker, tokens, *[value for pair in parts for value in pair])


def add(a, b):
    return (a.astype(F32) + b.astype(F32)).astype(BF)


def split_rows(value, count):
    rows = value.shape[-2] // count
    return [value[..., i * rows : (i + 1) * rows, :] for i in range(count)]


def scatter_dp(value, count):
    pieces = split_rows(value, count)
    total = pieces[0].astype(F32)
    for s in range(1, count):
        total = total + shift(pieces[s], "dp", count, s).astype(F32)
    return total


def gather_dp_parts(value, count):
    return [value] + [shift(value, "dp", count, -s) for s in range(1, count)]


def gather_dp(value, count):
    return jnp.concatenate(gather_dp_parts(value, count), axis=-2)


def exchange_dp(value, count, same_order):
    if count == 2:
        return value, shift(value, "dp", count, 1), "add" if same_order else "swap"
    total = gather_dp(scatter_dp(value, count).astype(BF), count)
    return total, total, "whole"


def body(
    tokens,
    routes,
    gate_weights,
    teacher_gate,
    teacher_up,
    teacher_down,
    expert_gate,
    expert_up,
    expert_down,
):
    ranks = lax.axis_size("expert")
    dps = lax.axis_size("dp")
    pipes = lax.axis_size("pipe")
    rank = lax.axis_index("expert")
    dp = lax.axis_index("dp")
    pipe = lax.axis_index("pipe")
    block, width = tokens.shape
    token_count = block * ranks
    experts = expert_gate.shape[1] // H
    slots = block // 2 * ranks
    place = jnp.stack([rank, dp, pipe]).astype(jnp.int32)

    near_first = (ranks, dps, pipes) == (4, 2, 2)
    offset = rank // 2 * 2 if near_first else 0
    capacity = slots // ranks
    if near_first:
        cuts = [(capacity, 2 * capacity), (0, capacity)]
        token_cuts = [(token_count // 2, token_count), (0, token_count // 2)]
    else:
        cuts = [(0, slots // 2)]
        token_cuts = [(0, token_count)]

    paired = ranks & (ranks - 1) == 0

    def to_partner(value, s):
        if paired:
            return lax.ppermute(value, "expert", [(i, i ^ s) for i in range(ranks)])
        return shift(value, "expert", ranks, s)

    def target_of(s):
        return rank ^ s if paired else (rank + s) % ranks

    def source_of(s):
        return rank ^ s if paired else (rank + ranks - s) % ranks

    def place_rows(rows, blocks):
        for s, value in blocks:
            at = (source_of(s) ^ offset) * block
            rows = lax.dynamic_update_slice(rows, value, (at, 0))
        return rows

    def gather_tokens(mine):
        rows = place_rows(jnp.zeros((token_count, mine.shape[1]), BF), [(0, mine)])
        near = range(1, 2 if near_first else ranks)
        near_rows = place_rows(rows, [(s, to_partner(mine, s)) for s in near])
        rest = range(2, ranks if near_first else 2)
        return near_rows, place_rows(near_rows, [(s, to_partner(mine, s)) for s in rest])

    def to_owners(product, first, count, low):
        received = []
        for s in range(first, first + count):
            at = (target_of(s) ^ offset) * block - low
            sent = lax.dynamic_slice_in_dim(product, at, block, axis=0)
            received.append(to_partner(sent, s) if s else sent)
        return received

    _, base = gather_tokens(tokens)
    picker, slot_weight, gate_near, up_near = prepare(
        place,
        routes.T,
        gate_weights.T,
        teacher_gate,
        teacher_up,
        near_first,
        ranks,
        dps,
        pipes,
        block,
        experts,
    )

    chunks = 2 if teacher_gate.shape[1] % 512 == 0 else 1
    size = teacher_gate.shape[1] // chunks
    halves = []
    for i in range(chunks):
        keep, send = teacher_pre(place, base, gate_near, up_near, i * size, size, dps, pipes)
        halves.append(add(keep, shift(send, "pipe", pipes, 1)))

    outs = expert_pre(picker, base, expert_gate, expert_up, halves[-1], cuts)
    parts, half = [], halves[-1]
    for i in range(len(cuts)):
        half = add_after(outs[2 * i], shift(outs[2 * i + 1], "pipe", pipes, 1), half)
        parts.append(exchange_dp(half, dps, near_first))
    hiddens = []
    for half in halves:
        total = scatter_dp(half, dps)
        hidden = (jax.nn.silu(total[0]) * total[1]).astype(BF)
        hidden = pair(gather_dp_parts(hidden, dps), parts[0][0])
        hiddens.append((hidden, shift(hidden, "pipe", pipes, 1)))
    hidden = join(place, hiddens, dps, pipes)
    product = jnp.dot(hidden, teacher_down, preferred_element_type=F32).astype(BF)
    target = to_owners(product, 0, ranks, 0)

    pre, dense, student = [], [], []
    wait = [target[1], target[-1]]
    for (mine, other, mode), cut, rows in zip(parts, cuts, token_cuts):
        total, part = hidden_act(mine, other, mode, slot_weight, wait, cut[0])
        pre.append(total)
        dense.append(spread(picker, part, shift(part, "pipe", pipes, 1), cut, rows))
        wait = dense[-1:]
        product = jnp.dot(dense[-1], expert_down, preferred_element_type=F32).astype(BF)
        count = (rows[1] - rows[0]) // block
        student = to_owners(product, rows[0] // block, count, rows[0]) + student
    dense_flipped, base_flipped = flip(dense[::-1], base, product)
    student_sum, residual = residual_of(student, target, (base_flipped,))

    _, residual = gather_tokens(residual)
    group = 2 if experts % 2 == 0 else 1
    firsts = range(0, experts, group)
    sums, last = [], residual
    for first in firsts:
        keep, send = hidden_grad_parts(picker, residual, expert_down, last, first, group)
        last = keep
        sums.append(add(keep, shift(send, "pipe", pipes, 1)))
    exchanged = [exchange_dp(value, dps, near_first) for value in sums]
    grad_down, done = down_grad(dense_flipped, residual, sums[-1])
    grads = []
    for first, (own, other, mode) in zip(firsts, exchanged):
        part = hidden_grad_act(own, other, mode, pre[::-1], slot_weight, done, first)
        grads.append((part, shift(part, "pipe", pipes, 1)))
    grads = input_grads(picker, base_flipped, grads)
    return (student_sum.astype(BF), grads[0], grads[1], grad_down)


def solution(mesh):
    placed = (
        P(("groups", "expert"), ("dp", "pipe")),
        P("groups", None),
        P("groups", None),
        P(("dp", "pipe"), "expert"),
        P(("dp", "pipe"), "expert"),
        P("expert", ("dp", "pipe")),
        P(("dp", "pipe"), "expert"),
        P(("dp", "pipe"), "expert"),
        P("expert", ("dp", "pipe")),
    )
    return jax.shard_map(
        body,
        mesh=mesh,
        in_specs=placed,
        out_specs=(
            P(("groups", "expert"), ("dp", "pipe")),
            P(("groups", "dp", "pipe"), "expert"),
            P(("groups", "dp", "pipe"), "expert"),
            P(("groups", "expert"), ("dp", "pipe")),
        ),
        check_vma=False,
    )
```

```python
import functools

import jax
import jax.numpy as jnp
from jax import lax
from jax.experimental import pallas as pl
from jax.experimental.pallas import tpu as pltpu
from jax.sharding import PartitionSpec as P

H = 896
BF = jnp.bfloat16
F32 = jnp.float32


def shift(value, axis, count, by):
    return lax.ppermute(value, axis, [(i, (i + by) % count) for i in range(count)])


def dot(a, b, contract_a=1, contract_b=0):
    return lax.dot_general(
        a, b, (((contract_a,), (contract_b,)), ((), ())), preferred_element_type=F32
    )


def whole():
    return pl.BlockSpec(memory_space=pltpu.VMEM)


def in_hbm():
    return pl.BlockSpec(memory_space=pltpu.HBM)


def anywhere():
    return pl.BlockSpec(memory_space=pl.ANY)


def scalars():
    return pl.BlockSpec(memory_space=pltpu.SMEM)


def load_start(pairs, sems, pieces):
    copies = []
    for which, (source, target) in enumerate(pairs):
        rows = source.shape[0] // pieces
        for i in range(pieces):
            part = pl.ds(i * rows, rows)
            copies.append(
                pltpu.make_async_copy(source.at[part], target.at[part], sems.at[which, i])
            )
    for copy in copies:
        copy.start()
    return copies


def far(value):
    return pltpu.with_memory_space_constraint(value, pltpu.HBM)


def prepare_kernel(
    near_first,
    ranks,
    capacity,
    dps,
    pipes,
    place,
    far_routes,
    far_shares,
    gate,
    up,
    picker,
    weights,
    gate_out,
    up_out,
    routes,
    shares,
    sems,
    table_sems,
):
    tables = [
        pltpu.make_async_copy(far_routes, routes, table_sems.at[0]),
        pltpu.make_async_copy(far_shares, shares, table_sems.at[1]),
    ]
    for copy in tables:
        copy.start()
    copies = load_start(((gate, gate_out), (up, up_out)), sems, 8)
    for copy in tables:
        copy.wait()
    rank, dp, pipe = place[0], place[1], place[2]
    experts, slots, token_count = picker.shape
    block = token_count // ranks
    per_piece = ranks // (dps * pipes)
    row = lax.broadcasted_iota(jnp.int32, (8, token_count), 0)
    names = row + rank * experts
    weight = jnp.zeros((8, token_count), F32)
    routed = jnp.zeros((8, token_count), F32)
    for k in range(routes.shape[0]):
        hit = (routes[k : k + 1, :] == names) & (row < experts)
        weight = weight + jnp.where(hit, shares[k : k + 1, :], 0.0)
        routed = routed + jnp.where(hit, 1.0, 0.0)
    if near_first:
        swapped = rank // 2 == 1
        weight = jnp.where(swapped, pltpu.roll(weight, token_count // 2, 1), weight)
        routed = jnp.where(swapped, pltpu.roll(routed, token_count // 2, 1), routed)
    t_from = lax.broadcasted_iota(jnp.int32, (token_count, token_count), 0)
    t_to = lax.broadcasted_iota(jnp.int32, (token_count, token_count), 1)
    earlier = jnp.where((t_from // block == t_to // block) & (t_from < t_to), 1.0, 0.0)
    within = dot(routed.astype(BF), earlier.astype(BF)).astype(jnp.int32)
    at_block = lax.broadcasted_iota(jnp.int32, (1, token_count), 1) // block
    if near_first:
        at_pipe = lax.rem(at_block + pipe, 2)
        first = (at_pipe * 2 + at_block // 2) * capacity
    else:
        at_pipe = lax.rem(at_block // (dps * per_piece) + pipes - pipe, pipes)
        at_dp = lax.rem(lax.rem(at_block // per_piece, dps) + dps - dp, dps)
        first = ((at_pipe * dps + at_dp) * per_piece + lax.rem(at_block, per_piece)) * capacity
    slot = jnp.where(routed > 0.0, within + first, -1)
    ids = lax.broadcasted_iota(jnp.int32, (slots, token_count), 0)
    for e in range(experts):
        hit = slot[e : e + 1] == ids
        picker[e] = jnp.where(hit, 1.0, 0.0).astype(BF)
        weights[e] = jnp.sum(jnp.where(hit, weight[e : e + 1], 0.0), axis=1, keepdims=True)
    for copy in copies:
        copy.wait()


def prepare(place, routes, shares, gate, up, near_first, ranks, dps, pipes, block, experts):
    assert experts <= 8
    capacity = block // 2
    token_count = block * ranks
    slots = capacity * ranks
    return pl.pallas_call(
        functools.partial(prepare_kernel, near_first, ranks, capacity, dps, pipes),
        in_specs=[scalars(), in_hbm(), in_hbm(), in_hbm(), in_hbm()],
        out_specs=(whole(), whole(), whole(), whole()),
        out_shape=(
            jax.ShapeDtypeStruct((experts, slots, token_count), BF),
            jax.ShapeDtypeStruct((experts, slots, 1), F32),
            pltpu.VMEM(gate.shape, BF),
            pltpu.VMEM(up.shape, BF),
        ),
        scratch_shapes=[
            pltpu.VMEM(routes.shape, routes.dtype),
            pltpu.VMEM(shares.shape, shares.dtype),
            pltpu.SemaphoreType.DMA((2, 8)),
            pltpu.SemaphoreType.DMA((2,)),
        ],
        compiler_params=pltpu.CompilerParams(vmem_limit_bytes=8 * 1024 * 1024),
        cost_estimate=pl.CostEstimate(
            flops=0, bytes_accessed=4 * gate.size, transcendentals=0
        ),
    )(place, far(routes), far(shares), far(gate), far(up))


def load_kernel(source, before, out, sems):
    for copy in load_start(((source, out),), sems, 8):
        copy.wait()


def load(source, before):
    return pl.pallas_call(
        load_kernel,
        in_specs=[in_hbm(), anywhere()],
        out_specs=whole(),
        out_shape=pltpu.VMEM(source.shape, source.dtype),
        scratch_shapes=[pltpu.SemaphoreType.DMA((1, 8))],
        compiler_params=pltpu.CompilerParams(vmem_limit_bytes=4 * 1024 * 1024),
    )(far(source), before)


def teacher_act_kernel(count, *refs):
    out = refs[-1]
    rows = out.shape[0]
    totals = []
    for which in range(2):
        total = refs[0][which, :rows].astype(F32)
        for theirs in refs[1:count]:
            total = total + theirs[which].astype(F32)
        totals.append(total)
    gate, up = totals
    out[...] = (gate * jax.nn.sigmoid(gate) * up).astype(BF)


def teacher_act(half, dps, before):
    pieces = split_rows(half, dps)
    received = [shift(pieces[r], "dp", dps, r) for r in range(1, dps)]
    return pl.pallas_call(
        functools.partial(teacher_act_kernel, dps),
        in_specs=[whole()] * dps + [anywhere()] * len(before),
        out_specs=whole(),
        out_shape=jax.ShapeDtypeStruct((half.shape[1] // dps, half.shape[2]), BF),
        compiler_params=pltpu.CompilerParams(vmem_limit_bytes=4 * 1024 * 1024),
    )(half, *received, *before)


def residual_kernel(ranks, *refs):
    student = refs[0][...].astype(F32)
    target = refs[ranks][...].astype(F32)
    for i in range(1, ranks):
        student = student + refs[i][...].astype(F32)
        target = target + refs[ranks + i][...].astype(F32)
    refs[-2][...] = student
    refs[-1][...] = (student - target).astype(BF)


def residual_of(student, target, before):
    ranks = len(student)
    shape = student[0].shape
    return pl.pallas_call(
        functools.partial(residual_kernel, ranks),
        in_specs=[whole()] * (2 * ranks) + [anywhere()] * len(before),
        out_specs=(whole(), whole()),
        out_shape=(jax.ShapeDtypeStruct(shape, F32), jax.ShapeDtypeStruct(shape, BF)),
        compiler_params=pltpu.CompilerParams(vmem_limit_bytes=4 * 1024 * 1024),
    )(*student, *target, *before)


def tile_of(size):
    return 256 if size % 256 == 0 else 128


def teacher_kernel(first, size, dps, pipes, place, tokens, gate, up, keep, send):
    dp, pipe = place[1], place[2]
    rows = tokens.shape[0] // (dps * pipes)
    half = dps * rows
    parts = []
    for j1 in range(pipes):
        for j0 in range(dps):
            piece = lax.rem(pipe + j1, pipes) * dps + lax.rem(dp + j0, dps)
            parts.append(tokens[pl.ds(pl.multiple_of(piece * rows, rows), rows), :])
    ordered = jnp.concatenate(parts, axis=0)
    tile = tile_of(size)
    for which, weight in enumerate((gate, up)):
        for i in range(size // tile):
            product = dot(ordered, weight[:, first + i * tile : first + (i + 1) * tile]).astype(BF)
            keep[which, :, i * tile : (i + 1) * tile] = product[:half]
            send[which, :, i * tile : (i + 1) * tile] = product[half:]


def teacher_pre(place, tokens, gate, up, first, size, dps, pipes):
    token_count, width = tokens.shape
    half = jax.ShapeDtypeStruct((2, token_count // pipes, size), BF)
    return pl.pallas_call(
        functools.partial(teacher_kernel, first, size, dps, pipes),
        in_specs=[scalars(), whole(), whole(), whole()],
        out_specs=(whole(), whole()),
        out_shape=(half, half),
        compiler_params=pltpu.CompilerParams(vmem_limit_bytes=8 * 1024 * 1024),
        cost_estimate=pl.CostEstimate(
            flops=4 * token_count * width * size, bytes_accessed=4 * width * size, transcendentals=0
        ),
    )(place, tokens, gate, up)


def expert_kernel(cuts, picker, tokens, gate, up, before, *rest):
    outs, held, sems = rest[:-2], rest[-2], rest[-1]
    count, slots = picker.shape[:2]
    depth, _, pieces = sems.shape
    rows_each = gate.shape[0] // pieces

    def copies(e, which):
        weight = (gate, up)[which]
        found = []
        for p in range(pieces):
            part = pl.ds(p * rows_each, rows_each)
            found.append(
                pltpu.make_async_copy(
                    weight.at[part, pl.ds(e * H, H)],
                    held.at[e % depth, which, part],
                    sems.at[e % depth, which, p],
                )
            )
        return found

    for e in range(min(depth, count)):
        for which in range(2):
            for copy in copies(e, which):
                copy.start()
    for e in range(count):
        rows = dot(picker[e], tokens[...]).astype(BF)
        for which in range(2):
            for copy in copies(e, which):
                copy.wait()
            product = dot(rows, held[e % depth, which]).astype(BF)
            for i, (low, high) in enumerate(cuts):
                outs[2 * i][e, which] = product[low:high]
                outs[2 * i + 1][e, which] = product[slots // 2 + low : slots // 2 + high]
            if e + depth < count:
                for copy in copies(e + depth, which):
                    copy.start()


def expert_pre(picker, tokens, gate, up, before, cuts):
    count, slots = picker.shape[:2]
    width = tokens.shape[1]
    outs = []
    for low, high in cuts:
        outs += [jax.ShapeDtypeStruct((count, 2, high - low, H), BF)] * 2
    return pl.pallas_call(
        functools.partial(expert_kernel, cuts),
        in_specs=[whole(), whole(), in_hbm(), in_hbm(), anywhere()],
        out_specs=tuple(whole() for _ in outs),
        out_shape=tuple(outs),
        scratch_shapes=[
            pltpu.VMEM((min(count, 2), 2, width, H), BF),
            pltpu.SemaphoreType.DMA((min(count, 2), 2, 4)),
        ],
        compiler_params=pltpu.CompilerParams(vmem_limit_bytes=12 * 1024 * 1024),
        cost_estimate=pl.CostEstimate(
            flops=count * 4 * slots * width * H,
            bytes_accessed=count * 4 * width * H,
            transcendentals=0,
        ),
    )(picker, tokens, far(gate), far(up), before)


def add_kernel(a, b, before, out):
    out[...] = (a[...].astype(F32) + b[...].astype(F32)).astype(BF)


def add_after(a, b, before):
    return pl.pallas_call(
        add_kernel,
        in_specs=[whole(), whole(), anywhere()],
        out_specs=whole(),
        out_shape=jax.ShapeDtypeStruct(a.shape, BF),
        compiler_params=pltpu.CompilerParams(vmem_limit_bytes=4 * 1024 * 1024),
    )(a, b, before)


def dp_total(mode, mine, other):
    total = mine.astype(F32)
    if mode == "add":
        total = total + other.astype(F32)
    if mode == "swap":
        theirs = other.astype(F32)
        rows = theirs.shape[0]
        total = total + jnp.concatenate([theirs[rows // 2 :], theirs[: rows // 2]], axis=0)
    return total


def hidden_act_kernel(mode, low, mine, other, weight, *rest):
    pre, out = rest[-2:]
    count, _, rows = mine.shape[:3]
    for i in range(count):
        gate = dp_total(mode, mine[i, 0], other[i, 0])
        up = dp_total(mode, mine[i, 1], other[i, 1])
        pre[i, 0] = gate
        pre[i, 1] = up
        out[i] = (gate * jax.nn.sigmoid(gate) * up * weight[i, low : low + rows]).astype(BF)


def hidden_act(mine, other, mode, weight, before, low):
    count, _, rows, width = mine.shape
    return pl.pallas_call(
        functools.partial(hidden_act_kernel, mode, low),
        in_specs=[whole(), whole(), whole()] + [anywhere()] * len(before),
        out_specs=(whole(), whole()),
        out_shape=(
            jax.ShapeDtypeStruct(mine.shape, F32),
            jax.ShapeDtypeStruct((count, rows, width), BF),
        ),
        compiler_params=pltpu.CompilerParams(vmem_limit_bytes=8 * 1024 * 1024),
    )(mine, other, weight, *before)


def pair_kernel(*refs):
    values, out = refs[:-2], refs[-1]
    rows = out.shape[0] // len(values)
    for i, value in enumerate(values):
        out[i * rows : (i + 1) * rows, :] = value[...]


def pair(values, before):
    rows, width = values[0].shape
    return pl.pallas_call(
        pair_kernel,
        in_specs=[whole()] * len(values) + [anywhere()],
        out_specs=whole(),
        out_shape=jax.ShapeDtypeStruct((rows * len(values), width), BF),
        compiler_params=pltpu.CompilerParams(vmem_limit_bytes=4 * 1024 * 1024),
    )(*values, before)


def join_kernel(dps, pipes, place, *refs):
    out = refs[-1]
    dp, pipe = place[1], place[2]
    rows = out.shape[0] // (dps * pipes)
    at = 0
    for i in range((len(refs) - 1) // 2):
        size = refs[2 * i].shape[1]
        for j1 in range(pipes):
            for j0 in range(dps):
                piece = lax.rem(pipe + j1, pipes) * dps + lax.rem(dp + j0, dps)
                target = pl.ds(pl.multiple_of(piece * rows, rows), rows)
                out[target, at : at + size] = refs[2 * i + j1][j0 * rows : (j0 + 1) * rows, :]
        at += size


def join(place, parts, dps, pipes):
    assert pipes == 2
    flat = [value for pair in parts for value in pair]
    rows = flat[0].shape[0] * pipes
    width = sum(pair[0].shape[1] for pair in parts)
    return pl.pallas_call(
        functools.partial(join_kernel, dps, pipes),
        in_specs=[scalars()] + [whole()] * len(flat),
        out_specs=whole(),
        out_shape=jax.ShapeDtypeStruct((rows, width), BF),
        compiler_params=pltpu.CompilerParams(vmem_limit_bytes=8 * 1024 * 1024),
    )(place, *flat)


def slot_rows(table, low, high):
    half = table.shape[0] // 2
    return jnp.concatenate([table[low:high], table[half + low : half + high]], axis=0)


def spread_kernel(cut, tokens, picker, mine, theirs, out):
    for e in range(picker.shape[0]):
        hidden = jnp.concatenate([mine[e], theirs[e]], axis=0)
        dense = dot(slot_rows(picker[e], *cut), hidden, 0, 0)[tokens[0] : tokens[1]]
        out[:, e * H : (e + 1) * H] = dense.astype(BF)


def spread(picker, mine, theirs, cut, tokens):
    count = picker.shape[0]
    return pl.pallas_call(
        functools.partial(spread_kernel, cut, tokens),
        in_specs=[whole()] * 3,
        out_specs=whole(),
        out_shape=jax.ShapeDtypeStruct((tokens[1] - tokens[0], count * H), BF),
        compiler_params=pltpu.CompilerParams(vmem_limit_bytes=8 * 1024 * 1024),
    )(picker, mine, theirs)


def flip_kernel(*refs):
    dense_out, tokens_out = refs[-2:]
    tokens = refs[-4]
    dense = jnp.concatenate([value[...].astype(F32) for value in refs[:-4]], axis=0)
    dense_out[...] = dense.T.astype(BF)
    tokens_out[...] = tokens[...].astype(F32).T.astype(BF)


def flip(dense, tokens, before):
    return pl.pallas_call(
        flip_kernel,
        in_specs=[whole()] * (len(dense) + 1) + [anywhere()],
        out_specs=(whole(), whole()),
        out_shape=(
            jax.ShapeDtypeStruct((dense[0].shape[1], tokens.shape[0]), BF),
            jax.ShapeDtypeStruct(tokens.shape[::-1], BF),
        ),
        compiler_params=pltpu.CompilerParams(vmem_limit_bytes=16 * 1024 * 1024),
    )(*dense, tokens, before)


def hidden_grad_kernel(first, picker, residual, down, before, keep, send):
    rows = keep.shape[1]
    for i in range(keep.shape[0]):
        e = first + i
        picked = dot(picker[e], residual[...]).astype(BF)
        product = dot(down[e * H : (e + 1) * H, :], picked, 1, 1).T.astype(BF)
        keep[i] = product[:rows]
        send[i] = product[rows:]


def hidden_grad_parts(picker, residual, down, before, first, count):
    part = jax.ShapeDtypeStruct((count, picker.shape[1] // 2, H), BF)
    return pl.pallas_call(
        functools.partial(hidden_grad_kernel, first),
        in_specs=[whole(), whole(), whole(), anywhere()],
        out_specs=(whole(), whole()),
        out_shape=(part, part),
        compiler_params=pltpu.CompilerParams(vmem_limit_bytes=8 * 1024 * 1024),
    )(picker, residual, down, before)


def hidden_grad_act_kernel(mode, first, mine, other, weight, before, *rest):
    pres, out = rest[:-1], rest[-1]
    count, rows = mine.shape[:2]
    for i in range(count):
        e = first + i
        total = dp_total(mode, mine[i], other[i]) * weight[e, :rows]
        pre_gate = jnp.concatenate([pre[e, 0] for pre in pres], axis=0)
        pre_up = jnp.concatenate([pre[e, 1] for pre in pres], axis=0)
        sig = jax.nn.sigmoid(pre_gate)
        gate_grad = total * pre_up * sig * (1.0 + pre_gate * (1.0 - sig))
        up_grad = total * pre_gate * sig
        out[i, 0] = gate_grad.astype(BF)
        out[i, 1] = up_grad.astype(BF)


def hidden_grad_act(mine, other, mode, pres, weight, before, first):
    count, rows, width = mine.shape
    return pl.pallas_call(
        functools.partial(hidden_grad_act_kernel, mode, first),
        in_specs=[whole(), whole(), whole(), anywhere()] + [whole()] * len(pres),
        out_specs=whole(),
        out_shape=jax.ShapeDtypeStruct((count, 2, rows, width), BF),
        compiler_params=pltpu.CompilerParams(vmem_limit_bytes=8 * 1024 * 1024),
    )(mine, other, weight, before, *pres)


def down_grad_kernel(hidden, residual, before, out, done, held, sems):
    tiles = sems.shape[0]
    rows = hidden.shape[0] // tiles
    copies = []
    for i in range(tiles):
        part = pl.ds(i * rows, rows)
        held[part, :] = dot(hidden[part, :], residual[...]).astype(BF)
        copies.append(pltpu.make_async_copy(held.at[part], out.at[part], sems.at[i]))
        copies[-1].start()
    done[...] = jnp.zeros_like(done)
    for copy in copies:
        copy.wait()


def down_grad(hidden, residual, before):
    rows, token_count = hidden.shape
    width = residual.shape[1]
    return pl.pallas_call(
        down_grad_kernel,
        in_specs=[whole(), whole(), anywhere()],
        out_specs=(in_hbm(), whole()),
        out_shape=(
            jax.ShapeDtypeStruct((rows, width), BF),
            jax.ShapeDtypeStruct((8, 128), F32),
        ),
        scratch_shapes=[
            pltpu.VMEM((rows, width), BF),
            pltpu.SemaphoreType.DMA((rows // (H // 2),)),
        ],
        compiler_params=pltpu.CompilerParams(vmem_limit_bytes=16 * 1024 * 1024),
        cost_estimate=pl.CostEstimate(
            flops=2 * rows * width * token_count,
            bytes_accessed=2 * rows * width,
            transcendentals=0,
        ),
    )(hidden, residual, before)


def input_grad_kernel(group, picker, tokens, *rest):
    outs, held, sems = rest[-4:-2], rest[-2], rest[-1]
    count = picker.shape[0]
    splits = sems.shape[2]
    rows = tokens.shape[0] // splits
    copies = []
    for i in range(count):
        for which in range(2):
            mine, theirs = rest[i // group * 2], rest[i // group * 2 + 1]
            grad = jnp.concatenate([mine[i % group, which], theirs[i % group, which]], axis=0)
            dense = dot(picker[i], grad, 0, 0).astype(BF)
            for r in range(splits):
                part = pl.ds(r * rows, rows)
                columns = pl.ds(i * H, H)
                held[i, which, part] = dot(tokens[part, :], dense).astype(BF)
                copies.append(
                    pltpu.make_async_copy(
                        held.at[i, which, part], outs[which].at[part, columns], sems.at[i, which, r]
                    )
                )
                copies[-1].start()
    for copy in copies:
        copy.wait()


def input_grads(picker, tokens, parts):
    count, slots, token_count = picker.shape
    width = tokens.shape[0]
    out = jax.ShapeDtypeStruct((width, count * H), BF)
    return pl.pallas_call(
        functools.partial(input_grad_kernel, count // len(parts)),
        in_specs=[whole()] * (2 + 2 * len(parts)),
        out_specs=(in_hbm(), in_hbm()),
        out_shape=(out, out),
        scratch_shapes=[
            pltpu.VMEM((count, 2, width, H), BF),
            pltpu.SemaphoreType.DMA((count, 2, 2)),
        ],
        compiler_params=pltpu.CompilerParams(vmem_limit_bytes=24 * 1024 * 1024),
        cost_estimate=pl.CostEstimate(
            flops=count * 4 * token_count * width * H,
            bytes_accessed=count * 4 * width * H,
            transcendentals=0,
        ),
    )(picker, tokens, *[value for pair in parts for value in pair])


def add(a, b):
    return (a.astype(F32) + b.astype(F32)).astype(BF)


def split_rows(value, count):
    rows = value.shape[-2] // count
    return [value[..., i * rows : (i + 1) * rows, :] for i in range(count)]


def scatter_dp(value, count):
    pieces = split_rows(value, count)
    total = pieces[0].astype(F32)
    for s in range(1, count):
        total = total + shift(pieces[s], "dp", count, s).astype(F32)
    return total


def gather_dp_parts(value, count):
    return [value] + [shift(value, "dp", count, -s) for s in range(1, count)]


def gather_dp(value, count):
    return jnp.concatenate(gather_dp_parts(value, count), axis=-2)


def exchange_dp(value, count, same_order):
    if count == 2:
        return value, shift(value, "dp", count, 1), "add" if same_order else "swap"
    total = gather_dp(scatter_dp(value, count).astype(BF), count)
    return total, total, "whole"


def body(
    tokens,
    routes,
    gate_weights,
    teacher_gate,
    teacher_up,
    teacher_down,
    expert_gate,
    expert_up,
    expert_down,
):
    ranks = lax.axis_size("expert")
    dps = lax.axis_size("dp")
    pipes = lax.axis_size("pipe")
    rank = lax.axis_index("expert")
    dp = lax.axis_index("dp")
    pipe = lax.axis_index("pipe")
    block, width = tokens.shape
    token_count = block * ranks
    experts = expert_gate.shape[1] // H
    slots = block // 2 * ranks
    place = jnp.stack([rank, dp, pipe]).astype(jnp.int32)

    near_first = (ranks, dps, pipes) == (4, 2, 2)
    offset = rank // 2 * 2 if near_first else 0
    capacity = slots // ranks
    if near_first:
        cuts = [(capacity, 2 * capacity), (0, capacity)]
        token_cuts = [(token_count // 2, token_count), (0, token_count // 2)]
    else:
        cuts = [(0, slots // 2)]
        token_cuts = [(0, token_count)]

    paired = ranks & (ranks - 1) == 0

    def to_partner(value, s):
        if paired:
            return lax.ppermute(value, "expert", [(i, i ^ s) for i in range(ranks)])
        return shift(value, "expert", ranks, s)

    def target_of(s):
        return rank ^ s if paired else (rank + s) % ranks

    def source_of(s):
        return rank ^ s if paired else (rank + ranks - s) % ranks

    def place_rows(rows, blocks):
        for s, value in blocks:
            at = (source_of(s) ^ offset) * block
            rows = lax.dynamic_update_slice(rows, value, (at, 0))
        return rows

    def gather_tokens(mine):
        rows = place_rows(jnp.zeros((token_count, mine.shape[1]), BF), [(0, mine)])
        near = range(1, 2 if near_first else ranks)
        near_rows = place_rows(rows, [(s, to_partner(mine, s)) for s in near])
        rest = range(2, ranks if near_first else 2)
        return near_rows, place_rows(near_rows, [(s, to_partner(mine, s)) for s in rest])

    def to_owners(product, first, count, low):
        received = []
        for s in range(first, first + count):
            at = (target_of(s) ^ offset) * block - low
            sent = lax.dynamic_slice_in_dim(product, at, block, axis=0)
            received.append(to_partner(sent, s) if s else sent)
        return received

    _, base = gather_tokens(tokens)
    picker, slot_weight, gate_near, up_near = prepare(
        place,
        routes.T,
        gate_weights.T,
        teacher_gate,
        teacher_up,
        near_first,
        ranks,
        dps,
        pipes,
        block,
        experts,
    )

    chunks = 2 if teacher_gate.shape[1] % 512 == 0 else 1
    size = teacher_gate.shape[1] // chunks
    halves = []
    for i in range(chunks):
        keep, send = teacher_pre(place, base, gate_near, up_near, i * size, size, dps, pipes)
        halves.append(add(keep, shift(send, "pipe", pipes, 1)))

    outs = expert_pre(picker, base, expert_gate, expert_up, halves[-1], cuts)
    parts, half = [], halves[-1]
    for i in range(len(cuts)):
        half = add_after(outs[2 * i], shift(outs[2 * i + 1], "pipe", pipes, 1), half)
        parts.append(exchange_dp(half, dps, near_first))
    hiddens = []
    before = []
    for half in halves:
        hidden = teacher_act(half, dps, before)
        if not before:
            expert_near = load(expert_down, hidden)
            before = [expert_near]
        hidden = pair(gather_dp_parts(hidden, dps), parts[0][0])
        hiddens.append((hidden, shift(hidden, "pipe", pipes, 1)))
    hidden = join(place, hiddens, dps, pipes)
    product = jnp.dot(hidden, teacher_down, preferred_element_type=F32).astype(BF)
    target = to_owners(product, 0, ranks, 0)

    pre, dense, student = [], [], []
    wait = [target[1], target[-1]]
    for (mine, other, mode), cut, rows in zip(parts, cuts, token_cuts):
        total, part = hidden_act(mine, other, mode, slot_weight, wait, cut[0])
        pre.append(total)
        dense.append(spread(picker, part, shift(part, "pipe", pipes, 1), cut, rows))
        product = jnp.dot(dense[-1], expert_near, preferred_element_type=F32).astype(BF)
        count = (rows[1] - rows[0]) // block
        student = to_owners(product, rows[0] // block, count, rows[0]) + student
    dense_flipped, base_flipped = flip(dense[::-1], base, product)
    expert_near = load(expert_down, base_flipped)
    student_sum, residual = residual_of(student, target, (expert_near,))

    _, residual = gather_tokens(residual)
    group = 2 if experts % 2 == 0 else 1
    firsts = range(0, experts, group)
    sums, last = [], residual
    for first in firsts:
        keep, send = hidden_grad_parts(picker, residual, expert_near, last, first, group)
        last = keep
        sums.append(add(keep, shift(send, "pipe", pipes, 1)))
    exchanged = [exchange_dp(value, dps, near_first) for value in sums]
    grad_down, done = down_grad(dense_flipped, residual, sums[-1])
    grads = []
    for first, (own, other, mode) in zip(firsts, exchanged):
        part = hidden_grad_act(own, other, mode, pre[::-1], slot_weight, done, first)
        grads.append((part, shift(part, "pipe", pipes, 1)))
    grads = input_grads(picker, base_flipped, grads)
    return (student_sum.astype(BF), grads[0], grads[1], grad_down)


def solution(mesh):
    placed = (
        P(("groups", "expert"), ("dp", "pipe")),
        P("groups", None),
        P("groups", None),
        P(("dp", "pipe"), "expert"),
        P(("dp", "pipe"), "expert"),
        P("expert", ("dp", "pipe")),
        P(("dp", "pipe"), "expert"),
        P(("dp", "pipe"), "expert"),
        P("expert", ("dp", "pipe")),
    )
    return jax.shard_map(
        body,
        mesh=mesh,
        in_specs=placed,
        out_specs=(
            P(("groups", "expert"), ("dp", "pipe")),
            P(("groups", "dp", "pipe"), "expert"),
            P(("groups", "dp", "pipe"), "expert"),
            P(("groups", "expert"), ("dp", "pipe")),
        ),
        check_vma=False,
    )
```

```python
import functools

import jax
import jax.numpy as jnp
from jax import lax
from jax.experimental import pallas as pl
from jax.experimental.pallas import tpu as pltpu
from jax.sharding import PartitionSpec as P

H = 896
BF = jnp.bfloat16
F32 = jnp.float32


def shift(value, axis, count, by):
    return lax.ppermute(value, axis, [(i, (i + by) % count) for i in range(count)])


def dot(a, b, contract_a=1, contract_b=0):
    return lax.dot_general(
        a, b, (((contract_a,), (contract_b,)), ((), ())), preferred_element_type=F32
    )


def whole():
    return pl.BlockSpec(memory_space=pltpu.VMEM)


def in_hbm():
    return pl.BlockSpec(memory_space=pltpu.HBM)


def anywhere():
    return pl.BlockSpec(memory_space=pl.ANY)


def scalars():
    return pl.BlockSpec(memory_space=pltpu.SMEM)


def load_start(pairs, sems, pieces):
    copies = []
    for which, (source, target) in enumerate(pairs):
        rows = source.shape[0] // pieces
        for i in range(pieces):
            part = pl.ds(i * rows, rows)
            copies.append(
                pltpu.make_async_copy(source.at[part], target.at[part], sems.at[which, i])
            )
    for copy in copies:
        copy.start()
    return copies


def far(value):
    return pltpu.with_memory_space_constraint(value, pltpu.HBM)


def prepare_kernel(
    near_first,
    ranks,
    capacity,
    dps,
    pipes,
    place,
    far_routes,
    far_shares,
    gate,
    up,
    picker,
    weights,
    gate_out,
    up_out,
    routes,
    shares,
    sems,
    table_sems,
):
    tables = [
        pltpu.make_async_copy(far_routes, routes, table_sems.at[0]),
        pltpu.make_async_copy(far_shares, shares, table_sems.at[1]),
    ]
    for copy in tables:
        copy.start()
    copies = load_start(((gate, gate_out), (up, up_out)), sems, 8)
    for copy in tables:
        copy.wait()
    rank, dp, pipe = place[0], place[1], place[2]
    experts, slots, token_count = picker.shape
    block = token_count // ranks
    per_piece = ranks // (dps * pipes)
    row = lax.broadcasted_iota(jnp.int32, (8, token_count), 0)
    names = row + rank * experts
    weight = jnp.zeros((8, token_count), F32)
    routed = jnp.zeros((8, token_count), F32)
    for k in range(routes.shape[0]):
        hit = (routes[k : k + 1, :] == names) & (row < experts)
        weight = weight + jnp.where(hit, shares[k : k + 1, :], 0.0)
        routed = routed + jnp.where(hit, 1.0, 0.0)
    if near_first:
        swapped = rank // 2 == 1
        weight = jnp.where(swapped, pltpu.roll(weight, token_count // 2, 1), weight)
        routed = jnp.where(swapped, pltpu.roll(routed, token_count // 2, 1), routed)
    t_from = lax.broadcasted_iota(jnp.int32, (token_count, token_count), 0)
    t_to = lax.broadcasted_iota(jnp.int32, (token_count, token_count), 1)
    earlier = jnp.where((t_from // block == t_to // block) & (t_from < t_to), 1.0, 0.0)
    within = dot(routed.astype(BF), earlier.astype(BF)).astype(jnp.int32)
    at_block = lax.broadcasted_iota(jnp.int32, (1, token_count), 1) // block
    if near_first:
        at_pipe = lax.rem(at_block + pipe, 2)
        first = (at_pipe * 2 + at_block // 2) * capacity
    else:
        at_pipe = lax.rem(at_block // (dps * per_piece) + pipes - pipe, pipes)
        at_dp = lax.rem(lax.rem(at_block // per_piece, dps) + dps - dp, dps)
        first = ((at_pipe * dps + at_dp) * per_piece + lax.rem(at_block, per_piece)) * capacity
    slot = jnp.where(routed > 0.0, within + first, -1)
    ids = lax.broadcasted_iota(jnp.int32, (slots, token_count), 0)
    for e in range(experts):
        hit = slot[e : e + 1] == ids
        picker[e] = jnp.where(hit, 1.0, 0.0).astype(BF)
        weights[e] = jnp.sum(jnp.where(hit, weight[e : e + 1], 0.0), axis=1, keepdims=True)
    for copy in copies:
        copy.wait()


def prepare(place, routes, shares, gate, up, near_first, ranks, dps, pipes, block, experts):
    assert experts <= 8
    capacity = block // 2
    token_count = block * ranks
    slots = capacity * ranks
    return pl.pallas_call(
        functools.partial(prepare_kernel, near_first, ranks, capacity, dps, pipes),
        in_specs=[scalars(), in_hbm(), in_hbm(), in_hbm(), in_hbm()],
        out_specs=(whole(), whole(), whole(), whole()),
        out_shape=(
            jax.ShapeDtypeStruct((experts, slots, token_count), BF),
            jax.ShapeDtypeStruct((experts, slots, 1), F32),
            pltpu.VMEM(gate.shape, BF),
            pltpu.VMEM(up.shape, BF),
        ),
        scratch_shapes=[
            pltpu.VMEM(routes.shape, routes.dtype),
            pltpu.VMEM(shares.shape, shares.dtype),
            pltpu.SemaphoreType.DMA((2, 8)),
            pltpu.SemaphoreType.DMA((2,)),
        ],
        compiler_params=pltpu.CompilerParams(vmem_limit_bytes=8 * 1024 * 1024),
        cost_estimate=pl.CostEstimate(
            flops=0, bytes_accessed=4 * gate.size, transcendentals=0
        ),
    )(place, far(routes), far(shares), far(gate), far(up))


def load_kernel(source, before, out, sems):
    for copy in load_start(((source, out),), sems, 8):
        copy.wait()


def load(source, before):
    return pl.pallas_call(
        load_kernel,
        in_specs=[in_hbm(), anywhere()],
        out_specs=whole(),
        out_shape=pltpu.VMEM(source.shape, source.dtype),
        scratch_shapes=[pltpu.SemaphoreType.DMA((1, 8))],
        compiler_params=pltpu.CompilerParams(vmem_limit_bytes=4 * 1024 * 1024),
    )(far(source), before)


def residual_kernel(ranks, *refs):
    student = refs[0][...].astype(F32)
    target = refs[ranks][...].astype(F32)
    for i in range(1, ranks):
        student = student + refs[i][...].astype(F32)
        target = target + refs[ranks + i][...].astype(F32)
    refs[-2][...] = student
    refs[-1][...] = (student - target).astype(BF)


def residual_of(student, target, before):
    ranks = len(student)
    shape = student[0].shape
    return pl.pallas_call(
        functools.partial(residual_kernel, ranks),
        in_specs=[whole()] * (2 * ranks) + [anywhere()] * len(before),
        out_specs=(whole(), whole()),
        out_shape=(jax.ShapeDtypeStruct(shape, F32), jax.ShapeDtypeStruct(shape, BF)),
        compiler_params=pltpu.CompilerParams(vmem_limit_bytes=4 * 1024 * 1024),
    )(*student, *target, *before)


def tile_of(size):
    return 256 if size % 256 == 0 else 128


def teacher_kernel(first, size, dps, pipes, place, tokens, gate, up, keep, send):
    dp, pipe = place[1], place[2]
    rows = tokens.shape[0] // (dps * pipes)
    half = dps * rows
    parts = []
    for j1 in range(pipes):
        for j0 in range(dps):
            piece = lax.rem(pipe + j1, pipes) * dps + lax.rem(dp + j0, dps)
            parts.append(tokens[pl.ds(pl.multiple_of(piece * rows, rows), rows), :])
    ordered = jnp.concatenate(parts, axis=0)
    tile = tile_of(size)
    for which, weight in enumerate((gate, up)):
        for i in range(size // tile):
            product = dot(ordered, weight[:, first + i * tile : first + (i + 1) * tile]).astype(BF)
            keep[which, :, i * tile : (i + 1) * tile] = product[:half]
            send[which, :, i * tile : (i + 1) * tile] = product[half:]


def teacher_pre(place, tokens, gate, up, first, size, dps, pipes):
    token_count, width = tokens.shape
    half = jax.ShapeDtypeStruct((2, token_count // pipes, size), BF)
    return pl.pallas_call(
        functools.partial(teacher_kernel, first, size, dps, pipes),
        in_specs=[scalars(), whole(), whole(), whole()],
        out_specs=(whole(), whole()),
        out_shape=(half, half),
        compiler_params=pltpu.CompilerParams(vmem_limit_bytes=8 * 1024 * 1024),
        cost_estimate=pl.CostEstimate(
            flops=4 * token_count * width * size, bytes_accessed=4 * width * size, transcendentals=0
        ),
    )(place, tokens, gate, up)


def expert_kernel(cuts, picker, tokens, gate, up, before, *rest):
    outs, held, sems = rest[:-2], rest[-2], rest[-1]
    count, slots = picker.shape[:2]
    depth, _, pieces = sems.shape
    rows_each = gate.shape[0] // pieces

    def copies(e, which):
        weight = (gate, up)[which]
        found = []
        for p in range(pieces):
            part = pl.ds(p * rows_each, rows_each)
            found.append(
                pltpu.make_async_copy(
                    weight.at[part, pl.ds(e * H, H)],
                    held.at[e % depth, which, part],
                    sems.at[e % depth, which, p],
                )
            )
        return found

    for e in range(min(depth, count)):
        for which in range(2):
            for copy in copies(e, which):
                copy.start()
    for e in range(count):
        rows = dot(picker[e], tokens[...]).astype(BF)
        for which in range(2):
            for copy in copies(e, which):
                copy.wait()
            product = dot(rows, held[e % depth, which]).astype(BF)
            for i, (low, high) in enumerate(cuts):
                outs[2 * i][e, which] = product[low:high]
                outs[2 * i + 1][e, which] = product[slots // 2 + low : slots // 2 + high]
            if e + depth < count:
                for copy in copies(e + depth, which):
                    copy.start()


def expert_pre(picker, tokens, gate, up, before, cuts):
    count, slots = picker.shape[:2]
    width = tokens.shape[1]
    outs = []
    for low, high in cuts:
        outs += [jax.ShapeDtypeStruct((count, 2, high - low, H), BF)] * 2
    return pl.pallas_call(
        functools.partial(expert_kernel, cuts),
        in_specs=[whole(), whole(), in_hbm(), in_hbm(), anywhere()],
        out_specs=tuple(whole() for _ in outs),
        out_shape=tuple(outs),
        scratch_shapes=[
            pltpu.VMEM((min(count, 2), 2, width, H), BF),
            pltpu.SemaphoreType.DMA((min(count, 2), 2, 4)),
        ],
        compiler_params=pltpu.CompilerParams(vmem_limit_bytes=12 * 1024 * 1024),
        cost_estimate=pl.CostEstimate(
            flops=count * 4 * slots * width * H,
            bytes_accessed=count * 4 * width * H,
            transcendentals=0,
        ),
    )(picker, tokens, far(gate), far(up), before)


def add_kernel(a, b, before, out):
    out[...] = (a[...].astype(F32) + b[...].astype(F32)).astype(BF)


def add_after(a, b, before):
    return pl.pallas_call(
        add_kernel,
        in_specs=[whole(), whole(), anywhere()],
        out_specs=whole(),
        out_shape=jax.ShapeDtypeStruct(a.shape, BF),
        compiler_params=pltpu.CompilerParams(vmem_limit_bytes=4 * 1024 * 1024),
    )(a, b, before)


def dp_total(mode, mine, other):
    total = mine.astype(F32)
    if mode == "add":
        total = total + other.astype(F32)
    if mode == "swap":
        theirs = other.astype(F32)
        rows = theirs.shape[0]
        total = total + jnp.concatenate([theirs[rows // 2 :], theirs[: rows // 2]], axis=0)
    return total


def hidden_act_kernel(mode, low, mine, other, weight, *rest):
    pre, out = rest[-2:]
    count, _, rows = mine.shape[:3]
    for i in range(count):
        gate = dp_total(mode, mine[i, 0], other[i, 0])
        up = dp_total(mode, mine[i, 1], other[i, 1])
        pre[i, 0] = gate
        pre[i, 1] = up
        out[i] = (gate * jax.nn.sigmoid(gate) * up * weight[i, low : low + rows]).astype(BF)


def hidden_act(mine, other, mode, weight, before, low):
    count, _, rows, width = mine.shape
    return pl.pallas_call(
        functools.partial(hidden_act_kernel, mode, low),
        in_specs=[whole(), whole(), whole()] + [anywhere()] * len(before),
        out_specs=(whole(), whole()),
        out_shape=(
            jax.ShapeDtypeStruct(mine.shape, F32),
            jax.ShapeDtypeStruct((count, rows, width), BF),
        ),
        compiler_params=pltpu.CompilerParams(vmem_limit_bytes=8 * 1024 * 1024),
    )(mine, other, weight, *before)


def pair_kernel(*refs):
    values, out = refs[:-2], refs[-1]
    rows = out.shape[0] // len(values)
    for i, value in enumerate(values):
        out[i * rows : (i + 1) * rows, :] = value[...]


def pair(values, before):
    rows, width = values[0].shape
    return pl.pallas_call(
        pair_kernel,
        in_specs=[whole()] * len(values) + [anywhere()],
        out_specs=whole(),
        out_shape=jax.ShapeDtypeStruct((rows * len(values), width), BF),
        compiler_params=pltpu.CompilerParams(vmem_limit_bytes=4 * 1024 * 1024),
    )(*values, before)


def join_kernel(dps, pipes, place, *refs):
    out = refs[-1]
    dp, pipe = place[1], place[2]
    rows = out.shape[0] // (dps * pipes)
    at = 0
    for i in range((len(refs) - 1) // 2):
        size = refs[2 * i].shape[1]
        for j1 in range(pipes):
            for j0 in range(dps):
                piece = lax.rem(pipe + j1, pipes) * dps + lax.rem(dp + j0, dps)
                target = pl.ds(pl.multiple_of(piece * rows, rows), rows)
                out[target, at : at + size] = refs[2 * i + j1][j0 * rows : (j0 + 1) * rows, :]
        at += size


def join(place, parts, dps, pipes):
    assert pipes == 2
    flat = [value for pair in parts for value in pair]
    rows = flat[0].shape[0] * pipes
    width = sum(pair[0].shape[1] for pair in parts)
    return pl.pallas_call(
        functools.partial(join_kernel, dps, pipes),
        in_specs=[scalars()] + [whole()] * len(flat),
        out_specs=whole(),
        out_shape=jax.ShapeDtypeStruct((rows, width), BF),
        compiler_params=pltpu.CompilerParams(vmem_limit_bytes=8 * 1024 * 1024),
    )(place, *flat)


def slot_rows(table, low, high):
    half = table.shape[0] // 2
    return jnp.concatenate([table[low:high], table[half + low : half + high]], axis=0)


def spread_kernel(cut, tokens, picker, mine, theirs, out):
    for e in range(picker.shape[0]):
        hidden = jnp.concatenate([mine[e], theirs[e]], axis=0)
        dense = dot(slot_rows(picker[e], *cut), hidden, 0, 0)[tokens[0] : tokens[1]]
        out[:, e * H : (e + 1) * H] = dense.astype(BF)


def spread(picker, mine, theirs, cut, tokens):
    count = picker.shape[0]
    return pl.pallas_call(
        functools.partial(spread_kernel, cut, tokens),
        in_specs=[whole()] * 3,
        out_specs=whole(),
        out_shape=jax.ShapeDtypeStruct((tokens[1] - tokens[0], count * H), BF),
        compiler_params=pltpu.CompilerParams(vmem_limit_bytes=8 * 1024 * 1024),
    )(picker, mine, theirs)


def flip_kernel(*refs):
    dense_out, tokens_out = refs[-2:]
    tokens = refs[-4]
    dense = jnp.concatenate([value[...].astype(F32) for value in refs[:-4]], axis=0)
    dense_out[...] = dense.T.astype(BF)
    tokens_out[...] = tokens[...].astype(F32).T.astype(BF)


def flip(dense, tokens, before):
    return pl.pallas_call(
        flip_kernel,
        in_specs=[whole()] * (len(dense) + 1) + [anywhere()],
        out_specs=(whole(), whole()),
        out_shape=(
            jax.ShapeDtypeStruct((dense[0].shape[1], tokens.shape[0]), BF),
            jax.ShapeDtypeStruct(tokens.shape[::-1], BF),
        ),
        compiler_params=pltpu.CompilerParams(vmem_limit_bytes=16 * 1024 * 1024),
    )(*dense, tokens, before)


def hidden_grad_kernel(first, picker, residual, down, before, keep, send):
    rows = keep.shape[1]
    for i in range(keep.shape[0]):
        e = first + i
        picked = dot(picker[e], residual[...]).astype(BF)
        product = dot(down[e * H : (e + 1) * H, :], picked, 1, 1).T.astype(BF)
        keep[i] = product[:rows]
        send[i] = product[rows:]


def hidden_grad_parts(picker, residual, down, before, first, count):
    part = jax.ShapeDtypeStruct((count, picker.shape[1] // 2, H), BF)
    return pl.pallas_call(
        functools.partial(hidden_grad_kernel, first),
        in_specs=[whole(), whole(), whole(), anywhere()],
        out_specs=(whole(), whole()),
        out_shape=(part, part),
        compiler_params=pltpu.CompilerParams(vmem_limit_bytes=8 * 1024 * 1024),
    )(picker, residual, down, before)


def hidden_grad_act_kernel(mode, first, mine, other, weight, before, *rest):
    pres, out = rest[:-1], rest[-1]
    count, rows = mine.shape[:2]
    for i in range(count):
        e = first + i
        total = dp_total(mode, mine[i], other[i]) * weight[e, :rows]
        pre_gate = jnp.concatenate([pre[e, 0] for pre in pres], axis=0)
        pre_up = jnp.concatenate([pre[e, 1] for pre in pres], axis=0)
        sig = jax.nn.sigmoid(pre_gate)
        gate_grad = total * pre_up * sig * (1.0 + pre_gate * (1.0 - sig))
        up_grad = total * pre_gate * sig
        out[i, 0] = gate_grad.astype(BF)
        out[i, 1] = up_grad.astype(BF)


def hidden_grad_act(mine, other, mode, pres, weight, before, first):
    count, rows, width = mine.shape
    return pl.pallas_call(
        functools.partial(hidden_grad_act_kernel, mode, first),
        in_specs=[whole(), whole(), whole(), anywhere()] + [whole()] * len(pres),
        out_specs=whole(),
        out_shape=jax.ShapeDtypeStruct((count, 2, rows, width), BF),
        compiler_params=pltpu.CompilerParams(vmem_limit_bytes=8 * 1024 * 1024),
    )(mine, other, weight, before, *pres)


def down_grad_kernel(hidden, residual, before, out, done, held, sems):
    tiles = sems.shape[0]
    rows = hidden.shape[0] // tiles
    copies = []
    for i in range(tiles):
        part = pl.ds(i * rows, rows)
        held[part, :] = dot(hidden[part, :], residual[...]).astype(BF)
        copies.append(pltpu.make_async_copy(held.at[part], out.at[part], sems.at[i]))
        copies[-1].start()
    done[...] = jnp.zeros_like(done)
    for copy in copies:
        copy.wait()


def down_grad(hidden, residual, before):
    rows, token_count = hidden.shape
    width = residual.shape[1]
    return pl.pallas_call(
        down_grad_kernel,
        in_specs=[whole(), whole(), anywhere()],
        out_specs=(in_hbm(), whole()),
        out_shape=(
            jax.ShapeDtypeStruct((rows, width), BF),
            jax.ShapeDtypeStruct((8, 128), F32),
        ),
        scratch_shapes=[
            pltpu.VMEM((rows, width), BF),
            pltpu.SemaphoreType.DMA((rows // (H // 2),)),
        ],
        compiler_params=pltpu.CompilerParams(vmem_limit_bytes=16 * 1024 * 1024),
        cost_estimate=pl.CostEstimate(
            flops=2 * rows * width * token_count,
            bytes_accessed=2 * rows * width,
            transcendentals=0,
        ),
    )(hidden, residual, before)


def input_grad_kernel(group, picker, tokens, *rest):
    outs, held, sems = rest[-4:-2], rest[-2], rest[-1]
    count = picker.shape[0]
    splits = sems.shape[2]
    rows = tokens.shape[0] // splits
    copies = []
    for i in range(count):
        for which in range(2):
            mine, theirs = rest[i // group * 2], rest[i // group * 2 + 1]
            grad = jnp.concatenate([mine[i % group, which], theirs[i % group, which]], axis=0)
            dense = dot(picker[i], grad, 0, 0).astype(BF)
            for r in range(splits):
                part = pl.ds(r * rows, rows)
                columns = pl.ds(i * H, H)
                held[i, which, part] = dot(tokens[part, :], dense).astype(BF)
                copies.append(
                    pltpu.make_async_copy(
                        held.at[i, which, part], outs[which].at[part, columns], sems.at[i, which, r]
                    )
                )
                copies[-1].start()
    for copy in copies:
        copy.wait()


def input_grads(picker, tokens, parts):
    count, slots, token_count = picker.shape
    width = tokens.shape[0]
    out = jax.ShapeDtypeStruct((width, count * H), BF)
    return pl.pallas_call(
        functools.partial(input_grad_kernel, count // len(parts)),
        in_specs=[whole()] * (2 + 2 * len(parts)),
        out_specs=(in_hbm(), in_hbm()),
        out_shape=(out, out),
        scratch_shapes=[
            pltpu.VMEM((count, 2, width, H), BF),
            pltpu.SemaphoreType.DMA((count, 2, 2)),
        ],
        compiler_params=pltpu.CompilerParams(vmem_limit_bytes=24 * 1024 * 1024),
        cost_estimate=pl.CostEstimate(
            flops=count * 4 * token_count * width * H,
            bytes_accessed=count * 4 * width * H,
            transcendentals=0,
        ),
    )(picker, tokens, *[value for pair in parts for value in pair])


def add(a, b):
    return (a.astype(F32) + b.astype(F32)).astype(BF)


def split_rows(value, count):
    rows = value.shape[-2] // count
    return [value[..., i * rows : (i + 1) * rows, :] for i in range(count)]


def scatter_dp(value, count):
    pieces = split_rows(value, count)
    total = pieces[0].astype(F32)
    for s in range(1, count):
        total = total + shift(pieces[s], "dp", count, s).astype(F32)
    return total


def gather_dp_parts(value, count):
    return [value] + [shift(value, "dp", count, -s) for s in range(1, count)]


def gather_dp(value, count):
    return jnp.concatenate(gather_dp_parts(value, count), axis=-2)


def exchange_dp(value, count, same_order):
    if count == 2:
        return value, shift(value, "dp", count, 1), "add" if same_order else "swap"
    total = gather_dp(scatter_dp(value, count).astype(BF), count)
    return total, total, "whole"


def body(
    tokens,
    routes,
    gate_weights,
    teacher_gate,
    teacher_up,
    teacher_down,
    expert_gate,
    expert_up,
    expert_down,
):
    ranks = lax.axis_size("expert")
    dps = lax.axis_size("dp")
    pipes = lax.axis_size("pipe")
    rank = lax.axis_index("expert")
    dp = lax.axis_index("dp")
    pipe = lax.axis_index("pipe")
    block, width = tokens.shape
    token_count = block * ranks
    experts = expert_gate.shape[1] // H
    slots = block // 2 * ranks
    place = jnp.stack([rank, dp, pipe]).astype(jnp.int32)

    near_first = (ranks, dps, pipes) == (4, 2, 2)
    offset = rank // 2 * 2 if near_first else 0
    capacity = slots // ranks
    if near_first:
        cuts = [(capacity, 2 * capacity), (0, capacity)]
        token_cuts = [(token_count // 2, token_count), (0, token_count // 2)]
    else:
        cuts = [(0, slots // 2)]
        token_cuts = [(0, token_count)]

    paired = ranks & (ranks - 1) == 0

    def to_partner(value, s):
        if paired:
            return lax.ppermute(value, "expert", [(i, i ^ s) for i in range(ranks)])
        return shift(value, "expert", ranks, s)

    def target_of(s):
        return rank ^ s if paired else (rank + s) % ranks

    def source_of(s):
        return rank ^ s if paired else (rank + ranks - s) % ranks

    def place_rows(rows, blocks):
        for s, value in blocks:
            at = (source_of(s) ^ offset) * block
            rows = lax.dynamic_update_slice(rows, value, (at, 0))
        return rows

    def gather_tokens(mine):
        rows = place_rows(jnp.zeros((token_count, mine.shape[1]), BF), [(0, mine)])
        near = range(1, 2 if near_first else ranks)
        near_rows = place_rows(rows, [(s, to_partner(mine, s)) for s in near])
        rest = range(2, ranks if near_first else 2)
        return near_rows, place_rows(near_rows, [(s, to_partner(mine, s)) for s in rest])

    def to_owners(product, first, count, low):
        received = []
        for s in range(first, first + count):
            at = (target_of(s) ^ offset) * block - low
            sent = lax.dynamic_slice_in_dim(product, at, block, axis=0)
            received.append(to_partner(sent, s) if s else sent)
        return received

    _, base = gather_tokens(tokens)
    picker, slot_weight, gate_near, up_near = prepare(
        place,
        routes.T,
        gate_weights.T,
        teacher_gate,
        teacher_up,
        near_first,
        ranks,
        dps,
        pipes,
        block,
        experts,
    )

    chunks = 2 if teacher_gate.shape[1] % 512 == 0 else 1
    size = teacher_gate.shape[1] // chunks
    halves = []
    for i in range(chunks):
        keep, send = teacher_pre(place, base, gate_near, up_near, i * size, size, dps, pipes)
        halves.append(add(keep, shift(send, "pipe", pipes, 1)))

    outs = expert_pre(picker, base, expert_gate, expert_up, halves[-1], cuts)
    parts, half = [], halves[-1]
    for i in range(len(cuts)):
        half = add_after(outs[2 * i], shift(outs[2 * i + 1], "pipe", pipes, 1), half)
        parts.append(exchange_dp(half, dps, near_first))
    hiddens = []
    for half in halves:
        total = scatter_dp(half, dps)
        hidden = (jax.nn.silu(total[0]) * total[1]).astype(BF)
        hidden = pair(gather_dp_parts(hidden, dps), parts[0][0])
        hiddens.append((hidden, shift(hidden, "pipe", pipes, 1)))
    hidden = join(place, hiddens, dps, pipes)
    product = jnp.dot(hidden, teacher_down, preferred_element_type=F32).astype(BF)
    target = to_owners(product, 0, ranks, 0)

    pre, dense, student = [], [], []
    expert_near = load(expert_down, product)
    wait = [target[1], target[-1], expert_near]
    for (mine, other, mode), cut, rows in zip(parts, cuts, token_cuts):
        total, part = hidden_act(mine, other, mode, slot_weight, wait, cut[0])
        pre.append(total)
        dense.append(spread(picker, part, shift(part, "pipe", pipes, 1), cut, rows))
        product = jnp.dot(dense[-1], expert_near, preferred_element_type=F32).astype(BF)
        count = (rows[1] - rows[0]) // block
        student = to_owners(product, rows[0] // block, count, rows[0]) + student
    dense_flipped, base_flipped = flip(dense[::-1], base, product)
    expert_near = load(expert_down, base_flipped)
    student_sum, residual = residual_of(student, target, (expert_near,))

    _, residual = gather_tokens(residual)
    group = 2 if experts % 2 == 0 else 1
    firsts = range(0, experts, group)
    sums, last = [], residual
    for first in firsts:
        keep, send = hidden_grad_parts(picker, residual, expert_near, last, first, group)
        last = keep
        sums.append(add(keep, shift(send, "pipe", pipes, 1)))
    exchanged = [exchange_dp(value, dps, near_first) for value in sums]
    grad_down, done = down_grad(dense_flipped, residual, sums[-1])
    grads = []
    for first, (own, other, mode) in zip(firsts, exchanged):
        part = hidden_grad_act(own, other, mode, pre[::-1], slot_weight, done, first)
        grads.append((part, shift(part, "pipe", pipes, 1)))
    grads = input_grads(picker, base_flipped, grads)
    return (student_sum.astype(BF), grads[0], grads[1], grad_down)


def solution(mesh):
    placed = (
        P(("groups", "expert"), ("dp", "pipe")),
        P("groups", None),
        P("groups", None),
        P(("dp", "pipe"), "expert"),
        P(("dp", "pipe"), "expert"),
        P("expert", ("dp", "pipe")),
        P(("dp", "pipe"), "expert"),
        P(("dp", "pipe"), "expert"),
        P("expert", ("dp", "pipe")),
    )
    return jax.shard_map(
        body,
        mesh=mesh,
        in_specs=placed,
        out_specs=(
            P(("groups", "expert"), ("dp", "pipe")),
            P(("groups", "dp", "pipe"), "expert"),
            P(("groups", "dp", "pipe"), "expert"),
            P(("groups", "expert"), ("dp", "pipe")),
        ),
        check_vma=False,
    )
```

```python
import functools

import jax
import jax.numpy as jnp
from jax import lax
from jax.experimental import pallas as pl
from jax.experimental.pallas import tpu as pltpu
from jax.sharding import PartitionSpec as P

H = 896
BF = jnp.bfloat16
F32 = jnp.float32


def shift(value, axis, count, by):
    return lax.ppermute(value, axis, [(i, (i + by) % count) for i in range(count)])


def dot(a, b, contract_a=1, contract_b=0):
    return lax.dot_general(
        a, b, (((contract_a,), (contract_b,)), ((), ())), preferred_element_type=F32
    )


def whole():
    return pl.BlockSpec(memory_space=pltpu.VMEM)


def in_hbm():
    return pl.BlockSpec(memory_space=pltpu.HBM)


def anywhere():
    return pl.BlockSpec(memory_space=pl.ANY)


def scalars():
    return pl.BlockSpec(memory_space=pltpu.SMEM)


def load_start(pairs, sems, pieces):
    copies = []
    for which, (source, target) in enumerate(pairs):
        rows = source.shape[0] // pieces
        for i in range(pieces):
            part = pl.ds(i * rows, rows)
            copies.append(
                pltpu.make_async_copy(source.at[part], target.at[part], sems.at[which, i])
            )
    for copy in copies:
        copy.start()
    return copies


def far(value):
    return pltpu.with_memory_space_constraint(value, pltpu.HBM)


def prepare_kernel(
    near_first,
    ranks,
    capacity,
    dps,
    pipes,
    place,
    far_routes,
    far_shares,
    gate,
    up,
    picker,
    weights,
    gate_out,
    up_out,
    routes,
    shares,
    sems,
    table_sems,
):
    tables = [
        pltpu.make_async_copy(far_routes, routes, table_sems.at[0]),
        pltpu.make_async_copy(far_shares, shares, table_sems.at[1]),
    ]
    for copy in tables:
        copy.start()
    copies = load_start(((gate, gate_out), (up, up_out)), sems, 8)
    for copy in tables:
        copy.wait()
    rank, dp, pipe = place[0], place[1], place[2]
    experts, slots, token_count = picker.shape
    block = token_count // ranks
    per_piece = ranks // (dps * pipes)
    row = lax.broadcasted_iota(jnp.int32, (8, token_count), 0)
    names = row + rank * experts
    weight = jnp.zeros((8, token_count), F32)
    routed = jnp.zeros((8, token_count), F32)
    for k in range(routes.shape[0]):
        hit = (routes[k : k + 1, :] == names) & (row < experts)
        weight = weight + jnp.where(hit, shares[k : k + 1, :], 0.0)
        routed = routed + jnp.where(hit, 1.0, 0.0)
    if near_first:
        swapped = rank // 2 == 1
        weight = jnp.where(swapped, pltpu.roll(weight, token_count // 2, 1), weight)
        routed = jnp.where(swapped, pltpu.roll(routed, token_count // 2, 1), routed)
    t_from = lax.broadcasted_iota(jnp.int32, (token_count, token_count), 0)
    t_to = lax.broadcasted_iota(jnp.int32, (token_count, token_count), 1)
    earlier = jnp.where((t_from // block == t_to // block) & (t_from < t_to), 1.0, 0.0)
    within = dot(routed.astype(BF), earlier.astype(BF)).astype(jnp.int32)
    at_block = lax.broadcasted_iota(jnp.int32, (1, token_count), 1) // block
    if near_first:
        at_pipe = lax.rem(at_block + pipe, 2)
        first = (at_pipe * 2 + at_block // 2) * capacity
    else:
        at_pipe = lax.rem(at_block // (dps * per_piece) + pipes - pipe, pipes)
        at_dp = lax.rem(lax.rem(at_block // per_piece, dps) + dps - dp, dps)
        first = ((at_pipe * dps + at_dp) * per_piece + lax.rem(at_block, per_piece)) * capacity
    slot = jnp.where(routed > 0.0, within + first, -1)
    ids = lax.broadcasted_iota(jnp.int32, (slots, token_count), 0)
    for e in range(experts):
        hit = slot[e : e + 1] == ids
        picker[e] = jnp.where(hit, 1.0, 0.0).astype(BF)
        weights[e] = jnp.sum(jnp.where(hit, weight[e : e + 1], 0.0), axis=1, keepdims=True)
    for copy in copies:
        copy.wait()


def prepare(place, routes, shares, gate, up, near_first, ranks, dps, pipes, block, experts):
    assert experts <= 8
    capacity = block // 2
    token_count = block * ranks
    slots = capacity * ranks
    return pl.pallas_call(
        functools.partial(prepare_kernel, near_first, ranks, capacity, dps, pipes),
        in_specs=[scalars(), in_hbm(), in_hbm(), in_hbm(), in_hbm()],
        out_specs=(whole(), whole(), whole(), whole()),
        out_shape=(
            jax.ShapeDtypeStruct((experts, slots, token_count), BF),
            jax.ShapeDtypeStruct((experts, slots, 1), F32),
            pltpu.VMEM(gate.shape, BF),
            pltpu.VMEM(up.shape, BF),
        ),
        scratch_shapes=[
            pltpu.VMEM(routes.shape, routes.dtype),
            pltpu.VMEM(shares.shape, shares.dtype),
            pltpu.SemaphoreType.DMA((2, 8)),
            pltpu.SemaphoreType.DMA((2,)),
        ],
        compiler_params=pltpu.CompilerParams(vmem_limit_bytes=3 * 1024 * 1024),
        cost_estimate=pl.CostEstimate(
            flops=0, bytes_accessed=4 * gate.size, transcendentals=0
        ),
    )(place, far(routes), far(shares), far(gate), far(up))


def residual_kernel(ranks, *refs):
    student = refs[0][...].astype(F32)
    target = refs[ranks][...].astype(F32)
    for i in range(1, ranks):
        student = student + refs[i][...].astype(F32)
        target = target + refs[ranks + i][...].astype(F32)
    refs[-2][...] = student
    refs[-1][...] = (student - target).astype(BF)


def residual_of(student, target, before):
    ranks = len(student)
    shape = student[0].shape
    return pl.pallas_call(
        functools.partial(residual_kernel, ranks),
        in_specs=[whole()] * (2 * ranks) + [anywhere()] * len(before),
        out_specs=(whole(), whole()),
        out_shape=(jax.ShapeDtypeStruct(shape, F32), jax.ShapeDtypeStruct(shape, BF)),
        compiler_params=pltpu.CompilerParams(vmem_limit_bytes=2 * 1024 * 1024),
    )(*student, *target, *before)


def tile_of(size):
    return 256 if size % 256 == 0 else 128


def teacher_kernel(first, size, dps, pipes, place, tokens, gate, up, keep, send):
    dp, pipe = place[1], place[2]
    rows = tokens.shape[0] // (dps * pipes)
    half = dps * rows
    parts = []
    for j1 in range(pipes):
        for j0 in range(dps):
            piece = lax.rem(pipe + j1, pipes) * dps + lax.rem(dp + j0, dps)
            parts.append(tokens[pl.ds(pl.multiple_of(piece * rows, rows), rows), :])
    ordered = jnp.concatenate(parts, axis=0)
    tile = tile_of(size)
    for which, weight in enumerate((gate, up)):
        for i in range(size // tile):
            product = dot(ordered, weight[:, first + i * tile : first + (i + 1) * tile]).astype(BF)
            keep[which, :, i * tile : (i + 1) * tile] = product[:half]
            send[which, :, i * tile : (i + 1) * tile] = product[half:]


def teacher_pre(place, tokens, gate, up, first, size, dps, pipes):
    token_count, width = tokens.shape
    half = jax.ShapeDtypeStruct((2, token_count // pipes, size), BF)
    return pl.pallas_call(
        functools.partial(teacher_kernel, first, size, dps, pipes),
        in_specs=[scalars(), whole(), whole(), whole()],
        out_specs=(whole(), whole()),
        out_shape=(half, half),
        compiler_params=pltpu.CompilerParams(vmem_limit_bytes=4 * 1024 * 1024),
        cost_estimate=pl.CostEstimate(
            flops=4 * token_count * width * size, bytes_accessed=4 * width * size, transcendentals=0
        ),
    )(place, tokens, gate, up)


def expert_kernel(cuts, picker, tokens, gate, up, before, *rest):
    outs, held, sems = rest[:-2], rest[-2], rest[-1]
    count, slots = picker.shape[:2]
    depth, _, pieces = sems.shape
    rows_each = gate.shape[0] // pieces

    def copies(e, which):
        weight = (gate, up)[which]
        found = []
        for p in range(pieces):
            part = pl.ds(p * rows_each, rows_each)
            found.append(
                pltpu.make_async_copy(
                    weight.at[part, pl.ds(e * H, H)],
                    held.at[e % depth, which, part],
                    sems.at[e % depth, which, p],
                )
            )
        return found

    for e in range(min(depth, count)):
        for which in range(2):
            for copy in copies(e, which):
                copy.start()
    for e in range(count):
        rows = dot(picker[e], tokens[...]).astype(BF)
        for which in range(2):
            for copy in copies(e, which):
                copy.wait()
            product = dot(rows, held[e % depth, which]).astype(BF)
            for i, (low, high) in enumerate(cuts):
                outs[2 * i][e, which] = product[low:high]
                outs[2 * i + 1][e, which] = product[slots // 2 + low : slots // 2 + high]
            if e + depth < count:
                for copy in copies(e + depth, which):
                    copy.start()


def expert_pre(picker, tokens, gate, up, before, cuts):
    count, slots = picker.shape[:2]
    width = tokens.shape[1]
    outs = []
    for low, high in cuts:
        outs += [jax.ShapeDtypeStruct((count, 2, high - low, H), BF)] * 2
    return pl.pallas_call(
        functools.partial(expert_kernel, cuts),
        in_specs=[whole(), whole(), in_hbm(), in_hbm(), anywhere()],
        out_specs=tuple(whole() for _ in outs),
        out_shape=tuple(outs),
        scratch_shapes=[
            pltpu.VMEM((min(count, 2), 2, width, H), BF),
            pltpu.SemaphoreType.DMA((min(count, 2), 2, 4)),
        ],
        compiler_params=pltpu.CompilerParams(vmem_limit_bytes=10 * 1024 * 1024),
        cost_estimate=pl.CostEstimate(
            flops=count * 4 * slots * width * H,
            bytes_accessed=count * 4 * width * H,
            transcendentals=0,
        ),
    )(picker, tokens, far(gate), far(up), before)


def add_kernel(a, b, before, out):
    out[...] = (a[...].astype(F32) + b[...].astype(F32)).astype(BF)


def add_after(a, b, before):
    return pl.pallas_call(
        add_kernel,
        in_specs=[whole(), whole(), anywhere()],
        out_specs=whole(),
        out_shape=jax.ShapeDtypeStruct(a.shape, BF),
        compiler_params=pltpu.CompilerParams(vmem_limit_bytes=2 * 1024 * 1024),
    )(a, b, before)


def dp_total(mode, mine, other):
    total = mine.astype(F32)
    if mode == "add":
        total = total + other.astype(F32)
    if mode == "swap":
        theirs = other.astype(F32)
        rows = theirs.shape[0]
        total = total + jnp.concatenate([theirs[rows // 2 :], theirs[: rows // 2]], axis=0)
    return total


def hidden_act_kernel(mode, low, mine, other, weight, *rest):
    pre, out = rest[-2:]
    count, _, rows = mine.shape[:3]
    for i in range(count):
        gate = dp_total(mode, mine[i, 0], other[i, 0])
        up = dp_total(mode, mine[i, 1], other[i, 1])
        pre[i, 0] = gate
        pre[i, 1] = up
        out[i] = (gate * jax.nn.sigmoid(gate) * up * weight[i, low : low + rows]).astype(BF)


def hidden_act(mine, other, mode, weight, before, low):
    count, _, rows, width = mine.shape
    return pl.pallas_call(
        functools.partial(hidden_act_kernel, mode, low),
        in_specs=[whole(), whole(), whole()] + [anywhere()] * len(before),
        out_specs=(whole(), whole()),
        out_shape=(
            jax.ShapeDtypeStruct(mine.shape, F32),
            jax.ShapeDtypeStruct((count, rows, width), BF),
        ),
        compiler_params=pltpu.CompilerParams(vmem_limit_bytes=2 * 1024 * 1024),
    )(mine, other, weight, *before)


def pair_kernel(*refs):
    values, out = refs[:-2], refs[-1]
    rows = out.shape[0] // len(values)
    for i, value in enumerate(values):
        out[i * rows : (i + 1) * rows, :] = value[...]


def pair(values, before):
    rows, width = values[0].shape
    return pl.pallas_call(
        pair_kernel,
        in_specs=[whole()] * len(values) + [anywhere()],
        out_specs=whole(),
        out_shape=jax.ShapeDtypeStruct((rows * len(values), width), BF),
        compiler_params=pltpu.CompilerParams(vmem_limit_bytes=2 * 1024 * 1024),
    )(*values, before)


def join_kernel(dps, pipes, place, *refs):
    out = refs[-1]
    dp, pipe = place[1], place[2]
    rows = out.shape[0] // (dps * pipes)
    at = 0
    for i in range((len(refs) - 1) // 2):
        size = refs[2 * i].shape[1]
        for j1 in range(pipes):
            for j0 in range(dps):
                piece = lax.rem(pipe + j1, pipes) * dps + lax.rem(dp + j0, dps)
                target = pl.ds(pl.multiple_of(piece * rows, rows), rows)
                out[target, at : at + size] = refs[2 * i + j1][j0 * rows : (j0 + 1) * rows, :]
        at += size


def join(place, parts, dps, pipes):
    assert pipes == 2
    flat = [value for pair in parts for value in pair]
    rows = flat[0].shape[0] * pipes
    width = sum(pair[0].shape[1] for pair in parts)
    return pl.pallas_call(
        functools.partial(join_kernel, dps, pipes),
        in_specs=[scalars()] + [whole()] * len(flat),
        out_specs=whole(),
        out_shape=jax.ShapeDtypeStruct((rows, width), BF),
        compiler_params=pltpu.CompilerParams(vmem_limit_bytes=2 * 1024 * 1024),
    )(place, *flat)


def slot_rows(table, low, high):
    half = table.shape[0] // 2
    return jnp.concatenate([table[low:high], table[half + low : half + high]], axis=0)


def spread_kernel(cut, tokens, picker, mine, theirs, out):
    for e in range(picker.shape[0]):
        hidden = jnp.concatenate([mine[e], theirs[e]], axis=0)
        dense = dot(slot_rows(picker[e], *cut), hidden, 0, 0)[tokens[0] : tokens[1]]
        out[:, e * H : (e + 1) * H] = dense.astype(BF)


def spread(picker, mine, theirs, cut, tokens):
    count = picker.shape[0]
    return pl.pallas_call(
        functools.partial(spread_kernel, cut, tokens),
        in_specs=[whole()] * 3,
        out_specs=whole(),
        out_shape=jax.ShapeDtypeStruct((tokens[1] - tokens[0], count * H), BF),
        compiler_params=pltpu.CompilerParams(vmem_limit_bytes=3 * 1024 * 1024),
    )(picker, mine, theirs)


def flip_kernel(*refs):
    dense_out, tokens_out = refs[-2:]
    tokens = refs[-4]
    dense = jnp.concatenate([value[...].astype(F32) for value in refs[:-4]], axis=0)
    dense_out[...] = dense.T.astype(BF)
    tokens_out[...] = tokens[...].astype(F32).T.astype(BF)


def flip(dense, tokens, before):
    return pl.pallas_call(
        flip_kernel,
        in_specs=[whole()] * (len(dense) + 1) + [anywhere()],
        out_specs=(whole(), whole()),
        out_shape=(
            jax.ShapeDtypeStruct((dense[0].shape[1], tokens.shape[0]), BF),
            jax.ShapeDtypeStruct(tokens.shape[::-1], BF),
        ),
        compiler_params=pltpu.CompilerParams(vmem_limit_bytes=6 * 1024 * 1024),
    )(*dense, tokens, before)


def hidden_grad_kernel(first, picker, residual, down, before, keep, send):
    rows = keep.shape[1]
    for i in range(keep.shape[0]):
        e = first + i
        picked = dot(picker[e], residual[...]).astype(BF)
        product = dot(down[e * H : (e + 1) * H, :], picked, 1, 1).T.astype(BF)
        keep[i] = product[:rows]
        send[i] = product[rows:]


def hidden_grad_parts(picker, residual, down, before, first, count):
    part = jax.ShapeDtypeStruct((count, picker.shape[1] // 2, H), BF)
    return pl.pallas_call(
        functools.partial(hidden_grad_kernel, first),
        in_specs=[whole(), whole(), whole(), anywhere()],
        out_specs=(whole(), whole()),
        out_shape=(part, part),
        compiler_params=pltpu.CompilerParams(vmem_limit_bytes=3 * 1024 * 1024),
    )(picker, residual, down, before)


def hidden_grad_act_kernel(mode, first, mine, other, weight, before, *rest):
    pres, out = rest[:-1], rest[-1]
    count, rows = mine.shape[:2]
    for i in range(count):
        e = first + i
        total = dp_total(mode, mine[i], other[i]) * weight[e, :rows]
        pre_gate = jnp.concatenate([pre[e, 0] for pre in pres], axis=0)
        pre_up = jnp.concatenate([pre[e, 1] for pre in pres], axis=0)
        sig = jax.nn.sigmoid(pre_gate)
        gate_grad = total * pre_up * sig * (1.0 + pre_gate * (1.0 - sig))
        up_grad = total * pre_gate * sig
        out[i, 0] = gate_grad.astype(BF)
        out[i, 1] = up_grad.astype(BF)


def hidden_grad_act(mine, other, mode, pres, weight, before, first):
    count, rows, width = mine.shape
    return pl.pallas_call(
        functools.partial(hidden_grad_act_kernel, mode, first),
        in_specs=[whole(), whole(), whole(), anywhere()] + [whole()] * len(pres),
        out_specs=whole(),
        out_shape=jax.ShapeDtypeStruct((count, 2, rows, width), BF),
        compiler_params=pltpu.CompilerParams(vmem_limit_bytes=2 * 1024 * 1024),
    )(mine, other, weight, before, *pres)


def down_grad_kernel(hidden, residual, before, out, done, held, sems):
    tiles = sems.shape[0]
    rows = hidden.shape[0] // tiles
    copies = []
    for i in range(tiles):
        part = pl.ds(i * rows, rows)
        held[part, :] = dot(hidden[part, :], residual[...]).astype(BF)
        copies.append(pltpu.make_async_copy(held.at[part], out.at[part], sems.at[i]))
        copies[-1].start()
    done[...] = jnp.zeros_like(done)
    for copy in copies:
        copy.wait()


def down_grad(hidden, residual, before):
    rows, token_count = hidden.shape
    width = residual.shape[1]
    return pl.pallas_call(
        down_grad_kernel,
        in_specs=[whole(), whole(), anywhere()],
        out_specs=(in_hbm(), whole()),
        out_shape=(
            jax.ShapeDtypeStruct((rows, width), BF),
            jax.ShapeDtypeStruct((8, 128), F32),
        ),
        scratch_shapes=[
            pltpu.VMEM((rows, width), BF),
            pltpu.SemaphoreType.DMA((rows // (H // 2),)),
        ],
        compiler_params=pltpu.CompilerParams(vmem_limit_bytes=10 * 1024 * 1024),
        cost_estimate=pl.CostEstimate(
            flops=2 * rows * width * token_count,
            bytes_accessed=2 * rows * width,
            transcendentals=0,
        ),
    )(hidden, residual, before)


def input_grad_kernel(group, picker, tokens, *rest):
    outs, held, sems = rest[-4:-2], rest[-2], rest[-1]
    count = picker.shape[0]
    splits = sems.shape[2]
    rows = tokens.shape[0] // splits
    copies = []
    for i in range(count):
        for which in range(2):
            mine, theirs = rest[i // group * 2], rest[i // group * 2 + 1]
            grad = jnp.concatenate([mine[i % group, which], theirs[i % group, which]], axis=0)
            dense = dot(picker[i], grad, 0, 0).astype(BF)
            for r in range(splits):
                part = pl.ds(r * rows, rows)
                columns = pl.ds(i * H, H)
                held[i, which, part] = dot(tokens[part, :], dense).astype(BF)
                copies.append(
                    pltpu.make_async_copy(
                        held.at[i, which, part], outs[which].at[part, columns], sems.at[i, which, r]
                    )
                )
                copies[-1].start()
    for copy in copies:
        copy.wait()


def input_grads(picker, tokens, parts):
    count, slots, token_count = picker.shape
    width = tokens.shape[0]
    out = jax.ShapeDtypeStruct((width, count * H), BF)
    return pl.pallas_call(
        functools.partial(input_grad_kernel, count // len(parts)),
        in_specs=[whole()] * (2 + 2 * len(parts)),
        out_specs=(in_hbm(), in_hbm()),
        out_shape=(out, out),
        scratch_shapes=[
            pltpu.VMEM((count, 2, width, H), BF),
            pltpu.SemaphoreType.DMA((count, 2, 2)),
        ],
        compiler_params=pltpu.CompilerParams(vmem_limit_bytes=18 * 1024 * 1024),
        cost_estimate=pl.CostEstimate(
            flops=count * 4 * token_count * width * H,
            bytes_accessed=count * 4 * width * H,
            transcendentals=0,
        ),
    )(picker, tokens, *[value for pair in parts for value in pair])


def add(a, b):
    return (a.astype(F32) + b.astype(F32)).astype(BF)


def split_rows(value, count):
    rows = value.shape[-2] // count
    return [value[..., i * rows : (i + 1) * rows, :] for i in range(count)]


def scatter_dp(value, count):
    pieces = split_rows(value, count)
    total = pieces[0].astype(F32)
    for s in range(1, count):
        total = total + shift(pieces[s], "dp", count, s).astype(F32)
    return total


def gather_dp_parts(value, count):
    return [value] + [shift(value, "dp", count, -s) for s in range(1, count)]


def gather_dp(value, count):
    return jnp.concatenate(gather_dp_parts(value, count), axis=-2)


def exchange_dp(value, count, same_order):
    if count == 2:
        return value, shift(value, "dp", count, 1), "add" if same_order else "swap"
    total = gather_dp(scatter_dp(value, count).astype(BF), count)
    return total, total, "whole"


def body(
    tokens,
    routes,
    gate_weights,
    teacher_gate,
    teacher_up,
    teacher_down,
    expert_gate,
    expert_up,
    expert_down,
):
    ranks = lax.axis_size("expert")
    dps = lax.axis_size("dp")
    pipes = lax.axis_size("pipe")
    rank = lax.axis_index("expert")
    dp = lax.axis_index("dp")
    pipe = lax.axis_index("pipe")
    block, width = tokens.shape
    token_count = block * ranks
    experts = expert_gate.shape[1] // H
    slots = block // 2 * ranks
    place = jnp.stack([rank, dp, pipe]).astype(jnp.int32)

    near_first = (ranks, dps, pipes) == (4, 2, 2)
    offset = rank // 2 * 2 if near_first else 0
    capacity = slots // ranks
    if near_first:
        cuts = [(capacity, 2 * capacity), (0, capacity)]
        token_cuts = [(token_count // 2, token_count), (0, token_count // 2)]
    else:
        cuts = [(0, slots // 2)]
        token_cuts = [(0, token_count)]

    paired = ranks & (ranks - 1) == 0

    def to_partner(value, s):
        if paired:
            return lax.ppermute(value, "expert", [(i, i ^ s) for i in range(ranks)])
        return shift(value, "expert", ranks, s)

    def target_of(s):
        return rank ^ s if paired else (rank + s) % ranks

    def source_of(s):
        return rank ^ s if paired else (rank + ranks - s) % ranks

    def place_rows(rows, blocks):
        for s, value in blocks:
            at = (source_of(s) ^ offset) * block
            rows = lax.dynamic_update_slice(rows, value, (at, 0))
        return rows

    def gather_tokens(mine):
        rows = place_rows(jnp.zeros((token_count, mine.shape[1]), BF), [(0, mine)])
        near = range(1, 2 if near_first else ranks)
        near_rows = place_rows(rows, [(s, to_partner(mine, s)) for s in near])
        rest = range(2, ranks if near_first else 2)
        return near_rows, place_rows(near_rows, [(s, to_partner(mine, s)) for s in rest])

    def to_owners(product, first, count, low):
        received = []
        for s in range(first, first + count):
            at = (target_of(s) ^ offset) * block - low
            sent = lax.dynamic_slice_in_dim(product, at, block, axis=0)
            received.append(to_partner(sent, s) if s else sent)
        return received

    _, base = gather_tokens(tokens)
    picker, slot_weight, gate_near, up_near = prepare(
        place,
        routes.T,
        gate_weights.T,
        teacher_gate,
        teacher_up,
        near_first,
        ranks,
        dps,
        pipes,
        block,
        experts,
    )

    chunks = 2 if teacher_gate.shape[1] % 512 == 0 else 1
    size = teacher_gate.shape[1] // chunks
    halves = []
    for i in range(chunks):
        keep, send = teacher_pre(place, base, gate_near, up_near, i * size, size, dps, pipes)
        halves.append(add(keep, shift(send, "pipe", pipes, 1)))

    outs = expert_pre(picker, base, expert_gate, expert_up, halves[-1], cuts)
    parts, half = [], halves[-1]
    for i in range(len(cuts)):
        half = add_after(outs[2 * i], shift(outs[2 * i + 1], "pipe", pipes, 1), half)
        parts.append(exchange_dp(half, dps, near_first))
    hiddens = []
    for half in halves:
        total = scatter_dp(half, dps)
        hidden = (jax.nn.silu(total[0]) * total[1]).astype(BF)
        hidden = pair(gather_dp_parts(hidden, dps), parts[0][0])
        hiddens.append((hidden, shift(hidden, "pipe", pipes, 1)))
    hidden = join(place, hiddens, dps, pipes)
    product = jnp.dot(hidden, teacher_down, preferred_element_type=F32).astype(BF)
    target = to_owners(product, 0, ranks, 0)

    pre, dense, student = [], [], []
    wait = [target[1], target[-1]]
    for (mine, other, mode), cut, rows in zip(parts, cuts, token_cuts):
        total, part = hidden_act(mine, other, mode, slot_weight, wait, cut[0])
        pre.append(total)
        dense.append(spread(picker, part, shift(part, "pipe", pipes, 1), cut, rows))
        wait = dense[-1:]
        product = jnp.dot(dense[-1], expert_down, preferred_element_type=F32).astype(BF)
        count = (rows[1] - rows[0]) // block
        student = to_owners(product, rows[0] // block, count, rows[0]) + student
    dense_flipped, base_flipped = flip(dense[::-1], base, product)
    student_sum, residual = residual_of(student, target, (base_flipped,))

    _, residual = gather_tokens(residual)
    group = 2 if experts % 2 == 0 else 1
    firsts = range(0, experts, group)
    sums, last = [], residual
    for first in firsts:
        keep, send = hidden_grad_parts(picker, residual, expert_down, last, first, group)
        last = keep
        sums.append(add(keep, shift(send, "pipe", pipes, 1)))
    exchanged = [exchange_dp(value, dps, near_first) for value in sums]
    grad_down, done = down_grad(dense_flipped, residual, sums[-1])
    grads = []
    for first, (own, other, mode) in zip(firsts, exchanged):
        part = hidden_grad_act(own, other, mode, pre[::-1], slot_weight, done, first)
        grads.append((part, shift(part, "pipe", pipes, 1)))
    grads = input_grads(picker, base_flipped, grads)
    return (student_sum.astype(BF), grads[0], grads[1], grad_down)


def solution(mesh):
    placed = (
        P(("groups", "expert"), ("dp", "pipe")),
        P("groups", None),
        P("groups", None),
        P(("dp", "pipe"), "expert"),
        P(("dp", "pipe"), "expert"),
        P("expert", ("dp", "pipe")),
        P(("dp", "pipe"), "expert"),
        P(("dp", "pipe"), "expert"),
        P("expert", ("dp", "pipe")),
    )
    return jax.shard_map(
        body,
        mesh=mesh,
        in_specs=placed,
        out_specs=(
            P(("groups", "expert"), ("dp", "pipe")),
            P(("groups", "dp", "pipe"), "expert"),
            P(("groups", "dp", "pipe"), "expert"),
            P(("groups", "expert"), ("dp", "pipe")),
        ),
        check_vma=False,
    )
```

```python
import functools

import jax
import jax.numpy as jnp
from jax import lax
from jax.experimental import pallas as pl
from jax.experimental.pallas import tpu as pltpu
from jax.sharding import PartitionSpec as P

H = 896
BF = jnp.bfloat16
F32 = jnp.float32


def shift(value, axis, count, by):
    return lax.ppermute(value, axis, [(i, (i + by) % count) for i in range(count)])


def dot(a, b, contract_a=1, contract_b=0):
    return lax.dot_general(
        a, b, (((contract_a,), (contract_b,)), ((), ())), preferred_element_type=F32
    )


def whole():
    return pl.BlockSpec(memory_space=pltpu.VMEM)


def in_hbm():
    return pl.BlockSpec(memory_space=pltpu.HBM)


def anywhere():
    return pl.BlockSpec(memory_space=pl.ANY)


def scalars():
    return pl.BlockSpec(memory_space=pltpu.SMEM)


def load_start(pairs, sems, pieces):
    copies = []
    for which, (source, target) in enumerate(pairs):
        rows = source.shape[0] // pieces
        for i in range(pieces):
            part = pl.ds(i * rows, rows)
            copies.append(
                pltpu.make_async_copy(source.at[part], target.at[part], sems.at[which, i])
            )
    for copy in copies:
        copy.start()
    return copies


def far(value):
    return pltpu.with_memory_space_constraint(value, pltpu.HBM)


def prepare_kernel(
    near_first,
    ranks,
    capacity,
    dps,
    pipes,
    place,
    far_routes,
    far_shares,
    gate,
    up,
    picker,
    weights,
    gate_out,
    up_out,
    routes,
    shares,
    sems,
    table_sems,
):
    tables = [
        pltpu.make_async_copy(far_routes, routes, table_sems.at[0]),
        pltpu.make_async_copy(far_shares, shares, table_sems.at[1]),
    ]
    for copy in tables:
        copy.start()
    copies = load_start(((gate, gate_out), (up, up_out)), sems, 8)
    for copy in tables:
        copy.wait()
    rank, dp, pipe = place[0], place[1], place[2]
    experts, slots, token_count = picker.shape
    block = token_count // ranks
    per_piece = ranks // (dps * pipes)
    row = lax.broadcasted_iota(jnp.int32, (8, token_count), 0)
    names = row + rank * experts
    weight = jnp.zeros((8, token_count), F32)
    routed = jnp.zeros((8, token_count), F32)
    for k in range(routes.shape[0]):
        hit = (routes[k : k + 1, :] == names) & (row < experts)
        weight = weight + jnp.where(hit, shares[k : k + 1, :], 0.0)
        routed = routed + jnp.where(hit, 1.0, 0.0)
    if near_first:
        swapped = rank // 2 == 1
        weight = jnp.where(swapped, pltpu.roll(weight, token_count // 2, 1), weight)
        routed = jnp.where(swapped, pltpu.roll(routed, token_count // 2, 1), routed)
    t_from = lax.broadcasted_iota(jnp.int32, (token_count, token_count), 0)
    t_to = lax.broadcasted_iota(jnp.int32, (token_count, token_count), 1)
    earlier = jnp.where((t_from // block == t_to // block) & (t_from < t_to), 1.0, 0.0)
    within = dot(routed.astype(BF), earlier.astype(BF)).astype(jnp.int32)
    at_block = lax.broadcasted_iota(jnp.int32, (1, token_count), 1) // block
    if near_first:
        at_pipe = lax.rem(at_block + pipe, 2)
        first = (at_pipe * 2 + at_block // 2) * capacity
    else:
        at_pipe = lax.rem(at_block // (dps * per_piece) + pipes - pipe, pipes)
        at_dp = lax.rem(lax.rem(at_block // per_piece, dps) + dps - dp, dps)
        first = ((at_pipe * dps + at_dp) * per_piece + lax.rem(at_block, per_piece)) * capacity
    slot = jnp.where(routed > 0.0, within + first, -1)
    ids = lax.broadcasted_iota(jnp.int32, (slots, token_count), 0)
    for e in range(experts):
        hit = slot[e : e + 1] == ids
        picker[e] = jnp.where(hit, 1.0, 0.0).astype(BF)
        weights[e] = jnp.sum(jnp.where(hit, weight[e : e + 1], 0.0), axis=1, keepdims=True)
    for copy in copies:
        copy.wait()


def prepare(place, routes, shares, gate, up, near_first, ranks, dps, pipes, block, experts):
    assert experts <= 8
    capacity = block // 2
    token_count = block * ranks
    slots = capacity * ranks
    return pl.pallas_call(
        functools.partial(prepare_kernel, near_first, ranks, capacity, dps, pipes),
        in_specs=[scalars(), in_hbm(), in_hbm(), in_hbm(), in_hbm()],
        out_specs=(whole(), whole(), whole(), whole()),
        out_shape=(
            jax.ShapeDtypeStruct((experts, slots, token_count), BF),
            jax.ShapeDtypeStruct((experts, slots, 1), F32),
            pltpu.VMEM(gate.shape, BF),
            pltpu.VMEM(up.shape, BF),
        ),
        scratch_shapes=[
            pltpu.VMEM(routes.shape, routes.dtype),
            pltpu.VMEM(shares.shape, shares.dtype),
            pltpu.SemaphoreType.DMA((2, 8)),
            pltpu.SemaphoreType.DMA((2,)),
        ],
        compiler_params=pltpu.CompilerParams(vmem_limit_bytes=8 * 1024 * 1024),
        cost_estimate=pl.CostEstimate(
            flops=0, bytes_accessed=4 * gate.size, transcendentals=0
        ),
    )(place, far(routes), far(shares), far(gate), far(up))


def residual_kernel(ranks, *refs):
    student = refs[0][...].astype(F32)
    target = refs[ranks][...].astype(F32)
    for i in range(1, ranks):
        student = student + refs[i][...].astype(F32)
        target = target + refs[ranks + i][...].astype(F32)
    refs[-2][...] = student
    refs[-1][...] = (student - target).astype(BF)


def residual_of(student, target, before):
    ranks = len(student)
    shape = student[0].shape
    return pl.pallas_call(
        functools.partial(residual_kernel, ranks),
        in_specs=[whole()] * (2 * ranks) + [anywhere()] * len(before),
        out_specs=(whole(), whole()),
        out_shape=(jax.ShapeDtypeStruct(shape, F32), jax.ShapeDtypeStruct(shape, BF)),
        compiler_params=pltpu.CompilerParams(vmem_limit_bytes=4 * 1024 * 1024),
    )(*student, *target, *before)


def tile_of(size):
    return 256 if size % 256 == 0 else 128


def teacher_kernel(first, size, dps, pipes, place, tokens, gate, up, keep, send):
    dp, pipe = place[1], place[2]
    rows = tokens.shape[0] // (dps * pipes)
    half = dps * rows
    parts = []
    for j1 in range(pipes):
        for j0 in range(dps):
            piece = lax.rem(pipe + j1, pipes) * dps + lax.rem(dp + j0, dps)
            parts.append(tokens[pl.ds(pl.multiple_of(piece * rows, rows), rows), :])
    ordered = jnp.concatenate(parts, axis=0)
    tile = tile_of(size)
    for which, weight in enumerate((gate, up)):
        for i in range(size // tile):
            product = dot(ordered, weight[:, first + i * tile : first + (i + 1) * tile]).astype(BF)
            keep[which, :, i * tile : (i + 1) * tile] = product[:half]
            send[which, :, i * tile : (i + 1) * tile] = product[half:]


def teacher_pre(place, tokens, gate, up, first, size, dps, pipes):
    token_count, width = tokens.shape
    half = jax.ShapeDtypeStruct((2, token_count // pipes, size), BF)
    return pl.pallas_call(
        functools.partial(teacher_kernel, first, size, dps, pipes),
        in_specs=[scalars(), whole(), whole(), whole()],
        out_specs=(whole(), whole()),
        out_shape=(half, half),
        compiler_params=pltpu.CompilerParams(vmem_limit_bytes=8 * 1024 * 1024),
        cost_estimate=pl.CostEstimate(
            flops=4 * token_count * width * size, bytes_accessed=4 * width * size, transcendentals=0
        ),
    )(place, tokens, gate, up)


def expert_kernel(cuts, picker, tokens, gate, up, before, *rest):
    outs, held, sems = rest[:-2], rest[-2], rest[-1]
    count, slots = picker.shape[:2]
    pieces = sems.shape[2]
    rows_each = gate.shape[0] // pieces
    copies = {}
    for e in range(count):
        for which, weight in enumerate((gate, up)):
            for p in range(pieces):
                part = pl.ds(p * rows_each, rows_each)
                columns = pl.ds(e * H, H)
                copies[e, which, p] = pltpu.make_async_copy(
                    weight.at[part, columns], held.at[e, which, part], sems.at[e, which, p]
                )
                copies[e, which, p].start()
    for e in range(count):
        rows = dot(picker[e], tokens[...]).astype(BF)
        for which in range(2):
            for p in range(pieces):
                copies[e, which, p].wait()
            product = dot(rows, held[e, which]).astype(BF)
            for i, (low, high) in enumerate(cuts):
                outs[2 * i][e, which] = product[low:high]
                outs[2 * i + 1][e, which] = product[slots // 2 + low : slots // 2 + high]


def expert_pre(picker, tokens, gate, up, before, cuts):
    count, slots = picker.shape[:2]
    width = tokens.shape[1]
    outs = []
    for low, high in cuts:
        outs += [jax.ShapeDtypeStruct((count, 2, high - low, H), BF)] * 2
    return pl.pallas_call(
        functools.partial(expert_kernel, cuts),
        in_specs=[whole(), whole(), in_hbm(), in_hbm(), anywhere()],
        out_specs=tuple(whole() for _ in outs),
        out_shape=tuple(outs),
        scratch_shapes=[
            pltpu.VMEM((count, 2, width, H), BF),
            pltpu.SemaphoreType.DMA((count, 2, 4)),
        ],
        compiler_params=pltpu.CompilerParams(vmem_limit_bytes=24 * 1024 * 1024),
        cost_estimate=pl.CostEstimate(
            flops=count * 4 * slots * width * H,
            bytes_accessed=count * 4 * width * H,
            transcendentals=0,
        ),
    )(picker, tokens, far(gate), far(up), before)


def add_kernel(a, b, before, out):
    out[...] = (a[...].astype(F32) + b[...].astype(F32)).astype(BF)


def add_after(a, b, before):
    return pl.pallas_call(
        add_kernel,
        in_specs=[whole(), whole(), anywhere()],
        out_specs=whole(),
        out_shape=jax.ShapeDtypeStruct(a.shape, BF),
        compiler_params=pltpu.CompilerParams(vmem_limit_bytes=4 * 1024 * 1024),
    )(a, b, before)


def dp_total(mode, mine, other):
    total = mine.astype(F32)
    if mode == "add":
        total = total + other.astype(F32)
    if mode == "swap":
        theirs = other.astype(F32)
        rows = theirs.shape[0]
        total = total + jnp.concatenate([theirs[rows // 2 :], theirs[: rows // 2]], axis=0)
    return total


def hidden_act_kernel(mode, low, mine, other, weight, *rest):
    pre, out = rest[-2:]
    count, _, rows = mine.shape[:3]
    for i in range(count):
        gate = dp_total(mode, mine[i, 0], other[i, 0])
        up = dp_total(mode, mine[i, 1], other[i, 1])
        pre[i, 0] = gate
        pre[i, 1] = up
        out[i] = (gate * jax.nn.sigmoid(gate) * up * weight[i, low : low + rows]).astype(BF)


def hidden_act(mine, other, mode, weight, before, low):
    count, _, rows, width = mine.shape
    return pl.pallas_call(
        functools.partial(hidden_act_kernel, mode, low),
        in_specs=[whole(), whole(), whole()] + [anywhere()] * len(before),
        out_specs=(whole(), whole()),
        out_shape=(
            jax.ShapeDtypeStruct(mine.shape, F32),
            jax.ShapeDtypeStruct((count, rows, width), BF),
        ),
        compiler_params=pltpu.CompilerParams(vmem_limit_bytes=8 * 1024 * 1024),
    )(mine, other, weight, *before)


def pair_kernel(*refs):
    values, out = refs[:-2], refs[-1]
    rows = out.shape[0] // len(values)
    for i, value in enumerate(values):
        out[i * rows : (i + 1) * rows, :] = value[...]


def pair(values, before):
    rows, width = values[0].shape
    return pl.pallas_call(
        pair_kernel,
        in_specs=[whole()] * len(values) + [anywhere()],
        out_specs=whole(),
        out_shape=jax.ShapeDtypeStruct((rows * len(values), width), BF),
        compiler_params=pltpu.CompilerParams(vmem_limit_bytes=4 * 1024 * 1024),
    )(*values, before)


def join_kernel(dps, pipes, place, *refs):
    out = refs[-1]
    dp, pipe = place[1], place[2]
    rows = out.shape[0] // (dps * pipes)
    at = 0
    for i in range((len(refs) - 1) // 2):
        size = refs[2 * i].shape[1]
        for j1 in range(pipes):
            for j0 in range(dps):
                piece = lax.rem(pipe + j1, pipes) * dps + lax.rem(dp + j0, dps)
                target = pl.ds(pl.multiple_of(piece * rows, rows), rows)
                out[target, at : at + size] = refs[2 * i + j1][j0 * rows : (j0 + 1) * rows, :]
        at += size


def join(place, parts, dps, pipes):
    assert pipes == 2
    flat = [value for pair in parts for value in pair]
    rows = flat[0].shape[0] * pipes
    width = sum(pair[0].shape[1] for pair in parts)
    return pl.pallas_call(
        functools.partial(join_kernel, dps, pipes),
        in_specs=[scalars()] + [whole()] * len(flat),
        out_specs=whole(),
        out_shape=jax.ShapeDtypeStruct((rows, width), BF),
        compiler_params=pltpu.CompilerParams(vmem_limit_bytes=8 * 1024 * 1024),
    )(place, *flat)


def slot_rows(table, low, high):
    half = table.shape[0] // 2
    return jnp.concatenate([table[low:high], table[half + low : half + high]], axis=0)


def spread_kernel(cut, tokens, picker, mine, theirs, out):
    for e in range(picker.shape[0]):
        hidden = jnp.concatenate([mine[e], theirs[e]], axis=0)
        dense = dot(slot_rows(picker[e], *cut), hidden, 0, 0)[tokens[0] : tokens[1]]
        out[:, e * H : (e + 1) * H] = dense.astype(BF)


def spread(picker, mine, theirs, cut, tokens):
    count = picker.shape[0]
    return pl.pallas_call(
        functools.partial(spread_kernel, cut, tokens),
        in_specs=[whole()] * 3,
        out_specs=whole(),
        out_shape=jax.ShapeDtypeStruct((tokens[1] - tokens[0], count * H), BF),
        compiler_params=pltpu.CompilerParams(vmem_limit_bytes=8 * 1024 * 1024),
    )(picker, mine, theirs)


def flip_kernel(*refs):
    dense_out, tokens_out = refs[-2:]
    tokens = refs[-4]
    dense = jnp.concatenate([value[...].astype(F32) for value in refs[:-4]], axis=0)
    dense_out[...] = dense.T.astype(BF)
    tokens_out[...] = tokens[...].astype(F32).T.astype(BF)


def flip(dense, tokens, before):
    return pl.pallas_call(
        flip_kernel,
        in_specs=[whole()] * (len(dense) + 1) + [anywhere()],
        out_specs=(whole(), whole()),
        out_shape=(
            jax.ShapeDtypeStruct((dense[0].shape[1], tokens.shape[0]), BF),
            jax.ShapeDtypeStruct(tokens.shape[::-1], BF),
        ),
        compiler_params=pltpu.CompilerParams(vmem_limit_bytes=16 * 1024 * 1024),
    )(*dense, tokens, before)


def hidden_grad_kernel(first, picker, residual, down, before, keep, send):
    rows = keep.shape[1]
    for i in range(keep.shape[0]):
        e = first + i
        picked = dot(picker[e], residual[...]).astype(BF)
        product = dot(down[e * H : (e + 1) * H, :], picked, 1, 1).T.astype(BF)
        keep[i] = product[:rows]
        send[i] = product[rows:]


def hidden_grad_parts(picker, residual, down, before, first, count):
    part = jax.ShapeDtypeStruct((count, picker.shape[1] // 2, H), BF)
    return pl.pallas_call(
        functools.partial(hidden_grad_kernel, first),
        in_specs=[whole(), whole(), whole(), anywhere()],
        out_specs=(whole(), whole()),
        out_shape=(part, part),
        compiler_params=pltpu.CompilerParams(vmem_limit_bytes=8 * 1024 * 1024),
    )(picker, residual, down, before)


def hidden_grad_act_kernel(mode, first, mine, other, weight, before, *rest):
    pres, out = rest[:-1], rest[-1]
    count, rows = mine.shape[:2]
    for i in range(count):
        e = first + i
        total = dp_total(mode, mine[i], other[i]) * weight[e, :rows]
        pre_gate = jnp.concatenate([pre[e, 0] for pre in pres], axis=0)
        pre_up = jnp.concatenate([pre[e, 1] for pre in pres], axis=0)
        sig = jax.nn.sigmoid(pre_gate)
        gate_grad = total * pre_up * sig * (1.0 + pre_gate * (1.0 - sig))
        up_grad = total * pre_gate * sig
        out[i, 0] = gate_grad.astype(BF)
        out[i, 1] = up_grad.astype(BF)


def hidden_grad_act(mine, other, mode, pres, weight, before, first):
    count, rows, width = mine.shape
    return pl.pallas_call(
        functools.partial(hidden_grad_act_kernel, mode, first),
        in_specs=[whole(), whole(), whole(), anywhere()] + [whole()] * len(pres),
        out_specs=whole(),
        out_shape=jax.ShapeDtypeStruct((count, 2, rows, width), BF),
        compiler_params=pltpu.CompilerParams(vmem_limit_bytes=8 * 1024 * 1024),
    )(mine, other, weight, before, *pres)


def down_grad_kernel(hidden, residual, before, out, done, held, sems):
    tiles = sems.shape[0]
    rows = hidden.shape[0] // tiles
    copies = []
    for i in range(tiles):
        part = pl.ds(i * rows, rows)
        held[part, :] = dot(hidden[part, :], residual[...]).astype(BF)
        copies.append(pltpu.make_async_copy(held.at[part], out.at[part], sems.at[i]))
        copies[-1].start()
    done[...] = jnp.zeros_like(done)
    for copy in copies:
        copy.wait()


def down_grad(hidden, residual, before):
    rows, token_count = hidden.shape
    width = residual.shape[1]
    return pl.pallas_call(
        down_grad_kernel,
        in_specs=[whole(), whole(), anywhere()],
        out_specs=(in_hbm(), whole()),
        out_shape=(
            jax.ShapeDtypeStruct((rows, width), BF),
            jax.ShapeDtypeStruct((8, 128), F32),
        ),
        scratch_shapes=[
            pltpu.VMEM((rows, width), BF),
            pltpu.SemaphoreType.DMA((rows // (H // 2),)),
        ],
        compiler_params=pltpu.CompilerParams(vmem_limit_bytes=16 * 1024 * 1024),
        cost_estimate=pl.CostEstimate(
            flops=2 * rows * width * token_count,
            bytes_accessed=2 * rows * width,
            transcendentals=0,
        ),
    )(hidden, residual, before)


def input_grad_kernel(group, picker, tokens, *rest):
    outs, held, sems = rest[-4:-2], rest[-2], rest[-1]
    count = picker.shape[0]
    splits = sems.shape[2]
    rows = tokens.shape[0] // splits
    copies = []
    for i in range(count):
        for which in range(2):
            mine, theirs = rest[i // group * 2], rest[i // group * 2 + 1]
            grad = jnp.concatenate([mine[i % group, which], theirs[i % group, which]], axis=0)
            dense = dot(picker[i], grad, 0, 0).astype(BF)
            for r in range(splits):
                part = pl.ds(r * rows, rows)
                columns = pl.ds(i * H, H)
                held[i, which, part] = dot(tokens[part, :], dense).astype(BF)
                copies.append(
                    pltpu.make_async_copy(
                        held.at[i, which, part], outs[which].at[part, columns], sems.at[i, which, r]
                    )
                )
                copies[-1].start()
    for copy in copies:
        copy.wait()


def input_grads(picker, tokens, parts):
    count, slots, token_count = picker.shape
    width = tokens.shape[0]
    out = jax.ShapeDtypeStruct((width, count * H), BF)
    return pl.pallas_call(
        functools.partial(input_grad_kernel, count // len(parts)),
        in_specs=[whole()] * (2 + 2 * len(parts)),
        out_specs=(in_hbm(), in_hbm()),
        out_shape=(out, out),
        scratch_shapes=[
            pltpu.VMEM((count, 2, width, H), BF),
            pltpu.SemaphoreType.DMA((count, 2, 2)),
        ],
        compiler_params=pltpu.CompilerParams(vmem_limit_bytes=24 * 1024 * 1024),
        cost_estimate=pl.CostEstimate(
            flops=count * 4 * token_count * width * H,
            bytes_accessed=count * 4 * width * H,
            transcendentals=0,
        ),
    )(picker, tokens, *[value for pair in parts for value in pair])


def add(a, b):
    return (a.astype(F32) + b.astype(F32)).astype(BF)


def split_rows(value, count):
    rows = value.shape[-2] // count
    return [value[..., i * rows : (i + 1) * rows, :] for i in range(count)]


def scatter_dp(value, count):
    pieces = split_rows(value, count)
    total = pieces[0].astype(F32)
    for s in range(1, count):
        total = total + shift(pieces[s], "dp", count, s).astype(F32)
    return total


def gather_dp_parts(value, count):
    return [value] + [shift(value, "dp", count, -s) for s in range(1, count)]


def gather_dp(value, count):
    return jnp.concatenate(gather_dp_parts(value, count), axis=-2)


def exchange_dp(value, count, same_order):
    if count == 2:
        return value, shift(value, "dp", count, 1), "add" if same_order else "swap"
    total = gather_dp(scatter_dp(value, count).astype(BF), count)
    return total, total, "whole"


def body(
    tokens,
    routes,
    gate_weights,
    teacher_gate,
    teacher_up,
    teacher_down,
    expert_gate,
    expert_up,
    expert_down,
):
    ranks = lax.axis_size("expert")
    dps = lax.axis_size("dp")
    pipes = lax.axis_size("pipe")
    rank = lax.axis_index("expert")
    dp = lax.axis_index("dp")
    pipe = lax.axis_index("pipe")
    block, width = tokens.shape
    token_count = block * ranks
    experts = expert_gate.shape[1] // H
    slots = block // 2 * ranks
    place = jnp.stack([rank, dp, pipe]).astype(jnp.int32)

    near_first = (ranks, dps, pipes) == (4, 2, 2)
    offset = rank // 2 * 2 if near_first else 0
    capacity = slots // ranks
    if near_first:
        cuts = [(capacity, 2 * capacity), (0, capacity)]
        token_cuts = [(token_count // 2, token_count), (0, token_count // 2)]
    else:
        cuts = [(0, slots // 2)]
        token_cuts = [(0, token_count)]

    paired = ranks & (ranks - 1) == 0

    def to_partner(value, s):
        if paired:
            return lax.ppermute(value, "expert", [(i, i ^ s) for i in range(ranks)])
        return shift(value, "expert", ranks, s)

    def target_of(s):
        return rank ^ s if paired else (rank + s) % ranks

    def source_of(s):
        return rank ^ s if paired else (rank + ranks - s) % ranks

    def place_rows(rows, blocks):
        for s, value in blocks:
            at = (source_of(s) ^ offset) * block
            rows = lax.dynamic_update_slice(rows, value, (at, 0))
        return rows

    def gather_tokens(mine):
        rows = place_rows(jnp.zeros((token_count, mine.shape[1]), BF), [(0, mine)])
        near = range(1, 2 if near_first else ranks)
        near_rows = place_rows(rows, [(s, to_partner(mine, s)) for s in near])
        rest = range(2, ranks if near_first else 2)
        return near_rows, place_rows(near_rows, [(s, to_partner(mine, s)) for s in rest])

    def to_owners(product, first, count, low):
        received = []
        for s in range(first, first + count):
            at = (target_of(s) ^ offset) * block - low
            sent = lax.dynamic_slice_in_dim(product, at, block, axis=0)
            received.append(to_partner(sent, s) if s else sent)
        return received

    _, base = gather_tokens(tokens)
    picker, slot_weight, gate_near, up_near = prepare(
        place,
        routes.T,
        gate_weights.T,
        teacher_gate,
        teacher_up,
        near_first,
        ranks,
        dps,
        pipes,
        block,
        experts,
    )

    chunks = 2 if teacher_gate.shape[1] % 512 == 0 else 1
    size = teacher_gate.shape[1] // chunks
    halves = []
    for i in range(chunks):
        keep, send = teacher_pre(place, base, gate_near, up_near, i * size, size, dps, pipes)
        halves.append(add(keep, shift(send, "pipe", pipes, 1)))

    outs = expert_pre(picker, base, expert_gate, expert_up, halves[-1], cuts)
    parts, half = [], halves[-1]
    for i in range(len(cuts)):
        half = add_after(outs[2 * i], shift(outs[2 * i + 1], "pipe", pipes, 1), half)
        parts.append(exchange_dp(half, dps, near_first))
    hiddens = []
    for half in halves:
        total = scatter_dp(half, dps)
        hidden = (jax.nn.silu(total[0]) * total[1]).astype(BF)
        hidden = pair(gather_dp_parts(hidden, dps), parts[0][0])
        hiddens.append((hidden, shift(hidden, "pipe", pipes, 1)))
    hidden = join(place, hiddens, dps, pipes)
    product = jnp.dot(hidden, teacher_down, preferred_element_type=F32).astype(BF)
    target = to_owners(product, 0, ranks, 0)

    pre, dense, student = [], [], []
    for (mine, other, mode), cut, rows in zip(parts, cuts, token_cuts):
        total, part = hidden_act(mine, other, mode, slot_weight, [product], cut[0])
        pre.append(total)
        dense.append(spread(picker, part, shift(part, "pipe", pipes, 1), cut, rows))
        product = jnp.dot(dense[-1], expert_down, preferred_element_type=F32).astype(BF)
        count = (rows[1] - rows[0]) // block
        student = to_owners(product, rows[0] // block, count, rows[0]) + student
    dense_flipped, base_flipped = flip(dense[::-1], base, product)
    student_sum, residual = residual_of(student, target, (base_flipped,))

    _, residual = gather_tokens(residual)
    group = 2 if experts % 2 == 0 else 1
    firsts = range(0, experts, group)
    sums, last = [], residual
    for first in firsts:
        keep, send = hidden_grad_parts(picker, residual, expert_down, last, first, group)
        last = keep
        sums.append(add(keep, shift(send, "pipe", pipes, 1)))
    exchanged = [exchange_dp(value, dps, near_first) for value in sums]
    grad_down, done = down_grad(dense_flipped, residual, sums[-1])
    grads = []
    for first, (own, other, mode) in zip(firsts, exchanged):
        part = hidden_grad_act(own, other, mode, pre[::-1], slot_weight, done, first)
        grads.append((part, shift(part, "pipe", pipes, 1)))
    grads = input_grads(picker, base_flipped, grads)
    return (student_sum.astype(BF), grads[0], grads[1], grad_down)


def solution(mesh):
    placed = (
        P(("groups", "expert"), ("dp", "pipe")),
        P("groups", None),
        P("groups", None),
        P(("dp", "pipe"), "expert"),
        P(("dp", "pipe"), "expert"),
        P("expert", ("dp", "pipe")),
        P(("dp", "pipe"), "expert"),
        P(("dp", "pipe"), "expert"),
        P("expert", ("dp", "pipe")),
    )
    return jax.shard_map(
        body,
        mesh=mesh,
        in_specs=placed,
        out_specs=(
            P(("groups", "expert"), ("dp", "pipe")),
            P(("groups", "dp", "pipe"), "expert"),
            P(("groups", "dp", "pipe"), "expert"),
            P(("groups", "expert"), ("dp", "pipe")),
        ),
        check_vma=False,
    )
```

```python
import functools

import jax
import jax.numpy as jnp
from jax import lax
from jax.experimental import pallas as pl
from jax.experimental.pallas import tpu as pltpu
from jax.sharding import PartitionSpec as P

H = 896
BF = jnp.bfloat16
F32 = jnp.float32


def shift(value, axis, count, by):
    return lax.ppermute(value, axis, [(i, (i + by) % count) for i in range(count)])


def dot(a, b, contract_a=1, contract_b=0):
    return lax.dot_general(
        a, b, (((contract_a,), (contract_b,)), ((), ())), preferred_element_type=F32
    )


def whole():
    return pl.BlockSpec(memory_space=pltpu.VMEM)


def in_hbm():
    return pl.BlockSpec(memory_space=pltpu.HBM)


def anywhere():
    return pl.BlockSpec(memory_space=pl.ANY)


def scalars():
    return pl.BlockSpec(memory_space=pltpu.SMEM)


def load_start(pairs, sems, pieces):
    copies = []
    for which, (source, target) in enumerate(pairs):
        rows = source.shape[0] // pieces
        for i in range(pieces):
            part = pl.ds(i * rows, rows)
            copies.append(
                pltpu.make_async_copy(source.at[part], target.at[part], sems.at[which, i])
            )
    for copy in copies:
        copy.start()
    return copies


def far(value):
    return pltpu.with_memory_space_constraint(value, pltpu.HBM)


def prepare_kernel(
    near_first,
    ranks,
    capacity,
    dps,
    pipes,
    place,
    far_routes,
    far_shares,
    gate,
    up,
    picker,
    weights,
    gate_out,
    up_out,
    routes,
    shares,
    sems,
    table_sems,
):
    tables = [
        pltpu.make_async_copy(far_routes, routes, table_sems.at[0]),
        pltpu.make_async_copy(far_shares, shares, table_sems.at[1]),
    ]
    for copy in tables:
        copy.start()
    copies = load_start(((gate, gate_out), (up, up_out)), sems, 8)
    for copy in tables:
        copy.wait()
    rank, dp, pipe = place[0], place[1], place[2]
    experts, slots, token_count = picker.shape
    block = token_count // ranks
    per_piece = ranks // (dps * pipes)
    row = lax.broadcasted_iota(jnp.int32, (8, token_count), 0)
    names = row + rank * experts
    weight = jnp.zeros((8, token_count), F32)
    routed = jnp.zeros((8, token_count), F32)
    for k in range(routes.shape[0]):
        hit = (routes[k : k + 1, :] == names) & (row < experts)
        weight = weight + jnp.where(hit, shares[k : k + 1, :], 0.0)
        routed = routed + jnp.where(hit, 1.0, 0.0)
    if near_first:
        swapped = rank // 2 == 1
        weight = jnp.where(swapped, pltpu.roll(weight, token_count // 2, 1), weight)
        routed = jnp.where(swapped, pltpu.roll(routed, token_count // 2, 1), routed)
    t_from = lax.broadcasted_iota(jnp.int32, (token_count, token_count), 0)
    t_to = lax.broadcasted_iota(jnp.int32, (token_count, token_count), 1)
    earlier = jnp.where((t_from // block == t_to // block) & (t_from < t_to), 1.0, 0.0)
    within = dot(routed.astype(BF), earlier.astype(BF)).astype(jnp.int32)
    at_block = lax.broadcasted_iota(jnp.int32, (1, token_count), 1) // block
    if near_first:
        at_pipe = lax.rem(at_block + pipe, 2)
        first = (at_pipe * 2 + at_block // 2) * capacity
    else:
        at_pipe = lax.rem(at_block // (dps * per_piece) + pipes - pipe, pipes)
        at_dp = lax.rem(lax.rem(at_block // per_piece, dps) + dps - dp, dps)
        first = ((at_pipe * dps + at_dp) * per_piece + lax.rem(at_block, per_piece)) * capacity
    slot = jnp.where(routed > 0.0, within + first, -1)
    ids = lax.broadcasted_iota(jnp.int32, (slots, token_count), 0)
    for e in range(experts):
        hit = slot[e : e + 1] == ids
        picker[e] = jnp.where(hit, 1.0, 0.0).astype(BF)
        weights[e] = jnp.sum(jnp.where(hit, weight[e : e + 1], 0.0), axis=1, keepdims=True)
    for copy in copies:
        copy.wait()


def prepare(place, routes, shares, gate, up, near_first, ranks, dps, pipes, block, experts):
    assert experts <= 8
    capacity = block // 2
    token_count = block * ranks
    slots = capacity * ranks
    return pl.pallas_call(
        functools.partial(prepare_kernel, near_first, ranks, capacity, dps, pipes),
        in_specs=[scalars(), in_hbm(), in_hbm(), in_hbm(), in_hbm()],
        out_specs=(whole(), whole(), whole(), whole()),
        out_shape=(
            jax.ShapeDtypeStruct((experts, slots, token_count), BF),
            jax.ShapeDtypeStruct((experts, slots, 1), F32),
            pltpu.VMEM(gate.shape, BF),
            pltpu.VMEM(up.shape, BF),
        ),
        scratch_shapes=[
            pltpu.VMEM(routes.shape, routes.dtype),
            pltpu.VMEM(shares.shape, shares.dtype),
            pltpu.SemaphoreType.DMA((2, 8)),
            pltpu.SemaphoreType.DMA((2,)),
        ],
        compiler_params=pltpu.CompilerParams(vmem_limit_bytes=8 * 1024 * 1024),
        cost_estimate=pl.CostEstimate(
            flops=0, bytes_accessed=4 * gate.size, transcendentals=0
        ),
    )(place, far(routes), far(shares), far(gate), far(up))


def residual_kernel(ranks, *refs):
    student = refs[0][...].astype(F32)
    target = refs[ranks][...].astype(F32)
    for i in range(1, ranks):
        student = student + refs[i][...].astype(F32)
        target = target + refs[ranks + i][...].astype(F32)
    refs[-2][...] = student
    refs[-1][...] = (student - target).astype(BF)


def residual_of(student, target, before):
    ranks = len(student)
    shape = student[0].shape
    return pl.pallas_call(
        functools.partial(residual_kernel, ranks),
        in_specs=[whole()] * (2 * ranks) + [anywhere()] * len(before),
        out_specs=(whole(), whole()),
        out_shape=(jax.ShapeDtypeStruct(shape, F32), jax.ShapeDtypeStruct(shape, BF)),
        compiler_params=pltpu.CompilerParams(vmem_limit_bytes=4 * 1024 * 1024),
    )(*student, *target, *before)


def tile_of(size):
    return 256 if size % 256 == 0 else 128


def teacher_kernel(first, size, dps, pipes, place, tokens, gate, up, keep, send):
    dp, pipe = place[1], place[2]
    rows = tokens.shape[0] // (dps * pipes)
    half = dps * rows
    parts = []
    for j1 in range(pipes):
        for j0 in range(dps):
            piece = lax.rem(pipe + j1, pipes) * dps + lax.rem(dp + j0, dps)
            parts.append(tokens[pl.ds(pl.multiple_of(piece * rows, rows), rows), :])
    ordered = jnp.concatenate(parts, axis=0)
    tile = tile_of(size)
    for which, weight in enumerate((gate, up)):
        for i in range(size // tile):
            product = dot(ordered, weight[:, first + i * tile : first + (i + 1) * tile]).astype(BF)
            keep[which, :, i * tile : (i + 1) * tile] = product[:half]
            send[which, :, i * tile : (i + 1) * tile] = product[half:]


def teacher_pre(place, tokens, gate, up, first, size, dps, pipes):
    token_count, width = tokens.shape
    half = jax.ShapeDtypeStruct((2, token_count // pipes, size), BF)
    return pl.pallas_call(
        functools.partial(teacher_kernel, first, size, dps, pipes),
        in_specs=[scalars(), whole(), whole(), whole()],
        out_specs=(whole(), whole()),
        out_shape=(half, half),
        compiler_params=pltpu.CompilerParams(vmem_limit_bytes=8 * 1024 * 1024),
        cost_estimate=pl.CostEstimate(
            flops=4 * token_count * width * size, bytes_accessed=4 * width * size, transcendentals=0
        ),
    )(place, tokens, gate, up)


def expert_kernel(cuts, picker, tokens, gate, up, before, *rest):
    outs, held, sems = rest[:-2], rest[-2], rest[-1]
    count, slots = picker.shape[:2]
    depth, _, pieces = sems.shape
    rows_each = gate.shape[0] // pieces

    def copies(e, which):
        weight = (gate, up)[which]
        found = []
        for p in range(pieces):
            part = pl.ds(p * rows_each, rows_each)
            found.append(
                pltpu.make_async_copy(
                    weight.at[part, pl.ds(e * H, H)],
                    held.at[e % depth, which, part],
                    sems.at[e % depth, which, p],
                )
            )
        return found

    for e in range(min(depth, count)):
        for which in range(2):
            for copy in copies(e, which):
                copy.start()
    for e in range(count):
        rows = dot(picker[e], tokens[...]).astype(BF)
        for which in range(2):
            for copy in copies(e, which):
                copy.wait()
            product = dot(rows, held[e % depth, which]).astype(BF)
            for i, (low, high) in enumerate(cuts):
                outs[2 * i][e, which] = product[low:high]
                outs[2 * i + 1][e, which] = product[slots // 2 + low : slots // 2 + high]
            if e + depth < count:
                for copy in copies(e + depth, which):
                    copy.start()


def expert_pre(picker, tokens, gate, up, before, cuts):
    count, slots = picker.shape[:2]
    width = tokens.shape[1]
    outs = []
    for low, high in cuts:
        outs += [jax.ShapeDtypeStruct((count, 2, high - low, H), BF)] * 2
    return pl.pallas_call(
        functools.partial(expert_kernel, cuts),
        in_specs=[whole(), whole(), in_hbm(), in_hbm(), anywhere()],
        out_specs=tuple(whole() for _ in outs),
        out_shape=tuple(outs),
        scratch_shapes=[
            pltpu.VMEM((min(count, 2), 2, width, H), BF),
            pltpu.SemaphoreType.DMA((min(count, 2), 2, 4)),
        ],
        compiler_params=pltpu.CompilerParams(vmem_limit_bytes=12 * 1024 * 1024),
        cost_estimate=pl.CostEstimate(
            flops=count * 4 * slots * width * H,
            bytes_accessed=count * 4 * width * H,
            transcendentals=0,
        ),
    )(picker, tokens, far(gate), far(up), before)


def add_kernel(a, b, before, out):
    out[...] = (a[...].astype(F32) + b[...].astype(F32)).astype(BF)


def add_after(a, b, before):
    return pl.pallas_call(
        add_kernel,
        in_specs=[whole(), whole(), anywhere()],
        out_specs=whole(),
        out_shape=jax.ShapeDtypeStruct(a.shape, BF),
        compiler_params=pltpu.CompilerParams(vmem_limit_bytes=4 * 1024 * 1024),
    )(a, b, before)


def dp_total(mode, mine, other):
    total = mine.astype(F32)
    if mode == "add":
        total = total + other.astype(F32)
    if mode == "swap":
        theirs = other.astype(F32)
        rows = theirs.shape[0]
        total = total + jnp.concatenate([theirs[rows // 2 :], theirs[: rows // 2]], axis=0)
    return total


def hidden_act_kernel(mode, low, mine, other, weight, *rest):
    pre, out = rest[-2:]
    count, _, rows = mine.shape[:3]
    for i in range(count):
        gate = dp_total(mode, mine[i, 0], other[i, 0])
        up = dp_total(mode, mine[i, 1], other[i, 1])
        pre[i, 0] = gate
        pre[i, 1] = up
        out[i] = (gate * jax.nn.sigmoid(gate) * up * weight[i, low : low + rows]).astype(BF)


def hidden_act(mine, other, mode, weight, before, low):
    count, _, rows, width = mine.shape
    return pl.pallas_call(
        functools.partial(hidden_act_kernel, mode, low),
        in_specs=[whole(), whole(), whole()] + [anywhere()] * len(before),
        out_specs=(whole(), whole()),
        out_shape=(
            jax.ShapeDtypeStruct(mine.shape, F32),
            jax.ShapeDtypeStruct((count, rows, width), BF),
        ),
        compiler_params=pltpu.CompilerParams(vmem_limit_bytes=8 * 1024 * 1024),
    )(mine, other, weight, *before)


def pair_kernel(*refs):
    values, out = refs[:-2], refs[-1]
    rows = out.shape[0] // len(values)
    for i, value in enumerate(values):
        out[i * rows : (i + 1) * rows, :] = value[...]


def pair(values, before):
    rows, width = values[0].shape
    return pl.pallas_call(
        pair_kernel,
        in_specs=[whole()] * len(values) + [anywhere()],
        out_specs=whole(),
        out_shape=jax.ShapeDtypeStruct((rows * len(values), width), BF),
        compiler_params=pltpu.CompilerParams(vmem_limit_bytes=4 * 1024 * 1024),
    )(*values, before)


def join_kernel(dps, pipes, place, *refs):
    out = refs[-1]
    dp, pipe = place[1], place[2]
    rows = out.shape[0] // (dps * pipes)
    at = 0
    for i in range((len(refs) - 1) // 2):
        size = refs[2 * i].shape[1]
        for j1 in range(pipes):
            for j0 in range(dps):
                piece = lax.rem(pipe + j1, pipes) * dps + lax.rem(dp + j0, dps)
                target = pl.ds(pl.multiple_of(piece * rows, rows), rows)
                out[target, at : at + size] = refs[2 * i + j1][j0 * rows : (j0 + 1) * rows, :]
        at += size


def join(place, parts, dps, pipes):
    assert pipes == 2
    flat = [value for pair in parts for value in pair]
    rows = flat[0].shape[0] * pipes
    width = sum(pair[0].shape[1] for pair in parts)
    return pl.pallas_call(
        functools.partial(join_kernel, dps, pipes),
        in_specs=[scalars()] + [whole()] * len(flat),
        out_specs=whole(),
        out_shape=jax.ShapeDtypeStruct((rows, width), BF),
        compiler_params=pltpu.CompilerParams(vmem_limit_bytes=8 * 1024 * 1024),
        cost_estimate=pl.CostEstimate(flops=0, bytes_accessed=16 * 2**20, transcendentals=0),
    )(place, *flat)


def slot_rows(table, low, high):
    half = table.shape[0] // 2
    return jnp.concatenate([table[low:high], table[half + low : half + high]], axis=0)


def spread_kernel(cut, tokens, picker, mine, theirs, out):
    for e in range(picker.shape[0]):
        hidden = jnp.concatenate([mine[e], theirs[e]], axis=0)
        dense = dot(slot_rows(picker[e], *cut), hidden, 0, 0)[tokens[0] : tokens[1]]
        out[:, e * H : (e + 1) * H] = dense.astype(BF)


def spread(picker, mine, theirs, cut, tokens):
    count = picker.shape[0]
    return pl.pallas_call(
        functools.partial(spread_kernel, cut, tokens),
        in_specs=[whole()] * 3,
        out_specs=whole(),
        out_shape=jax.ShapeDtypeStruct((tokens[1] - tokens[0], count * H), BF),
        compiler_params=pltpu.CompilerParams(vmem_limit_bytes=8 * 1024 * 1024),
    )(picker, mine, theirs)


def flip_kernel(*refs):
    dense_out, tokens_out = refs[-2:]
    tokens = refs[-4]
    dense = jnp.concatenate([value[...].astype(F32) for value in refs[:-4]], axis=0)
    dense_out[...] = dense.T.astype(BF)
    tokens_out[...] = tokens[...].astype(F32).T.astype(BF)


def flip(dense, tokens, before):
    return pl.pallas_call(
        flip_kernel,
        in_specs=[whole()] * (len(dense) + 1) + [anywhere()],
        out_specs=(whole(), whole()),
        out_shape=(
            jax.ShapeDtypeStruct((dense[0].shape[1], tokens.shape[0]), BF),
            jax.ShapeDtypeStruct(tokens.shape[::-1], BF),
        ),
        compiler_params=pltpu.CompilerParams(vmem_limit_bytes=16 * 1024 * 1024),
    )(*dense, tokens, before)


def hidden_grad_kernel(first, picker, residual, down, before, keep, send):
    rows = keep.shape[1]
    for i in range(keep.shape[0]):
        e = first + i
        picked = dot(picker[e], residual[...]).astype(BF)
        product = dot(down[e * H : (e + 1) * H, :], picked, 1, 1).T.astype(BF)
        keep[i] = product[:rows]
        send[i] = product[rows:]


def hidden_grad_parts(picker, residual, down, before, first, count):
    part = jax.ShapeDtypeStruct((count, picker.shape[1] // 2, H), BF)
    return pl.pallas_call(
        functools.partial(hidden_grad_kernel, first),
        in_specs=[whole(), whole(), whole(), anywhere()],
        out_specs=(whole(), whole()),
        out_shape=(part, part),
        compiler_params=pltpu.CompilerParams(vmem_limit_bytes=8 * 1024 * 1024),
    )(picker, residual, down, before)


def hidden_grad_act_kernel(mode, first, mine, other, weight, before, *rest):
    pres, out = rest[:-1], rest[-1]
    count, rows = mine.shape[:2]
    for i in range(count):
        e = first + i
        total = dp_total(mode, mine[i], other[i]) * weight[e, :rows]
        pre_gate = jnp.concatenate([pre[e, 0] for pre in pres], axis=0)
        pre_up = jnp.concatenate([pre[e, 1] for pre in pres], axis=0)
        sig = jax.nn.sigmoid(pre_gate)
        gate_grad = total * pre_up * sig * (1.0 + pre_gate * (1.0 - sig))
        up_grad = total * pre_gate * sig
        out[i, 0] = gate_grad.astype(BF)
        out[i, 1] = up_grad.astype(BF)


def hidden_grad_act(mine, other, mode, pres, weight, before, first):
    count, rows, width = mine.shape
    return pl.pallas_call(
        functools.partial(hidden_grad_act_kernel, mode, first),
        in_specs=[whole(), whole(), whole(), anywhere()] + [whole()] * len(pres),
        out_specs=whole(),
        out_shape=jax.ShapeDtypeStruct((count, 2, rows, width), BF),
        compiler_params=pltpu.CompilerParams(vmem_limit_bytes=8 * 1024 * 1024),
    )(mine, other, weight, before, *pres)


def down_grad_kernel(hidden, residual, before, out, done, held, sems):
    tiles = sems.shape[0]
    rows = hidden.shape[0] // tiles
    copies = []
    for i in range(tiles):
        part = pl.ds(i * rows, rows)
        held[part, :] = dot(hidden[part, :], residual[...]).astype(BF)
        copies.append(pltpu.make_async_copy(held.at[part], out.at[part], sems.at[i]))
        copies[-1].start()
    done[...] = jnp.zeros_like(done)
    for copy in copies:
        copy.wait()


def down_grad(hidden, residual, before):
    rows, token_count = hidden.shape
    width = residual.shape[1]
    return pl.pallas_call(
        down_grad_kernel,
        in_specs=[whole(), whole(), anywhere()],
        out_specs=(in_hbm(), whole()),
        out_shape=(
            jax.ShapeDtypeStruct((rows, width), BF),
            jax.ShapeDtypeStruct((8, 128), F32),
        ),
        scratch_shapes=[
            pltpu.VMEM((rows, width), BF),
            pltpu.SemaphoreType.DMA((rows // (H // 2),)),
        ],
        compiler_params=pltpu.CompilerParams(vmem_limit_bytes=16 * 1024 * 1024),
        cost_estimate=pl.CostEstimate(
            flops=2 * rows * width * token_count,
            bytes_accessed=2 * rows * width,
            transcendentals=0,
        ),
    )(hidden, residual, before)


def input_grad_kernel(group, picker, tokens, *rest):
    outs, held, sems = rest[-4:-2], rest[-2], rest[-1]
    count = picker.shape[0]
    splits = sems.shape[2]
    rows = tokens.shape[0] // splits
    copies = []
    for i in range(count):
        for which in range(2):
            mine, theirs = rest[i // group * 2], rest[i // group * 2 + 1]
            grad = jnp.concatenate([mine[i % group, which], theirs[i % group, which]], axis=0)
            dense = dot(picker[i], grad, 0, 0).astype(BF)
            for r in range(splits):
                part = pl.ds(r * rows, rows)
                columns = pl.ds(i * H, H)
                held[i, which, part] = dot(tokens[part, :], dense).astype(BF)
                copies.append(
                    pltpu.make_async_copy(
                        held.at[i, which, part], outs[which].at[part, columns], sems.at[i, which, r]
                    )
                )
                copies[-1].start()
    for copy in copies:
        copy.wait()


def input_grads(picker, tokens, parts):
    count, slots, token_count = picker.shape
    width = tokens.shape[0]
    out = jax.ShapeDtypeStruct((width, count * H), BF)
    return pl.pallas_call(
        functools.partial(input_grad_kernel, count // len(parts)),
        in_specs=[whole()] * (2 + 2 * len(parts)),
        out_specs=(in_hbm(), in_hbm()),
        out_shape=(out, out),
        scratch_shapes=[
            pltpu.VMEM((count, 2, width, H), BF),
            pltpu.SemaphoreType.DMA((count, 2, 2)),
        ],
        compiler_params=pltpu.CompilerParams(vmem_limit_bytes=24 * 1024 * 1024),
        cost_estimate=pl.CostEstimate(
            flops=count * 4 * token_count * width * H,
            bytes_accessed=count * 4 * width * H,
            transcendentals=0,
        ),
    )(picker, tokens, *[value for pair in parts for value in pair])


def add(a, b):
    return (a.astype(F32) + b.astype(F32)).astype(BF)


def split_rows(value, count):
    rows = value.shape[-2] // count
    return [value[..., i * rows : (i + 1) * rows, :] for i in range(count)]


def scatter_dp(value, count):
    pieces = split_rows(value, count)
    total = pieces[0].astype(F32)
    for s in range(1, count):
        total = total + shift(pieces[s], "dp", count, s).astype(F32)
    return total


def gather_dp_parts(value, count):
    return [value] + [shift(value, "dp", count, -s) for s in range(1, count)]


def gather_dp(value, count):
    return jnp.concatenate(gather_dp_parts(value, count), axis=-2)


def exchange_dp(value, count, same_order):
    if count == 2:
        return value, shift(value, "dp", count, 1), "add" if same_order else "swap"
    total = gather_dp(scatter_dp(value, count).astype(BF), count)
    return total, total, "whole"


def body(
    tokens,
    routes,
    gate_weights,
    teacher_gate,
    teacher_up,
    teacher_down,
    expert_gate,
    expert_up,
    expert_down,
):
    ranks = lax.axis_size("expert")
    dps = lax.axis_size("dp")
    pipes = lax.axis_size("pipe")
    rank = lax.axis_index("expert")
    dp = lax.axis_index("dp")
    pipe = lax.axis_index("pipe")
    block, width = tokens.shape
    token_count = block * ranks
    experts = expert_gate.shape[1] // H
    slots = block // 2 * ranks
    place = jnp.stack([rank, dp, pipe]).astype(jnp.int32)

    near_first = (ranks, dps, pipes) == (4, 2, 2)
    offset = rank // 2 * 2 if near_first else 0
    capacity = slots // ranks
    if near_first:
        cuts = [(capacity, 2 * capacity), (0, capacity)]
        token_cuts = [(token_count // 2, token_count), (0, token_count // 2)]
    else:
        cuts = [(0, slots // 2)]
        token_cuts = [(0, token_count)]

    paired = ranks & (ranks - 1) == 0

    def to_partner(value, s):
        if paired:
            return lax.ppermute(value, "expert", [(i, i ^ s) for i in range(ranks)])
        return shift(value, "expert", ranks, s)

    def target_of(s):
        return rank ^ s if paired else (rank + s) % ranks

    def source_of(s):
        return rank ^ s if paired else (rank + ranks - s) % ranks

    def place_rows(rows, blocks):
        for s, value in blocks:
            at = (source_of(s) ^ offset) * block
            rows = lax.dynamic_update_slice(rows, value, (at, 0))
        return rows

    def gather_tokens(mine):
        rows = place_rows(jnp.zeros((token_count, mine.shape[1]), BF), [(0, mine)])
        near = range(1, 2 if near_first else ranks)
        near_rows = place_rows(rows, [(s, to_partner(mine, s)) for s in near])
        rest = range(2, ranks if near_first else 2)
        return near_rows, place_rows(near_rows, [(s, to_partner(mine, s)) for s in rest])

    def to_owners(product, first, count, low):
        received = []
        for s in range(first, first + count):
            at = (target_of(s) ^ offset) * block - low
            sent = lax.dynamic_slice_in_dim(product, at, block, axis=0)
            received.append(to_partner(sent, s) if s else sent)
        return received

    _, base = gather_tokens(tokens)
    picker, slot_weight, gate_near, up_near = prepare(
        place,
        routes.T,
        gate_weights.T,
        teacher_gate,
        teacher_up,
        near_first,
        ranks,
        dps,
        pipes,
        block,
        experts,
    )

    chunks = 2 if teacher_gate.shape[1] % 512 == 0 else 1
    size = teacher_gate.shape[1] // chunks
    halves = []
    for i in range(chunks):
        keep, send = teacher_pre(place, base, gate_near, up_near, i * size, size, dps, pipes)
        halves.append(add(keep, shift(send, "pipe", pipes, 1)))

    outs = expert_pre(picker, base, expert_gate, expert_up, halves[-1], cuts)
    parts, half = [], halves[-1]
    for i in range(len(cuts)):
        half = add_after(outs[2 * i], shift(outs[2 * i + 1], "pipe", pipes, 1), half)
        parts.append(exchange_dp(half, dps, near_first))
    hiddens = []
    for half in halves:
        total = scatter_dp(half, dps)
        hidden = (jax.nn.silu(total[0]) * total[1]).astype(BF)
        hidden = pair(gather_dp_parts(hidden, dps), parts[0][0])
        hiddens.append((hidden, shift(hidden, "pipe", pipes, 1)))
    hidden = join(place, hiddens, dps, pipes)
    product = jnp.dot(hidden, teacher_down, preferred_element_type=F32).astype(BF)
    target = to_owners(product, 0, ranks, 0)

    pre, dense, student = [], [], []
    wait = [target[1], target[-1]]
    for (mine, other, mode), cut, rows in zip(parts, cuts, token_cuts):
        total, part = hidden_act(mine, other, mode, slot_weight, wait, cut[0])
        pre.append(total)
        dense.append(spread(picker, part, shift(part, "pipe", pipes, 1), cut, rows))
        wait = dense[-1:]
        product = jnp.dot(dense[-1], expert_down, preferred_element_type=F32).astype(BF)
        count = (rows[1] - rows[0]) // block
        student = to_owners(product, rows[0] // block, count, rows[0]) + student
    dense_flipped, base_flipped = flip(dense[::-1], base, product)
    student_sum, residual = residual_of(student, target, (base_flipped,))

    _, residual = gather_tokens(residual)
    group = 2 if experts % 2 == 0 else 1
    firsts = range(0, experts, group)
    sums, last = [], residual
    for first in firsts:
        keep, send = hidden_grad_parts(picker, residual, expert_down, last, first, group)
        last = keep
        sums.append(add(keep, shift(send, "pipe", pipes, 1)))
    exchanged = [exchange_dp(value, dps, near_first) for value in sums]
    grad_down, done = down_grad(dense_flipped, residual, sums[-1])
    grads = []
    for first, (own, other, mode) in zip(firsts, exchanged):
        part = hidden_grad_act(own, other, mode, pre[::-1], slot_weight, done, first)
        grads.append((part, shift(part, "pipe", pipes, 1)))
    grads = input_grads(picker, base_flipped, grads)
    return (student_sum.astype(BF), grads[0], grads[1], grad_down)


def solution(mesh):
    placed = (
        P(("groups", "expert"), ("dp", "pipe")),
        P("groups", None),
        P("groups", None),
        P(("dp", "pipe"), "expert"),
        P(("dp", "pipe"), "expert"),
        P("expert", ("dp", "pipe")),
        P(("dp", "pipe"), "expert"),
        P(("dp", "pipe"), "expert"),
        P("expert", ("dp", "pipe")),
    )
    return jax.shard_map(
        body,
        mesh=mesh,
        in_specs=placed,
        out_specs=(
            P(("groups", "expert"), ("dp", "pipe")),
            P(("groups", "dp", "pipe"), "expert"),
            P(("groups", "dp", "pipe"), "expert"),
            P(("groups", "expert"), ("dp", "pipe")),
        ),
        check_vma=False,
    )
```
